32 devices in a mesh: groups: 2 (over x), wide: 16 (over z, y, core).
Axes of the slice: x: 2, y: 2, z: 4, core: 2. Of those that a mesh axis runs over, the one named last changes fastest.
Arguments:
- train_act: bfloat16 [512, 4096], P(('groups', 'wide')), parts along dimension 0, may hold values from -6 to 6
- train_grad: bfloat16 [512, 32768], P(('groups', 'wide')), parts along dimension 0, may hold values from -6 to 6
- seq_ids: int32 [512], P(('groups', 'wide')), parts along dimension 0, may hold values from 0 to 7, never falling along the last dimension, each value on 1 to 64 neighbouring positions
- act_basis: bfloat16 [512, 4096], replicated, may hold values from -0.25 to 0.25
- grad_basis: bfloat16 [512, 32768], P(None, 'wide'), may hold values from -0.25 to 0.25
- eigenvalues: bfloat16 [32768, 4096], P('wide'), may hold values from 0.099609375 to 10
- query_factors: bfloat16 [32, 16, 36864], P('wide'), may hold values from -6 to 6
- owners: int32 [2], replicated, may hold values from 0 to 15, as said below
Outputs:
- scores: float32 [16, 2], P('groups'), parts along dimension 0
The draws below stay inside these ranges and needn't reach their ends.
There are 2 independent parts, one for each index of `groups`. The reference program is written for one: setup_inputs(seed, part) draws one part's arguments, and reference() takes and returns one part's arrays. A program takes and returns all parts, laid end to end along the dimension named above; an argument that names none is the same for every part. Nothing has to cross between parts.
Inputs may be any that keep to these rules, and one draw needn't show every extreme that they name: The owners of different query batches are different devices, and one batch is always owned by the last device along wide.
All inputs are finite; a program needn't handle non-finite values.
Results may differ from the reference program's by a relative error of at most 0.0065.
Values may be sent and summed in bfloat16 or wider, within the bound.
No kernel may reach another device: no remote copies, remote signals or barrier semaphores. Data moves between devices by JAX's collectives and lax.ppermute only.
A program may use at most 192 MiB of HBM per device.

```python
import math
import jax
import jax.numpy as jnp
import numpy as np
from jax import lax

D = 4096
FF = 32768
BLOCK = 512
SEQ_MEAN = 32
QT = 16
QB = 2
TOKENS = 256
SEQS = 8
QSLOTS = 32
N_WIDE = 16


def draw_owners(key, part):
    key = jax.random.fold_in(key, 5)
    first_key = jax.random.fold_in(key, 11)
    second_key = jax.random.fold_in(key, 13)
    others = jax.random.permutation(first_key, jnp.arange(N_WIDE - 1, dtype=jnp.int32))
    chosen = jnp.concatenate((jnp.full((1,), N_WIDE - 1, jnp.int32), others[:QB - 1]))
    return jax.random.permutation(second_key, chosen).astype(jnp.int32)


def block_scale(stream_key, dims, pieces, smallest, top_value):
    loudness = 1.0
    for axis_at, parts in pieces:
        draws = jax.random.uniform(jax.random.fold_in(jax.random.fold_in(stream_key, 6), axis_at), (parts,), jnp.float32, smallest / len(pieces), top_value / len(pieces))
        loudness = loudness * jnp.repeat(jnp.exp(draws), dims[axis_at] // parts).reshape((-1,) + (1,) * (len(dims) - 1 - axis_at))
    return loudness


def split_up(number_of, total, reach, lean):
    weights = [(1 << 20) // math.isqrt(rank ** lean) + 1 for rank in range(2, number_of + 1)]
    spare, counts = total - reach - (number_of - 1), [1] * (number_of - 1)
    while spare > 0:
        free = [i for i in range(number_of - 1) if counts[i] < reach]
        whole, budget = sum([weights[i] for i in free]), spare
        for i in free:
            addition = min(reach - counts[i], max(1, budget * weights[i] // whole), spare)
            counts[i] = counts[i] + addition
            spare = spare - addition
    return np.array([reach] + counts)


def uneven_parts(key, amount, total, reach, skew):
    if amount == 2:
        one = jax.random.randint(key, (), max(1, total - reach), min(reach, total - 1) + 1)
        return jnp.stack([one, total - one])
    sizes = jnp.asarray(split_up(amount, total, reach, skew), jnp.int32)
    pairs = (amount - 1) // 2
    giver, sink = sizes[1:1 + 2 * pairs:2], sizes[2:2 + 2 * pairs:2]
    slack = jnp.minimum(giver - 1, reach - sink)
    passed = jax.random.randint(jax.random.fold_in(key, 1), (pairs,), 0, 1 << 20) % (slack + 1)
    sizes = sizes.at[1:1 + 2 * pairs:2].set(giver - passed).at[2:2 + 2 * pairs:2].set(sink + passed)
    return sizes[jax.random.permutation(jax.random.fold_in(key, 2), amount)]


def gaussian(key, shape, scale, most, cuts=(), kind=jnp.bfloat16):
    array = jax.random.normal(key, shape, jnp.float32) * scale
    if len(cuts) > 0:
        array = block_scale(key, shape, cuts, -0.22, 0.18) * array
    return jnp.clip(array, min=-most, max=most).astype(kind)


def setup_inputs(seed: int = 0, part: int = 0) -> dict:
    keys = jax.random.split(jax.random.key(seed), 9)
    part_keys = jax.random.split(jax.random.fold_in(keys[8], part), 9)
    return {
        "train_act": gaussian(part_keys[0], (TOKENS, D), 1.0, 6.0, ((0, 16),)),
        "train_grad": gaussian(part_keys[1], (TOKENS, FF), 1.0, 6.0, ((0, 16),)),
        "seq_ids": jnp.searchsorted(jnp.cumsum(uneven_parts(part_keys[2], SEQS, TOKENS, 2 * SEQ_MEAN, 1)), jnp.arange(TOKENS), side="right").astype(jnp.int32),
        "act_basis": gaussian(keys[3], (BLOCK, D), BLOCK ** -0.5, 0.25),
        "grad_basis": gaussian(keys[4], (BLOCK, FF), BLOCK ** -0.5, 0.25, ((1, 16),)),
        "eigenvalues": jnp.clip(jnp.exp(math.log(10.0) - 4.609084 * jax.random.uniform(keys[5], (FF, D), jnp.float32) ** block_scale(keys[5], (FF, D), ((0, 16),), -0.2, 0.2)), 0.099609375, 10.0).astype(jnp.bfloat16),
        "query_factors": gaussian(keys[6], (QSLOTS, QT, FF + D), 1.0, 6.0, ((0, 16),)),
        "owners": draw_owners(jax.random.fold_in(keys[8], 71), part),
    }


damping = 0.1

def rotate_blocks(values, basis_cols):
    row_count = values.shape[0]
    out_width = basis_cols.shape[1]
    block_size = basis_cols.shape[0]
    block_count = max(1, out_width // block_size)
    inner_width = values.shape[1] // block_count
    outer_width = out_width // block_count
    blocks = values.reshape(row_count, block_count, inner_width).astype(jnp.float32)
    table_view = basis_cols.reshape(inner_width, block_count, outer_width).astype(jnp.float32)
    turned = jnp.einsum('tkr,rkc->tkc', blocks, table_view, precision=lax.Precision.HIGHEST)
    return turned.reshape(row_count, out_width).astype(jnp.bfloat16)

def reference(train_act, train_grad, seq_ids, act_basis, grad_basis, eigenvalues, query_factors, owners):
    rot_act = rotate_blocks(train_act, act_basis)
    rot_grad = rotate_blocks(train_grad, grad_basis)
    onehot = (seq_ids[:, None] == jnp.arange(SEQS, dtype=jnp.int32)[None, :]).astype(jnp.bfloat16).astype(jnp.float32)
    inverse = 1.0 / (eigenvalues.astype(jnp.float32) + damping)
    score_scale = 1.0 / math.sqrt(FF * D * QT * SEQ_MEAN)
    columns = []
    for batch_index in range(QB):
        slot_index = owners[batch_index] * QB + batch_index
        factors = lax.dynamic_index_in_dim(query_factors, slot_index, 0, keepdims=False)
        grad_side = factors[:, :FF]
        act_side = factors[:, FF:]
        outer_sum = jnp.dot(grad_side.T, act_side, preferred_element_type=jnp.float32)
        precond = (outer_sum * inverse).astype(jnp.bfloat16)
        image_rows = jnp.dot(rot_act.astype(jnp.float32), precond.astype(jnp.float32).T, precision=lax.Precision.HIGHEST)
        token_score = lax.optimization_barrier(jnp.sum(image_rows * rot_grad.astype(jnp.float32), axis=1))
        columns.append(jnp.dot(onehot.T, token_score, precision=lax.Precision.HIGHEST))
    return jnp.stack(columns, axis=1) * score_scale
```

```python
import functools
import math

import jax
import jax.numpy as jnp
from jax import lax
from jax.experimental import pallas as pl
from jax.experimental.pallas import tpu as pltpu
from jax.sharding import PartitionSpec as P

D = 4096
FF = 32768
SEQ_MEAN = 32
QT = 16


damping = 0.1


def image_kernel(batch_count, act_ref, basis_ref, left_ref, right_ref, eig_ref, out_ref, rot_ref, pre_ref):
    rows = eig_ref.shape[0]
    depth = basis_ref.shape[0]
    width = act_ref.shape[1]
    blocks = width // depth

    @pl.when(pl.program_id(0) == 0)
    def _():
        for k in range(blocks):
            cols = slice(k * depth, (k + 1) * depth)
            turned = jnp.dot(act_ref[:, cols], basis_ref[:, cols], preferred_element_type=jnp.float32)
            rot_ref[cols, :] = turned.astype(jnp.bfloat16).T

    def produce(k, carry):
        cols = pl.ds(pl.multiple_of(k * depth, depth), depth)
        inverse = 1.0 / (eig_ref[:, cols].astype(jnp.float32) + damping)
        for b in range(batch_count):
            u = slice(b * QT, (b + 1) * QT)
            outer_sum = lax.dot_general(
                left_ref[u, :], right_ref[u, cols], (((0,), (0,)), ((), ())),
                preferred_element_type=jnp.float32,
            )
            pre_ref[b * rows:(b + 1) * rows, cols] = (outer_sum * inverse).astype(jnp.bfloat16)
        return carry

    lax.fori_loop(0, blocks, produce, 0)
    for b in range(batch_count):
        out_ref[b] = jnp.dot(
            pre_ref[b * rows:(b + 1) * rows, :], rot_ref[...], preferred_element_type=jnp.float32
        )


def images(act_all, act_basis, left, right, eigenvalues, batch_count):
    tokens, width = act_all.shape
    hidden = eigenvalues.shape[0]
    rows = min(256, hidden)
    whole = lambda s: pl.BlockSpec(s, lambda i: (0, 0), pipeline_mode=pl.Buffered(1))
    return pl.pallas_call(
        functools.partial(image_kernel, batch_count),
        grid=(hidden // rows,),
        in_specs=[
            whole(act_all.shape),
            whole(act_basis.shape),
            pl.BlockSpec((left.shape[0], rows), lambda i: (0, i)),
            whole(right.shape),
            pl.BlockSpec((rows, width), lambda i: (i, 0)),
        ],
        out_specs=pl.BlockSpec((batch_count, rows, tokens), lambda i: (0, i, 0)),
        out_shape=jax.ShapeDtypeStruct((batch_count, hidden, tokens), jnp.float32),
        scratch_shapes=[
            pltpu.VMEM((width, tokens), jnp.bfloat16),
            pltpu.VMEM((batch_count * rows, width), jnp.bfloat16),
        ],
        compiler_params=pltpu.CompilerParams(vmem_limit_bytes=56 * 1024 * 1024),
        cost_estimate=pl.CostEstimate(
            flops=2 * hidden * width * (tokens + 256) * batch_count,
            bytes_accessed=2 * hidden * width,
            transcendentals=0,
        ),
    )(act_all, act_basis, left, right, eigenvalues)


def score_kernel(batch_count, seq_count, grad_ref, basis_ref, image_ref, ids_ref, out_ref):
    depth = basis_ref.shape[0]
    hidden = basis_ref.shape[1]
    tokens = grad_ref.shape[0]
    inner = min(depth, hidden)
    token = [jnp.zeros((1, tokens), jnp.float32) for _ in range(batch_count)]
    for k in range(hidden // inner):
        cols = slice(k * inner, (k + 1) * inner)
        turned = jnp.dot(
            grad_ref[:, cols], basis_ref[:, cols], preferred_element_type=jnp.float32
        ).astype(jnp.bfloat16).T.astype(jnp.float32)
        for b in range(batch_count):
            token[b] += jnp.sum(image_ref[b, cols, :] * turned, axis=0, keepdims=True)
    seqs = lax.broadcasted_iota(jnp.int32, (seq_count, tokens), 0)
    member = ids_ref[...] == seqs
    for b in range(batch_count):
        out_ref[b] = jnp.sum(jnp.where(member, token[b], 0.0), axis=1, keepdims=True)


def score_parts(grads, grad_basis, image, ids, batch_count, seq_count):
    return pl.pallas_call(
        functools.partial(score_kernel, batch_count, seq_count),
        out_shape=jax.ShapeDtypeStruct((batch_count, seq_count, 1), jnp.float32),
        compiler_params=pltpu.CompilerParams(vmem_limit_bytes=56 * 1024 * 1024),
        cost_estimate=pl.CostEstimate(
            flops=2 * grads.shape[0] * grads.shape[1] * grad_basis.shape[0],
            bytes_accessed=4 * image.size,
            transcendentals=0,
        ),
    )(grads, grad_basis, image, ids)


def swap(x, axis, bit):
    count = lax.axis_size(axis)
    return lax.ppermute(x, axis, [(i, i ^ bit) for i in range(count)])


def per_device(
    train_act, train_grad, seq_ids, act_basis, grad_basis, eigenvalues, query_factors, owners
):
    wide_count = lax.axis_size("wide")
    me = lax.axis_index("wide")
    group = lax.axis_index("groups")
    tok_local = train_act.shape[0]
    seq_count = tok_local * wide_count // SEQ_MEAN
    cols = grad_basis.shape[1]
    hidden = train_grad.shape[1]
    batch_count = owners.shape[0]
    score_scale = 1.0 / math.sqrt(FF * D * QT * SEQ_MEAN)

    raw_cols = lax.all_to_all(train_grad, "wide", split_axis=1, concat_axis=0, tiled=True)

    ids_cols = jnp.broadcast_to(seq_ids[:, None].astype(jnp.bfloat16), (tok_local, 128))
    act_ids = lax.all_gather(jnp.concatenate([train_act, ids_cols], axis=1), "wide", axis=0, tiled=True)
    act_all = act_ids[:, :train_act.shape[1]]
    ids = act_ids[:, train_act.shape[1]].astype(jnp.int32)[None, :]

    batch = group % batch_count
    owner = owners[batch]
    mine = query_factors[batch]
    act_piece = (mine.shape[1] - hidden) // wide_count
    held = jnp.concatenate(
        [
            mine[:, :hidden].reshape(QT, wide_count, cols),
            mine[:, hidden:].reshape(QT, wide_count, act_piece),
        ],
        axis=2,
    ).transpose(1, 0, 2)
    bit = 1
    while bit < wide_count:
        pairs = held.reshape(held.shape[0] // 2, 2, QT, cols + act_piece)
        my_bit = (me // bit) % 2
        keep = jnp.where(my_bit == 1, pairs[:, 1], pairs[:, 0])
        give = jnp.where(my_bit == 1, pairs[:, 0], pairs[:, 1])
        got = swap(give, "wide", bit)
        held = jnp.where((owner // bit) % 2 == my_bit, keep, got)
        bit *= 2
    first = held[0]
    other = swap(first, "groups", 1)
    both = jnp.where(batch == 0, jnp.stack([first, other]), jnp.stack([other, first]))
    left = both[:, :, :cols].reshape(batch_count * QT, cols)
    right = lax.all_gather(
        both[:, :, cols:].reshape(batch_count * QT, act_piece), "wide", axis=1, tiled=True
    )

    image = images(act_all, act_basis, left, right, eigenvalues, batch_count)
    parts = score_parts(raw_cols, grad_basis, image, ids, batch_count, seq_count)
    totals = parts[:, :, 0].T
    bit = 1
    while bit < wide_count:
        totals = totals + swap(totals, "wide", bit)
        bit *= 2
    return totals * score_scale


def solution(mesh):
    return jax.shard_map(
        per_device,
        mesh=mesh,
        in_specs=(
            P(("groups", "wide"), None),
            P(("groups", "wide"), None),
            P(("groups", "wide")),
            P(),
            P(None, "wide"),
            P("wide", None),
            P("wide", None, None),
            P(),
        ),
        out_specs=P("groups", None),
        check_vma=False,
    )
```

```python
import functools
import math

import jax
import jax.numpy as jnp
from jax import lax
from jax.experimental import pallas as pl
from jax.experimental.pallas import tpu as pltpu
from jax.sharding import PartitionSpec as P

D = 4096
FF = 32768
SEQ_MEAN = 32
QT = 16
LANES = 128


damping = 0.1


def params(mib):
    return pltpu.CompilerParams(vmem_limit_bytes=mib * 1024 * 1024)


def whole_block(shape):
    return pl.BlockSpec(shape, lambda *_: (0,) * len(shape), pipeline_mode=pl.Buffered(1))


def swap(x, axis, bit):
    count = lax.axis_size(axis)
    return lax.ppermute(x, axis, [(i, i ^ bit) for i in range(count)])


def cut_grads_kernel(me_ref, grad_ref, *out_refs):
    cols = out_refs[0].shape[1]
    for r, out_ref in enumerate(out_refs):
        at = pl.multiple_of((me_ref[0] ^ r) * cols, cols)
        out_ref[...] = grad_ref[:, pl.ds(at, cols)]


def cut_grads(me, grads, count):
    rows, hidden = grads.shape
    piece = jax.ShapeDtypeStruct((rows, hidden // count), grads.dtype)
    return pl.pallas_call(
        cut_grads_kernel,
        in_specs=[pl.BlockSpec(memory_space=pltpu.SMEM), pl.BlockSpec(memory_space=pltpu.VMEM)],
        out_specs=[pl.BlockSpec(memory_space=pltpu.VMEM)] * count,
        out_shape=[piece] * count,
        compiler_params=params(16),
        cost_estimate=pl.CostEstimate(flops=0, bytes_accessed=4 * grads.size, transcendentals=0),
    )(me, grads)


def cut_factors_kernel(order, hidden, me_ref, fac_ref, keep_ref, give_ref):
    cols = hidden // len(order)
    half = (fac_ref.shape[2] - hidden) // 2
    batch = me_ref[1]
    mine = me_ref[0]
    for part, out_ref in enumerate((keep_ref, give_ref)):
        picked = order[part * len(order) // 2:(part + 1) * len(order) // 2]
        for place, r in enumerate(picked):
            at = pl.multiple_of((mine ^ r) * cols, cols)
            out_ref[:, place * cols:(place + 1) * cols] = fac_ref[batch, :, pl.ds(at, cols)]
        at = pl.multiple_of(hidden + ((mine & 1) ^ part) * half, LANES)
        out_ref[:, len(picked) * cols:] = fac_ref[batch, :, pl.ds(at, half)]


def cut_factors(me_batch, factors, order, hidden):
    rows, width = factors.shape[1:]
    half = jax.ShapeDtypeStruct((rows, width // 2), factors.dtype)
    return pl.pallas_call(
        functools.partial(cut_factors_kernel, order, hidden),
        in_specs=[pl.BlockSpec(memory_space=pltpu.SMEM), pl.BlockSpec(memory_space=pltpu.VMEM)],
        out_specs=[pl.BlockSpec(memory_space=pltpu.VMEM)] * 2,
        out_shape=[half] * 2,
        compiler_params=params(16),
        cost_estimate=pl.CostEstimate(flops=0, bytes_accessed=4 * factors.size, transcendentals=0),
    )(me_batch, factors)


def image_kernel(count, batch_count, me_ref, *refs):
    act_refs = refs[:count]
    basis_ref = refs[count]
    left_refs = refs[count + 1:count + 1 + batch_count]
    half_refs = refs[count + 1 + batch_count:count + 1 + 3 * batch_count]
    eig_ref, out_ref, ids_ref = refs[count + 1 + 3 * batch_count:count + 4 + 3 * batch_count]
    rot_ref, right_ref, turn_ref, pre_a, pre_b = refs[count + 4 + 3 * batch_count:]
    rows = eig_ref.shape[0]
    depth, width = basis_ref.shape
    half = pre_a.shape[0] // batch_count
    chunk = pre_a.shape[1]
    per = width // chunk
    phases = (rows // half) * per
    tile = min(256, chunk)

    @pl.when(pl.program_id(0) == 0)
    def _():
        for k in range(width // depth):
            cols = slice(k * depth, (k + 1) * depth)
            act = jnp.concatenate([ref[:, cols] for ref in act_refs], axis=0)
            turned = jnp.dot(act, basis_ref[:, cols], preferred_element_type=jnp.float32)
            rot_ref[cols, :] = turned.astype(jnp.bfloat16).T
        ids = jnp.concatenate([ref[:, width:] for ref in act_refs], axis=0)
        ids_ref[...] = ids.astype(jnp.float32).T[:ids_ref.shape[0], :]
        side = width // 2
        for b in range(batch_count):
            for other in range(2):
                at = pl.multiple_of(((me_ref[0] & 1) ^ other) * side, side)
                right_ref[b, :, pl.ds(at, side)] = half_refs[2 * b + other][...]

    for b in range(batch_count):
        turn_ref[b] = left_refs[b][...].T
    out_ref[...] = jnp.zeros_like(out_ref)

    def place(k):
        return pl.multiple_of((k // per) * half, half), (k % per) * chunk

    def produce(k, s, pre):
        row, col = place(k)
        cols = pl.ds(pl.multiple_of(col + s * tile, tile), tile)
        damped = eig_ref[pl.ds(row, half), cols].astype(jnp.float32) + damping
        guess = pl.reciprocal(damped, approx=True)
        inverse = guess * (2.0 - damped * guess)
        for b in range(batch_count):
            outer_sum = jnp.dot(
                turn_ref[b, pl.ds(row, half), :], right_ref[b, :, cols],
                preferred_element_type=jnp.float32,
            )
            pre[b * half:(b + 1) * half, s * tile:(s + 1) * tile] = (
                outer_sum * inverse
            ).astype(jnp.bfloat16)

    def absorb(k, b, pre):
        row, col = place(k)
        rot = rot_ref[pl.ds(pl.multiple_of(col, chunk), chunk), :]
        out_ref[b, pl.ds(row, half), :] += jnp.dot(
            pre[b * half:(b + 1) * half, :], rot, preferred_element_type=jnp.float32
        )

    def both(k, pre_now, pre_next):
        subs = chunk // tile
        for b in range(batch_count):
            for s in range(b * subs // batch_count, (b + 1) * subs // batch_count):
                produce(k + 1, s, pre_next)
            absorb(k, b, pre_now)

    for s in range(chunk // tile):
        produce(0, s, pre_a)

    def pair(q, carry):
        both(2 * q, pre_a, pre_b)
        both(2 * q + 1, pre_b, pre_a)
        return carry

    lax.fori_loop(0, phases // 2 - 1, pair, 0)
    both(phases - 2, pre_a, pre_b)
    for b in range(batch_count):
        absorb(phases - 1, b, pre_b)


def images(me, act_pieces, act_basis, lefts, halves, eigenvalues):
    count, batch_count = len(act_pieces), len(lefts)
    tokens = count * act_pieces[0].shape[0]
    hidden, width = eigenvalues.shape
    rows = min(512, hidden)
    half = min(256, rows)
    chunk = min(1024, width // 2)
    return pl.pallas_call(
        functools.partial(image_kernel, count, batch_count),
        grid=(hidden // rows,),
        in_specs=[pl.BlockSpec(memory_space=pltpu.SMEM)]
        + [whole_block(x.shape) for x in act_pieces]
        + [whole_block(act_basis.shape)]
        + [pl.BlockSpec((QT, rows), lambda i: (0, i)) for x in lefts]
        + [whole_block(x.shape) for x in halves]
        + [pl.BlockSpec((rows, width), lambda i: (i, 0))],
        out_specs=[
            pl.BlockSpec((batch_count, rows, tokens), lambda i: (0, i, 0)),
            pl.BlockSpec((8, tokens), lambda i: (0, 0)),
        ],
        out_shape=[
            jax.ShapeDtypeStruct((batch_count, hidden, tokens), jnp.float32),
            jax.ShapeDtypeStruct((8, tokens), jnp.float32),
        ],
        scratch_shapes=[
            pltpu.VMEM((width, tokens), jnp.bfloat16),
            pltpu.VMEM((batch_count, QT, width), jnp.bfloat16),
            pltpu.VMEM((batch_count, rows, QT), jnp.bfloat16),
            pltpu.VMEM((batch_count * half, chunk), jnp.bfloat16),
            pltpu.VMEM((batch_count * half, chunk), jnp.bfloat16),
        ],
        compiler_params=params(32 if tokens <= 256 else 56),
        cost_estimate=pl.CostEstimate(
            flops=2 * hidden * width * (tokens + 256) * batch_count,
            bytes_accessed=2 * hidden * width,
            transcendentals=0,
        ),
    )(me, *act_pieces, act_basis, *lefts, *halves, eigenvalues)


def score_kernel(count, batch_count, seq_count, *refs):
    grad_refs = refs[:count]
    basis_ref, image_ref, ids_ref, out_ref, token_ref = refs[count:]
    step = pl.program_id(0)

    @pl.when(step == 0)
    def _():
        token_ref[...] = jnp.zeros_like(token_ref)

    grads = jnp.concatenate([ref[...] for ref in grad_refs], axis=0)
    turned = jnp.dot(grads, basis_ref[...], preferred_element_type=jnp.float32)
    turned = turned.astype(jnp.bfloat16).T.astype(jnp.float32)
    for b in range(batch_count):
        token_ref[b:b + 1, :] += jnp.sum(image_ref[b] * turned, axis=0, keepdims=True)

    @pl.when(step == pl.num_programs(0) - 1)
    def _():
        tokens = token_ref.shape[1]
        seqs = lax.broadcasted_iota(jnp.int32, (seq_count, tokens), 0).astype(jnp.float32)
        member = ids_ref[0:1, :] == seqs
        for b in range(batch_count):
            out_ref[b] = jnp.sum(jnp.where(member, token_ref[b:b + 1, :], 0.0), axis=1, keepdims=True)


def score_parts(grad_pieces, grad_basis, image, ids, seq_count):
    count, batch_count = len(grad_pieces), image.shape[0]
    rows, hidden = grad_pieces[0].shape
    inner = min(grad_basis.shape[0], hidden)
    tokens = count * rows
    return pl.pallas_call(
        functools.partial(score_kernel, count, batch_count, seq_count),
        grid=(hidden // inner,),
        in_specs=[pl.BlockSpec((rows, inner), lambda i: (0, i)) for _ in grad_pieces]
        + [
            pl.BlockSpec((grad_basis.shape[0], inner), lambda i: (0, i)),
            pl.BlockSpec((batch_count, inner, tokens), lambda i: (0, i, 0)),
            pl.BlockSpec(ids.shape, lambda i: (0, 0)),
        ],
        out_specs=pl.BlockSpec((batch_count, seq_count, 1), lambda i: (0, 0, 0)),
        out_shape=jax.ShapeDtypeStruct((batch_count, seq_count, 1), jnp.float32),
        scratch_shapes=[pltpu.VMEM((8, tokens), jnp.float32)],
        compiler_params=params(16 if tokens <= 256 else 40),
        cost_estimate=pl.CostEstimate(
            flops=2 * tokens * hidden * grad_basis.shape[0],
            bytes_accessed=4 * image.size,
            transcendentals=0,
        ),
    )(*grad_pieces, grad_basis, image, ids)


def per_device(
    train_act, train_grad, seq_ids, act_basis, grad_basis, eigenvalues, query_factors, owners
):
    wide_count = lax.axis_size("wide")
    bits = [1 << n for n in range(wide_count.bit_length() - 1)]
    me = lax.axis_index("wide")
    tok_local = train_act.shape[0]
    seq_count = tok_local * wide_count // SEQ_MEAN
    cols = grad_basis.shape[1]
    hidden = train_grad.shape[1]
    batch_count = owners.shape[0]
    score_scale = 1.0 / math.sqrt(FF * D * QT * SEQ_MEAN)
    batch = lax.axis_index("groups") % batch_count
    place = jnp.stack([me, batch]).astype(jnp.int32)

    order = [0]
    for bit in reversed(bits):
        order = order + [r + bit for r in order]
    order = sorted(order, key=lambda r: [r & bit for bit in bits])
    keep, give = cut_factors(place, query_factors, order, hidden)
    owner = owners[batch]
    got = swap(give, "wide", 1)
    held = jnp.where((owner & 1) == (me & 1), keep, got)
    count = wide_count // 2
    for bit in bits[1:]:
        count //= 2
        got = swap(held[:, count * cols:], "wide", bit)
        keep = jnp.concatenate([held[:, :count * cols], held[:, 2 * count * cols:]], axis=1)
        held = jnp.where((owner & bit) == (me & bit), keep, got)
    other = swap(held, "groups", 1)
    lefts = [held[:, :cols], other[:, :cols]]
    halves = []
    for x in (held, other):
        halves += [x[:, cols:], swap(x[:, cols:], "wide", 1)]

    ids_cols = jnp.broadcast_to(seq_ids[:, None].astype(jnp.bfloat16), (tok_local, LANES))
    acts = {0: jnp.concatenate([train_act, ids_cols], axis=1)}
    for bit in reversed(bits):
        acts.update({r + bit: swap(x, "wide", bit) for r, x in acts.items()})
    act_pieces = [acts[r] for r in range(wide_count)]

    sent = cut_grads(place, train_grad, wide_count)
    grad_pieces = [sent[0]] + [swap(sent[r], "wide", r) for r in range(1, wide_count)]

    image, ids = images(place, act_pieces, act_basis, lefts, halves, eigenvalues)
    parts = score_parts(grad_pieces, grad_basis, image, ids, seq_count)[:, :, 0]
    for bit in bits:
        parts = parts + swap(parts, "wide", bit)
    mine, others = parts[0], parts[1]
    first = jnp.where(batch == 0, mine, others)
    second = jnp.where(batch == 0, others, mine)
    return jnp.stack([first, second], axis=1) * score_scale


def solution(mesh):
    return jax.shard_map(
        per_device,
        mesh=mesh,
        in_specs=(
            P(("groups", "wide"), None),
            P(("groups", "wide"), None),
            P(("groups", "wide")),
            P(),
            P(None, "wide"),
            P("wide", None),
            P("wide", None, None),
            P(),
        ),
        out_specs=P("groups", None),
        check_vma=False,
    )
```

```python
import functools
import math

import jax
import jax.numpy as jnp
from jax import lax
from jax.experimental import pallas as pl
from jax.experimental.pallas import tpu as pltpu
from jax.sharding import PartitionSpec as P

D = 4096
FF = 32768
SEQ_MEAN = 32
QT = 16
LANES = 128


damping = 0.1


def params(mib):
    return pltpu.CompilerParams(vmem_limit_bytes=mib * 1024 * 1024)


def whole_block(shape):
    return pl.BlockSpec(shape, lambda *_: (0,) * len(shape), pipeline_mode=pl.Buffered(1))


def swap(x, axis, bit):
    count = lax.axis_size(axis)
    return lax.ppermute(x, axis, [(i, i ^ bit) for i in range(count)])


def run_copies(pairs, sems):
    copies = [pltpu.make_async_copy(src, dst, sems.at[n]) for n, (src, dst) in enumerate(pairs)]
    for copy in copies:
        copy.start()
    for copy in copies:
        copy.wait()


def in_smem(n):
    return [pl.BlockSpec(memory_space=pltpu.SMEM)] * n


def in_vmem(n):
    return [pl.BlockSpec(memory_space=pltpu.VMEM)] * n


def in_place(n):
    return [pl.BlockSpec(memory_space=pl.ANY)] * n


def in_hbm(n):
    return [pl.BlockSpec(memory_space=pltpu.HBM)] * n


def cut_factors_kernel(order, hidden, place_ref, fac_ref, keep_ref, give_ref, sems):
    cols = hidden // len(order)
    half = (fac_ref.shape[2] - hidden) // 2
    me, batch = place_ref[0], place_ref[1]
    pairs = []
    for part, out_ref in enumerate((keep_ref, give_ref)):
        picked = order[part * len(order) // 2:(part + 1) * len(order) // 2]
        for at, r in enumerate(picked):
            src = pl.multiple_of((me ^ r) * cols, cols)
            pairs.append((
                fac_ref.at[batch, :, pl.ds(src, cols)],
                out_ref.at[:, at * cols:(at + 1) * cols],
            ))
        src = pl.multiple_of(hidden + ((me & 1) ^ part) * half, LANES)
        pairs.append((fac_ref.at[batch, :, pl.ds(src, half)], out_ref.at[:, len(picked) * cols:]))
    run_copies(pairs, sems)


def cut_factors(place, factors, order, hidden):
    rows, width = factors.shape[1:]
    half = jax.ShapeDtypeStruct((rows, width // 2), factors.dtype)
    return pl.pallas_call(
        functools.partial(cut_factors_kernel, order, hidden),
        in_specs=in_smem(1) + in_hbm(1),
        out_specs=in_vmem(2),
        out_shape=[half] * 2,
        scratch_shapes=[pltpu.SemaphoreType.DMA((len(order) + 2,))],
        compiler_params=params(60),
        cost_estimate=pl.CostEstimate(flops=0, bytes_accessed=2 * factors.size, transcendentals=0),
    )(place, factors)


def pick_kernel(bit, cols, place_ref, owners_ref, keep_ref, got_ref, *out_refs):
    owner = owners_ref[place_ref[1]]
    same = ((owner ^ place_ref[0]) & bit) == 0
    count = (keep_ref.shape[1] - out_refs[0].shape[1]) // cols

    def fill(ref):
        if len(out_refs) == 1:
            out_refs[0][...] = ref[...]
        else:
            for part, out_ref in enumerate(out_refs):
                out_ref[:, :count * cols] = ref[:, part * count * cols:(part + 1) * count * cols]
                out_ref[:, count * cols:] = ref[:, 2 * count * cols:]

    @pl.when(same)
    def _():
        fill(keep_ref)

    @pl.when(jnp.logical_not(same))
    def _():
        fill(got_ref)


def pick(place, owners, keep, got, bit, cols, count):
    rows, width = keep.shape
    if count > 1:
        out = [jax.ShapeDtypeStruct((rows, width - count // 2 * cols), keep.dtype)] * 2
    else:
        out = [jax.ShapeDtypeStruct((rows, width), keep.dtype)]
    return pl.pallas_call(
        functools.partial(pick_kernel, bit, cols),
        in_specs=in_smem(2) + in_vmem(2),
        out_specs=in_vmem(len(out)),
        out_shape=out,
        compiler_params=params(16),
        cost_estimate=pl.CostEstimate(flops=0, bytes_accessed=6 * keep.size, transcendentals=0),
    )(place, owners, keep, got)


def cut_grads_kernel(place_ref, grad_ref, _, out_ref, sems):
    count = sems.shape[0]
    cols = out_ref.shape[1] // count
    pairs = []
    for q in range(count):
        src = pl.multiple_of((place_ref[0] ^ (2 * q + 1)) * cols, cols)
        pairs.append((grad_ref.at[:, pl.ds(src, cols)], out_ref.at[:, q * cols:(q + 1) * cols]))
    run_copies(pairs, sems)


def cut_grads(place, grads, after, wide_count):
    rows, hidden = grads.shape
    return pl.pallas_call(
        cut_grads_kernel,
        in_specs=in_smem(1) + in_place(2),
        out_specs=in_vmem(1)[0],
        out_shape=jax.ShapeDtypeStruct((rows, hidden // 2), grads.dtype),
        scratch_shapes=[pltpu.SemaphoreType.DMA((wide_count // 2,))],
        compiler_params=params(16),
        cost_estimate=pl.CostEstimate(flops=0, bytes_accessed=2 * grads.size, transcendentals=0),
    )(place, grads, after)


def pack_grads_kernel(count, place_ref, grad_ref, got_ref, *refs):
    out_refs, sems = refs[-count - 1:-1], refs[-1]
    rows, cols = grad_ref.shape[0], out_refs[0].shape[1]
    pairs = []
    for q, out_ref in enumerate(out_refs):
        src = pl.multiple_of((place_ref[0] ^ (2 * q)) * cols, cols)
        pairs.append((grad_ref.at[:, pl.ds(src, cols)], out_ref.at[:rows, :]))
        pairs.append((got_ref.at[:, q * cols:(q + 1) * cols], out_ref.at[rows:, :]))
    run_copies(pairs, sems)


def pack_grads(place, grads, got, after, wide_count):
    rows, hidden = grads.shape
    count = wide_count // 2
    piece = jax.ShapeDtypeStruct((2 * rows, hidden // wide_count), grads.dtype)
    return pl.pallas_call(
        functools.partial(pack_grads_kernel, count),
        in_specs=in_smem(1) + in_place(2 + len(after)),
        out_specs=in_vmem(count),
        out_shape=[piece] * count,
        scratch_shapes=[pltpu.SemaphoreType.DMA((2 * count,))],
        compiler_params=params(16),
        cost_estimate=pl.CostEstimate(flops=0, bytes_accessed=4 * grads.size, transcendentals=0),
    )(place, grads, got, *after)


def rotate_kernel(ids_ref, act_ref, basis_ref, _, out_ref):
    rows, width = act_ref.shape
    depth = basis_ref.shape[0]
    for k in range(width // depth):
        cols = slice(k * depth, (k + 1) * depth)
        out_ref[:, cols] = jnp.dot(
            act_ref[:, cols], basis_ref[:, cols], preferred_element_type=jnp.float32
        ).astype(jnp.bfloat16)
    row = lax.broadcasted_iota(jnp.int32, (rows, LANES), 0)
    ids = jnp.zeros((rows, LANES), jnp.int32)
    for t in range(rows):
        ids = jnp.where(row == t, ids_ref[t], ids)
    out_ref[:, width:] = ids.astype(jnp.float32).astype(jnp.bfloat16)


def rotate(ids, act, basis, after):
    rows, width = act.shape
    return pl.pallas_call(
        rotate_kernel,
        in_specs=in_smem(1) + in_vmem(2) + in_place(1),
        out_specs=in_vmem(1)[0],
        out_shape=jax.ShapeDtypeStruct((rows, width + LANES), act.dtype),
        compiler_params=params(16),
        cost_estimate=pl.CostEstimate(
            flops=2 * rows * width * basis.shape[0], bytes_accessed=2 * basis.size, transcendentals=0
        ),
    )(ids, act, basis, after)


def image_kernel(order, count, batch_count, me_ref, *refs):
    act_refs = refs[:count]
    left_refs = refs[count:count + batch_count]
    half_refs = refs[count + batch_count:count + 3 * batch_count]
    eig_ref, out_ref, ids_ref = refs[count + 3 * batch_count:count + 3 + 3 * batch_count]
    rot_ref, right_ref, turn_ref, pre_a, pre_b = refs[count + 3 + 3 * batch_count:]
    act_refs = [act_refs[n].at[at:at + size, :] for n, at, size in order]
    rows, width = eig_ref.shape
    half = pre_a.shape[0] // batch_count
    chunk = pre_a.shape[1]
    per = width // chunk
    phases = (rows // half) * per
    tile = min(256, chunk)

    @pl.when(pl.program_id(0) == 0)
    def _():
        for k in range(width // chunk):
            cols = slice(k * chunk, (k + 1) * chunk)
            rot_ref[cols, :] = jnp.concatenate([ref[:, cols] for ref in act_refs], axis=0).T
        ids = jnp.concatenate([ref[:, width:] for ref in act_refs], axis=0)
        ids_ref[...] = ids.astype(jnp.float32).T[:ids_ref.shape[0], :]
        side = width // 2
        for b in range(batch_count):
            for other in range(2):
                at = pl.multiple_of(((me_ref[0] & 1) ^ other) * side, side)
                ref = half_refs[2 * b + other]
                right_ref[b, :, pl.ds(at, side)] = ref[:, ref.shape[1] - side:]

    for b in range(batch_count):
        turn_ref[b] = left_refs[b][...].T
    out_ref[...] = jnp.zeros_like(out_ref)

    def place(k):
        return pl.multiple_of((k // per) * half, half), (k % per) * chunk

    def produce(k, s, pre):
        row, col = place(k)
        cols = pl.ds(pl.multiple_of(col + s * tile, tile), tile)
        damped = eig_ref[pl.ds(row, half), cols].astype(jnp.float32) + damping
        guess = pl.reciprocal(damped, approx=True)
        inverse = guess * (2.0 - damped * guess)
        for b in range(batch_count):
            outer_sum = jnp.dot(
                turn_ref[b, pl.ds(row, half), :], right_ref[b, :, cols],
                preferred_element_type=jnp.float32,
            )
            pre[b * half:(b + 1) * half, s * tile:(s + 1) * tile] = (
                outer_sum * inverse
            ).astype(jnp.bfloat16)

    def absorb(k, pre):
        row, col = place(k)
        rot = rot_ref[pl.ds(pl.multiple_of(col, chunk), chunk), :]
        more = jnp.dot(pre[...], rot, preferred_element_type=jnp.float32)
        for b in range(batch_count):
            out_ref[b, pl.ds(row, half), :] += more[b * half:(b + 1) * half, :]

    def both(k, pre_now, pre_next):
        absorb(k, pre_now)
        for s in range(chunk // tile):
            produce(k + 1, s, pre_next)

    for s in range(chunk // tile):
        produce(0, s, pre_a)

    def pair(q, carry):
        both(2 * q, pre_a, pre_b)
        both(2 * q + 1, pre_b, pre_a)
        return carry

    lax.fori_loop(0, phases // 2 - 1, pair, 0)
    both(phases - 2, pre_a, pre_b)
    absorb(phases - 1, pre_b)


def images(me, act_pieces, order, lefts, halves, eigenvalues):
    count, batch_count = len(act_pieces), len(lefts)
    tokens = sum(x.shape[0] for x in act_pieces)
    hidden, width = eigenvalues.shape
    rows = min(512, hidden)
    half = min(256, rows)
    chunk = min(1024, width // 2)
    return pl.pallas_call(
        functools.partial(image_kernel, order, count, batch_count),
        grid=(hidden // rows,),
        in_specs=in_smem(1)
        + [whole_block(x.shape) for x in act_pieces]
        + [pl.BlockSpec((QT, rows), lambda i: (0, i)) for x in lefts]
        + [whole_block(x.shape) for x in halves]
        + [pl.BlockSpec((rows, width), lambda i: (i, 0))],
        out_specs=[
            pl.BlockSpec((batch_count, rows, tokens), lambda i: (0, i, 0)),
            pl.BlockSpec((8, tokens), lambda i: (0, 0)),
        ],
        out_shape=[
            jax.ShapeDtypeStruct((batch_count, hidden, tokens), jnp.float32),
            jax.ShapeDtypeStruct((8, tokens), jnp.float32),
        ],
        scratch_shapes=[
            pltpu.VMEM((width, tokens), jnp.bfloat16),
            pltpu.VMEM((batch_count, QT, width), jnp.bfloat16),
            pltpu.VMEM((batch_count, rows, QT), jnp.bfloat16),
            pltpu.VMEM((batch_count * half, chunk), jnp.bfloat16),
            pltpu.VMEM((batch_count * half, chunk), jnp.bfloat16),
        ],
        compiler_params=params(32 if tokens <= 256 else 56),
        cost_estimate=pl.CostEstimate(
            flops=2 * hidden * width * (tokens + 256) * batch_count,
            bytes_accessed=2 * hidden * width,
            transcendentals=0,
        ),
    )(me, *act_pieces, *lefts, *halves, eigenvalues)


def score_kernel(count, batch_count, seq_count, *refs):
    grad_refs = refs[:count]
    basis_ref, image_ref, ids_ref, out_ref, token_ref = refs[count:]
    step = pl.program_id(0)

    @pl.when(step == 0)
    def _():
        token_ref[...] = jnp.zeros_like(token_ref)

    grads = jnp.concatenate([ref[...] for ref in grad_refs], axis=0)
    turned = jnp.dot(grads, basis_ref[...], preferred_element_type=jnp.float32)
    turned = turned.astype(jnp.bfloat16).T.astype(jnp.float32)
    for b in range(batch_count):
        token_ref[b:b + 1, :] += jnp.sum(image_ref[b] * turned, axis=0, keepdims=True)

    @pl.when(step == pl.num_programs(0) - 1)
    def _():
        tokens = token_ref.shape[1]
        seqs = lax.broadcasted_iota(jnp.int32, (seq_count, tokens), 0).astype(jnp.float32)
        member = ids_ref[0:1, :] == seqs
        for b in range(batch_count):
            out_ref[b] = jnp.sum(jnp.where(member, token_ref[b:b + 1, :], 0.0), axis=1, keepdims=True)


def score_parts(grad_pieces, grad_basis, image, ids, seq_count):
    count, batch_count = len(grad_pieces), image.shape[0]
    rows, hidden = grad_pieces[0].shape
    inner = min(grad_basis.shape[0], hidden)
    tokens = count * rows
    return pl.pallas_call(
        functools.partial(score_kernel, count, batch_count, seq_count),
        grid=(hidden // inner,),
        in_specs=[pl.BlockSpec((rows, inner), lambda i: (0, i)) for _ in grad_pieces]
        + [
            pl.BlockSpec((grad_basis.shape[0], inner), lambda i: (0, i)),
            pl.BlockSpec((batch_count, inner, tokens), lambda i: (0, i, 0)),
            pl.BlockSpec(ids.shape, lambda i: (0, 0)),
        ],
        out_specs=pl.BlockSpec((batch_count, seq_count, 1), lambda i: (0, 0, 0)),
        out_shape=jax.ShapeDtypeStruct((batch_count, seq_count, 1), jnp.float32),
        scratch_shapes=[pltpu.VMEM((8, tokens), jnp.float32)],
        compiler_params=params(16 if tokens <= 256 else 40),
        cost_estimate=pl.CostEstimate(
            flops=2 * tokens * hidden * grad_basis.shape[0],
            bytes_accessed=4 * image.size,
            transcendentals=0,
        ),
    )(*grad_pieces, grad_basis, image, ids)


def per_device(
    train_act, train_grad, seq_ids, act_basis, grad_basis, eigenvalues, query_factors, owners
):
    wide_count = lax.axis_size("wide")
    bits = [1 << n for n in range(wide_count.bit_length() - 1)]
    me = lax.axis_index("wide")
    tok_local = train_act.shape[0]
    seq_count = tok_local * wide_count // SEQ_MEAN
    cols = grad_basis.shape[1]
    hidden = train_grad.shape[1]
    batch_count = owners.shape[0]
    score_scale = 1.0 / math.sqrt(FF * D * QT * SEQ_MEAN)
    batch = lax.axis_index("groups") % batch_count
    place = jnp.stack([me, batch]).astype(jnp.int32)

    order = [0]
    for bit in reversed(bits):
        order = order + [r + bit for r in order]
    order = sorted(order, key=lambda r: [r & bit for bit in bits])
    keep, give = cut_factors(place, query_factors, order, hidden)
    count = wide_count // 2
    for bit in bits:
        got = swap(give, "wide", bit)
        picked = pick(place, owners, keep, got, bit, cols, count)
        keep, give = picked[0], picked[-1]
        count //= 2
        if bit == 1:
            rot = rotate(seq_ids, train_act, act_basis, give)
            grads_out = cut_grads(place, train_grad, rot, wide_count)
    held = keep
    other = swap(held, "groups", 1)
    lefts = [held, other]
    halves = []
    for x in (held, other):
        halves += [x, swap(x[:, cols:], "wide", 1)]

    acts = {0: rot}
    for bit in reversed(bits[2:]):
        acts.update({r + bit: swap(x, "wide", bit) for r, x in acts.items()})
    far = jnp.concatenate([acts[r] for r in range(4, wide_count, 4)], axis=0)
    acts = [acts[0], far]
    for bit in (2, 1):
        acts = [x for piece in acts for x in (piece, swap(piece, "wide", bit))]
    token_order = [(r, 0, tok_local) for r in range(4)]
    token_order += [(4 + r % 4, (r // 4 - 1) * tok_local, tok_local) for r in range(4, wide_count)]

    grads_got = swap(grads_out, "wide", 1)
    sent = pack_grads(place, train_grad, grads_got, [far], wide_count)
    grad_pieces = [sent[0]] + [swap(sent[q], "wide", 2 * q) for q in range(1, wide_count // 2)]

    image, ids = images(place, acts, token_order, lefts, halves, eigenvalues)
    parts = score_parts(grad_pieces, grad_basis, image, ids, seq_count)[:, :, 0]
    parts = lax.all_to_all(
        jnp.broadcast_to(parts[None], (wide_count,) + parts.shape), "wide", 0, 0
    )
    parts = jnp.sum(parts, axis=0)
    mine, others = parts[0], parts[1]
    first = jnp.where(batch == 0, mine, others)
    second = jnp.where(batch == 0, others, mine)
    return jnp.stack([first, second], axis=1) * score_scale


def solution(mesh):
    return jax.shard_map(
        per_device,
        mesh=mesh,
        in_specs=(
            P(("groups", "wide"), None),
            P(("groups", "wide"), None),
            P(("groups", "wide")),
            P(),
            P(None, "wide"),
            P("wide", None),
            P("wide", None, None),
            P(),
        ),
        out_specs=P("groups", None),
        check_vma=False,
    )
```

```python
import functools
import math

import jax
import jax.numpy as jnp
from jax import lax
from jax.experimental import pallas as pl
from jax.experimental.pallas import tpu as pltpu
from jax.sharding import PartitionSpec as P

D = 4096
FF = 32768
SEQ_MEAN = 32
QT = 16
LANES = 128


damping = 0.1


def params(mib):
    return pltpu.CompilerParams(vmem_limit_bytes=mib * 1024 * 1024)


def whole_block(shape):
    return pl.BlockSpec(shape, lambda *_: (0,) * len(shape), pipeline_mode=pl.Buffered(1))


def swap(x, axis, bit):
    count = lax.axis_size(axis)
    return lax.ppermute(x, axis, [(i, i ^ bit) for i in range(count)])


def in_smem(n):
    return [pl.BlockSpec(memory_space=pltpu.SMEM)] * n


def in_vmem(n):
    return [pl.BlockSpec(memory_space=pltpu.VMEM)] * n


def in_place(n):
    return [pl.BlockSpec(memory_space=pl.ANY)] * n


def cut_factors_kernel(order, hidden, batch_count, fac_ref, keep_ref, give_ref):
    cols = hidden // len(order)
    half = (fac_ref.shape[2] - hidden) // 2
    me, batch = lax.axis_index("wide"), lax.rem(lax.axis_index("groups"), batch_count)
    for part, out_ref in enumerate((keep_ref, give_ref)):
        picked = order[part * len(order) // 2:(part + 1) * len(order) // 2]
        for at, r in enumerate(picked):
            src = pl.multiple_of((me ^ r) * cols, cols)
            out_ref[:, at * cols:(at + 1) * cols] = fac_ref[batch, :, pl.ds(src, cols)]
        src = pl.multiple_of(hidden + ((me & 1) ^ part) * half, LANES)
        out_ref[:, len(picked) * cols:] = fac_ref[batch, :, pl.ds(src, half)]


def cut_factors(factors, order, hidden, batch_count):
    rows, width = factors.shape[1:]
    half = jax.ShapeDtypeStruct((rows, width // 2), factors.dtype)
    return pl.pallas_call(
        functools.partial(cut_factors_kernel, order, hidden, batch_count),
        in_specs=in_vmem(1),
        out_specs=in_vmem(2),
        out_shape=[half] * 2,
        compiler_params=params(16),
        cost_estimate=pl.CostEstimate(flops=0, bytes_accessed=factors.size, transcendentals=0),
    )(factors)


def pick_kernel(bit, cols, batch_count, parts, join, owners_ref, keep_ref, got_ref, *refs):
    me, batch = lax.axis_index("wide"), lax.rem(lax.axis_index("groups"), batch_count)
    join_refs, out_refs = refs[:join], refs[join:]
    same = ((owners_ref[batch] ^ me) & bit) == 0
    count = (keep_ref.shape[1] - out_refs[0].shape[1]) // cols

    def fill(ref):
        if parts == 1:
            out_refs[0][...] = ref[...]
        else:
            for part in range(parts):
                out_ref = out_refs[part]
                out_ref[:, :count * cols] = ref[:, part * count * cols:(part + 1) * count * cols]
                out_ref[:, count * cols:] = ref[:, 2 * count * cols:]

    @pl.when(same)
    def _():
        fill(keep_ref)

    @pl.when(jnp.logical_not(same))
    def _():
        fill(got_ref)

    at = 0
    for ref in join_refs:
        out_refs[-1][at:at + ref.shape[0], :] = ref[...]
        at += ref.shape[0]


def pick(owners, keep, got, bit, cols, count, join=()):
    rows, width = keep.shape
    if count > 1:
        out = [jax.ShapeDtypeStruct((rows, width - count // 2 * cols), keep.dtype)] * 2
    else:
        out = [jax.ShapeDtypeStruct((rows, width), keep.dtype)]
    parts = len(out)
    if join:
        out.append(jax.ShapeDtypeStruct(
            (sum(x.shape[0] for x in join), join[0].shape[1]), join[0].dtype
        ))
    return pl.pallas_call(
        functools.partial(pick_kernel, bit, cols, owners.shape[0], parts, len(join)),
        in_specs=in_smem(1) + in_vmem(2 + len(join)),
        out_specs=in_vmem(len(out)),
        out_shape=out,
        compiler_params=params(16),
        cost_estimate=pl.CostEstimate(flops=0, bytes_accessed=2 * keep.size, transcendentals=0),
    )(owners, keep, got, *join)


def cut_grads_kernel(grad_ref, _, out_ref):
    count, rows, cols = out_ref.shape
    for to in range(count):
        out_ref[to] = grad_ref[:, to * cols:(to + 1) * cols]


def cut_grads(grads, after, count):
    rows, hidden = grads.shape
    return pl.pallas_call(
        cut_grads_kernel,
        in_specs=in_vmem(1) + in_place(1),
        out_specs=in_vmem(1)[0],
        out_shape=jax.ShapeDtypeStruct((count, rows, hidden // count), grads.dtype),
        compiler_params=params(16),
        cost_estimate=pl.CostEstimate(flops=0, bytes_accessed=grads.size, transcendentals=0),
    )(grads, after)


def rotate_kernel(ids_ref, act_ref, basis_ref, _, out_ref, held_ref, sems):
    rows, width = act_ref.shape
    depth = basis_ref.shape[0]
    copies = []
    for k in range(width // depth):
        cols = slice(k * depth, (k + 1) * depth)
        copy = pltpu.make_async_copy(basis_ref.at[:, cols], held_ref.at[k], sems.at[k])
        copy.start()
        copies.append(copy)
    row = lax.broadcasted_iota(jnp.int32, (rows, LANES), 0)
    ids = jnp.zeros((rows, LANES), jnp.int32)
    for t in range(rows):
        ids = jnp.where(row == t, ids_ref[t], ids)
    out_ref[:, width:] = ids.astype(jnp.float32).astype(jnp.bfloat16)
    for k, copy in enumerate(copies):
        cols = slice(k * depth, (k + 1) * depth)
        copy.wait()
        out_ref[:, cols] = jnp.dot(
            act_ref[:, cols], held_ref[k], preferred_element_type=jnp.float32
        ).astype(jnp.bfloat16)


def rotate(ids, act, basis, after):
    rows, width = act.shape
    depth = basis.shape[0]
    return pl.pallas_call(
        rotate_kernel,
        in_specs=in_smem(1) + in_vmem(1) + in_place(2),
        out_specs=in_vmem(1)[0],
        out_shape=jax.ShapeDtypeStruct((rows, width + LANES), act.dtype),
        scratch_shapes=[
            pltpu.VMEM((width // depth, depth, depth), jnp.bfloat16),
            pltpu.SemaphoreType.DMA((width // depth,)),
        ],
        compiler_params=params(55),
        cost_estimate=pl.CostEstimate(
            flops=2 * rows * width * basis.shape[0], bytes_accessed=basis.size, transcendentals=0
        ),
    )(ids, act, basis, after)


def image_kernel(order, count, batch_count, *refs):
    act_refs = refs[:count]
    left_refs = refs[count:count + batch_count]
    half_refs = refs[count + batch_count:count + 3 * batch_count]
    eig_ref, out_ref, ids_ref = refs[count + 3 * batch_count:count + 3 + 3 * batch_count]
    rot_ref, right_ref, turn_ref, pre_a, pre_b = refs[count + 3 + 3 * batch_count:]
    act_refs = [act_refs[n].at[at:at + size, :] for n, at, size in order]
    rows, width = eig_ref.shape
    half = pre_a.shape[0] // batch_count
    chunk = pre_a.shape[1]
    per = width // chunk
    phases = (rows // half) * per
    tile = min(256, chunk)

    @pl.when(pl.program_id(0) == 0)
    def _():
        for k in range(width // chunk):
            cols = slice(k * chunk, (k + 1) * chunk)
            rot_ref[cols, :] = jnp.concatenate([ref[:, cols] for ref in act_refs], axis=0).T
        ids = jnp.concatenate([ref[:, width:] for ref in act_refs], axis=0)
        ids_ref[...] = ids.astype(jnp.float32).T[:ids_ref.shape[0], :]
        side = width // 2
        for b in range(batch_count):
            for other in range(2):
                at = pl.multiple_of(((lax.axis_index("wide") & 1) ^ other) * side, side)
                ref = half_refs[2 * b + other]
                right_ref[b, :, pl.ds(at, side)] = ref[:, ref.shape[1] - side:]

    for b in range(batch_count):
        turn_ref[b] = left_refs[b][...].T
    out_ref[...] = jnp.zeros_like(out_ref)

    def place(k):
        return pl.multiple_of((k // per) * half, half), (k % per) * chunk

    def produce(k, s, pre):
        row, col = place(k)
        cols = pl.ds(pl.multiple_of(col + s * tile, tile), tile)
        damped = eig_ref[pl.ds(row, half), cols].astype(jnp.float32) + damping
        inverse = pl.reciprocal(damped, approx=True)
        for b in range(batch_count):
            outer_sum = jnp.dot(
                turn_ref[b, pl.ds(row, half), :], right_ref[b, :, cols],
                preferred_element_type=jnp.float32,
            )
            pre[b * half:(b + 1) * half, s * tile:(s + 1) * tile] = (
                outer_sum * inverse
            ).astype(jnp.bfloat16)

    def absorb(k, pre):
        row, col = place(k)
        rot = rot_ref[pl.ds(pl.multiple_of(col, chunk), chunk), :]
        more = jnp.dot(pre[...], rot, preferred_element_type=jnp.float32)
        for b in range(batch_count):
            out_ref[b, pl.ds(row, half), :] += more[b * half:(b + 1) * half, :]

    def both(k, pre_now, pre_next):
        absorb(k, pre_now)
        for s in range(chunk // tile):
            produce(k + 1, s, pre_next)

    for s in range(chunk // tile):
        produce(0, s, pre_a)

    def pair(q, carry):
        both(2 * q, pre_a, pre_b)
        both(2 * q + 1, pre_b, pre_a)
        return carry

    lax.fori_loop(0, phases // 2 - 1, pair, 0)
    both(phases - 2, pre_a, pre_b)
    absorb(phases - 1, pre_b)


def images(act_pieces, order, lefts, halves, eigenvalues):
    count, batch_count = len(act_pieces), len(lefts)
    tokens = sum(x.shape[0] for x in act_pieces)
    hidden, width = eigenvalues.shape
    rows = min(512, hidden)
    half = min(256, rows)
    chunk = min(1024, width // 2)
    return pl.pallas_call(
        functools.partial(image_kernel, order, count, batch_count),
        grid=(hidden // rows,),
        in_specs=[whole_block(x.shape) for x in act_pieces]
        + [pl.BlockSpec((QT, rows), lambda i: (0, i)) for x in lefts]
        + [whole_block(x.shape) for x in halves]
        + [pl.BlockSpec((rows, width), lambda i: (i, 0))],
        out_specs=[
            pl.BlockSpec((batch_count, rows, tokens), lambda i: (0, i, 0)),
            pl.BlockSpec((8, tokens), lambda i: (0, 0)),
        ],
        out_shape=[
            jax.ShapeDtypeStruct((batch_count, hidden, tokens), jnp.float32),
            jax.ShapeDtypeStruct((8, tokens), jnp.float32),
        ],
        scratch_shapes=[
            pltpu.VMEM((width, tokens), jnp.bfloat16),
            pltpu.VMEM((batch_count, QT, width), jnp.bfloat16),
            pltpu.VMEM((batch_count, rows, QT), jnp.bfloat16),
            pltpu.VMEM((batch_count * half, chunk), jnp.bfloat16),
            pltpu.VMEM((batch_count * half, chunk), jnp.bfloat16),
        ],
        compiler_params=params(32 if tokens <= 256 else 56),
        cost_estimate=pl.CostEstimate(
            flops=2 * hidden * width * (tokens + 256) * batch_count,
            bytes_accessed=2 * hidden * width,
            transcendentals=0,
        ),
    )(*act_pieces, *lefts, *halves, eigenvalues)


def score_kernel(batch_count, seq_count, grad_ref, basis_ref, image_ref, ids_ref, out_ref, token_ref):
    step = pl.program_id(0)
    me = lax.axis_index("wide")

    @pl.when(step == 0)
    def _():
        token_ref[...] = jnp.zeros_like(token_ref)

    grads = jnp.concatenate([grad_ref[me ^ r] for r in range(grad_ref.shape[0])], axis=0)
    turned = jnp.dot(grads, basis_ref[...], preferred_element_type=jnp.float32)
    turned = turned.astype(jnp.bfloat16).T.astype(jnp.float32)
    for b in range(batch_count):
        token_ref[b:b + 1, :] += jnp.sum(image_ref[b] * turned, axis=0, keepdims=True)

    @pl.when(step == pl.num_programs(0) - 1)
    def _():
        tokens = token_ref.shape[1]
        seqs = lax.broadcasted_iota(jnp.int32, (seq_count, tokens), 0).astype(jnp.float32)
        member = ids_ref[0:1, :] == seqs
        for b in range(batch_count):
            out_ref[b] = jnp.sum(jnp.where(member, token_ref[b:b + 1, :], 0.0), axis=1, keepdims=True)


def score_parts(grads, grad_basis, image, ids, seq_count):
    batch_count = image.shape[0]
    count, rows, hidden = grads.shape
    inner = min(grad_basis.shape[0], hidden)
    tokens = count * rows
    return pl.pallas_call(
        functools.partial(score_kernel, batch_count, seq_count),
        grid=(hidden // inner,),
        in_specs=[
            pl.BlockSpec((count, rows, inner), lambda i: (0, 0, i)),
            pl.BlockSpec((grad_basis.shape[0], inner), lambda i: (0, i)),
            pl.BlockSpec((batch_count, inner, tokens), lambda i: (0, i, 0)),
            pl.BlockSpec(ids.shape, lambda i: (0, 0)),
        ],
        out_specs=pl.BlockSpec((batch_count, seq_count, 1), lambda i: (0, 0, 0)),
        out_shape=jax.ShapeDtypeStruct((batch_count, seq_count, 1), jnp.float32),
        scratch_shapes=[pltpu.VMEM((8, tokens), jnp.float32)],
        compiler_params=params(16 if tokens <= 256 else 40),
        cost_estimate=pl.CostEstimate(
            flops=2 * tokens * hidden * grad_basis.shape[0],
            bytes_accessed=4 * image.size,
            transcendentals=0,
        ),
    )(grads, grad_basis, image, ids)


def per_device(
    train_act, train_grad, seq_ids, act_basis, grad_basis, eigenvalues, query_factors, owners
):
    wide_count = lax.axis_size("wide")
    bits = [1 << n for n in range(wide_count.bit_length() - 1)]
    me = lax.axis_index("wide")
    tok_local = train_act.shape[0]
    seq_count = tok_local * wide_count // SEQ_MEAN
    cols = grad_basis.shape[1]
    hidden = train_grad.shape[1]
    batch_count = owners.shape[0]
    score_scale = 1.0 / math.sqrt(FF * D * QT * SEQ_MEAN)
    batch = lax.axis_index("groups") % batch_count

    order = [0]
    for bit in reversed(bits):
        order = order + [r + bit for r in order]
    order = sorted(order, key=lambda r: [r & bit for bit in bits])
    keep, give = cut_factors(query_factors, order, hidden, batch_count)
    rot = rotate(seq_ids, train_act, act_basis, give)
    joined, ranks = rot, [0]
    far = bits[:1:-1]
    count = wide_count // 2
    for step, bit in enumerate(bits):
        got = swap(give, "wide", bit)
        join = ()
        if 1 <= step < len(far):
            join = (joined, swap(joined, "wide", far[step - 1]))
            ranks = ranks + [r + far[step - 1] for r in ranks]
        picked = list(pick(owners, keep, got, bit, cols, count, join))
        if join:
            joined = picked.pop()
        keep, give = picked[0], picked[-1]
        count //= 2
        if step == len(bits) - 2:
            sent = cut_grads(train_grad, give, wide_count)
            grads = lax.all_to_all(sent, "wide", 0, 0)
    held = keep
    acts = [(joined, ranks)]
    for bit in (far[-1], 2, 1):
        acts += [(swap(x, "wide", bit), [r + bit for r in has]) for x, has in acts]
    token_order = [None] * wide_count
    for n, (_, has) in enumerate(acts):
        for at, r in enumerate(has):
            token_order[r] = (n, at * tok_local, tok_local)
    acts = [x for x, _ in acts]

    other = swap(held, "groups", 1)
    lefts = [held, other]
    halves = []
    for x in (held, other):
        halves += [x, swap(x[:, cols:], "wide", 1)]

    image, ids = images(acts, token_order, lefts, halves, eigenvalues)
    parts = score_parts(grads, grad_basis, image, ids, seq_count)[:, :, 0]
    for near in (bits[:2], bits[2:]):
        step = near[0]
        others = [swap(parts, "wide", step * n) for n in range(1, 1 << len(near))]
        parts = parts + sum(others)
    mine, others = parts[0], parts[1]
    first = jnp.where(batch == 0, mine, others)
    second = jnp.where(batch == 0, others, mine)
    return jnp.stack([first, second], axis=1) * score_scale


def solution(mesh):
    return jax.shard_map(
        per_device,
        mesh=mesh,
        in_specs=(
            P(("groups", "wide"), None),
            P(("groups", "wide"), None),
            P(("groups", "wide")),
            P(),
            P(None, "wide"),
            P("wide", None),
            P("wide", None, None),
            P(),
        ),
        out_specs=P("groups", None),
        check_vma=False,
    )
```

```python
import functools
import math

import jax
import jax.numpy as jnp
from jax import lax
from jax.experimental import pallas as pl
from jax.experimental.pallas import tpu as pltpu
from jax.sharding import PartitionSpec as P

D = 4096
FF = 32768
SEQ_MEAN = 32
QT = 16
LANES = 128


damping = 0.1


def params(mib):
    return pltpu.CompilerParams(vmem_limit_bytes=mib * 1024 * 1024)


def whole_block(shape):
    return pl.BlockSpec(shape, lambda *_: (0,) * len(shape), pipeline_mode=pl.Buffered(1))


def swap(x, axis, bit):
    count = lax.axis_size(axis)
    return lax.ppermute(x, axis, [(i, i ^ bit) for i in range(count)])


def in_smem(n):
    return [pl.BlockSpec(memory_space=pltpu.SMEM)] * n


def in_vmem(n):
    return [pl.BlockSpec(memory_space=pltpu.VMEM)] * n


def in_place(n):
    return [pl.BlockSpec(memory_space=pl.ANY)] * n


def cut_factors_kernel(order, hidden, batch_count, fac_ref, keep_ref, give_ref):
    cols = hidden // len(order)
    half = (fac_ref.shape[2] - hidden) // 2
    me, batch = lax.axis_index("wide"), lax.rem(lax.axis_index("groups"), batch_count)
    for part, out_ref in enumerate((keep_ref, give_ref)):
        picked = order[part * len(order) // 2:(part + 1) * len(order) // 2]
        for at, r in enumerate(picked):
            src = pl.multiple_of((me ^ r) * cols, cols)
            out_ref[:, at * cols:(at + 1) * cols] = fac_ref[batch, :, pl.ds(src, cols)]
        src = pl.multiple_of(hidden + ((me & 1) ^ part) * half, LANES)
        out_ref[:, len(picked) * cols:] = fac_ref[batch, :, pl.ds(src, half)]


def cut_factors(factors, order, hidden, batch_count):
    rows, width = factors.shape[1:]
    half = jax.ShapeDtypeStruct((rows, width // 2), factors.dtype)
    return pl.pallas_call(
        functools.partial(cut_factors_kernel, order, hidden, batch_count),
        in_specs=in_vmem(1),
        out_specs=in_vmem(2),
        out_shape=[half] * 2,
        compiler_params=params(16),
        cost_estimate=pl.CostEstimate(flops=0, bytes_accessed=factors.size, transcendentals=0),
    )(factors)


def pick_kernel(bit, cols, batch_count, last, join, owners_ref, keep_ref, got_ref, *refs):
    me, batch = lax.axis_index("wide"), lax.rem(lax.axis_index("groups"), batch_count)
    join_refs, out_refs = refs[:join], refs[join:]
    same = ((owners_ref[batch] ^ me) & bit) == 0
    count = (keep_ref.shape[1] - out_refs[0].shape[1]) // cols

    def fill(ref):
        if last:
            out_refs[0][...] = ref[:, :cols]
            out_refs[1][...] = ref[:, cols:]
        else:
            for part in range(2):
                out_ref = out_refs[part]
                out_ref[:, :count * cols] = ref[:, part * count * cols:(part + 1) * count * cols]
                out_ref[:, count * cols:] = ref[:, 2 * count * cols:]

    @pl.when(same)
    def _():
        fill(keep_ref)

    @pl.when(jnp.logical_not(same))
    def _():
        fill(got_ref)

    at = 0
    for ref in join_refs:
        out_refs[-1][at:at + ref.shape[0], :] = ref[...]
        at += ref.shape[0]


def pick(owners, keep, got, bit, cols, count, join=()):
    rows, width = keep.shape
    if count > 1:
        widths = [width - count // 2 * cols] * 2
    else:
        widths = [cols, width - cols]
    out = [jax.ShapeDtypeStruct((rows, w), keep.dtype) for w in widths]
    if join:
        out.append(jax.ShapeDtypeStruct(
            (sum(x.shape[0] for x in join), join[0].shape[1]), join[0].dtype
        ))
    return pl.pallas_call(
        functools.partial(pick_kernel, bit, cols, owners.shape[0], count == 1, len(join)),
        in_specs=in_smem(1) + in_vmem(2 + len(join)),
        out_specs=in_vmem(len(out)),
        out_shape=out,
        compiler_params=params(16),
        cost_estimate=pl.CostEstimate(flops=0, bytes_accessed=2 * keep.size, transcendentals=0),
    )(owners, keep, got, *join)


def cut_grads_kernel(grad_ref, _, out_ref):
    count, rows, cols = out_ref.shape
    for to in range(count):
        out_ref[to] = grad_ref[:, to * cols:(to + 1) * cols]


def cut_grads(grads, after, count):
    rows, hidden = grads.shape
    return pl.pallas_call(
        cut_grads_kernel,
        in_specs=in_vmem(1) + in_place(1),
        out_specs=in_vmem(1)[0],
        out_shape=jax.ShapeDtypeStruct((count, rows, hidden // count), grads.dtype),
        compiler_params=params(16),
        cost_estimate=pl.CostEstimate(flops=0, bytes_accessed=grads.size, transcendentals=0),
    )(grads, after)


def label_kernel(ids_ref, act_ref, out_ref):
    rows, width = act_ref.shape
    row = lax.broadcasted_iota(jnp.int32, (rows, LANES), 0)
    ids = jnp.zeros((rows, LANES), jnp.int32)
    for t in range(rows):
        ids = jnp.where(row == t, ids_ref[t], ids)
    out_ref[:, :width] = act_ref[...]
    out_ref[:, width:] = ids.astype(jnp.float32).astype(jnp.bfloat16)


def label(ids, act):
    rows, width = act.shape
    return pl.pallas_call(
        label_kernel,
        in_specs=in_smem(1) + in_vmem(1),
        out_specs=in_vmem(1)[0],
        out_shape=jax.ShapeDtypeStruct((rows, width + LANES), act.dtype),
        compiler_params=params(16),
        cost_estimate=pl.CostEstimate(flops=0, bytes_accessed=act.size, transcendentals=0),
    )(ids, act)


def rotate_kernel(order, *refs):
    act_refs, (basis_ref, out_ref, ids_ref) = refs[:-3], refs[-3:]
    act_refs = [act_refs[n].at[at:at + size, :] for n, at, size in order]
    depth, width = basis_ref.shape
    for k in range(width // depth):
        cols = slice(k * depth, (k + 1) * depth)
        act = jnp.concatenate([ref[:, cols] for ref in act_refs], axis=0)
        out_ref[:, cols] = jnp.dot(
            act, basis_ref[:, cols], preferred_element_type=jnp.float32
        ).astype(jnp.bfloat16)
    ids = jnp.concatenate([ref[:, width:] for ref in act_refs], axis=0)
    ids_ref[...] = ids.astype(jnp.float32)


def rotate(act_pieces, order, basis):
    tokens = sum(x.shape[0] for x in act_pieces)
    width = basis.shape[1]
    return pl.pallas_call(
        functools.partial(rotate_kernel, order),
        in_specs=in_vmem(len(act_pieces) + 1),
        out_specs=in_vmem(2),
        out_shape=[
            jax.ShapeDtypeStruct((tokens, width), jnp.bfloat16),
            jax.ShapeDtypeStruct((tokens, LANES), jnp.float32),
        ],
        compiler_params=params(20 if tokens <= 256 else 40),
        cost_estimate=pl.CostEstimate(
            flops=2 * tokens * width * basis.shape[0], bytes_accessed=basis.size, transcendentals=0
        ),
    )(*act_pieces, basis)


def image_kernel(batch_count, rot_ref, *refs):
    left_refs, half_refs = refs[:batch_count], refs[batch_count:3 * batch_count]
    eig_ref, out_ref, right_ref, turn_ref, pre_a, pre_b = refs[3 * batch_count:]
    rows, width = eig_ref.shape
    half = pre_a.shape[0] // batch_count
    chunk = pre_a.shape[1]
    per = width // chunk
    phases = (rows // half) * per
    tile = min(256, chunk)

    @pl.when(pl.program_id(0) == 0)
    def _():
        side = width // 2
        for b in range(batch_count):
            for other in range(2):
                at = pl.multiple_of(((lax.axis_index("wide") & 1) ^ other) * side, side)
                right_ref[b, :, pl.ds(at, side)] = half_refs[2 * b + other][...]

    for b in range(batch_count):
        turn_ref[b] = left_refs[b][...].T
    out_ref[...] = jnp.zeros_like(out_ref)

    def place(k):
        return pl.multiple_of((k // per) * half, half), (k % per) * chunk

    def produce(k, s, pre):
        row, col = place(k)
        cols = pl.ds(pl.multiple_of(col + s * tile, tile), tile)
        damped = eig_ref[pl.ds(row, half), cols].astype(jnp.float32) + damping
        inverse = pl.reciprocal(damped, approx=True)
        for b in range(batch_count):
            outer_sum = jnp.dot(
                turn_ref[b, pl.ds(row, half), :], right_ref[b, :, cols],
                preferred_element_type=jnp.float32,
            )
            pre[b * half:(b + 1) * half, s * tile:(s + 1) * tile] = (
                outer_sum * inverse
            ).astype(jnp.bfloat16)

    def absorb(k, pre):
        row, col = place(k)
        rot = rot_ref[:, pl.ds(pl.multiple_of(col, chunk), chunk)]
        more = lax.dot_general(
            rot, pre[...], (((1,), (1,)), ((), ())), preferred_element_type=jnp.float32
        )
        for b in range(batch_count):
            out_ref[b, :, pl.ds(row, half)] += more[:, b * half:(b + 1) * half]

    def both(k, pre_now, pre_next):
        absorb(k, pre_now)
        for s in range(chunk // tile):
            produce(k + 1, s, pre_next)

    for s in range(chunk // tile):
        produce(0, s, pre_a)

    def pair(q, carry):
        both(2 * q, pre_a, pre_b)
        both(2 * q + 1, pre_b, pre_a)
        return carry

    lax.fori_loop(0, phases // 2 - 1, pair, 0)
    both(phases - 2, pre_a, pre_b)
    absorb(phases - 1, pre_b)


def images(rot, lefts, halves, eigenvalues):
    batch_count, tokens = len(lefts), rot.shape[0]
    hidden, width = eigenvalues.shape
    rows = min(512, hidden)
    half = min(256, rows)
    chunk = min(1024, width // 2)
    return pl.pallas_call(
        functools.partial(image_kernel, batch_count),
        grid=(hidden // rows,),
        in_specs=[whole_block(rot.shape)]
        + [pl.BlockSpec((QT, rows), lambda i: (0, i)) for x in lefts]
        + [whole_block(x.shape) for x in halves]
        + [pl.BlockSpec((rows, width), lambda i: (i, 0))],
        out_specs=pl.BlockSpec((batch_count, tokens, rows), lambda i: (0, 0, i)),
        out_shape=jax.ShapeDtypeStruct((batch_count, tokens, hidden), jnp.float32),
        scratch_shapes=[
            pltpu.VMEM((batch_count, QT, width), jnp.bfloat16),
            pltpu.VMEM((batch_count, rows, QT), jnp.bfloat16),
            pltpu.VMEM((batch_count * half, chunk), jnp.bfloat16),
            pltpu.VMEM((batch_count * half, chunk), jnp.bfloat16),
        ],
        compiler_params=params(32 if tokens <= 256 else 56),
        cost_estimate=pl.CostEstimate(
            flops=2 * hidden * width * (tokens + 256) * batch_count,
            bytes_accessed=2 * hidden * width,
            transcendentals=0,
        ),
    )(rot, *lefts, *halves, eigenvalues)


def score_kernel(batch_count, grad_ref, basis_ref, image_ref, ids_ref, out_ref, token_ref):
    step = pl.program_id(0)
    me = lax.axis_index("wide")

    @pl.when(step == 0)
    def _():
        token_ref[...] = jnp.zeros_like(token_ref)

    grads = jnp.concatenate([grad_ref[me ^ r] for r in range(grad_ref.shape[0])], axis=0)
    turned = jnp.dot(grads, basis_ref[...], preferred_element_type=jnp.float32)
    turned = turned.astype(jnp.bfloat16).astype(jnp.float32)
    for b in range(batch_count):
        token_ref[b] += jnp.sum(image_ref[b] * turned, axis=1, keepdims=True)

    @pl.when(step == pl.num_programs(0) - 1)
    def _():
        seqs = lax.broadcasted_iota(jnp.int32, ids_ref.shape, 1).astype(jnp.float32)
        member = ids_ref[...] == seqs
        for b in range(batch_count):
            sums = jnp.sum(jnp.where(member, token_ref[b], 0.0), axis=0, keepdims=True)
            out_ref[b:b + 1, :] = sums[:, :out_ref.shape[1]]


def score_parts(grads, grad_basis, image, ids, seq_count):
    batch_count, tokens = image.shape[:2]
    count, rows, hidden = grads.shape
    inner = min(grad_basis.shape[0], hidden)
    return pl.pallas_call(
        functools.partial(score_kernel, batch_count),
        grid=(hidden // inner,),
        in_specs=[
            pl.BlockSpec((count, rows, inner), lambda i: (0, 0, i)),
            pl.BlockSpec((grad_basis.shape[0], inner), lambda i: (0, i)),
            pl.BlockSpec((batch_count, tokens, inner), lambda i: (0, 0, i)),
            pl.BlockSpec(ids.shape, lambda i: (0, 0)),
        ],
        out_specs=pl.BlockSpec((batch_count, seq_count), lambda i: (0, 0)),
        out_shape=jax.ShapeDtypeStruct((batch_count, seq_count), jnp.float32),
        scratch_shapes=[pltpu.VMEM((batch_count, tokens, 1), jnp.float32)],
        compiler_params=params(16 if tokens <= 256 else 40),
        cost_estimate=pl.CostEstimate(
            flops=2 * tokens * hidden * grad_basis.shape[0],
            bytes_accessed=4 * image.size,
            transcendentals=0,
        ),
    )(grads, grad_basis, image, ids)


def per_device(
    train_act, train_grad, seq_ids, act_basis, grad_basis, eigenvalues, query_factors, owners
):
    wide_count = lax.axis_size("wide")
    bits = [1 << n for n in range(wide_count.bit_length() - 1)]
    me = lax.axis_index("wide")
    tok_local = train_act.shape[0]
    seq_count = tok_local * wide_count // SEQ_MEAN
    cols = grad_basis.shape[1]
    hidden = train_grad.shape[1]
    batch_count = owners.shape[0]
    score_scale = 1.0 / math.sqrt(FF * D * QT * SEQ_MEAN)
    batch = lax.axis_index("groups") % batch_count

    order = [0]
    for bit in reversed(bits):
        order = order + [r + bit for r in order]
    order = sorted(order, key=lambda r: [r & bit for bit in bits])
    joined, ranks = label(seq_ids, train_act), [0]
    far = bits[:1:-1]
    keep, give = cut_factors(query_factors, order, hidden, batch_count)
    count = wide_count // 2
    for step, bit in enumerate(bits):
        join = ()
        if step < len(far):
            join = (joined, swap(joined, "wide", far[step]))
            ranks = ranks + [r + far[step] for r in ranks]
        got = swap(give, "wide", bit)
        picked = list(pick(owners, keep, got, bit, cols, count, join))
        if join:
            joined = picked.pop()
        keep, give = picked
        count //= 2
    left, right = keep, give
    acts = [(joined, ranks)]
    for bit in (2, 1):
        acts += [(swap(x, "wide", bit), [r + bit for r in has]) for x, has in acts]
    token_order = [None] * wide_count
    for n, (_, has) in enumerate(acts):
        for at, r in enumerate(has):
            token_order[r] = (n, at * tok_local, tok_local)
    rot, ids = rotate([x for x, _ in acts], token_order, act_basis)

    lefts = [left, swap(left, "groups", 1)]
    halves = []
    for x in (right, swap(right, "groups", 1)):
        halves += [x, swap(x, "wide", 1)]

    grads = lax.all_to_all(cut_grads(train_grad, right, wide_count), "wide", 0, 0)

    image = images(rot, lefts, halves, eigenvalues)
    parts = score_parts(grads, grad_basis, image, ids, seq_count)
    for near in (bits[:2], bits[2:]):
        step = near[0]
        others = [swap(parts, "wide", step * n) for n in range(1, 1 << len(near))]
        parts = parts + sum(others)
    mine, others = parts[0], parts[1]
    first = jnp.where(batch == 0, mine, others)
    second = jnp.where(batch == 0, others, mine)
    return jnp.stack([first, second], axis=1) * score_scale


def solution(mesh):
    return jax.shard_map(
        per_device,
        mesh=mesh,
        in_specs=(
            P(("groups", "wide"), None),
            P(("groups", "wide"), None),
            P(("groups", "wide")),
            P(),
            P(None, "wide"),
            P("wide", None),
            P("wide", None, None),
            P(),
        ),
        out_specs=P("groups", None),
        check_vma=False,
    )
```

```python
import functools
import math

import jax
import jax.numpy as jnp
from jax import lax
from jax.experimental import pallas as pl
from jax.experimental.pallas import tpu as pltpu
from jax.sharding import PartitionSpec as P

D = 4096
FF = 32768
SEQ_MEAN = 32
QT = 16
LANES = 128


damping = 0.1


def params(mib):
    return pltpu.CompilerParams(vmem_limit_bytes=mib * 1024 * 1024)


def whole_block(shape):
    return pl.BlockSpec(shape, lambda *_: (0,) * len(shape), pipeline_mode=pl.Buffered(1))


def swap(x, axis, bit):
    count = lax.axis_size(axis)
    return lax.ppermute(x, axis, [(i, i ^ bit) for i in range(count)])


def in_smem(n):
    return [pl.BlockSpec(memory_space=pltpu.SMEM)] * n


def in_vmem(n):
    return [pl.BlockSpec(memory_space=pltpu.VMEM)] * n


def in_place(n):
    return [pl.BlockSpec(memory_space=pl.ANY)] * n


def cut_factors_kernel(order, hidden, batch_count, owners_ref, fac_ref, keep_ref, give_ref, flag_ref):
    cols = hidden // len(order)
    half = (fac_ref.shape[2] - hidden) // 2
    me, batch = lax.axis_index("wide"), lax.rem(lax.axis_index("groups"), batch_count)
    for part, out_ref in enumerate((keep_ref, give_ref)):
        picked = order[part * len(order) // 2:(part + 1) * len(order) // 2]
        for at, r in enumerate(picked):
            src = pl.multiple_of((me ^ r) * cols, cols)
            out_ref[:, at * cols:(at + 1) * cols] = fac_ref[batch, :, pl.ds(src, cols)]
        src = pl.multiple_of(hidden + ((me & 1) ^ part) * half, LANES)
        out_ref[:, len(picked) * cols:] = fac_ref[batch, :, pl.ds(src, half)]
    apart = owners_ref[batch] ^ me
    lane = lax.broadcasted_iota(jnp.int32, flag_ref.shape, 1)
    flags = jnp.zeros(flag_ref.shape, jnp.float32)
    for step in range(len(order).bit_length() - 1):
        same = jnp.where((apart & (1 << step)) == 0, 1.0, 0.0)
        flags = jnp.where(lane == step, same, flags)
    flag_ref[...] = flags.astype(flag_ref.dtype)


def cut_factors(owners, factors, order, hidden):
    batch_count, rows, width = owners.shape[0], *factors.shape[1:]
    half = jax.ShapeDtypeStruct((rows, width // 2), factors.dtype)
    return pl.pallas_call(
        functools.partial(cut_factors_kernel, order, hidden, batch_count),
        in_specs=in_smem(1) + in_vmem(1),
        out_specs=in_vmem(3),
        out_shape=[half] * 2 + [jax.ShapeDtypeStruct((rows, LANES), factors.dtype)],
        compiler_params=params(16),
        cost_estimate=pl.CostEstimate(flops=0, bytes_accessed=factors.size, transcendentals=0),
    )(owners, factors)


def pick_kernel(step, cols, last, flag_ref, keep_ref, got_ref, *refs):
    first_ref, second_ref = refs[-2:]
    same = flag_ref[:, step:step + 1]
    differs = 1 - same

    def chosen(at, size):
        place = slice(at, at + size)
        return keep_ref[:, place] * same + got_ref[:, place] * differs

    if last:
        first_ref[...] = chosen(0, cols)
        second_ref[...] = chosen(cols, keep_ref.shape[1] - cols)
    else:
        size = keep_ref.shape[1] - first_ref.shape[1]
        shared = chosen(2 * size, keep_ref.shape[1] - 2 * size)
        for part, out_ref in enumerate((first_ref, second_ref)):
            out_ref[:, :size] = chosen(part * size, size)
            out_ref[:, size:] = shared


def pick(flags, keep, got, step, cols, count, after):
    rows, width = keep.shape
    if count > 1:
        widths = [width - count // 2 * cols] * 2
    else:
        widths = [cols, width - cols]
    return pl.pallas_call(
        functools.partial(pick_kernel, step, cols, count == 1),
        in_specs=in_vmem(3) + in_place(len(after)),
        out_specs=in_vmem(2),
        out_shape=[jax.ShapeDtypeStruct((rows, w), keep.dtype) for w in widths],
        compiler_params=params(16),
        cost_estimate=pl.CostEstimate(flops=0, bytes_accessed=2 * keep.size, transcendentals=0),
    )(flags, keep, got, *after)


def join_kernel(first_ref, second_ref, _, out_ref):
    rows = first_ref.shape[0]
    out_ref[:rows, :] = first_ref[...]
    out_ref[rows:, :] = second_ref[...]


def join(first, second, after):
    rows, width = first.shape
    return pl.pallas_call(
        join_kernel,
        in_specs=in_vmem(2) + in_place(1),
        out_specs=in_vmem(1)[0],
        out_shape=jax.ShapeDtypeStruct((2 * rows, width), first.dtype),
        compiler_params=params(16),
        cost_estimate=pl.CostEstimate(flops=0, bytes_accessed=first.size, transcendentals=0),
    )(first, second, after)


def mark_kernel(give_ref, out_ref):
    out_ref[...] = give_ref[:, :out_ref.shape[1]]


def mark(give):
    return pl.pallas_call(
        mark_kernel,
        in_specs=in_vmem(1),
        out_specs=in_vmem(1)[0],
        out_shape=jax.ShapeDtypeStruct((give.shape[0], LANES), give.dtype),
        compiler_params=params(16),
        cost_estimate=pl.CostEstimate(flops=0, bytes_accessed=1, transcendentals=0),
    )(give)


def cut_grads_kernel(ids_ref, grad_ref, _, out_ref):
    count, rows, width = out_ref.shape
    cols = width - LANES
    row = lax.broadcasted_iota(jnp.int32, (rows, LANES), 0)
    ids = jnp.zeros((rows, LANES), jnp.int32)
    for t in range(rows):
        ids = jnp.where(row == t, ids_ref[t], ids)
    ids = ids.astype(jnp.float32).astype(out_ref.dtype)
    for to in range(count):
        out_ref[to, :, :cols] = grad_ref[:, to * cols:(to + 1) * cols]
        out_ref[to, :, cols:] = ids


def cut_grads(ids, grads, after, count):
    rows, hidden = grads.shape
    return pl.pallas_call(
        cut_grads_kernel,
        in_specs=in_smem(1) + in_vmem(1) + in_place(1),
        out_specs=in_vmem(1)[0],
        out_shape=jax.ShapeDtypeStruct((count, rows, hidden // count + LANES), grads.dtype),
        compiler_params=params(16),
        cost_estimate=pl.CostEstimate(flops=0, bytes_accessed=grads.size, transcendentals=0),
    )(ids, grads, after)


def rotate_kernel(order, *refs):
    act_refs, (basis_ref, out_ref, held_ref, sems) = refs[:-4], refs[-4:]
    act_refs = [act_refs[n].at[at:at + size, :] for n, at, size in order]
    depth, width = basis_ref.shape
    places = [slice(k * depth, (k + 1) * depth) for k in range(width // depth)]
    copies = [
        pltpu.make_async_copy(basis_ref.at[:, cols], held_ref.at[k], sems.at[k])
        for k, cols in enumerate(places)
    ]
    for copy in copies:
        copy.start()
    for k, cols in enumerate(places):
        act = jnp.concatenate([ref[:, cols] for ref in act_refs], axis=0)
        copies[k].wait()
        out_ref[:, cols] = jnp.dot(
            act, held_ref[k], preferred_element_type=jnp.float32
        ).astype(jnp.bfloat16)


def rotate(act_pieces, order, basis):
    tokens = sum(x.shape[0] for x in act_pieces)
    depth, width = basis.shape
    count = width // depth
    return pl.pallas_call(
        functools.partial(rotate_kernel, order),
        in_specs=in_vmem(len(act_pieces)) + in_place(1),
        out_specs=in_vmem(1)[0],
        out_shape=jax.ShapeDtypeStruct((tokens, width), jnp.bfloat16),
        scratch_shapes=[
            pltpu.VMEM((count, depth, depth), jnp.bfloat16),
            pltpu.SemaphoreType.DMA((count,)),
        ],
        compiler_params=params(48 if tokens <= 256 else 40),
        cost_estimate=pl.CostEstimate(
            flops=2 * tokens * width * depth, bytes_accessed=basis.size, transcendentals=0
        ),
    )(*act_pieces, basis)


def image_kernel(batch_count, rot_ref, *refs):
    left_refs, half_refs = refs[:batch_count], refs[batch_count:3 * batch_count]
    eig_ref, out_ref, right_ref, turn_ref, pre_a, pre_b = refs[3 * batch_count:]
    rows, width = eig_ref.shape
    half = pre_a.shape[0] // batch_count
    chunk = pre_a.shape[1]
    per = width // chunk
    phases = (rows // half) * per
    tile = min(256, chunk)

    @pl.when(pl.program_id(0) == 0)
    def _():
        side = width // 2
        for b in range(batch_count):
            for other in range(2):
                at = pl.multiple_of(((lax.axis_index("wide") & 1) ^ other) * side, side)
                right_ref[b, :, pl.ds(at, side)] = half_refs[2 * b + other][...]

    for b in range(batch_count):
        turn_ref[b] = left_refs[b][...].T
    out_ref[...] = jnp.zeros_like(out_ref)

    def place(k):
        return pl.multiple_of((k // per) * half, half), (k % per) * chunk

    def produce(k, s, pre):
        row, col = place(k)
        cols = pl.ds(pl.multiple_of(col + s * tile, tile), tile)
        part = min(128, half)
        for at in range(0, half, part):
            some = pl.ds(pl.multiple_of(row + at, part), part)
            damped = eig_ref[some, cols].astype(jnp.float32) + damping
            inverse = pl.reciprocal(damped, approx=True)
            for b in range(batch_count):
                outer_sum = jnp.dot(
                    turn_ref[b, some, :], right_ref[b, :, cols], preferred_element_type=jnp.float32
                )
                pre[b * half + at:b * half + at + part, s * tile:(s + 1) * tile] = (
                    outer_sum * inverse
                ).astype(jnp.bfloat16)

    def absorb(k, pre):
        row, col = place(k)
        rot = rot_ref[:, pl.ds(pl.multiple_of(col, chunk), chunk)]
        for b in range(batch_count):
            out_ref[b, :, pl.ds(row, half)] += lax.dot_general(
                rot, pre[b * half:(b + 1) * half, :], (((1,), (1,)), ((), ())),
                preferred_element_type=jnp.float32,
            )

    def both(k, pre_now, pre_next):
        absorb(k, pre_now)
        for s in range(chunk // tile):
            produce(k + 1, s, pre_next)

    for s in range(chunk // tile):
        produce(0, s, pre_a)

    def pair(q, carry):
        both(2 * q, pre_a, pre_b)
        both(2 * q + 1, pre_b, pre_a)
        return carry

    lax.fori_loop(0, phases // 2 - 1, pair, 0)
    both(phases - 2, pre_a, pre_b)
    absorb(phases - 1, pre_b)


def images(rot, lefts, halves, eigenvalues):
    batch_count, tokens = len(lefts), rot.shape[0]
    hidden, width = eigenvalues.shape
    rows = min(512, hidden)
    half = min(256, rows)
    chunk = min(1024, width // 2)
    return pl.pallas_call(
        functools.partial(image_kernel, batch_count),
        grid=(hidden // rows,),
        in_specs=[whole_block(rot.shape)]
        + [pl.BlockSpec((QT, rows), lambda i: (0, i)) for x in lefts]
        + [whole_block(x.shape) for x in halves]
        + [pl.BlockSpec((rows, width), lambda i: (i, 0))],
        out_specs=pl.BlockSpec((batch_count, tokens, rows), lambda i: (0, 0, i)),
        out_shape=jax.ShapeDtypeStruct((batch_count, tokens, hidden), jnp.float32),
        scratch_shapes=[
            pltpu.VMEM((batch_count, QT, width), jnp.bfloat16),
            pltpu.VMEM((batch_count, rows, QT), jnp.bfloat16),
            pltpu.VMEM((batch_count * half, chunk), jnp.bfloat16),
            pltpu.VMEM((batch_count * half, chunk), jnp.bfloat16),
        ],
        compiler_params=params(32 if tokens <= 256 else 56),
        cost_estimate=pl.CostEstimate(
            flops=2 * hidden * width * (tokens + 256) * batch_count,
            bytes_accessed=2 * hidden * width,
            transcendentals=0,
        ),
    )(rot, *lefts, *halves, eigenvalues)


def score_kernel(batch_count, grad_ref, basis_ref, image_ref, ids_ref, out_ref, token_ref):
    step = pl.program_id(0)
    me = lax.axis_index("wide")

    @pl.when(step == 0)
    def _():
        token_ref[...] = jnp.zeros_like(token_ref)

    order = [me ^ r for r in range(grad_ref.shape[0])]
    grads = jnp.concatenate([grad_ref[n] for n in order], axis=0)
    turned = jnp.dot(grads, basis_ref[...], preferred_element_type=jnp.float32)
    turned = turned.astype(jnp.bfloat16).astype(jnp.float32)
    for b in range(batch_count):
        token_ref[b] += jnp.sum(image_ref[b] * turned, axis=1, keepdims=True)

    @pl.when(step == pl.num_programs(0) - 1)
    def _():
        ids = jnp.concatenate([ids_ref[n] for n in order], axis=0).astype(jnp.float32)
        seqs = lax.broadcasted_iota(jnp.int32, ids.shape, 1).astype(jnp.float32)
        member = ids == seqs
        for b in range(batch_count):
            sums = jnp.sum(jnp.where(member, token_ref[b], 0.0), axis=0, keepdims=True)
            out_ref[b:b + 1, :] = sums[:, :out_ref.shape[1]]


def score_parts(grads, grad_basis, image, seq_count):
    batch_count, tokens = image.shape[:2]
    count, rows, width = grads.shape
    hidden = width - LANES
    inner = min(grad_basis.shape[0], hidden)
    return pl.pallas_call(
        functools.partial(score_kernel, batch_count),
        grid=(hidden // inner,),
        in_specs=[
            pl.BlockSpec((count, rows, inner), lambda i: (0, 0, i)),
            pl.BlockSpec((grad_basis.shape[0], inner), lambda i: (0, i)),
            pl.BlockSpec((batch_count, tokens, inner), lambda i: (0, 0, i)),
            pl.BlockSpec((count, rows, LANES), lambda i: (0, 0, hidden // LANES)),
        ],
        out_specs=pl.BlockSpec((batch_count, seq_count), lambda i: (0, 0)),
        out_shape=jax.ShapeDtypeStruct((batch_count, seq_count), jnp.float32),
        scratch_shapes=[pltpu.VMEM((batch_count, tokens, 1), jnp.float32)],
        compiler_params=params(44),
        cost_estimate=pl.CostEstimate(
            flops=2 * tokens * hidden * grad_basis.shape[0],
            bytes_accessed=4 * image.size,
            transcendentals=0,
        ),
    )(grads, grad_basis, image, grads)


def per_device(
    train_act, train_grad, seq_ids, act_basis, grad_basis, eigenvalues, query_factors, owners
):
    wide_count = lax.axis_size("wide")
    bits = [1 << n for n in range(wide_count.bit_length() - 1)]
    me = lax.axis_index("wide")
    tok_local = train_act.shape[0]
    seq_count = tok_local * wide_count // SEQ_MEAN
    cols = grad_basis.shape[1]
    hidden = train_grad.shape[1]
    batch_count = owners.shape[0]
    score_scale = 1.0 / math.sqrt(FF * D * QT * SEQ_MEAN)
    batch = lax.axis_index("groups") % batch_count

    order = [0]
    for bit in reversed(bits):
        order = order + [r + bit for r in order]
    order = sorted(order, key=lambda r: [r & bit for bit in bits])
    acts, ranks = train_act, [0]
    far = bits[:1:-1]
    keep, give, flags = cut_factors(owners, query_factors, order, hidden)
    count = wide_count // 2
    after = []
    for step, bit in enumerate(bits):
        got = swap(give, "wide", bit)
        keep, give = pick(flags, keep, got, step, cols, count, after)
        count //= 2
        after = []
        if step < len(far):
            acts = join(acts, swap(acts, "wide", far[step]), give)
            ranks = ranks + [r + far[step] for r in ranks]
            after = [acts]
        if step == len(bits) - 2:
            sent = cut_grads(seq_ids, train_grad, swap(mark(give), "wide", 1), wide_count)
            grads = lax.all_to_all(sent, "wide", 0, 0)
    left, right = keep, give
    pieces = [(acts, ranks)]
    for bit in (2, 1):
        pieces += [(swap(x, "wide", bit), [r + bit for r in has]) for x, has in pieces]
    token_order = [None] * wide_count
    for n, (_, has) in enumerate(pieces):
        for at, r in enumerate(has):
            token_order[r] = (n, at * tok_local, tok_local)
    rot = rotate([x for x, _ in pieces], token_order, act_basis)

    lefts = [left, swap(left, "groups", 1)]
    halves = []
    for x in (right, swap(right, "groups", 1)):
        halves += [x, swap(x, "wide", 1)]

    image = images(rot, lefts, halves, eigenvalues)
    parts = score_parts(grads, grad_basis, image, seq_count)
    for near in (bits[:2], bits[2:]):
        step = near[0]
        others = [swap(parts, "wide", step * n) for n in range(1, 1 << len(near))]
        parts = parts + sum(others)
    mine, others = parts[0], parts[1]
    first = jnp.where(batch == 0, mine, others)
    second = jnp.where(batch == 0, others, mine)
    return jnp.stack([first, second], axis=1) * score_scale


def solution(mesh):
    return jax.shard_map(
        per_device,
        mesh=mesh,
        in_specs=(
            P(("groups", "wide"), None),
            P(("groups", "wide"), None),
            P(("groups", "wide")),
            P(),
            P(None, "wide"),
            P("wide", None),
            P("wide", None, None),
            P(),
        ),
        out_specs=P("groups", None),
        check_vma=False,
    )
```

```python
import functools
import math

import jax
import jax.numpy as jnp
from jax import lax
from jax.experimental import pallas as pl
from jax.experimental.pallas import tpu as pltpu
from jax.sharding import PartitionSpec as P

D = 4096
FF = 32768
SEQ_MEAN = 32
QT = 16
LANES = 128


damping = 0.1


def params(mib):
    return pltpu.CompilerParams(vmem_limit_bytes=mib * 1024 * 1024)


def whole_block(shape):
    return pl.BlockSpec(shape, lambda *_: (0,) * len(shape), pipeline_mode=pl.Buffered(1))


def swap(x, axis, bit):
    count = lax.axis_size(axis)
    return lax.ppermute(x, axis, [(i, i ^ bit) for i in range(count)])


def in_smem(n):
    return [pl.BlockSpec(memory_space=pltpu.SMEM)] * n


def in_vmem(n):
    return [pl.BlockSpec(memory_space=pltpu.VMEM)] * n


def in_place(n):
    return [pl.BlockSpec(memory_space=pl.ANY)] * n


def cut_factors_kernel(order, hidden, batch_count, owners_ref, fac_ref, keep_ref, give_ref, flag_ref):
    cols = hidden // len(order)
    half = (fac_ref.shape[2] - hidden) // 2
    me, batch = lax.axis_index("wide"), lax.rem(lax.axis_index("groups"), batch_count)
    for part, out_ref in enumerate((keep_ref, give_ref)):
        picked = order[part * len(order) // 2:(part + 1) * len(order) // 2]
        for at, r in enumerate(picked):
            src = pl.multiple_of((me ^ r) * cols, cols)
            out_ref[:, at * cols:(at + 1) * cols] = fac_ref[batch, :, pl.ds(src, cols)]
        src = pl.multiple_of(hidden + ((me & 1) ^ part) * half, LANES)
        out_ref[:, len(picked) * cols:] = fac_ref[batch, :, pl.ds(src, half)]
    apart = owners_ref[batch] ^ me
    lane = lax.broadcasted_iota(jnp.int32, flag_ref.shape, 1)
    flags = jnp.zeros(flag_ref.shape, jnp.float32)
    for step in range(len(order).bit_length() - 1):
        same = jnp.where((apart & (1 << step)) == 0, 1.0, 0.0)
        flags = jnp.where(lane == step, same, flags)
    flag_ref[...] = flags.astype(flag_ref.dtype)


def cut_factors(owners, factors, order, hidden):
    batch_count, rows, width = owners.shape[0], *factors.shape[1:]
    half = jax.ShapeDtypeStruct((rows, width // 2), factors.dtype)
    return pl.pallas_call(
        functools.partial(cut_factors_kernel, order, hidden, batch_count),
        in_specs=in_smem(1) + in_vmem(1),
        out_specs=in_vmem(3),
        out_shape=[half] * 2 + [jax.ShapeDtypeStruct((rows, LANES), factors.dtype)],
        compiler_params=params(16),
        cost_estimate=pl.CostEstimate(flops=0, bytes_accessed=factors.size, transcendentals=0),
    )(owners, factors)


def pick_kernel(step, cols, last, flag_ref, keep_ref, got_ref, *refs):
    first_ref, second_ref = refs[-2:]
    same = flag_ref[:, step:step + 1]
    differs = 1 - same

    def chosen(at, size):
        place = slice(at, at + size)
        return keep_ref[:, place] * same + got_ref[:, place] * differs

    if last:
        first_ref[...] = chosen(0, cols)
        second_ref[...] = chosen(cols, keep_ref.shape[1] - cols)
    else:
        size = keep_ref.shape[1] - first_ref.shape[1]
        shared = chosen(2 * size, keep_ref.shape[1] - 2 * size)
        for part, out_ref in enumerate((first_ref, second_ref)):
            out_ref[:, :size] = chosen(part * size, size)
            out_ref[:, size:] = shared


def pick(flags, keep, got, step, cols, count, after):
    rows, width = keep.shape
    if count > 1:
        widths = [width - count // 2 * cols] * 2
    else:
        widths = [cols, width - cols]
    return pl.pallas_call(
        functools.partial(pick_kernel, step, cols, count == 1),
        in_specs=in_vmem(3) + in_place(len(after)),
        out_specs=in_vmem(2),
        out_shape=[jax.ShapeDtypeStruct((rows, w), keep.dtype) for w in widths],
        compiler_params=params(16),
        cost_estimate=pl.CostEstimate(flops=0, bytes_accessed=2 * keep.size, transcendentals=0),
    )(flags, keep, got, *after)


def join_kernel(first_ref, second_ref, _, out_ref):
    rows = first_ref.shape[0]
    out_ref[:rows, :] = first_ref[...]
    out_ref[rows:, :] = second_ref[...]


def join(first, second, after):
    rows, width = first.shape
    return pl.pallas_call(
        join_kernel,
        in_specs=in_vmem(2) + in_place(1),
        out_specs=in_vmem(1)[0],
        out_shape=jax.ShapeDtypeStruct((2 * rows, width), first.dtype),
        compiler_params=params(16),
        cost_estimate=pl.CostEstimate(flops=0, bytes_accessed=first.size, transcendentals=0),
    )(first, second, after)


def gate_kernel(*_):
    pass


def gate(array, after):
    return pl.pallas_call(
        gate_kernel,
        in_specs=in_place(1 + len(after)),
        out_specs=in_place(1)[0],
        out_shape=jax.ShapeDtypeStruct(array.shape, array.dtype),
        input_output_aliases={0: 0},
        compiler_params=params(1),
        cost_estimate=pl.CostEstimate(flops=0, bytes_accessed=1, transcendentals=0),
    )(array, *after)


def cut_grads_kernel(ids_ref, grad_ref, _, out_ref):
    count, rows, width = out_ref.shape
    cols = width - LANES
    row = lax.broadcasted_iota(jnp.int32, (rows, LANES), 0)
    ids = jnp.zeros((rows, LANES), jnp.int32)
    for t in range(rows):
        ids = jnp.where(row == t, ids_ref[t], ids)
    ids = ids.astype(jnp.float32).astype(out_ref.dtype)
    for to in range(count):
        out_ref[to, :, :cols] = grad_ref[:, to * cols:(to + 1) * cols]
        out_ref[to, :, cols:] = ids


def cut_grads(ids, grads, after, count):
    rows, hidden = grads.shape
    return pl.pallas_call(
        cut_grads_kernel,
        in_specs=in_smem(1) + in_vmem(1) + in_place(1),
        out_specs=in_vmem(1)[0],
        out_shape=jax.ShapeDtypeStruct((count, rows, hidden // count + LANES), grads.dtype),
        compiler_params=params(16),
        cost_estimate=pl.CostEstimate(flops=0, bytes_accessed=grads.size, transcendentals=0),
    )(ids, grads, after)


def rotate_kernel(*refs):
    act_refs, (basis_ref, out_ref, held_ref, sems) = refs[:-4], refs[-4:]
    depth, width = basis_ref.shape
    places = [slice(k * depth, (k + 1) * depth) for k in range(width // depth)]
    copies = [
        pltpu.make_async_copy(basis_ref.at[:, cols], held_ref.at[k], sems.at[k])
        for k, cols in enumerate(places)
    ]
    for copy in copies:
        copy.start()
    for k, cols in enumerate(places):
        act = jnp.concatenate([ref[:, cols] for ref in act_refs], axis=0)
        copies[k].wait()
        turned = jnp.dot(act, held_ref[k], preferred_element_type=jnp.float32)
        out_ref[cols, :] = turned.astype(jnp.bfloat16).T


def rotate(act_pieces, basis):
    tokens = sum(x.shape[0] for x in act_pieces)
    depth, width = basis.shape
    count = width // depth
    return pl.pallas_call(
        rotate_kernel,
        in_specs=in_vmem(len(act_pieces)) + in_place(1),
        out_specs=in_vmem(1)[0],
        out_shape=jax.ShapeDtypeStruct((width, tokens), jnp.bfloat16),
        scratch_shapes=[
            pltpu.VMEM((count, depth, depth), jnp.bfloat16),
            pltpu.SemaphoreType.DMA((count,)),
        ],
        compiler_params=params(48 if tokens <= 256 else 40),
        cost_estimate=pl.CostEstimate(
            flops=2 * tokens * width * depth, bytes_accessed=basis.size, transcendentals=0
        ),
    )(*act_pieces, basis)


def image_kernel(batch_count, rot_ref, *refs):
    left_refs, half_refs = refs[:batch_count], refs[batch_count:3 * batch_count]
    eig_ref, out_ref, right_ref, turn_ref, pre_a, pre_b = refs[3 * batch_count:]
    rows, width = eig_ref.shape
    chunk = pre_a.shape[1]
    phases = width // chunk
    tile = min(256, chunk)

    @pl.when(pl.program_id(0) == 0)
    def _():
        side = width // 2
        for b in range(batch_count):
            for other in range(2):
                at = pl.multiple_of(((lax.axis_index("wide") & 1) ^ other) * side, side)
                right_ref[b, :, pl.ds(at, side)] = half_refs[2 * b + other][...]

    for b in range(batch_count):
        turn_ref[b] = left_refs[b][...].T

    def produce(k, s, pre):
        cols = slice(k * chunk + s * tile, k * chunk + (s + 1) * tile)
        damped = eig_ref[:, cols].astype(jnp.float32) + damping
        inverse = pl.reciprocal(damped, approx=True)
        for b in range(batch_count):
            outer_sum = jnp.dot(
                turn_ref[b], right_ref[b, :, cols], preferred_element_type=jnp.float32
            )
            pre[b * rows:(b + 1) * rows, s * tile:(s + 1) * tile] = (
                outer_sum * inverse
            ).astype(jnp.bfloat16)

    def absorb(k, pre):
        more = jnp.dot(
            pre[...], rot_ref[k * chunk:(k + 1) * chunk, :], preferred_element_type=jnp.float32
        )
        for b in range(batch_count):
            part = more[b * rows:(b + 1) * rows, :]
            out_ref[b] = part if k == 0 else out_ref[b] + part

    for s in range(chunk // tile):
        produce(0, s, pre_a)
    for k in range(phases):
        now, later = (pre_a, pre_b) if k % 2 == 0 else (pre_b, pre_a)
        if k + 1 < phases:
            for s in range(chunk // tile):
                produce(k + 1, s, later)
        absorb(k, now)


def images(rot, lefts, halves, eigenvalues):
    batch_count, tokens = len(lefts), rot.shape[1]
    hidden, width = eigenvalues.shape
    rows = min(512, hidden)
    chunk = min(1024 if tokens <= 256 else 512, width // 2)
    return pl.pallas_call(
        functools.partial(image_kernel, batch_count),
        grid=(hidden // rows,),
        in_specs=[whole_block(rot.shape)]
        + [pl.BlockSpec((QT, rows), lambda i: (0, i)) for x in lefts]
        + [whole_block(x.shape) for x in halves]
        + [pl.BlockSpec((rows, width), lambda i: (i, 0))],
        out_specs=pl.BlockSpec((batch_count, rows, tokens), lambda i: (0, i, 0)),
        out_shape=jax.ShapeDtypeStruct((batch_count, hidden, tokens), jnp.float32),
        scratch_shapes=[
            pltpu.VMEM((batch_count, QT, width), jnp.bfloat16),
            pltpu.VMEM((batch_count, rows, QT), jnp.bfloat16),
            pltpu.VMEM((batch_count * rows, chunk), jnp.bfloat16),
            pltpu.VMEM((batch_count * rows, chunk), jnp.bfloat16),
        ],
        compiler_params=params(50),
        cost_estimate=pl.CostEstimate(
            flops=2 * hidden * width * (tokens + 256) * batch_count,
            bytes_accessed=2 * hidden * width,
            transcendentals=0,
        ),
    )(rot, *lefts, *halves, eigenvalues)


def score_kernel(batch_count, ranks, grad_ref, basis_ref, image_ref, ids_ref, out_ref, token_ref):
    step = pl.program_id(0)
    me = lax.axis_index("wide")

    @pl.when(step == 0)
    def _():
        token_ref[...] = jnp.zeros_like(token_ref)

    grads = jnp.concatenate([grad_ref[me ^ r] for r in ranks], axis=0)
    turned = jnp.dot(grads, basis_ref[...], preferred_element_type=jnp.float32)
    turned = turned.astype(jnp.bfloat16).T.astype(jnp.float32)
    for b in range(batch_count):
        token_ref[b:b + 1, :] += jnp.sum(image_ref[b] * turned, axis=0, keepdims=True)

    @pl.when(step == pl.num_programs(0) - 1)
    def _():
        ids = jnp.concatenate([ids_ref[me ^ r] for r in ranks], axis=0).astype(jnp.float32)
        seqs = lax.broadcasted_iota(jnp.int32, ids.shape, 1).astype(jnp.float32)
        member = jnp.where(ids == seqs, 1.0, 0.0).T
        for b in range(batch_count):
            sums = jnp.sum(member * token_ref[b:b + 1, :], axis=1, keepdims=True)
            out_ref[b] = sums[:out_ref.shape[1], :]


def score_parts(grads, ranks, grad_basis, image, seq_count):
    batch_count, _, tokens = image.shape
    count, rows, width = grads.shape
    hidden = width - LANES
    inner = min(grad_basis.shape[0], hidden)
    return pl.pallas_call(
        functools.partial(score_kernel, batch_count, ranks),
        grid=(hidden // inner,),
        in_specs=[
            pl.BlockSpec((count, rows, inner), lambda i: (0, 0, i)),
            pl.BlockSpec((grad_basis.shape[0], inner), lambda i: (0, i)),
            pl.BlockSpec((batch_count, inner, tokens), lambda i: (0, i, 0)),
            pl.BlockSpec((count, rows, LANES), lambda i: (0, 0, hidden // LANES)),
        ],
        out_specs=pl.BlockSpec((batch_count, seq_count, 1), lambda i: (0, 0, 0)),
        out_shape=jax.ShapeDtypeStruct((batch_count, seq_count, 1), jnp.float32),
        scratch_shapes=[pltpu.VMEM((8, tokens), jnp.float32)],
        compiler_params=params(56),
        cost_estimate=pl.CostEstimate(
            flops=2 * tokens * hidden * grad_basis.shape[0],
            bytes_accessed=4 * image.size,
            transcendentals=0,
        ),
    )(grads, grad_basis, image, grads)[:, :, 0]


def per_device(
    train_act, train_grad, seq_ids, act_basis, grad_basis, eigenvalues, query_factors, owners
):
    wide_count = lax.axis_size("wide")
    bits = [1 << n for n in range(wide_count.bit_length() - 1)]
    me = lax.axis_index("wide")
    tok_local = train_act.shape[0]
    seq_count = tok_local * wide_count // SEQ_MEAN
    cols = grad_basis.shape[1]
    hidden = train_grad.shape[1]
    batch_count = owners.shape[0]
    score_scale = 1.0 / math.sqrt(FF * D * QT * SEQ_MEAN)
    batch = lax.axis_index("groups") % batch_count

    order = [0]
    for bit in reversed(bits):
        order = order + [r + bit for r in order]
    order = sorted(order, key=lambda r: [r & bit for bit in bits])
    acts, ranks = train_act, [0]
    far = bits[:1:-1]
    keep, give, flags = cut_factors(owners, query_factors, order, hidden)
    count = wide_count // 2
    after = []
    pieces = []
    for step, bit in enumerate(bits):
        got = swap(give, "wide", bit)
        keep, give = pick(flags, keep, got, step, cols, count, after)
        count //= 2
        after = []
        if step < len(far) - 1:
            acts = join(acts, swap(acts, "wide", far[step]), give)
            ranks = ranks + [r + far[step] for r in ranks]
            after = [acts]
        elif step == len(far) - 1:
            last = swap(acts, "wide", far[step])
            held = gate(acts, [give])
            pieces = [(acts, ranks), (swap(held, "wide", 2), [r + 2 for r in ranks])]
            after = [held]
        elif step == len(far):
            ranks = [r + far[-1] for r in ranks]
            held = gate(last, [give])
            pieces += [(held, ranks), (swap(held, "wide", 2), [r + 2 for r in ranks])]
            sent = cut_grads(seq_ids, train_grad, give, wide_count)
    left, right = keep, give
    for n in (1, 3):
        pieces[n] = (gate(pieces[n][0], [right]), pieces[n][1])
    pieces += [(swap(x, "wide", 1), [r + 1 for r in has]) for x, has in pieces]
    rot = rotate([x for x, _ in pieces], act_basis)
    ranks = [r for _, has in pieces for r in has]

    lefts = [left, swap(left, "groups", 1)]
    other = swap(right, "groups", 1)
    halves = []
    for x in (right, other):
        halves += [x, swap(x, "wide", 1)]

    grads = lax.all_to_all(gate(sent, [rot, other]), "wide", 0, 0)

    image = images(rot, lefts, halves, eigenvalues)
    parts = score_parts(grads, ranks, grad_basis, image, seq_count)
    for near in (bits[:2], bits[2:]):
        step = near[0]
        others = [swap(parts, "wide", step * n) for n in range(1, 1 << len(near))]
        parts = parts + sum(others)
    mine, others = parts[0], parts[1]
    first = jnp.where(batch == 0, mine, others)
    second = jnp.where(batch == 0, others, mine)
    return jnp.stack([first, second], axis=1) * score_scale


def solution(mesh):
    return jax.shard_map(
        per_device,
        mesh=mesh,
        in_specs=(
            P(("groups", "wide"), None),
            P(("groups", "wide"), None),
            P(("groups", "wide")),
            P(),
            P(None, "wide"),
            P("wide", None),
            P("wide", None, None),
            P(),
        ),
        out_specs=P("groups", None),
        check_vma=False,
    )
```

```python
import functools
import math

import jax
import jax.numpy as jnp
from jax import lax
from jax.experimental import pallas as pl
from jax.experimental.pallas import tpu as pltpu
from jax.sharding import PartitionSpec as P

D = 4096
FF = 32768
SEQ_MEAN = 32
QT = 16
LANES = 128


damping = 0.1


def params(mib):
    return pltpu.CompilerParams(vmem_limit_bytes=mib * 1024 * 1024)


def whole_block(shape):
    return pl.BlockSpec(shape, lambda *_: (0,) * len(shape), pipeline_mode=pl.Buffered(1))


def swap(x, axis, bit):
    count = lax.axis_size(axis)
    return lax.ppermute(x, axis, [(i, i ^ bit) for i in range(count)])


def in_smem(n):
    return [pl.BlockSpec(memory_space=pltpu.SMEM)] * n


def in_vmem(n):
    return [pl.BlockSpec(memory_space=pltpu.VMEM)] * n


def in_place(n):
    return [pl.BlockSpec(memory_space=pl.ANY)] * n


def cut_factors_kernel(order, hidden, batch_count, fac_ref, keep_ref, give_ref):
    cols = hidden // len(order)
    half = (fac_ref.shape[2] - hidden) // 2
    me, batch = lax.axis_index("wide"), lax.rem(lax.axis_index("groups"), batch_count)
    for part, out_ref in enumerate((keep_ref, give_ref)):
        picked = order[part * len(order) // 2:(part + 1) * len(order) // 2]
        for at, r in enumerate(picked):
            src = pl.multiple_of((me ^ r) * cols, cols)
            out_ref[:, at * cols:(at + 1) * cols] = fac_ref[batch, :, pl.ds(src, cols)]
        src = pl.multiple_of(hidden + ((me & 1) ^ part) * half, LANES)
        out_ref[:, len(picked) * cols:] = fac_ref[batch, :, pl.ds(src, half)]


def cut_factors(factors, order, hidden, batch_count):
    rows, width = factors.shape[1:]
    half = jax.ShapeDtypeStruct((rows, width // 2), factors.dtype)
    return pl.pallas_call(
        functools.partial(cut_factors_kernel, order, hidden, batch_count),
        in_specs=in_vmem(1),
        out_specs=in_vmem(2),
        out_shape=[half] * 2,
        compiler_params=params(16),
        cost_estimate=pl.CostEstimate(flops=0, bytes_accessed=factors.size, transcendentals=0),
    )(factors)


def flags_kernel(ways, batch_count, owners_ref, _, flag_ref):
    me, batch = lax.axis_index("wide"), lax.rem(lax.axis_index("groups"), batch_count)
    apart = owners_ref[batch] ^ me
    lane = lax.broadcasted_iota(jnp.int32, flag_ref.shape, 1)
    flags = jnp.zeros(flag_ref.shape, jnp.float32)
    for step, bit in enumerate(ways):
        same = jnp.where((apart & bit) == 0, 1.0, 0.0)
        flags = jnp.where(lane == step, same, flags)
    flag_ref[...] = flags.astype(flag_ref.dtype)


def owner_flags(owners, ways, after):
    return pl.pallas_call(
        functools.partial(flags_kernel, ways, owners.shape[0]),
        in_specs=in_smem(1) + in_place(1),
        out_specs=in_vmem(1)[0],
        out_shape=jax.ShapeDtypeStruct((after.shape[0], LANES), after.dtype),
        compiler_params=params(16),
        cost_estimate=pl.CostEstimate(flops=0, bytes_accessed=1, transcendentals=0),
    )(owners, after)


def pick_kernel(step, cols, last, flag_ref, keep_ref, got_ref, *refs):
    first_ref, second_ref = refs[-2:]
    same = flag_ref[:, step:step + 1]
    differs = 1 - same

    def chosen(at, size):
        place = slice(at, at + size)
        return keep_ref[:, place] * same + got_ref[:, place] * differs

    if last:
        first_ref[...] = chosen(0, cols)
        second_ref[...] = chosen(cols, keep_ref.shape[1] - cols)
    else:
        size = keep_ref.shape[1] - first_ref.shape[1]
        shared = chosen(2 * size, keep_ref.shape[1] - 2 * size)
        for part, out_ref in enumerate((first_ref, second_ref)):
            out_ref[:, :size] = chosen(part * size, size)
            out_ref[:, size:] = shared


def pick(flags, keep, got, step, cols, count, after):
    rows, width = keep.shape
    if count > 1:
        widths = [width - count // 2 * cols] * 2
    else:
        widths = [cols, width - cols]
    return pl.pallas_call(
        functools.partial(pick_kernel, step, cols, count == 1),
        in_specs=in_vmem(3) + in_place(len(after)),
        out_specs=in_vmem(2),
        out_shape=[jax.ShapeDtypeStruct((rows, w), keep.dtype) for w in widths],
        compiler_params=params(16),
        cost_estimate=pl.CostEstimate(flops=0, bytes_accessed=2 * keep.size, transcendentals=0),
    )(flags, keep, got, *after)


def join_kernel(first_ref, second_ref, _, out_ref):
    rows = first_ref.shape[0]
    out_ref[:rows, :] = first_ref[...]
    out_ref[rows:, :] = second_ref[...]


def join(first, second, after):
    rows, width = first.shape
    return pl.pallas_call(
        join_kernel,
        in_specs=in_vmem(2) + in_place(1),
        out_specs=in_vmem(1)[0],
        out_shape=jax.ShapeDtypeStruct((2 * rows, width), first.dtype),
        compiler_params=params(16),
        cost_estimate=pl.CostEstimate(flops=0, bytes_accessed=first.size, transcendentals=0),
    )(first, second, after)


def gate_kernel(*_):
    pass


def gate(array, after):
    return pl.pallas_call(
        gate_kernel,
        in_specs=in_place(1 + len(after)),
        out_specs=in_place(1)[0],
        out_shape=jax.ShapeDtypeStruct(array.shape, array.dtype),
        input_output_aliases={0: 0},
        compiler_params=params(1),
        cost_estimate=pl.CostEstimate(flops=0, bytes_accessed=1, transcendentals=0),
    )(array, *after)


def cut_grads_kernel(ids_ref, grad_ref, _, out_ref):
    count, rows, width = out_ref.shape
    cols = width - LANES
    row = lax.broadcasted_iota(jnp.int32, (rows, LANES), 0)
    ids = jnp.zeros((rows, LANES), jnp.int32)
    for t in range(rows):
        ids = jnp.where(row == t, ids_ref[t], ids)
    ids = ids.astype(jnp.float32).astype(out_ref.dtype)
    for to in range(count):
        out_ref[to, :, :cols] = grad_ref[:, to * cols:(to + 1) * cols]
        out_ref[to, :, cols:] = ids


def cut_grads(ids, grads, after, count):
    rows, hidden = grads.shape
    return pl.pallas_call(
        cut_grads_kernel,
        in_specs=in_smem(1) + in_vmem(1) + in_place(1),
        out_specs=in_vmem(1)[0],
        out_shape=jax.ShapeDtypeStruct((count, rows, hidden // count + LANES), grads.dtype),
        compiler_params=params(16),
        cost_estimate=pl.CostEstimate(flops=0, bytes_accessed=grads.size, transcendentals=0),
    )(ids, grads, after)


def rotate_kernel(act_count, *refs):
    act_refs, (basis_ref, out_ref, held_ref, sems) = refs[:act_count], refs[act_count:]
    depth, width = basis_ref.shape
    places = [slice(k * depth, (k + 1) * depth) for k in range(width // depth)]
    copies = [
        pltpu.make_async_copy(basis_ref.at[:, cols], held_ref.at[k], sems.at[k])
        for k, cols in enumerate(places)
    ]
    for copy in copies:
        copy.start()
    for k, cols in enumerate(places):
        act = jnp.concatenate([ref[:, cols] for ref in act_refs], axis=0)
        copies[k].wait()
        turned = jnp.dot(act, held_ref[k], preferred_element_type=jnp.float32)
        out_ref[cols, :] = turned.astype(jnp.bfloat16).T


def rotate(act_pieces, basis):
    tokens = sum(x.shape[0] for x in act_pieces)
    depth, width = basis.shape
    count = width // depth
    return pl.pallas_call(
        functools.partial(rotate_kernel, len(act_pieces)),
        in_specs=in_vmem(len(act_pieces)) + in_place(1),
        out_specs=in_vmem(2),
        out_shape=[
            jax.ShapeDtypeStruct((width, tokens), jnp.bfloat16),
            jax.ShapeDtypeStruct((count, depth, depth), jnp.bfloat16),
        ],
        scratch_shapes=[pltpu.SemaphoreType.DMA((count,))],
        compiler_params=params(46 if tokens <= 256 else 32),
        cost_estimate=pl.CostEstimate(
            flops=2 * tokens * width * depth, bytes_accessed=basis.size, transcendentals=0
        ),
    )(*act_pieces, basis)


def rotate_rest_kernel(act_count, *refs):
    act_refs, (held_ref, first_ref, out_ref) = refs[:act_count], refs[act_count:]
    depth = held_ref.shape[1]
    done = first_ref.shape[1]
    out_ref[:, :done] = first_ref[...]
    for k in range(held_ref.shape[0]):
        cols = slice(k * depth, (k + 1) * depth)
        act = jnp.concatenate([ref[:, cols] for ref in act_refs], axis=0)
        turned = jnp.dot(act, held_ref[k], preferred_element_type=jnp.float32)
        out_ref[cols, done:] = turned.astype(jnp.bfloat16).T


def rotate_rest(act_pieces, held, first):
    width, done = first.shape
    tokens = done + sum(x.shape[0] for x in act_pieces)
    return pl.pallas_call(
        functools.partial(rotate_rest_kernel, len(act_pieces)),
        in_specs=in_vmem(len(act_pieces) + 2),
        out_specs=in_vmem(1)[0],
        out_shape=jax.ShapeDtypeStruct((width, tokens), jnp.bfloat16),
        compiler_params=params(16 if tokens <= 256 else 32),
        cost_estimate=pl.CostEstimate(
            flops=2 * tokens * held.size, bytes_accessed=held.size, transcendentals=0
        ),
    )(*act_pieces, held, first)


def image_kernel(batch_count, total, per, rot_ref, *refs):
    left_refs, half_refs = refs[:batch_count], refs[batch_count:3 * batch_count]
    eig_ref, out_ref, right_ref, turn_ref, pre_a, pre_b = refs[3 * batch_count:]
    rows, chunk = eig_ref.shape
    tile = min(256, chunk)
    s = pl.program_id(0)

    @pl.when(s == 0)
    def _():
        side = right_ref.shape[2] // 2
        for b in range(batch_count):
            for other in range(2):
                at = pl.multiple_of(((lax.axis_index("wide") & 1) ^ other) * side, side)
                right_ref[b, :, pl.ds(at, side)] = half_refs[2 * b + other][...]

    @pl.when(jnp.logical_and(lax.rem(s, per) == 0, s < total))
    def _():
        for b in range(batch_count):
            turn_ref[b] = left_refs[b][...].T

    @pl.when(lax.rem(s, per) == 1)
    def _():
        out_ref[...] = jnp.zeros_like(out_ref)

    def produce(pre):
        start = lax.rem(s, per) * chunk
        for at in range(0, chunk, tile):
            cols = pl.ds(pl.multiple_of(start + at, tile), tile)
            damped = eig_ref[:, at:at + tile].astype(jnp.float32) + damping
            inverse = pl.reciprocal(damped, approx=True)
            for b in range(batch_count):
                outer_sum = jnp.dot(
                    turn_ref[b], right_ref[b, :, cols], preferred_element_type=jnp.float32
                )
                pre[b * rows:(b + 1) * rows, at:at + tile] = (
                    outer_sum * inverse
                ).astype(jnp.bfloat16)

    def absorb(pre):
        rot = rot_ref[pl.ds(pl.multiple_of(lax.rem(s - 1, per) * chunk, chunk), chunk), :]
        for b in range(batch_count):
            out_ref[b] += jnp.dot(
                pre[b * rows:(b + 1) * rows, :], rot, preferred_element_type=jnp.float32
            )

    between = jnp.logical_and(s > 0, s < total)
    odd = lax.rem(s, 2) == 1

    @pl.when(s == 0)
    def _():
        produce(pre_a)

    @pl.when(jnp.logical_and(between, odd))
    def _():
        produce(pre_b)
        absorb(pre_a)

    @pl.when(jnp.logical_and(between, jnp.logical_not(odd)))
    def _():
        produce(pre_a)
        absorb(pre_b)

    @pl.when(s == total)
    def _():
        absorb(pre_a if total % 2 else pre_b)


def images(rot, lefts, halves, eigenvalues):
    batch_count, tokens = len(lefts), rot.shape[1]
    hidden, width = eigenvalues.shape
    rows = min(1024, hidden)
    chunk = min(1024, width // 2)
    per = width // chunk
    total = hidden // rows * per
    now = lambda s: jnp.minimum(s, total - 1)
    before = lambda s: jnp.maximum(s - 1, 0)
    return pl.pallas_call(
        functools.partial(image_kernel, batch_count, total, per),
        grid=(total + 1,),
        in_specs=[whole_block(rot.shape)]
        + [pl.BlockSpec((QT, rows), lambda s: (0, now(s) // per)) for _ in lefts]
        + [whole_block(x.shape) for x in halves]
        + [pl.BlockSpec((rows, chunk), lambda s: (now(s) // per, now(s) % per))],
        out_specs=pl.BlockSpec((batch_count, rows, tokens), lambda s: (0, before(s) // per, 0)),
        out_shape=jax.ShapeDtypeStruct((batch_count, hidden, tokens), jnp.float32),
        scratch_shapes=[
            pltpu.VMEM((batch_count, QT, width), jnp.bfloat16),
            pltpu.VMEM((batch_count, rows, QT), jnp.bfloat16),
            pltpu.VMEM((batch_count * rows, chunk), jnp.bfloat16),
            pltpu.VMEM((batch_count * rows, chunk), jnp.bfloat16),
        ],
        compiler_params=params(44),
        cost_estimate=pl.CostEstimate(
            flops=2 * hidden * width * (tokens + 256) * batch_count,
            bytes_accessed=2 * hidden * width,
            transcendentals=0,
        ),
    )(rot, *lefts, *halves, eigenvalues)


def score_kernel(batch_count, ranks, grad_ref, basis_ref, image_ref, ids_ref, out_ref, token_ref):
    step = pl.program_id(0)
    me = lax.axis_index("wide")

    @pl.when(step == 0)
    def _():
        token_ref[...] = jnp.zeros_like(token_ref)

    grads = jnp.concatenate([grad_ref[me ^ r] for r in ranks], axis=0)
    turned = jnp.dot(grads, basis_ref[...], preferred_element_type=jnp.float32)
    turned = turned.astype(jnp.bfloat16).T.astype(jnp.float32)
    for b in range(batch_count):
        token_ref[b:b + 1, :] += jnp.sum(image_ref[b] * turned, axis=0, keepdims=True)

    @pl.when(step == pl.num_programs(0) - 1)
    def _():
        ids = jnp.concatenate([ids_ref[me ^ r] for r in ranks], axis=0).astype(jnp.float32)
        seqs = lax.broadcasted_iota(jnp.int32, ids.shape, 1).astype(jnp.float32)
        member = jnp.where(ids == seqs, 1.0, 0.0).T
        for b in range(batch_count):
            sums = jnp.sum(member * token_ref[b:b + 1, :], axis=1, keepdims=True)
            out_ref[b] = sums[:out_ref.shape[1], :]


def score_parts(grads, ranks, grad_basis, image, seq_count):
    batch_count, _, tokens = image.shape
    count, rows, width = grads.shape
    hidden = width - LANES
    inner = min(grad_basis.shape[0], hidden)
    return pl.pallas_call(
        functools.partial(score_kernel, batch_count, ranks),
        grid=(hidden // inner,),
        in_specs=[
            pl.BlockSpec((count, rows, inner), lambda i: (0, 0, i)),
            pl.BlockSpec((grad_basis.shape[0], inner), lambda i: (0, i)),
            pl.BlockSpec((batch_count, inner, tokens), lambda i: (0, i, 0)),
            pl.BlockSpec((count, rows, LANES), lambda i: (0, 0, hidden // LANES)),
        ],
        out_specs=pl.BlockSpec((batch_count, seq_count, 1), lambda i: (0, 0, 0)),
        out_shape=jax.ShapeDtypeStruct((batch_count, seq_count, 1), jnp.float32),
        scratch_shapes=[pltpu.VMEM((8, tokens), jnp.float32)],
        compiler_params=params(44),
        cost_estimate=pl.CostEstimate(
            flops=2 * tokens * hidden * grad_basis.shape[0],
            bytes_accessed=4 * image.size,
            transcendentals=0,
        ),
    )(grads, grad_basis, image, grads)


def per_device(
    train_act, train_grad, seq_ids, act_basis, grad_basis, eigenvalues, query_factors, owners
):
    wide_count = lax.axis_size("wide")
    bits = [1 << n for n in range(wide_count.bit_length() - 1)]
    me = lax.axis_index("wide")
    tok_local = train_act.shape[0]
    seq_count = tok_local * wide_count // SEQ_MEAN
    cols = grad_basis.shape[1]
    hidden = train_grad.shape[1]
    batch_count = owners.shape[0]
    score_scale = 1.0 / math.sqrt(FF * D * QT * SEQ_MEAN)
    batch = lax.axis_index("groups") % batch_count

    ways = bits[:2] + bits[:1:-1]
    order = [0]
    for bit in reversed(bits):
        order = order + [r + bit for r in order]
    order = sorted(order, key=lambda r: [r & bit for bit in ways])
    acts, ranks = train_act, [0]
    far = bits[:1:-1]
    keep, give = cut_factors(query_factors, order, hidden, batch_count)
    flags = owner_flags(owners, ways, keep)
    count = wide_count // 2
    after = []
    pieces = []
    for step, bit in enumerate(ways):
        got = swap(give, "wide", bit)
        keep, give = pick(flags, keep, got, step, cols, count, after)
        count //= 2
        after = []
        if step < len(far) - 1:
            acts = join(acts, swap(acts, "wide", far[step]), give)
            ranks = ranks + [r + far[step] for r in ranks]
            after = [acts]
        elif step == len(far) - 1:
            last = swap(acts, "wide", far[step])
            held = gate(acts, [give])
            near = [(acts, ranks)]
            over = [(swap(held, "wide", 2), [r + 2 for r in ranks])]
            sent = cut_grads(seq_ids, train_grad, give, wide_count)
            after = [held, sent]
        elif step == len(far):
            ranks = [r + far[-1] for r in ranks]
            held = gate(last, [give])
            near += [(held, ranks)]
            over += [(swap(held, "wide", 2), [r + 2 for r in ranks])]
            near += [(swap(x, "wide", 1), [r + 1 for r in has]) for x, has in near]
            first, basis = rotate([x for x, _ in near], act_basis)
            after = [first]
    left, right = keep, give

    lefts = [left, swap(left, "groups", 1)]
    other = swap(right, "groups", 1)
    halves = []
    for x in (right, other):
        halves += [x, swap(x, "wide", 1)]
    over = [(gate(x, [right]), has) for x, has in over]
    over += [(swap(x, "wide", 1), [r + 1 for r in has]) for x, has in over]
    rot = rotate_rest([x for x, _ in over], basis, first)
    ranks = [r for _, has in near + over for r in has]

    grads = lax.all_to_all(gate(sent, [rot, halves[-1]]), "wide", 0, 0)

    image = images(rot, lefts, halves, eigenvalues)
    parts = score_parts(grads, ranks, grad_basis, image, seq_count)
    for some in (bits[:2], bits[2:]):
        others = [swap(parts, "wide", some[0] * n) for n in range(1, 1 << len(some))]
        parts = parts + sum(others)
    mine, others = parts[0, :, 0], parts[1, :, 0]
    first = jnp.where(batch == 0, mine, others)
    second = jnp.where(batch == 0, others, mine)
    return jnp.stack([first, second], axis=1) * score_scale


def solution(mesh):
    return jax.shard_map(
        per_device,
        mesh=mesh,
        in_specs=(
            P(("groups", "wide"), None),
            P(("groups", "wide"), None),
            P(("groups", "wide")),
            P(),
            P(None, "wide"),
            P("wide", None),
            P("wide", None, None),
            P(),
        ),
        out_specs=P("groups", None),
        check_vma=False,
    )
```

```python
import functools
import math

import jax
import jax.numpy as jnp
from jax import lax
from jax.experimental import pallas as pl
from jax.experimental.pallas import tpu as pltpu
from jax.sharding import PartitionSpec as P

D = 4096
FF = 32768
SEQ_MEAN = 32
QT = 16
LANES = 128


damping = 0.1


def params(mib):
    return pltpu.CompilerParams(vmem_limit_bytes=mib * 1024 * 1024)


def whole_block(shape):
    return pl.BlockSpec(shape, lambda *_: (0,) * len(shape), pipeline_mode=pl.Buffered(1))


def swap(x, axis, bit):
    count = lax.axis_size(axis)
    return lax.ppermute(x, axis, [(i, i ^ bit) for i in range(count)])


def in_smem(n):
    return [pl.BlockSpec(memory_space=pltpu.SMEM)] * n


def in_vmem(n):
    return [pl.BlockSpec(memory_space=pltpu.VMEM)] * n


def in_place(n):
    return [pl.BlockSpec(memory_space=pl.ANY)] * n


def cut_factors_kernel(order, hidden, batch_count, fac_ref, keep_ref, give_ref):
    cols = hidden // len(order)
    half = (fac_ref.shape[2] - hidden) // 2
    me, batch = lax.axis_index("wide"), lax.rem(lax.axis_index("groups"), batch_count)
    for part, out_ref in enumerate((keep_ref, give_ref)):
        picked = order[part * len(order) // 2:(part + 1) * len(order) // 2]
        for at, r in enumerate(picked):
            src = pl.multiple_of((me ^ r) * cols, cols)
            out_ref[:, at * cols:(at + 1) * cols] = fac_ref[batch, :, pl.ds(src, cols)]
        src = pl.multiple_of(hidden + ((me & 1) ^ part) * half, LANES)
        out_ref[:, len(picked) * cols:] = fac_ref[batch, :, pl.ds(src, half)]


def cut_factors(factors, order, hidden, batch_count):
    rows, width = factors.shape[1:]
    half = jax.ShapeDtypeStruct((rows, width // 2), factors.dtype)
    return pl.pallas_call(
        functools.partial(cut_factors_kernel, order, hidden, batch_count),
        in_specs=in_vmem(1),
        out_specs=in_vmem(2),
        out_shape=[half] * 2,
        compiler_params=params(16),
        cost_estimate=pl.CostEstimate(flops=0, bytes_accessed=1, transcendentals=0),
    )(factors)


def flags_kernel(ways, batch_count, owners_ref, _, flag_ref):
    me, batch = lax.axis_index("wide"), lax.rem(lax.axis_index("groups"), batch_count)
    apart = owners_ref[batch] ^ me
    lane = lax.broadcasted_iota(jnp.int32, flag_ref.shape, 1)
    flags = jnp.zeros(flag_ref.shape, jnp.float32)
    for step, bit in enumerate(ways):
        same = jnp.where((apart & bit) == 0, 1.0, 0.0)
        flags = jnp.where(lane == step, same, flags)
    flag_ref[...] = flags.astype(flag_ref.dtype)


def owner_flags(owners, ways, after):
    return pl.pallas_call(
        functools.partial(flags_kernel, ways, owners.shape[0]),
        in_specs=in_smem(1) + in_place(1),
        out_specs=in_vmem(1)[0],
        out_shape=jax.ShapeDtypeStruct((after.shape[0], LANES), after.dtype),
        compiler_params=params(16),
        cost_estimate=pl.CostEstimate(flops=0, bytes_accessed=1, transcendentals=0),
    )(owners, after)


def pick_kernel(step, cols, last, flag_ref, keep_ref, got_ref, *refs):
    first_ref, second_ref = refs[-2:]
    same = flag_ref[:, step:step + 1]
    differs = 1 - same

    def chosen(at, size):
        place = slice(at, at + size)
        return keep_ref[:, place] * same + got_ref[:, place] * differs

    if last:
        first_ref[...] = chosen(0, cols)
        second_ref[...] = chosen(cols, keep_ref.shape[1] - cols)
    else:
        size = keep_ref.shape[1] - first_ref.shape[1]
        shared = chosen(2 * size, keep_ref.shape[1] - 2 * size)
        for part, out_ref in enumerate((first_ref, second_ref)):
            out_ref[:, :size] = chosen(part * size, size)
            out_ref[:, size:] = shared


def pick(flags, keep, got, step, cols, count, after):
    rows, width = keep.shape
    if count > 1:
        widths = [width - count // 2 * cols] * 2
    else:
        widths = [cols, width - cols]
    return pl.pallas_call(
        functools.partial(pick_kernel, step, cols, count == 1),
        in_specs=in_vmem(3) + in_place(len(after)),
        out_specs=in_vmem(2),
        out_shape=[jax.ShapeDtypeStruct((rows, w), keep.dtype) for w in widths],
        compiler_params=params(16),
        cost_estimate=pl.CostEstimate(flops=0, bytes_accessed=1, transcendentals=0),
    )(flags, keep, got, *after)


def join_kernel(first_ref, second_ref, out_ref):
    rows = first_ref.shape[0]
    out_ref[:rows, :] = first_ref[...]
    out_ref[rows:, :] = second_ref[...]


def join(first, second):
    rows, width = first.shape
    return pl.pallas_call(
        join_kernel,
        in_specs=in_vmem(2),
        out_specs=in_vmem(1)[0],
        out_shape=jax.ShapeDtypeStruct((2 * rows, width), first.dtype),
        compiler_params=params(16),
        cost_estimate=pl.CostEstimate(flops=0, bytes_accessed=1, transcendentals=0),
    )(first, second)


def gate_kernel(*_):
    pass


def gate(array, after):
    return pl.pallas_call(
        gate_kernel,
        in_specs=in_place(1 + len(after)),
        out_specs=in_place(1)[0],
        out_shape=jax.ShapeDtypeStruct(array.shape, array.dtype),
        input_output_aliases={0: 0},
        compiler_params=params(1),
        cost_estimate=pl.CostEstimate(flops=0, bytes_accessed=1, transcendentals=0),
    )(array, *after)


def cut_grads_kernel(ids_ref, grad_ref, _, out_ref):
    count, rows, width = out_ref.shape
    cols = width - LANES
    row = lax.broadcasted_iota(jnp.int32, (rows, LANES), 0)
    ids = jnp.zeros((rows, LANES), jnp.int32)
    for t in range(rows):
        ids = jnp.where(row == t, ids_ref[t], ids)
    ids = ids.astype(jnp.float32).astype(out_ref.dtype)
    for to in range(count):
        out_ref[to, :, :cols] = grad_ref[:, to * cols:(to + 1) * cols]
        out_ref[to, :, cols:] = ids


def cut_grads(ids, grads, after, count):
    rows, hidden = grads.shape
    return pl.pallas_call(
        cut_grads_kernel,
        in_specs=in_smem(1) + in_vmem(1) + in_place(1),
        out_specs=in_vmem(1)[0],
        out_shape=jax.ShapeDtypeStruct((count, rows, hidden // count + LANES), grads.dtype),
        compiler_params=params(16),
        cost_estimate=pl.CostEstimate(flops=0, bytes_accessed=1, transcendentals=0),
    )(ids, grads, after)


def rotate_kernel(act_count, *refs):
    act_refs, (basis_ref, _, out_ref, held_ref, sems) = refs[:act_count], refs[act_count:]
    depth, width = basis_ref.shape
    places = [slice(k * depth, (k + 1) * depth) for k in range(width // depth)]
    copies = [
        pltpu.make_async_copy(basis_ref.at[:, cols], held_ref.at[k], sems.at[k])
        for k, cols in enumerate(places)
    ]
    for copy in copies:
        copy.start()
    for k, cols in enumerate(places):
        act = jnp.concatenate([ref[:, cols] for ref in act_refs], axis=0)
        copies[k].wait()
        turned = jnp.dot(act, held_ref[k], preferred_element_type=jnp.float32)
        out_ref[cols, :] = turned.astype(jnp.bfloat16).T


def rotate(act_pieces, basis, after):
    tokens = sum(x.shape[0] for x in act_pieces)
    depth, width = basis.shape
    count = width // depth
    return pl.pallas_call(
        functools.partial(rotate_kernel, len(act_pieces)),
        in_specs=in_vmem(len(act_pieces)) + in_place(2),
        out_specs=in_vmem(2),
        out_shape=[
            jax.ShapeDtypeStruct((width, tokens), jnp.bfloat16),
            jax.ShapeDtypeStruct((count, depth, depth), jnp.bfloat16),
        ],
        scratch_shapes=[pltpu.SemaphoreType.DMA((count,))],
        compiler_params=params(46 if tokens <= 256 else 32),
        cost_estimate=pl.CostEstimate(flops=0, bytes_accessed=1, transcendentals=0),
    )(*act_pieces, basis, after)


def rotate_rest_kernel(act_count, *refs):
    act_refs, (held_ref, first_ref, out_ref) = refs[:act_count], refs[act_count:]
    depth = held_ref.shape[1]
    done = first_ref.shape[1]
    out_ref[:, :done] = first_ref[...]
    for k in range(held_ref.shape[0]):
        cols = slice(k * depth, (k + 1) * depth)
        act = jnp.concatenate([ref[:, cols] for ref in act_refs], axis=0)
        turned = jnp.dot(act, held_ref[k], preferred_element_type=jnp.float32)
        out_ref[cols, done:] = turned.astype(jnp.bfloat16).T


def rotate_rest(act_pieces, held, first):
    width, done = first.shape
    tokens = done + sum(x.shape[0] for x in act_pieces)
    return pl.pallas_call(
        functools.partial(rotate_rest_kernel, len(act_pieces)),
        in_specs=in_vmem(len(act_pieces) + 2),
        out_specs=in_vmem(1)[0],
        out_shape=jax.ShapeDtypeStruct((width, tokens), jnp.bfloat16),
        compiler_params=params(16 if tokens <= 256 else 32),
        cost_estimate=pl.CostEstimate(flops=0, bytes_accessed=1, transcendentals=0),
    )(*act_pieces, held, first)


def image_kernel(batch_count, total, per, rot_ref, *refs):
    left_refs, half_refs = refs[:batch_count], refs[batch_count:3 * batch_count]
    eig_ref, out_ref, right_ref, turn_ref, pre_a, pre_b = refs[3 * batch_count:]
    rows, chunk = eig_ref.shape
    tile = min(256, chunk)
    s = pl.program_id(0)

    @pl.when(s == 0)
    def _():
        side = right_ref.shape[2] // 2
        for b in range(batch_count):
            for other in range(2):
                at = pl.multiple_of(((lax.axis_index("wide") & 1) ^ other) * side, side)
                right_ref[b, :, pl.ds(at, side)] = half_refs[2 * b + other][...]

    @pl.when(jnp.logical_and(lax.rem(s, per) == 0, s < total))
    def _():
        for b in range(batch_count):
            turn_ref[b] = left_refs[b][...].T

    @pl.when(lax.rem(s, per) == 1)
    def _():
        out_ref[...] = jnp.zeros_like(out_ref)

    def produce(pre):
        start = lax.rem(s, per) * chunk
        for at in range(0, chunk, tile):
            cols = pl.ds(pl.multiple_of(start + at, tile), tile)
            damped = eig_ref[:, at:at + tile].astype(jnp.float32) + damping
            inverse = pl.reciprocal(damped, approx=True)
            for b in range(batch_count):
                outer_sum = jnp.dot(
                    turn_ref[b], right_ref[b, :, cols], preferred_element_type=jnp.float32
                )
                pre[b * rows:(b + 1) * rows, at:at + tile] = (
                    outer_sum * inverse
                ).astype(jnp.bfloat16)

    def absorb(pre):
        rot = rot_ref[pl.ds(pl.multiple_of(lax.rem(s - 1, per) * chunk, chunk), chunk), :]
        for b in range(batch_count):
            out_ref[b] += jnp.dot(
                pre[b * rows:(b + 1) * rows, :], rot, preferred_element_type=jnp.float32
            )

    between = jnp.logical_and(s > 0, s < total)
    odd = lax.rem(s, 2) == 1

    @pl.when(s == 0)
    def _():
        produce(pre_a)

    @pl.when(jnp.logical_and(between, odd))
    def _():
        produce(pre_b)
        absorb(pre_a)

    @pl.when(jnp.logical_and(between, jnp.logical_not(odd)))
    def _():
        produce(pre_a)
        absorb(pre_b)

    @pl.when(s == total)
    def _():
        absorb(pre_a if total % 2 else pre_b)


def images(rot, lefts, halves, eigenvalues):
    batch_count, tokens = len(lefts), rot.shape[1]
    hidden, width = eigenvalues.shape
    rows = min(1024, hidden)
    chunk = min(1024, width // 2)
    per = width // chunk
    total = hidden // rows * per
    now = lambda s: jnp.minimum(s, total - 1)
    before = lambda s: jnp.maximum(s - 1, 0)
    return pl.pallas_call(
        functools.partial(image_kernel, batch_count, total, per),
        grid=(total + 1,),
        in_specs=[whole_block(rot.shape)]
        + [pl.BlockSpec((QT, rows), lambda s: (0, now(s) // per)) for _ in lefts]
        + [whole_block(x.shape) for x in halves]
        + [pl.BlockSpec((rows, chunk), lambda s: (now(s) // per, now(s) % per))],
        out_specs=pl.BlockSpec((batch_count, rows, tokens), lambda s: (0, before(s) // per, 0)),
        out_shape=jax.ShapeDtypeStruct((batch_count, hidden, tokens), jnp.float32),
        scratch_shapes=[
            pltpu.VMEM((batch_count, QT, width), jnp.bfloat16),
            pltpu.VMEM((batch_count, rows, QT), jnp.bfloat16),
            pltpu.VMEM((batch_count * rows, chunk), jnp.bfloat16),
            pltpu.VMEM((batch_count * rows, chunk), jnp.bfloat16),
        ],
        compiler_params=params(50),
        cost_estimate=pl.CostEstimate(
            flops=2 * hidden * width * (tokens + 256) * batch_count,
            bytes_accessed=2 * hidden * width,
            transcendentals=0,
        ),
    )(rot, *lefts, *halves, eigenvalues)


def score_kernel(batch_count, ranks, grad_ref, basis_ref, image_ref, ids_ref, out_ref, token_ref):
    step = pl.program_id(0)
    me = lax.axis_index("wide")

    @pl.when(step == 0)
    def _():
        token_ref[...] = jnp.zeros_like(token_ref)

    grads = jnp.concatenate([grad_ref[me ^ r] for r in ranks], axis=0)
    turned = jnp.dot(grads, basis_ref[...], preferred_element_type=jnp.float32)
    turned = turned.astype(jnp.bfloat16).T.astype(jnp.float32)
    for b in range(batch_count):
        token_ref[b:b + 1, :] += jnp.sum(image_ref[b] * turned, axis=0, keepdims=True)

    @pl.when(step == pl.num_programs(0) - 1)
    def _():
        ids = jnp.concatenate([ids_ref[me ^ r] for r in ranks], axis=0).astype(jnp.float32)
        seqs = lax.broadcasted_iota(jnp.int32, ids.shape, 1).astype(jnp.float32)
        member = jnp.where(ids == seqs, 1.0, 0.0).T
        for b in range(batch_count):
            sums = jnp.sum(member * token_ref[b:b + 1, :], axis=1, keepdims=True)
            out_ref[b] = sums[:out_ref.shape[1], :]


def score_parts(grads, ranks, grad_basis, image, seq_count):
    batch_count, _, tokens = image.shape
    count, rows, width = grads.shape
    hidden = width - LANES
    inner = min(grad_basis.shape[0], hidden)
    return pl.pallas_call(
        functools.partial(score_kernel, batch_count, ranks),
        grid=(hidden // inner,),
        in_specs=[
            pl.BlockSpec((count, rows, inner), lambda i: (0, 0, i)),
            pl.BlockSpec((grad_basis.shape[0], inner), lambda i: (0, i)),
            pl.BlockSpec((batch_count, inner, tokens), lambda i: (0, i, 0)),
            pl.BlockSpec((count, rows, LANES), lambda i: (0, 0, hidden // LANES)),
        ],
        out_specs=pl.BlockSpec((batch_count, seq_count, 1), lambda i: (0, 0, 0)),
        out_shape=jax.ShapeDtypeStruct((batch_count, seq_count, 1), jnp.float32),
        scratch_shapes=[pltpu.VMEM((8, tokens), jnp.float32)],
        compiler_params=params(56),
        cost_estimate=pl.CostEstimate(
            flops=2 * tokens * hidden * grad_basis.shape[0],
            bytes_accessed=4 * image.size,
            transcendentals=0,
        ),
    )(grads, grad_basis, image, grads)


def per_device(
    train_act, train_grad, seq_ids, act_basis, grad_basis, eigenvalues, query_factors, owners
):
    wide_count = lax.axis_size("wide")
    bits = [1 << n for n in range(wide_count.bit_length() - 1)]
    me = lax.axis_index("wide")
    tok_local = train_act.shape[0]
    seq_count = tok_local * wide_count // SEQ_MEAN
    cols = grad_basis.shape[1]
    hidden = train_grad.shape[1]
    batch_count = owners.shape[0]
    score_scale = 1.0 / math.sqrt(FF * D * QT * SEQ_MEAN)
    batch = lax.axis_index("groups") % batch_count

    ways = bits[:2] + bits[:1:-1]
    order = [0]
    for bit in reversed(bits):
        order = order + [r + bit for r in order]
    order = sorted(order, key=lambda r: [r & bit for bit in ways])
    acts, ranks = train_act, [0]
    far = bits[:1:-1]
    keep, give = cut_factors(query_factors, order, hidden, batch_count)
    flags = owner_flags(owners, ways, keep)
    count = wide_count // 2
    for step, bit in enumerate(ways):
        got = swap(give, "wide", bit)
        if step < len(far) - 1:
            acts = join(acts, swap(acts, "wide", far[step]))
            ranks = ranks + [r + far[step] for r in ranks]
            after = [acts]
        elif step == len(far) - 1:
            last = swap(acts, "wide", far[step])
            sent = cut_grads(seq_ids, train_grad, give, wide_count)
            after = [last, sent]
        elif step == len(far):
            after = [over[0][0], first]
        else:
            after = []
        keep, give = pick(flags, keep, got, step, cols, count, after)
        count //= 2
        if step == len(far) - 1:
            near = [(gate(acts, [give]), ranks), (gate(last, [give]), [r + far[step] for r in ranks])]
            over = [(swap(x, "wide", 2), [r + 2 for r in has]) for x, has in near]
            near += [(swap(x, "wide", 1), [r + 1 for r in has]) for x, has in near]
            first, basis = rotate([x for x, _ in near], act_basis, give)
    left, right = keep, give

    lefts = [left, swap(left, "groups", 1)]
    other = swap(right, "groups", 1)
    halves = []
    for x in (right, other):
        halves += [x, swap(x, "wide", 1)]
    over = [(gate(x, [wait]), has) for (x, has), wait in zip(over, (right, other))]
    over += [(swap(x, "wide", 1), [r + 1 for r in has]) for x, has in over]
    rot = rotate_rest([x for x, _ in over], basis, first)
    ranks = [r for _, has in near + over for r in has]

    grads = lax.all_to_all(gate(sent, [rot, lefts[1], halves[1], halves[3]]), "wide", 0, 0)

    image = images(rot, lefts, halves, eigenvalues)
    parts = score_parts(grads, ranks, grad_basis, image, seq_count)
    for some in (bits[:2], bits[2:]):
        others = [swap(parts, "wide", some[0] * n) for n in range(1, 1 << len(some))]
        parts = parts + sum(others)
    mine, others = parts[0, :, 0], parts[1, :, 0]
    first = jnp.where(batch == 0, mine, others)
    second = jnp.where(batch == 0, others, mine)
    return jnp.stack([first, second], axis=1) * score_scale


def solution(mesh):
    return jax.shard_map(
        per_device,
        mesh=mesh,
        in_specs=(
            P(("groups", "wide"), None),
            P(("groups", "wide"), None),
            P(("groups", "wide")),
            P(),
            P(None, "wide"),
            P("wide", None),
            P("wide", None, None),
            P(),
        ),
        out_specs=P("groups", None),
        check_vma=False,
    )
```

```python
import functools
import math

import jax
import jax.numpy as jnp
from jax import lax
from jax.experimental import pallas as pl
from jax.experimental.pallas import tpu as pltpu
from jax.sharding import PartitionSpec as P

D = 4096
FF = 32768
SEQ_MEAN = 32
QT = 16
LANES = 128


damping = 0.1


def params(mib):
    return pltpu.CompilerParams(vmem_limit_bytes=mib * 1024 * 1024)


def whole_block(shape):
    return pl.BlockSpec(shape, lambda *_: (0,) * len(shape), pipeline_mode=pl.Buffered(1))


def swap(x, axis, bit):
    count = lax.axis_size(axis)
    return lax.ppermute(x, axis, [(i, i ^ bit) for i in range(count)])


def in_smem(n):
    return [pl.BlockSpec(memory_space=pltpu.SMEM)] * n


def in_vmem(n):
    return [pl.BlockSpec(memory_space=pltpu.VMEM)] * n


def in_place(n):
    return [pl.BlockSpec(memory_space=pl.ANY)] * n


def cut_factors_kernel(order, hidden, batch_count, fac_ref, keep_ref, give_ref):
    cols = hidden // len(order)
    half = (fac_ref.shape[2] - hidden) // 2
    me, batch = lax.axis_index("wide"), lax.rem(lax.axis_index("groups"), batch_count)
    for part, out_ref in enumerate((keep_ref, give_ref)):
        picked = order[part * len(order) // 2:(part + 1) * len(order) // 2]
        for at, r in enumerate(picked):
            src = pl.multiple_of((me ^ r) * cols, cols)
            out_ref[:, at * cols:(at + 1) * cols] = fac_ref[batch, :, pl.ds(src, cols)]
        src = pl.multiple_of(hidden + ((me & 1) ^ part) * half, LANES)
        out_ref[:, len(picked) * cols:] = fac_ref[batch, :, pl.ds(src, half)]


def cut_factors(factors, order, hidden, batch_count):
    rows, width = factors.shape[1:]
    half = jax.ShapeDtypeStruct((rows, width // 2), factors.dtype)
    return pl.pallas_call(
        functools.partial(cut_factors_kernel, order, hidden, batch_count),
        in_specs=in_vmem(1),
        out_specs=in_vmem(2),
        out_shape=[half] * 2,
        compiler_params=params(16),
        cost_estimate=pl.CostEstimate(flops=0, bytes_accessed=1, transcendentals=0),
    )(factors)


def flags_kernel(ways, batch_count, owners_ref, _, flag_ref):
    me, batch = lax.axis_index("wide"), lax.rem(lax.axis_index("groups"), batch_count)
    apart = owners_ref[batch] ^ me
    lane = lax.broadcasted_iota(jnp.int32, flag_ref.shape, 1)
    flags = jnp.zeros(flag_ref.shape, jnp.float32)
    for step, bit in enumerate(ways):
        same = jnp.where((apart & bit) == 0, 1.0, 0.0)
        flags = jnp.where(lane == step, same, flags)
    flag_ref[...] = flags.astype(flag_ref.dtype)


def owner_flags(owners, ways, after):
    return pl.pallas_call(
        functools.partial(flags_kernel, ways, owners.shape[0]),
        in_specs=in_smem(1) + in_place(1),
        out_specs=in_vmem(1)[0],
        out_shape=jax.ShapeDtypeStruct((after.shape[0], LANES), after.dtype),
        compiler_params=params(16),
        cost_estimate=pl.CostEstimate(flops=0, bytes_accessed=1, transcendentals=0),
    )(owners, after)


def pick_kernel(step, cols, last, flag_ref, keep_ref, got_ref, *refs):
    first_ref, second_ref = refs[-2:]
    same = flag_ref[:, step:step + 1]
    differs = 1 - same

    def chosen(at, size):
        place = slice(at, at + size)
        return keep_ref[:, place] * same + got_ref[:, place] * differs

    if last:
        first_ref[...] = chosen(0, cols)
        second_ref[...] = chosen(cols, keep_ref.shape[1] - cols)
    else:
        size = keep_ref.shape[1] - first_ref.shape[1]
        shared = chosen(2 * size, keep_ref.shape[1] - 2 * size)
        for part, out_ref in enumerate((first_ref, second_ref)):
            out_ref[:, :size] = chosen(part * size, size)
            out_ref[:, size:] = shared


def pick(flags, keep, got, step, cols, count, after):
    rows, width = keep.shape
    if count > 1:
        widths = [width - count // 2 * cols] * 2
    else:
        widths = [cols, width - cols]
    return pl.pallas_call(
        functools.partial(pick_kernel, step, cols, count == 1),
        in_specs=in_vmem(3) + in_place(len(after)),
        out_specs=in_vmem(2),
        out_shape=[jax.ShapeDtypeStruct((rows, w), keep.dtype) for w in widths],
        compiler_params=params(16),
        cost_estimate=pl.CostEstimate(flops=0, bytes_accessed=1, transcendentals=0),
    )(flags, keep, got, *after)


def join_kernel(first_ref, second_ref, _, out_ref):
    rows = first_ref.shape[0]
    out_ref[:rows, :] = first_ref[...]
    out_ref[rows:, :] = second_ref[...]


def join(first, second, after):
    rows, width = first.shape
    return pl.pallas_call(
        join_kernel,
        in_specs=in_vmem(2) + in_place(1),
        out_specs=in_vmem(1)[0],
        out_shape=jax.ShapeDtypeStruct((2 * rows, width), first.dtype),
        compiler_params=params(16),
        cost_estimate=pl.CostEstimate(flops=0, bytes_accessed=1, transcendentals=0),
    )(first, second, after)


def gate_kernel(*_):
    pass


def gate(array, after):
    return pl.pallas_call(
        gate_kernel,
        in_specs=in_place(1 + len(after)),
        out_specs=in_place(1)[0],
        out_shape=jax.ShapeDtypeStruct(array.shape, array.dtype),
        input_output_aliases={0: 0},
        compiler_params=params(1),
        cost_estimate=pl.CostEstimate(flops=0, bytes_accessed=1, transcendentals=0),
    )(array, *after)


def grads_core_kernel(ids_ref, grad_ref, _, out_ref):
    rows, hidden = grad_ref.shape
    wide = lax.axis_size("wide")
    cols = hidden // wide
    me = lax.axis_index("wide")
    row = lax.broadcasted_iota(jnp.int32, (rows, LANES), 0)
    ids = jnp.zeros((rows, LANES), jnp.int32)
    for t in range(rows):
        ids = jnp.where(row == t, ids_ref[t], ids)
    out_ref[:, wide // 2 * cols:] = ids.astype(jnp.float32).astype(out_ref.dtype)
    for q in range(wide // 2):
        src = pl.multiple_of((me ^ (2 * q + 1)) * cols, cols)
        out_ref[:, q * cols:(q + 1) * cols] = grad_ref[:, pl.ds(src, cols)]


def grads_core(ids, grads, after):
    rows, hidden = grads.shape
    return pl.pallas_call(
        grads_core_kernel,
        in_specs=in_smem(1) + in_vmem(1) + in_place(1),
        out_specs=in_vmem(1)[0],
        out_shape=jax.ShapeDtypeStruct((rows, hidden // 2 + LANES), grads.dtype),
        compiler_params=params(16),
        cost_estimate=pl.CostEstimate(flops=0, bytes_accessed=1, transcendentals=0),
    )(ids, grads, after)


def grads_y_kernel(grad_ref, sent_ref, got_ref, _, out_ref):
    rows, hidden = grad_ref.shape
    wide = lax.axis_size("wide")
    cols = hidden // wide
    me = lax.axis_index("wide")
    for k in range(wide // 4):
        src = pl.multiple_of((me ^ (4 * k + 2)) * cols, cols)
        place = slice(k * cols, (k + 1) * cols)
        out_ref[:rows, place] = grad_ref[:, pl.ds(src, cols)]
        out_ref[rows:, place] = got_ref[:, (2 * k + 1) * cols:(2 * k + 2) * cols]
    ids = slice(wide // 4 * cols, wide // 4 * cols + LANES)
    out_ref[:rows, ids] = sent_ref[:, wide // 2 * cols:]
    out_ref[rows:, ids] = got_ref[:, wide // 2 * cols:]


def grads_y(grads, sent, got, after):
    rows, hidden = grads.shape
    return pl.pallas_call(
        grads_y_kernel,
        in_specs=in_vmem(3) + in_place(1),
        out_specs=in_vmem(1)[0],
        out_shape=jax.ShapeDtypeStruct((2 * rows, hidden // 4 + LANES), grads.dtype),
        compiler_params=params(16),
        cost_estimate=pl.CostEstimate(flops=0, bytes_accessed=1, transcendentals=0),
    )(grads, sent, got, after)


def grads_z_kernel(grad_ref, sent_ref, got_ref, over_ref, *out_refs):
    rows = grad_ref.shape[0]
    cols = out_refs[0].shape[1] - LANES
    me = lax.axis_index("wide")
    for k, out_ref in enumerate(out_refs):
        src = pl.multiple_of((me ^ (4 * k)) * cols, cols)
        out_ref[:rows, :cols] = grad_ref[:, pl.ds(src, cols)]
        out_ref[rows:2 * rows, :cols] = got_ref[:, 2 * k * cols:(2 * k + 1) * cols]
        out_ref[2 * rows:, :cols] = over_ref[:, k * cols:(k + 1) * cols]
        out_ref[:rows, cols:] = sent_ref[:, 2 * len(out_refs) * cols:]
        out_ref[rows:2 * rows, cols:] = got_ref[:, 2 * len(out_refs) * cols:]
        out_ref[2 * rows:, cols:] = over_ref[:, len(out_refs) * cols:]


def grads_z(grads, sent, got, over, wide_count):
    rows, hidden = grads.shape
    count = wide_count // 4
    piece = jax.ShapeDtypeStruct((4 * rows, hidden // wide_count + LANES), grads.dtype)
    return pl.pallas_call(
        grads_z_kernel,
        in_specs=in_vmem(4),
        out_specs=in_vmem(count),
        out_shape=[piece] * count,
        compiler_params=params(16),
        cost_estimate=pl.CostEstimate(flops=0, bytes_accessed=1, transcendentals=0),
    )(grads, sent, got, over)


def rotate_kernel(act_count, *refs):
    act_refs, (basis_ref, _, out_ref, held_ref, sems) = refs[:act_count], refs[act_count:]
    depth, width = basis_ref.shape
    places = [slice(k * depth, (k + 1) * depth) for k in range(width // depth)]
    copies = [
        pltpu.make_async_copy(basis_ref.at[:, cols], held_ref.at[k], sems.at[k])
        for k, cols in enumerate(places)
    ]
    for copy in copies:
        copy.start()
    for k, cols in enumerate(places):
        act = jnp.concatenate([ref[:, cols] for ref in act_refs], axis=0)
        copies[k].wait()
        turned = jnp.dot(act, held_ref[k], preferred_element_type=jnp.float32)
        out_ref[cols, :] = turned.astype(jnp.bfloat16).T


def rotate(act_pieces, basis, after):
    tokens = sum(x.shape[0] for x in act_pieces)
    depth, width = basis.shape
    count = width // depth
    return pl.pallas_call(
        functools.partial(rotate_kernel, len(act_pieces)),
        in_specs=in_vmem(len(act_pieces)) + in_place(2),
        out_specs=in_vmem(2),
        out_shape=[
            jax.ShapeDtypeStruct((width, tokens), jnp.bfloat16),
            jax.ShapeDtypeStruct((count, depth, depth), jnp.bfloat16),
        ],
        scratch_shapes=[pltpu.SemaphoreType.DMA((count,))],
        compiler_params=params(46 if tokens <= 256 else 32),
        cost_estimate=pl.CostEstimate(flops=0, bytes_accessed=1, transcendentals=0),
    )(*act_pieces, basis, after)


def rotate_rest_kernel(act_count, *refs):
    act_refs, (held_ref, first_ref, out_ref) = refs[:act_count], refs[act_count:]
    depth = held_ref.shape[1]
    done = first_ref.shape[1]
    out_ref[:, :done] = first_ref[...]
    for k in range(held_ref.shape[0]):
        cols = slice(k * depth, (k + 1) * depth)
        act = jnp.concatenate([ref[:, cols] for ref in act_refs], axis=0)
        turned = jnp.dot(act, held_ref[k], preferred_element_type=jnp.float32)
        out_ref[cols, done:] = turned.astype(jnp.bfloat16).T


def rotate_rest(act_pieces, held, first):
    width, done = first.shape
    tokens = done + sum(x.shape[0] for x in act_pieces)
    return pl.pallas_call(
        functools.partial(rotate_rest_kernel, len(act_pieces)),
        in_specs=in_vmem(len(act_pieces) + 2),
        out_specs=in_vmem(1)[0],
        out_shape=jax.ShapeDtypeStruct((width, tokens), jnp.bfloat16),
        compiler_params=params(16 if tokens <= 256 else 32),
        cost_estimate=pl.CostEstimate(flops=0, bytes_accessed=1, transcendentals=0),
    )(*act_pieces, held, first)


def image_kernel(batch_count, total, per, rot_ref, *refs):
    left_refs, half_refs = refs[:batch_count], refs[batch_count:3 * batch_count]
    eig_ref, out_ref, right_ref, turn_ref, pre_a, pre_b = refs[3 * batch_count:]
    rows, chunk = eig_ref.shape
    tile = min(256, chunk)
    s = pl.program_id(0)

    @pl.when(s == 0)
    def _():
        side = right_ref.shape[2] // 2
        for b in range(batch_count):
            for other in range(2):
                at = pl.multiple_of(((lax.axis_index("wide") & 1) ^ other) * side, side)
                right_ref[b, :, pl.ds(at, side)] = half_refs[2 * b + other][...]

    @pl.when(jnp.logical_and(lax.rem(s, per) == 0, s < total))
    def _():
        for b in range(batch_count):
            turn_ref[b] = left_refs[b][...].T

    @pl.when(lax.rem(s, per) == 1)
    def _():
        out_ref[...] = jnp.zeros_like(out_ref)

    def produce(pre):
        start = lax.rem(s, per) * chunk
        for at in range(0, chunk, tile):
            cols = pl.ds(pl.multiple_of(start + at, tile), tile)
            damped = eig_ref[:, at:at + tile].astype(jnp.float32) + damping
            inverse = pl.reciprocal(damped, approx=True)
            for b in range(batch_count):
                outer_sum = jnp.dot(
                    turn_ref[b], right_ref[b, :, cols], preferred_element_type=jnp.float32
                )
                pre[b * rows:(b + 1) * rows, at:at + tile] = (
                    outer_sum * inverse
                ).astype(jnp.bfloat16)

    def absorb(pre):
        rot = rot_ref[pl.ds(pl.multiple_of(lax.rem(s - 1, per) * chunk, chunk), chunk), :]
        for b in range(batch_count):
            out_ref[b] += jnp.dot(
                pre[b * rows:(b + 1) * rows, :], rot, preferred_element_type=jnp.float32
            )

    between = jnp.logical_and(s > 0, s < total)
    odd = lax.rem(s, 2) == 1

    @pl.when(s == 0)
    def _():
        produce(pre_a)

    @pl.when(jnp.logical_and(between, odd))
    def _():
        produce(pre_b)
        absorb(pre_a)

    @pl.when(jnp.logical_and(between, jnp.logical_not(odd)))
    def _():
        produce(pre_a)
        absorb(pre_b)

    @pl.when(s == total)
    def _():
        absorb(pre_a if total % 2 else pre_b)


def images(rot, lefts, halves, eigenvalues):
    batch_count, tokens = len(lefts), rot.shape[1]
    hidden, width = eigenvalues.shape
    rows = min(1024, hidden)
    chunk = min(1024, width // 2)
    per = width // chunk
    total = hidden // rows * per
    now = lambda s: jnp.minimum(s, total - 1)
    before = lambda s: jnp.maximum(s - 1, 0)
    return pl.pallas_call(
        functools.partial(image_kernel, batch_count, total, per),
        grid=(total + 1,),
        in_specs=[whole_block(rot.shape)]
        + [pl.BlockSpec((QT, rows), lambda s: (0, now(s) // per)) for _ in lefts]
        + [whole_block(x.shape) for x in halves]
        + [pl.BlockSpec((rows, chunk), lambda s: (now(s) // per, now(s) % per))],
        out_specs=pl.BlockSpec((batch_count, rows, tokens), lambda s: (0, before(s) // per, 0)),
        out_shape=jax.ShapeDtypeStruct((batch_count, hidden, tokens), jnp.float32),
        scratch_shapes=[
            pltpu.VMEM((batch_count, QT, width), jnp.bfloat16),
            pltpu.VMEM((batch_count, rows, QT), jnp.bfloat16),
            pltpu.VMEM((batch_count * rows, chunk), jnp.bfloat16),
            pltpu.VMEM((batch_count * rows, chunk), jnp.bfloat16),
        ],
        compiler_params=params(44),
        cost_estimate=pl.CostEstimate(
            flops=2 * hidden * width * (tokens + 256) * batch_count,
            bytes_accessed=2 * hidden * width,
            transcendentals=0,
        ),
    )(rot, *lefts, *halves, eigenvalues)


def score_kernel(batch_count, ranks, count, *refs):
    grad_refs, ids_refs = refs[:count], refs[count:2 * count]
    basis_ref, image_ref, out_ref, token_ref = refs[2 * count:]
    step = pl.program_id(0)
    rows = grad_refs[0].shape[0] // 4

    def tokens_of(pieces):
        return jnp.concatenate(
            [pieces[r // 4][r % 4 * rows:(r % 4 + 1) * rows, :] for r in ranks], axis=0
        )

    @pl.when(step == 0)
    def _():
        token_ref[...] = jnp.zeros_like(token_ref)

    turned = jnp.dot(tokens_of(grad_refs), basis_ref[...], preferred_element_type=jnp.float32)
    turned = turned.astype(jnp.bfloat16).T.astype(jnp.float32)
    for b in range(batch_count):
        token_ref[b:b + 1, :] += jnp.sum(image_ref[b] * turned, axis=0, keepdims=True)

    @pl.when(step == pl.num_programs(0) - 1)
    def _():
        ids = tokens_of(ids_refs).astype(jnp.float32)
        seqs = lax.broadcasted_iota(jnp.int32, ids.shape, 1).astype(jnp.float32)
        member = jnp.where(ids == seqs, 1.0, 0.0).T
        for b in range(batch_count):
            sums = jnp.sum(member * token_ref[b:b + 1, :], axis=1, keepdims=True)
            out_ref[b] = sums[:out_ref.shape[1], :]


def score_parts(grad_pieces, ranks, grad_basis, image, seq_count):
    batch_count, hidden, tokens = image.shape
    count = len(grad_pieces)
    rows = grad_pieces[0].shape[0]
    inner = min(grad_basis.shape[0], hidden)
    return pl.pallas_call(
        functools.partial(score_kernel, batch_count, ranks, count),
        grid=(hidden // inner,),
        in_specs=[pl.BlockSpec((rows, inner), lambda i: (0, i))] * count
        + [pl.BlockSpec((rows, LANES), lambda i: (0, hidden // LANES))] * count
        + [
            pl.BlockSpec((grad_basis.shape[0], inner), lambda i: (0, i)),
            pl.BlockSpec((batch_count, inner, tokens), lambda i: (0, i, 0)),
        ],
        out_specs=pl.BlockSpec((batch_count, seq_count, 1), lambda i: (0, 0, 0)),
        out_shape=jax.ShapeDtypeStruct((batch_count, seq_count, 1), jnp.float32),
        scratch_shapes=[pltpu.VMEM((8, tokens), jnp.float32)],
        compiler_params=params(44),
        cost_estimate=pl.CostEstimate(
            flops=2 * tokens * hidden * grad_basis.shape[0],
            bytes_accessed=4 * image.size,
            transcendentals=0,
        ),
    )(*grad_pieces, *grad_pieces, grad_basis, image)


def per_device(
    train_act, train_grad, seq_ids, act_basis, grad_basis, eigenvalues, query_factors, owners
):
    wide_count = lax.axis_size("wide")
    bits = [1 << n for n in range(wide_count.bit_length() - 1)]
    me = lax.axis_index("wide")
    tok_local = train_act.shape[0]
    seq_count = tok_local * wide_count // SEQ_MEAN
    cols = grad_basis.shape[1]
    hidden = train_grad.shape[1]
    batch_count = owners.shape[0]
    score_scale = 1.0 / math.sqrt(FF * D * QT * SEQ_MEAN)
    batch = lax.axis_index("groups") % batch_count

    ways = bits[:2] + bits[:1:-1]
    order = [0]
    for bit in reversed(bits):
        order = order + [r + bit for r in order]
    order = sorted(order, key=lambda r: [r & bit for bit in ways])
    acts, ranks = train_act, [0]
    far = bits[:1:-1]
    keep, give = cut_factors(query_factors, order, hidden, batch_count)
    flags = owner_flags(owners, ways, keep)
    count = wide_count // 2
    after = []
    for step, bit in enumerate(ways):
        got = swap(give, "wide", bit)
        keep, give = pick(flags, keep, got, step, cols, count, after)
        count //= 2
        if step == 0:
            grads_sent = grads_core(seq_ids, train_grad, give)
            grads_got = swap(grads_sent, "wide", 1)
        if step < len(far) - 1:
            acts = join(acts, swap(acts, "wide", far[step]), give)
            ranks = ranks + [r + far[step] for r in ranks]
            after = [acts, grads_sent]
        elif step == len(far) - 1:
            last = swap(acts, "wide", far[step])
            near = [(gate(acts, [give]), ranks)]
            over = [(swap(near[0][0], "wide", 2), [r + 2 for r in ranks])]
            grads_over = grads_y(train_grad, grads_sent, grads_got, give)
            after = [over[0][0], grads_over]
        elif step == len(far):
            near += [(gate(last, [give]), [r + far[-1] for r in ranks])]
            over += [(swap(near[1][0], "wide", 2), [r + 2 for r in near[1][1]])]
            near += [(swap(x, "wide", 1), [r + 1 for r in has]) for x, has in near]
            first, basis = rotate([x for x, _ in near], act_basis, give)
            after = [first]
    left, right = keep, give

    lefts = [left, swap(left, "groups", 1)]
    other = swap(right, "groups", 1)
    halves = []
    for x in (right, other):
        halves += [x, swap(x, "wide", 1)]
    over = [(gate(x, [wait]), has) for (x, has), wait in zip(over, (right, other))]
    over += [(swap(x, "wide", 1), [r + 1 for r in has]) for x, has in over]
    rot = rotate_rest([x for x, _ in over], basis, first)
    ranks = [r for _, has in near + over for r in has]

    grads_over = swap(grads_over, "wide", 2)
    sent = grads_z(train_grad, grads_sent, grads_got, grads_over, wide_count)
    grads = [sent[0]] + [swap(sent[k], "wide", 4 * k) for k in range(1, wide_count // 4)]

    image = images(rot, lefts, halves, eigenvalues)
    parts = score_parts(grads, ranks, grad_basis, image, seq_count)
    for some in (bits[:2], bits[2:]):
        others = [swap(parts, "wide", some[0] * n) for n in range(1, 1 << len(some))]
        parts = parts + sum(others)
    mine, others = parts[0, :, 0], parts[1, :, 0]
    first = jnp.where(batch == 0, mine, others)
    second = jnp.where(batch == 0, others, mine)
    return jnp.stack([first, second], axis=1) * score_scale


def solution(mesh):
    return jax.shard_map(
        per_device,
        mesh=mesh,
        in_specs=(
            P(("groups", "wide"), None),
            P(("groups", "wide"), None),
            P(("groups", "wide")),
            P(),
            P(None, "wide"),
            P("wide", None),
            P("wide", None, None),
            P(),
        ),
        out_specs=P("groups", None),
        check_vma=False,
    )
```

```python
import functools
import math

import jax
import jax.numpy as jnp
from jax import lax
from jax.experimental import pallas as pl
from jax.experimental.pallas import tpu as pltpu
from jax.sharding import PartitionSpec as P

D = 4096
FF = 32768
SEQ_MEAN = 32
QT = 16
LANES = 128


damping = 0.1


def params(mib):
    return pltpu.CompilerParams(vmem_limit_bytes=mib * 1024 * 1024)


def whole_block(shape):
    return pl.BlockSpec(shape, lambda *_: (0,) * len(shape), pipeline_mode=pl.Buffered(1))


def swap(x, axis, bit):
    count = lax.axis_size(axis)
    return lax.ppermute(x, axis, [(i, i ^ bit) for i in range(count)])


def in_smem(n):
    return [pl.BlockSpec(memory_space=pltpu.SMEM)] * n


def in_vmem(n):
    return [pl.BlockSpec(memory_space=pltpu.VMEM)] * n


def in_place(n):
    return [pl.BlockSpec(memory_space=pl.ANY)] * n


def cut_factors_kernel(order, hidden, batch_count, fac_ref, keep_ref, give_ref):
    cols = hidden // len(order)
    half = (fac_ref.shape[2] - hidden) // 2
    me, batch = lax.axis_index("wide"), lax.rem(lax.axis_index("groups"), batch_count)
    for part, out_ref in enumerate((keep_ref, give_ref)):
        picked = order[part * len(order) // 2:(part + 1) * len(order) // 2]
        for at, r in enumerate(picked):
            src = pl.multiple_of((me ^ r) * cols, cols)
            out_ref[:, at * cols:(at + 1) * cols] = fac_ref[batch, :, pl.ds(src, cols)]
        src = pl.multiple_of(hidden + ((me & 1) ^ part) * half, LANES)
        out_ref[:, len(picked) * cols:] = fac_ref[batch, :, pl.ds(src, half)]


def cut_factors(factors, order, hidden, batch_count):
    rows, width = factors.shape[1:]
    half = jax.ShapeDtypeStruct((rows, width // 2), factors.dtype)
    return pl.pallas_call(
        functools.partial(cut_factors_kernel, order, hidden, batch_count),
        in_specs=in_vmem(1),
        out_specs=in_vmem(2),
        out_shape=[half] * 2,
        compiler_params=params(16),
        cost_estimate=pl.CostEstimate(flops=0, bytes_accessed=1, transcendentals=0),
    )(factors)


def flags_kernel(ways, batch_count, owners_ref, _, flag_ref):
    me, batch = lax.axis_index("wide"), lax.rem(lax.axis_index("groups"), batch_count)
    apart = owners_ref[batch] ^ me
    lane = lax.broadcasted_iota(jnp.int32, flag_ref.shape, 1)
    flags = jnp.zeros(flag_ref.shape, jnp.float32)
    for step, bit in enumerate(ways):
        same = jnp.where((apart & bit) == 0, 1.0, 0.0)
        flags = jnp.where(lane == step, same, flags)
    flag_ref[...] = flags.astype(flag_ref.dtype)


def owner_flags(owners, ways, after):
    return pl.pallas_call(
        functools.partial(flags_kernel, ways, owners.shape[0]),
        in_specs=in_smem(1) + in_place(1),
        out_specs=in_vmem(1)[0],
        out_shape=jax.ShapeDtypeStruct((after.shape[0], LANES), after.dtype),
        compiler_params=params(16),
        cost_estimate=pl.CostEstimate(flops=0, bytes_accessed=1, transcendentals=0),
    )(owners, after)


def pick_kernel(step, cols, last, flag_ref, keep_ref, got_ref, *refs):
    first_ref, second_ref = refs[-2:]
    same = flag_ref[:, step:step + 1]
    differs = 1 - same

    def chosen(at, size):
        place = slice(at, at + size)
        return keep_ref[:, place] * same + got_ref[:, place] * differs

    if last:
        first_ref[...] = chosen(0, cols)
        second_ref[...] = chosen(cols, keep_ref.shape[1] - cols)
    else:
        size = keep_ref.shape[1] - first_ref.shape[1]
        shared = chosen(2 * size, keep_ref.shape[1] - 2 * size)
        for part, out_ref in enumerate((first_ref, second_ref)):
            out_ref[:, :size] = chosen(part * size, size)
            out_ref[:, size:] = shared


def pick(flags, keep, got, step, cols, count, after):
    rows, width = keep.shape
    if count > 1:
        widths = [width - count // 2 * cols] * 2
    else:
        widths = [cols, width - cols]
    return pl.pallas_call(
        functools.partial(pick_kernel, step, cols, count == 1),
        in_specs=in_vmem(3) + in_place(len(after)),
        out_specs=in_vmem(2),
        out_shape=[jax.ShapeDtypeStruct((rows, w), keep.dtype) for w in widths],
        compiler_params=params(16),
        cost_estimate=pl.CostEstimate(flops=0, bytes_accessed=1, transcendentals=0),
    )(flags, keep, got, *after)


def join_kernel(first_ref, second_ref, _, out_ref):
    rows = first_ref.shape[0]
    out_ref[:rows, :] = first_ref[...]
    out_ref[rows:, :] = second_ref[...]


def join(first, second, after):
    rows, width = first.shape
    return pl.pallas_call(
        join_kernel,
        in_specs=in_vmem(2) + in_place(1),
        out_specs=in_vmem(1)[0],
        out_shape=jax.ShapeDtypeStruct((2 * rows, width), first.dtype),
        compiler_params=params(16),
        cost_estimate=pl.CostEstimate(flops=0, bytes_accessed=1, transcendentals=0),
    )(first, second, after)


def gate_kernel(*_):
    pass


def gate(array, after):
    return pl.pallas_call(
        gate_kernel,
        in_specs=in_place(1 + len(after)),
        out_specs=in_place(1)[0],
        out_shape=jax.ShapeDtypeStruct(array.shape, array.dtype),
        input_output_aliases={0: 0},
        compiler_params=params(1),
        cost_estimate=pl.CostEstimate(flops=0, bytes_accessed=1, transcendentals=0),
    )(array, *after)


def grads_core_kernel(ids_ref, grad_ref, _, out_ref):
    rows, hidden = grad_ref.shape
    wide = lax.axis_size("wide")
    cols = hidden // wide
    me = lax.axis_index("wide")
    row = lax.broadcasted_iota(jnp.int32, (rows, LANES), 0)
    ids = jnp.zeros((rows, LANES), jnp.int32)
    for t in range(rows):
        ids = jnp.where(row == t, ids_ref[t], ids)
    out_ref[:, wide // 2 * cols:] = ids.astype(jnp.float32).astype(out_ref.dtype)
    for q in range(wide // 2):
        src = pl.multiple_of((me ^ (2 * q + 1)) * cols, cols)
        out_ref[:, q * cols:(q + 1) * cols] = grad_ref[:, pl.ds(src, cols)]


def grads_core(ids, grads, after):
    rows, hidden = grads.shape
    return pl.pallas_call(
        grads_core_kernel,
        in_specs=in_smem(1) + in_vmem(1) + in_place(1),
        out_specs=in_vmem(1)[0],
        out_shape=jax.ShapeDtypeStruct((rows, hidden // 2 + LANES), grads.dtype),
        compiler_params=params(16),
        cost_estimate=pl.CostEstimate(flops=0, bytes_accessed=1, transcendentals=0),
    )(ids, grads, after)


def grads_y_kernel(grad_ref, sent_ref, got_ref, _, out_ref):
    rows, hidden = grad_ref.shape
    wide = lax.axis_size("wide")
    cols = hidden // wide
    me = lax.axis_index("wide")
    for k in range(wide // 4):
        src = pl.multiple_of((me ^ (4 * k + 2)) * cols, cols)
        place = slice(k * cols, (k + 1) * cols)
        out_ref[:rows, place] = grad_ref[:, pl.ds(src, cols)]
        out_ref[rows:, place] = got_ref[:, (2 * k + 1) * cols:(2 * k + 2) * cols]
    ids = slice(wide // 4 * cols, wide // 4 * cols + LANES)
    out_ref[:rows, ids] = sent_ref[:, wide // 2 * cols:]
    out_ref[rows:, ids] = got_ref[:, wide // 2 * cols:]


def grads_y(grads, sent, got, after):
    rows, hidden = grads.shape
    return pl.pallas_call(
        grads_y_kernel,
        in_specs=in_vmem(3) + in_place(1),
        out_specs=in_vmem(1)[0],
        out_shape=jax.ShapeDtypeStruct((2 * rows, hidden // 4 + LANES), grads.dtype),
        compiler_params=params(16),
        cost_estimate=pl.CostEstimate(flops=0, bytes_accessed=1, transcendentals=0),
    )(grads, sent, got, after)


def grads_z_kernel(grad_ref, sent_ref, got_ref, over_ref, *out_refs):
    rows = grad_ref.shape[0]
    cols = out_refs[0].shape[1] - LANES
    me = lax.axis_index("wide")
    for k, out_ref in enumerate(out_refs):
        src = pl.multiple_of((me ^ (4 * k)) * cols, cols)
        out_ref[:rows, :cols] = grad_ref[:, pl.ds(src, cols)]
        out_ref[rows:2 * rows, :cols] = got_ref[:, 2 * k * cols:(2 * k + 1) * cols]
        out_ref[2 * rows:, :cols] = over_ref[:, k * cols:(k + 1) * cols]
        out_ref[:rows, cols:] = sent_ref[:, 2 * len(out_refs) * cols:]
        out_ref[rows:2 * rows, cols:] = got_ref[:, 2 * len(out_refs) * cols:]
        out_ref[2 * rows:, cols:] = over_ref[:, len(out_refs) * cols:]


def grads_z(grads, sent, got, over, wide_count):
    rows, hidden = grads.shape
    count = wide_count // 4
    piece = jax.ShapeDtypeStruct((4 * rows, hidden // wide_count + LANES), grads.dtype)
    return pl.pallas_call(
        grads_z_kernel,
        in_specs=in_vmem(4),
        out_specs=in_vmem(count),
        out_shape=[piece] * count,
        compiler_params=params(16),
        cost_estimate=pl.CostEstimate(flops=0, bytes_accessed=1, transcendentals=0),
    )(grads, sent, got, over)


def rotate_kernel(act_count, done, *refs):
    act_refs, basis_ref, out_ref = refs[:act_count], refs[act_count], refs[-1]
    depth, width = basis_ref.shape
    if done:
        out_ref[:, :done] = refs[act_count + 1][...]
    for k in range(width // depth):
        cols = slice(k * depth, (k + 1) * depth)
        act = jnp.concatenate([ref[:, cols] for ref in act_refs], axis=0)
        turned = jnp.dot(act, basis_ref[:, cols], preferred_element_type=jnp.float32)
        out_ref[cols, done:] = turned.astype(jnp.bfloat16).T


def rotate(act_pieces, basis, after, first=None):
    width = basis.shape[1]
    done = 0 if first is None else first.shape[1]
    tokens = done + sum(x.shape[0] for x in act_pieces)
    more = [after] if first is None else [first]
    return pl.pallas_call(
        functools.partial(rotate_kernel, len(act_pieces), done),
        in_specs=in_vmem(len(act_pieces) + 1) + (in_place(1) if first is None else in_vmem(1)),
        out_specs=in_vmem(1)[0],
        out_shape=jax.ShapeDtypeStruct((width, tokens), jnp.bfloat16),
        compiler_params=params(16 if tokens <= 256 else 32),
        cost_estimate=pl.CostEstimate(flops=0, bytes_accessed=1, transcendentals=0),
    )(*act_pieces, basis, *more)


def image_kernel(batch_count, total, per, rot_ref, *refs):
    left_refs, half_refs = refs[:batch_count], refs[batch_count:3 * batch_count]
    eig_ref, out_ref, right_ref, turn_ref, pre_a, pre_b = refs[3 * batch_count:]
    rows, chunk = eig_ref.shape
    tile = min(256, chunk)
    s = pl.program_id(0)

    @pl.when(s == 0)
    def _():
        side = right_ref.shape[2] // 2
        for b in range(batch_count):
            for other in range(2):
                at = pl.multiple_of(((lax.axis_index("wide") & 1) ^ other) * side, side)
                right_ref[b, :, pl.ds(at, side)] = half_refs[2 * b + other][...]

    @pl.when(jnp.logical_and(lax.rem(s, per) == 0, s < total))
    def _():
        for b in range(batch_count):
            turn_ref[b] = left_refs[b][...].T

    @pl.when(lax.rem(s, per) == 1)
    def _():
        out_ref[...] = jnp.zeros_like(out_ref)

    def produce(pre):
        start = lax.rem(s, per) * chunk
        for at in range(0, chunk, tile):
            cols = pl.ds(pl.multiple_of(start + at, tile), tile)
            damped = eig_ref[:, at:at + tile].astype(jnp.float32) + damping
            inverse = pl.reciprocal(damped, approx=True)
            for b in range(batch_count):
                outer_sum = jnp.dot(
                    turn_ref[b], right_ref[b, :, cols], preferred_element_type=jnp.float32
                )
                pre[b * rows:(b + 1) * rows, at:at + tile] = (
                    outer_sum * inverse
                ).astype(jnp.bfloat16)

    def absorb(pre):
        rot = rot_ref[pl.ds(pl.multiple_of(lax.rem(s - 1, per) * chunk, chunk), chunk), :]
        for b in range(batch_count):
            out_ref[b] += jnp.dot(
                pre[b * rows:(b + 1) * rows, :], rot, preferred_element_type=jnp.float32
            )

    between = jnp.logical_and(s > 0, s < total)
    odd = lax.rem(s, 2) == 1

    @pl.when(s == 0)
    def _():
        produce(pre_a)

    @pl.when(jnp.logical_and(between, odd))
    def _():
        produce(pre_b)
        absorb(pre_a)

    @pl.when(jnp.logical_and(between, jnp.logical_not(odd)))
    def _():
        produce(pre_a)
        absorb(pre_b)

    @pl.when(s == total)
    def _():
        absorb(pre_a if total % 2 else pre_b)


def images(rot, lefts, halves, eigenvalues):
    batch_count, tokens = len(lefts), rot.shape[1]
    hidden, width = eigenvalues.shape
    rows = min(1024, hidden)
    chunk = min(1024, width // 2)
    per = width // chunk
    total = hidden // rows * per
    now = lambda s: jnp.minimum(s, total - 1)
    before = lambda s: jnp.maximum(s - 1, 0)
    return pl.pallas_call(
        functools.partial(image_kernel, batch_count, total, per),
        grid=(total + 1,),
        in_specs=[whole_block(rot.shape)]
        + [pl.BlockSpec((QT, rows), lambda s: (0, now(s) // per)) for _ in lefts]
        + [whole_block(x.shape) for x in halves]
        + [pl.BlockSpec((rows, chunk), lambda s: (now(s) // per, now(s) % per))],
        out_specs=pl.BlockSpec((batch_count, rows, tokens), lambda s: (0, before(s) // per, 0)),
        out_shape=jax.ShapeDtypeStruct((batch_count, hidden, tokens), jnp.float32),
        scratch_shapes=[
            pltpu.VMEM((batch_count, QT, width), jnp.bfloat16),
            pltpu.VMEM((batch_count, rows, QT), jnp.bfloat16),
            pltpu.VMEM((batch_count * rows, chunk), jnp.bfloat16),
            pltpu.VMEM((batch_count * rows, chunk), jnp.bfloat16),
        ],
        compiler_params=params(32 if tokens <= 256 else 48),
        cost_estimate=pl.CostEstimate(
            flops=2 * hidden * width * (tokens + 256) * batch_count,
            bytes_accessed=2 * hidden * width,
            transcendentals=0,
        ),
    )(rot, *lefts, *halves, eigenvalues)


def score_kernel(batch_count, ranks, count, *refs):
    grad_refs, ids_refs = refs[:count], refs[count:2 * count]
    basis_ref, image_ref, out_ref, token_ref = refs[2 * count:]
    step = pl.program_id(0)
    rows = grad_refs[0].shape[0] // 4

    def tokens_of(pieces):
        return jnp.concatenate(
            [pieces[r // 4][r % 4 * rows:(r % 4 + 1) * rows, :] for r in ranks], axis=0
        )

    @pl.when(step == 0)
    def _():
        token_ref[...] = jnp.zeros_like(token_ref)

    turned = jnp.dot(tokens_of(grad_refs), basis_ref[...], preferred_element_type=jnp.float32)
    turned = turned.astype(jnp.bfloat16).T.astype(jnp.float32)
    for b in range(batch_count):
        token_ref[b:b + 1, :] += jnp.sum(image_ref[b] * turned, axis=0, keepdims=True)

    @pl.when(step == pl.num_programs(0) - 1)
    def _():
        ids = tokens_of(ids_refs).astype(jnp.float32)
        seqs = lax.broadcasted_iota(jnp.int32, ids.shape, 1).astype(jnp.float32)
        member = jnp.where(ids == seqs, 1.0, 0.0).T
        for b in range(batch_count):
            sums = jnp.sum(member * token_ref[b:b + 1, :], axis=1, keepdims=True)
            out_ref[b] = sums[:out_ref.shape[1], :]


def score_parts(grad_pieces, ranks, grad_basis, image, seq_count):
    batch_count, hidden, tokens = image.shape
    count = len(grad_pieces)
    rows = grad_pieces[0].shape[0]
    inner = min(grad_basis.shape[0], hidden)
    return pl.pallas_call(
        functools.partial(score_kernel, batch_count, ranks, count),
        grid=(hidden // inner,),
        in_specs=[pl.BlockSpec((rows, inner), lambda i: (0, i))] * count
        + [pl.BlockSpec((rows, LANES), lambda i: (0, hidden // LANES))] * count
        + [
            pl.BlockSpec((grad_basis.shape[0], inner), lambda i: (0, i)),
            pl.BlockSpec((batch_count, inner, tokens), lambda i: (0, i, 0)),
        ],
        out_specs=pl.BlockSpec((batch_count, seq_count, 1), lambda i: (0, 0, 0)),
        out_shape=jax.ShapeDtypeStruct((batch_count, seq_count, 1), jnp.float32),
        scratch_shapes=[pltpu.VMEM((8, tokens), jnp.float32)],
        compiler_params=params(32 if tokens <= 256 else 48),
        cost_estimate=pl.CostEstimate(
            flops=2 * tokens * hidden * grad_basis.shape[0],
            bytes_accessed=4 * image.size,
            transcendentals=0,
        ),
    )(*grad_pieces, *grad_pieces, grad_basis, image)


def per_device(
    train_act, train_grad, seq_ids, act_basis, grad_basis, eigenvalues, query_factors, owners
):
    wide_count = lax.axis_size("wide")
    bits = [1 << n for n in range(wide_count.bit_length() - 1)]
    me = lax.axis_index("wide")
    tok_local = train_act.shape[0]
    seq_count = tok_local * wide_count // SEQ_MEAN
    cols = grad_basis.shape[1]
    hidden = train_grad.shape[1]
    batch_count = owners.shape[0]
    score_scale = 1.0 / math.sqrt(FF * D * QT * SEQ_MEAN)
    batch = lax.axis_index("groups") % batch_count

    ways = bits[:2] + bits[:1:-1]
    order = [0]
    for bit in reversed(bits):
        order = order + [r + bit for r in order]
    order = sorted(order, key=lambda r: [r & bit for bit in ways])
    acts, ranks = train_act, [0]
    far = bits[:1:-1]
    keep, give = cut_factors(query_factors, order, hidden, batch_count)
    flags = owner_flags(owners, ways, keep)
    count = wide_count // 2
    after = []
    for step, bit in enumerate(ways):
        got = swap(give, "wide", bit)
        keep, give = pick(flags, keep, got, step, cols, count, after)
        count //= 2
        if step == 0:
            grads_sent = grads_core(seq_ids, train_grad, give)
            grads_got = swap(grads_sent, "wide", 1)
        if step < len(far) - 1:
            acts = join(acts, swap(acts, "wide", far[step]), give)
            ranks = ranks + [r + far[step] for r in ranks]
            after = [acts, grads_sent]
        elif step == len(far) - 1:
            last = swap(acts, "wide", far[step])
            near = [(gate(acts, [give]), ranks)]
            over = [(swap(near[0][0], "wide", 2), [r + 2 for r in ranks])]
            grads_over = grads_y(train_grad, grads_sent, grads_got, give)
            after = [over[0][0], grads_over]
        elif step == len(far):
            near += [(gate(last, [give]), [r + far[-1] for r in ranks])]
            over += [(swap(near[1][0], "wide", 2), [r + 2 for r in near[1][1]])]
            near += [(swap(x, "wide", 1), [r + 1 for r in has]) for x, has in near]
            first = rotate([x for x, _ in near], act_basis, give)
            after = [first]
    left, right = keep, give

    lefts = [left, swap(left, "groups", 1)]
    other = swap(right, "groups", 1)
    halves = []
    for x in (right, other):
        halves += [x, swap(x, "wide", 1)]
    over = [(gate(x, [wait]), has) for (x, has), wait in zip(over, (right, other))]
    over += [(swap(x, "wide", 1), [r + 1 for r in has]) for x, has in over]
    rot = rotate([x for x, _ in over], act_basis, None, first)
    ranks = [r for _, has in near + over for r in has]

    grads_over = swap(grads_over, "wide", 2)
    sent = grads_z(train_grad, grads_sent, grads_got, grads_over, wide_count)
    grads = [sent[0]] + [swap(sent[k], "wide", 4 * k) for k in range(1, wide_count // 4)]

    image = images(rot, lefts, halves, eigenvalues)
    parts = score_parts(grads, ranks, grad_basis, image, seq_count)
    for some in (bits[:2], bits[2:]):
        others = [swap(parts, "wide", some[0] * n) for n in range(1, 1 << len(some))]
        parts = parts + sum(others)
    mine, others = parts[0, :, 0], parts[1, :, 0]
    first = jnp.where(batch == 0, mine, others)
    second = jnp.where(batch == 0, others, mine)
    return jnp.stack([first, second], axis=1) * score_scale


def solution(mesh):
    return jax.shard_map(
        per_device,
        mesh=mesh,
        in_specs=(
            P(("groups", "wide"), None),
            P(("groups", "wide"), None),
            P(("groups", "wide")),
            P(),
            P(None, "wide"),
            P("wide", None),
            P("wide", None, None),
            P(),
        ),
        out_specs=P("groups", None),
        check_vma=False,
    )
```

```python
import functools
import math

import jax
import jax.numpy as jnp
from jax import lax
from jax.experimental import pallas as pl
from jax.experimental.pallas import tpu as pltpu
from jax.sharding import PartitionSpec as P

D = 4096
FF = 32768
SEQ_MEAN = 32
QT = 16
LANES = 128


damping = 0.1


def params(mib):
    return pltpu.CompilerParams(vmem_limit_bytes=mib * 1024 * 1024)


def whole_block(shape):
    return pl.BlockSpec(shape, lambda *_: (0,) * len(shape), pipeline_mode=pl.Buffered(1))


def swap(x, axis, bit):
    count = lax.axis_size(axis)
    return lax.ppermute(x, axis, [(i, i ^ bit) for i in range(count)])


def in_smem(n):
    return [pl.BlockSpec(memory_space=pltpu.SMEM)] * n


def in_vmem(n):
    return [pl.BlockSpec(memory_space=pltpu.VMEM)] * n


def in_place(n):
    return [pl.BlockSpec(memory_space=pl.ANY)] * n


def cut_factors_kernel(order, hidden, batch_count, fac_ref, keep_ref, give_ref):
    cols = hidden // len(order)
    half = (fac_ref.shape[2] - hidden) // 2
    me, batch = lax.axis_index("wide"), lax.rem(lax.axis_index("groups"), batch_count)
    for part, out_ref in enumerate((keep_ref, give_ref)):
        picked = order[part * len(order) // 2:(part + 1) * len(order) // 2]
        for at, r in enumerate(picked):
            src = pl.multiple_of((me ^ r) * cols, cols)
            out_ref[:, at * cols:(at + 1) * cols] = fac_ref[batch, :, pl.ds(src, cols)]
        src = pl.multiple_of(hidden + ((me & 1) ^ part) * half, LANES)
        out_ref[:, len(picked) * cols:] = fac_ref[batch, :, pl.ds(src, half)]


def cut_factors(factors, order, hidden, batch_count):
    rows, width = factors.shape[1:]
    half = jax.ShapeDtypeStruct((rows, width // 2), factors.dtype)
    return pl.pallas_call(
        functools.partial(cut_factors_kernel, order, hidden, batch_count),
        in_specs=in_vmem(1),
        out_specs=in_vmem(2),
        out_shape=[half] * 2,
        compiler_params=params(16),
        cost_estimate=pl.CostEstimate(flops=0, bytes_accessed=1, transcendentals=0),
    )(factors)


def flags_kernel(batch_count, owners_ref, _, flag_ref):
    me, batch = lax.axis_index("wide"), lax.rem(lax.axis_index("groups"), batch_count)
    apart = owners_ref[batch] ^ me
    lane = lax.broadcasted_iota(jnp.int32, flag_ref.shape, 1)
    flags = jnp.where(lane - 2 == apart // 4, 1.0, 0.0)
    for step in range(2):
        same = jnp.where((apart & (1 << step)) == 0, 1.0, 0.0)
        flags = jnp.where(lane == step, same, flags)
    flag_ref[...] = flags.astype(flag_ref.dtype)


def owner_flags(owners, after):
    return pl.pallas_call(
        functools.partial(flags_kernel, owners.shape[0]),
        in_specs=in_smem(1) + in_place(1),
        out_specs=in_vmem(1)[0],
        out_shape=jax.ShapeDtypeStruct((after.shape[0], LANES), after.dtype),
        compiler_params=params(16),
        cost_estimate=pl.CostEstimate(flops=0, bytes_accessed=1, transcendentals=0),
    )(owners, after)


def pick_kernel(step, cols, half, flag_ref, keep_ref, got_ref, *refs):
    out_refs = refs[-2:] if step == 0 else refs[-((keep_ref.shape[1] - half) // cols):]
    same = flag_ref[:, step:step + 1]
    differs = 1 - same

    def chosen(at, size):
        place = slice(at, at + size)
        return keep_ref[:, place] * same + got_ref[:, place] * differs

    size = out_refs[0].shape[1] - half
    shared = chosen(len(out_refs) * size, half)
    for n, out_ref in enumerate(out_refs):
        out_ref[:, :size] = chosen(n * size, size)
        out_ref[:, size:] = shared


def pick(flags, keep, got, step, cols, half, after):
    rows, width = keep.shape
    parts = 2 if step == 0 else (width - half) // cols
    size = (width - half) // parts + half
    return pl.pallas_call(
        functools.partial(pick_kernel, step, cols, half),
        in_specs=in_vmem(3) + in_place(len(after)),
        out_specs=in_vmem(parts),
        out_shape=[jax.ShapeDtypeStruct((rows, size), keep.dtype)] * parts,
        compiler_params=params(16),
        cost_estimate=pl.CostEstimate(flops=0, bytes_accessed=1, transcendentals=0),
    )(flags, keep, got, *after)


def pick_one_kernel(count, flag_ref, *refs):
    left_ref, right_ref = refs[-2:]
    cols = left_ref.shape[1]
    for out_ref, place in ((left_ref, slice(0, cols)), (right_ref, slice(cols, None))):
        out_ref[...] = sum(refs[k][:, place] * flag_ref[:, 2 + k:3 + k] for k in range(count))


def pick_one(flags, pieces, cols, after):
    rows, width = pieces[0].shape
    return pl.pallas_call(
        functools.partial(pick_one_kernel, len(pieces)),
        in_specs=in_vmem(1 + len(pieces)) + in_place(len(after)),
        out_specs=in_vmem(2),
        out_shape=[jax.ShapeDtypeStruct((rows, w), pieces[0].dtype) for w in (cols, width - cols)],
        compiler_params=params(16),
        cost_estimate=pl.CostEstimate(flops=0, bytes_accessed=1, transcendentals=0),
    )(flags, *pieces, *after)


def join_kernel(*refs):
    out_ref = refs[-1]
    rows = refs[0].shape[0]
    for n, ref in enumerate(refs[:-2]):
        out_ref[n * rows:(n + 1) * rows, :] = ref[...]


def join(pieces, after):
    rows, width = pieces[0].shape
    return pl.pallas_call(
        join_kernel,
        in_specs=in_vmem(len(pieces)) + in_place(1),
        out_specs=in_vmem(1)[0],
        out_shape=jax.ShapeDtypeStruct((len(pieces) * rows, width), pieces[0].dtype),
        compiler_params=params(16),
        cost_estimate=pl.CostEstimate(flops=0, bytes_accessed=1, transcendentals=0),
    )(*pieces, after)


def gate_kernel(*_):
    pass


def gate(array, after):
    return pl.pallas_call(
        gate_kernel,
        in_specs=in_place(1 + len(after)),
        out_specs=in_place(1)[0],
        out_shape=jax.ShapeDtypeStruct(array.shape, array.dtype),
        input_output_aliases={0: 0},
        compiler_params=params(1),
        cost_estimate=pl.CostEstimate(flops=0, bytes_accessed=1, transcendentals=0),
    )(array, *after)


def cut_grads_kernel(ids_ref, grad_ref, _, out_ref):
    count, rows, width = out_ref.shape
    cols = width - LANES
    row = lax.broadcasted_iota(jnp.int32, (rows, LANES), 0)
    ids = jnp.zeros((rows, LANES), jnp.int32)
    for t in range(rows):
        ids = jnp.where(row == t, ids_ref[t], ids)
    ids = ids.astype(jnp.float32).astype(out_ref.dtype)
    for to in range(count):
        out_ref[to, :, :cols] = grad_ref[:, to * cols:(to + 1) * cols]
        out_ref[to, :, cols:] = ids


def cut_grads(ids, grads, after, count):
    rows, hidden = grads.shape
    return pl.pallas_call(
        cut_grads_kernel,
        in_specs=in_smem(1) + in_vmem(1) + in_place(1),
        out_specs=in_vmem(1)[0],
        out_shape=jax.ShapeDtypeStruct((count, rows, hidden // count + LANES), grads.dtype),
        compiler_params=params(16),
        cost_estimate=pl.CostEstimate(flops=0, bytes_accessed=1, transcendentals=0),
    )(ids, grads, after)


def rotate_kernel(act_count, done, *refs):
    act_refs, basis_ref, out_ref = refs[:act_count], refs[act_count], refs[-1]
    depth, width = basis_ref.shape
    if done:
        out_ref[:, :done] = refs[act_count + 1][...]
    for k in range(width // depth):
        cols = slice(k * depth, (k + 1) * depth)
        act = jnp.concatenate([ref[:, cols] for ref in act_refs], axis=0)
        turned = jnp.dot(act, basis_ref[:, cols], preferred_element_type=jnp.float32)
        out_ref[cols, done:] = turned.astype(jnp.bfloat16).T


def rotate(act_pieces, basis, after, first=None):
    width = basis.shape[1]
    done = 0 if first is None else first.shape[1]
    tokens = done + sum(x.shape[0] for x in act_pieces)
    more = [after] if first is None else [first]
    return pl.pallas_call(
        functools.partial(rotate_kernel, len(act_pieces), done),
        in_specs=in_vmem(len(act_pieces) + 1) + (in_place(1) if first is None else in_vmem(1)),
        out_specs=in_vmem(1)[0],
        out_shape=jax.ShapeDtypeStruct((width, tokens), jnp.bfloat16),
        compiler_params=params(16 if tokens <= 256 else 32),
        cost_estimate=pl.CostEstimate(flops=0, bytes_accessed=1, transcendentals=0),
    )(*act_pieces, basis, *more)


def image_kernel(batch_count, total, per, rot_ref, *refs):
    left_refs, half_refs = refs[:batch_count], refs[batch_count:3 * batch_count]
    eig_ref, out_ref, right_ref, turn_ref, pre_a, pre_b = refs[3 * batch_count:]
    rows, chunk = eig_ref.shape
    tile = min(256, chunk)
    s = pl.program_id(0)

    @pl.when(s == 0)
    def _():
        side = right_ref.shape[2] // 2
        for b in range(batch_count):
            for other in range(2):
                at = pl.multiple_of(((lax.axis_index("wide") & 1) ^ other) * side, side)
                right_ref[b, :, pl.ds(at, side)] = half_refs[2 * b + other][...]

    @pl.when(jnp.logical_and(lax.rem(s, per) == 0, s < total))
    def _():
        for b in range(batch_count):
            turn_ref[b] = left_refs[b][...].T

    @pl.when(lax.rem(s, per) == 1)
    def _():
        out_ref[...] = jnp.zeros_like(out_ref)

    def produce(pre):
        start = lax.rem(s, per) * chunk
        for at in range(0, chunk, tile):
            cols = pl.ds(pl.multiple_of(start + at, tile), tile)
            damped = eig_ref[:, at:at + tile].astype(jnp.float32) + damping
            inverse = pl.reciprocal(damped, approx=True)
            for b in range(batch_count):
                outer_sum = jnp.dot(
                    turn_ref[b], right_ref[b, :, cols], preferred_element_type=jnp.float32
                )
                pre[b * rows:(b + 1) * rows, at:at + tile] = (
                    outer_sum * inverse
                ).astype(jnp.bfloat16)

    def absorb(pre):
        rot = rot_ref[pl.ds(pl.multiple_of(lax.rem(s - 1, per) * chunk, chunk), chunk), :]
        for b in range(batch_count):
            out_ref[b] += jnp.dot(
                pre[b * rows:(b + 1) * rows, :], rot, preferred_element_type=jnp.float32
            )

    between = jnp.logical_and(s > 0, s < total)
    odd = lax.rem(s, 2) == 1

    @pl.when(s == 0)
    def _():
        produce(pre_a)

    @pl.when(jnp.logical_and(between, odd))
    def _():
        produce(pre_b)
        absorb(pre_a)

    @pl.when(jnp.logical_and(between, jnp.logical_not(odd)))
    def _():
        produce(pre_a)
        absorb(pre_b)

    @pl.when(s == total)
    def _():
        absorb(pre_a if total % 2 else pre_b)


def images(rot, lefts, halves, eigenvalues):
    batch_count, tokens = len(lefts), rot.shape[1]
    hidden, width = eigenvalues.shape
    rows = min(1024, hidden)
    chunk = min(1024, width // 2)
    per = width // chunk
    total = hidden // rows * per
    now = lambda s: jnp.minimum(s, total - 1)
    before = lambda s: jnp.maximum(s - 1, 0)
    return pl.pallas_call(
        functools.partial(image_kernel, batch_count, total, per),
        grid=(total + 1,),
        in_specs=[whole_block(rot.shape)]
        + [pl.BlockSpec((QT, rows), lambda s: (0, now(s) // per)) for _ in lefts]
        + [whole_block(x.shape) for x in halves]
        + [pl.BlockSpec((rows, chunk), lambda s: (now(s) // per, now(s) % per))],
        out_specs=pl.BlockSpec((batch_count, rows, tokens), lambda s: (0, before(s) // per, 0)),
        out_shape=jax.ShapeDtypeStruct((batch_count, hidden, tokens), jnp.float32),
        scratch_shapes=[
            pltpu.VMEM((batch_count, QT, width), jnp.bfloat16),
            pltpu.VMEM((batch_count, rows, QT), jnp.bfloat16),
            pltpu.VMEM((batch_count * rows, chunk), jnp.bfloat16),
            pltpu.VMEM((batch_count * rows, chunk), jnp.bfloat16),
        ],
        compiler_params=params(50),
        cost_estimate=pl.CostEstimate(
            flops=2 * hidden * width * (tokens + 256) * batch_count,
            bytes_accessed=2 * hidden * width,
            transcendentals=0,
        ),
    )(rot, *lefts, *halves, eigenvalues)


def score_kernel(batch_count, ranks, grad_ref, basis_ref, image_ref, ids_ref, out_ref, token_ref):
    step = pl.program_id(0)
    me = lax.axis_index("wide")

    @pl.when(step == 0)
    def _():
        token_ref[...] = jnp.zeros_like(token_ref)

    grads = jnp.concatenate([grad_ref[me ^ r] for r in ranks], axis=0)
    turned = jnp.dot(grads, basis_ref[...], preferred_element_type=jnp.float32)
    turned = turned.astype(jnp.bfloat16).T.astype(jnp.float32)
    for b in range(batch_count):
        token_ref[b:b + 1, :] += jnp.sum(image_ref[b] * turned, axis=0, keepdims=True)

    @pl.when(step == pl.num_programs(0) - 1)
    def _():
        ids = jnp.concatenate([ids_ref[me ^ r] for r in ranks], axis=0).astype(jnp.float32)
        seqs = lax.broadcasted_iota(jnp.int32, ids.shape, 1).astype(jnp.float32)
        member = jnp.where(ids == seqs, 1.0, 0.0).T
        own = lax.rem(lax.axis_index("groups"), batch_count)
        for b in range(batch_count):
            sums = jnp.sum(member * token_ref[b:b + 1, :], axis=1, keepdims=True)
            out_ref[lax.rem(own + b, batch_count)] = sums[:out_ref.shape[1], :]


def score_parts(grads, ranks, grad_basis, image, seq_count):
    batch_count, _, tokens = image.shape
    count, rows, width = grads.shape
    hidden = width - LANES
    inner = min(grad_basis.shape[0], hidden)
    return pl.pallas_call(
        functools.partial(score_kernel, batch_count, ranks),
        grid=(hidden // inner,),
        in_specs=[
            pl.BlockSpec((count, rows, inner), lambda i: (0, 0, i)),
            pl.BlockSpec((grad_basis.shape[0], inner), lambda i: (0, i)),
            pl.BlockSpec((batch_count, inner, tokens), lambda i: (0, i, 0)),
            pl.BlockSpec((count, rows, LANES), lambda i: (0, 0, hidden // LANES)),
        ],
        out_specs=pl.BlockSpec((batch_count, seq_count, 1), lambda i: (0, 0, 0)),
        out_shape=jax.ShapeDtypeStruct((batch_count, seq_count, 1), jnp.float32),
        scratch_shapes=[pltpu.VMEM((8, tokens), jnp.float32)],
        compiler_params=params(56),
        cost_estimate=pl.CostEstimate(
            flops=2 * tokens * hidden * grad_basis.shape[0],
            bytes_accessed=4 * image.size,
            transcendentals=0,
        ),
    )(grads, grad_basis, image, grads)


def per_device(
    train_act, train_grad, seq_ids, act_basis, grad_basis, eigenvalues, query_factors, owners
):
    wide_count = lax.axis_size("wide")
    along_z = range(wide_count // 4)
    tok_local = train_act.shape[0]
    seq_count = tok_local * wide_count // SEQ_MEAN
    cols = grad_basis.shape[1]
    hidden = train_grad.shape[1]
    batch_count = owners.shape[0]
    score_scale = 1.0 / math.sqrt(FF * D * QT * SEQ_MEAN)

    half = (query_factors.shape[2] - hidden) // 2
    order = [4 * k + r for r in (0, 2, 1, 3) for k in along_z]
    keep, give = cut_factors(query_factors, order, hidden, batch_count)
    flags = owner_flags(owners, keep)
    keep, give = pick(flags, keep, swap(give, "wide", 1), 0, cols, half, [])
    sent = cut_grads(seq_ids, train_grad, give, wide_count)
    parts = pick(flags, keep, swap(give, "wide", 2), 1, cols, half, [sent])
    acts = join([train_act] + [swap(train_act, "wide", 4 * k) for k in along_z if k], parts[0])
    ranks = [4 * k for k in along_z]
    near = [(acts, ranks), (swap(acts, "wide", 1), [r + 1 for r in ranks])]
    over = [(swap(acts, "wide", 2), [r + 2 for r in ranks])]
    first = rotate([x for x, _ in near], act_basis, parts[0])
    parts = [swap(parts[k], "wide", 4 * k) if k else parts[0] for k in along_z]
    left, right = pick_one(flags, parts, cols, [over[0][0], first])

    lefts = [left, swap(left, "groups", 1)]
    other = swap(right, "groups", 1)
    halves = []
    for x in (right, other):
        halves += [x, swap(x, "wide", 1)]
    over += [(swap(x, "wide", 1), [r + 1 for r in has]) for x, has in over]
    rot = rotate([x for x, _ in over], act_basis, None, first)
    ranks = [r for _, has in near + over for r in has]

    grads = lax.all_to_all(gate(sent, [right]), "wide", 0, 0)

    image = images(rot, lefts, halves, eigenvalues)
    parts = score_parts(grads, ranks, grad_basis, image, seq_count)
    for step, count in ((1, 4), (4, wide_count // 4)):
        parts = parts + sum(swap(parts, "wide", step * n) for n in range(1, count))
    return parts[:, :, 0].T * score_scale


def solution(mesh):
    return jax.shard_map(
        per_device,
        mesh=mesh,
        in_specs=(
            P(("groups", "wide"), None),
            P(("groups", "wide"), None),
            P(("groups", "wide")),
            P(),
            P(None, "wide"),
            P("wide", None),
            P("wide", None, None),
            P(),
        ),
        out_specs=P("groups", None),
        check_vma=False,
    )
```

```python
import functools
import math

import jax
import jax.numpy as jnp
from jax import lax
from jax.experimental import pallas as pl
from jax.experimental.pallas import tpu as pltpu
from jax.sharding import PartitionSpec as P

D = 4096
FF = 32768
SEQ_MEAN = 32
QT = 16
LANES = 128


damping = 0.1


def params(mib):
    return pltpu.CompilerParams(vmem_limit_bytes=mib * 1024 * 1024)


def whole_block(shape):
    return pl.BlockSpec(shape, lambda *_: (0,) * len(shape), pipeline_mode=pl.Buffered(1))


def swap(x, axis, bit):
    count = lax.axis_size(axis)
    return lax.ppermute(x, axis, [(i, i ^ bit) for i in range(count)])


def in_smem(n):
    return [pl.BlockSpec(memory_space=pltpu.SMEM)] * n


def in_vmem(n):
    return [pl.BlockSpec(memory_space=pltpu.VMEM)] * n


def in_place(n):
    return [pl.BlockSpec(memory_space=pl.ANY)] * n


def cut_factors_kernel(order, hidden, batch_count, fac_ref, keep_ref, give_ref):
    cols = hidden // len(order)
    half = (fac_ref.shape[2] - hidden) // 2
    me, batch = lax.axis_index("wide"), lax.rem(lax.axis_index("groups"), batch_count)
    for part, out_ref in enumerate((keep_ref, give_ref)):
        picked = order[part * len(order) // 2:(part + 1) * len(order) // 2]
        for at, r in enumerate(picked):
            src = pl.multiple_of((me ^ r) * cols, cols)
            out_ref[:, at * cols:(at + 1) * cols] = fac_ref[batch, :, pl.ds(src, cols)]
        src = pl.multiple_of(hidden + ((me & 1) ^ part) * half, LANES)
        out_ref[:, len(picked) * cols:] = fac_ref[batch, :, pl.ds(src, half)]


def cut_factors(factors, order, hidden, batch_count):
    rows, width = factors.shape[1:]
    half = jax.ShapeDtypeStruct((rows, width // 2), factors.dtype)
    return pl.pallas_call(
        functools.partial(cut_factors_kernel, order, hidden, batch_count),
        in_specs=in_vmem(1),
        out_specs=in_vmem(2),
        out_shape=[half] * 2,
        compiler_params=params(16),
        cost_estimate=pl.CostEstimate(flops=0, bytes_accessed=1, transcendentals=0),
    )(factors)


def flags_kernel(batch_count, owners_ref, _, flag_ref):
    me, batch = lax.axis_index("wide"), lax.rem(lax.axis_index("groups"), batch_count)
    apart = owners_ref[batch] ^ me
    lane = lax.broadcasted_iota(jnp.int32, flag_ref.shape, 1)
    flags = jnp.where(lane - 2 == apart // 4, 1.0, 0.0)
    for step in range(2):
        same = jnp.where((apart & (1 << step)) == 0, 1.0, 0.0)
        flags = jnp.where(lane == step, same, flags)
    flag_ref[...] = flags.astype(flag_ref.dtype)


def owner_flags(owners, after):
    return pl.pallas_call(
        functools.partial(flags_kernel, owners.shape[0]),
        in_specs=in_smem(1) + in_place(1),
        out_specs=in_vmem(1)[0],
        out_shape=jax.ShapeDtypeStruct((after.shape[0], LANES), after.dtype),
        compiler_params=params(16),
        cost_estimate=pl.CostEstimate(flops=0, bytes_accessed=1, transcendentals=0),
    )(owners, after)


def pick_kernel(step, cols, half, flag_ref, keep_ref, got_ref, *refs):
    out_refs = refs[-2:] if step == 0 else refs[-((keep_ref.shape[1] - half) // cols):]
    same = flag_ref[:, step:step + 1]
    differs = 1 - same

    def chosen(at, size):
        place = slice(at, at + size)
        return keep_ref[:, place] * same + got_ref[:, place] * differs

    size = out_refs[0].shape[1] - half
    shared = chosen(len(out_refs) * size, half)
    for n, out_ref in enumerate(out_refs):
        out_ref[:, :size] = chosen(n * size, size)
        out_ref[:, size:] = shared


def pick(flags, keep, got, step, cols, half, after):
    rows, width = keep.shape
    parts = 2 if step == 0 else (width - half) // cols
    size = (width - half) // parts + half
    return pl.pallas_call(
        functools.partial(pick_kernel, step, cols, half),
        in_specs=in_vmem(3) + in_place(len(after)),
        out_specs=in_vmem(parts),
        out_shape=[jax.ShapeDtypeStruct((rows, size), keep.dtype)] * parts,
        compiler_params=params(16),
        cost_estimate=pl.CostEstimate(flops=0, bytes_accessed=1, transcendentals=0),
    )(flags, keep, got, *after)


def pick_one_kernel(count, flag_ref, *refs):
    left_ref, right_ref = refs[-2:]
    cols = left_ref.shape[1]
    for out_ref, place in ((left_ref, slice(0, cols)), (right_ref, slice(cols, None))):
        out_ref[...] = sum(refs[k][:, place] * flag_ref[:, 2 + k:3 + k] for k in range(count))


def pick_one(flags, pieces, cols, after):
    rows, width = pieces[0].shape
    return pl.pallas_call(
        functools.partial(pick_one_kernel, len(pieces)),
        in_specs=in_vmem(1 + len(pieces)) + in_place(len(after)),
        out_specs=in_vmem(2),
        out_shape=[jax.ShapeDtypeStruct((rows, w), pieces[0].dtype) for w in (cols, width - cols)],
        compiler_params=params(16),
        cost_estimate=pl.CostEstimate(flops=0, bytes_accessed=1, transcendentals=0),
    )(flags, *pieces, *after)


def join_kernel(*refs):
    out_ref = refs[-1]
    rows = refs[0].shape[0]
    for n, ref in enumerate(refs[:-2]):
        out_ref[n * rows:(n + 1) * rows, :] = ref[...]


def join(pieces, after):
    rows, width = pieces[0].shape
    return pl.pallas_call(
        join_kernel,
        in_specs=in_vmem(len(pieces)) + in_place(1),
        out_specs=in_vmem(1)[0],
        out_shape=jax.ShapeDtypeStruct((len(pieces) * rows, width), pieces[0].dtype),
        compiler_params=params(16),
        cost_estimate=pl.CostEstimate(flops=0, bytes_accessed=1, transcendentals=0),
    )(*pieces, after)


def gate_kernel(*_):
    pass


def gate(array, after):
    return pl.pallas_call(
        gate_kernel,
        in_specs=in_place(1 + len(after)),
        out_specs=in_place(1)[0],
        out_shape=jax.ShapeDtypeStruct(array.shape, array.dtype),
        input_output_aliases={0: 0},
        compiler_params=params(1),
        cost_estimate=pl.CostEstimate(flops=0, bytes_accessed=1, transcendentals=0),
    )(array, *after)


def grads_core_kernel(ids_ref, grad_ref, _, out_ref):
    rows, hidden = grad_ref.shape
    wide = lax.axis_size("wide")
    cols = hidden // wide
    me = lax.axis_index("wide")
    row = lax.broadcasted_iota(jnp.int32, (rows, LANES), 0)
    ids = jnp.zeros((rows, LANES), jnp.int32)
    for t in range(rows):
        ids = jnp.where(row == t, ids_ref[t], ids)
    out_ref[:, wide // 2 * cols:] = ids.astype(jnp.float32).astype(out_ref.dtype)
    for q in range(wide // 2):
        src = pl.multiple_of((me ^ (2 * q + 1)) * cols, cols)
        out_ref[:, q * cols:(q + 1) * cols] = grad_ref[:, pl.ds(src, cols)]


def grads_core(ids, grads, after):
    rows, hidden = grads.shape
    return pl.pallas_call(
        grads_core_kernel,
        in_specs=in_smem(1) + in_vmem(1) + in_place(1),
        out_specs=in_vmem(1)[0],
        out_shape=jax.ShapeDtypeStruct((rows, hidden // 2 + LANES), grads.dtype),
        compiler_params=params(16),
        cost_estimate=pl.CostEstimate(flops=0, bytes_accessed=1, transcendentals=0),
    )(ids, grads, after)


def grads_y_kernel(grad_ref, sent_ref, got_ref, _, out_ref):
    rows, hidden = grad_ref.shape
    wide = lax.axis_size("wide")
    cols = hidden // wide
    me = lax.axis_index("wide")
    for k in range(wide // 4):
        src = pl.multiple_of((me ^ (4 * k + 2)) * cols, cols)
        place = slice(k * cols, (k + 1) * cols)
        out_ref[:rows, place] = grad_ref[:, pl.ds(src, cols)]
        out_ref[rows:, place] = got_ref[:, (2 * k + 1) * cols:(2 * k + 2) * cols]
    ids = slice(wide // 4 * cols, wide // 4 * cols + LANES)
    out_ref[:rows, ids] = sent_ref[:, wide // 2 * cols:]
    out_ref[rows:, ids] = got_ref[:, wide // 2 * cols:]


def grads_y(grads, sent, got, after):
    rows, hidden = grads.shape
    return pl.pallas_call(
        grads_y_kernel,
        in_specs=in_vmem(3) + in_place(1),
        out_specs=in_vmem(1)[0],
        out_shape=jax.ShapeDtypeStruct((2 * rows, hidden // 4 + LANES), grads.dtype),
        compiler_params=params(16),
        cost_estimate=pl.CostEstimate(flops=0, bytes_accessed=1, transcendentals=0),
    )(grads, sent, got, after)


def grads_z_kernel(grad_ref, sent_ref, got_ref, over_ref, *out_refs):
    rows = grad_ref.shape[0]
    cols = out_refs[0].shape[1] - LANES
    me = lax.axis_index("wide")
    for k, out_ref in enumerate(out_refs):
        src = pl.multiple_of((me ^ (4 * k)) * cols, cols)
        out_ref[:rows, :cols] = grad_ref[:, pl.ds(src, cols)]
        out_ref[rows:2 * rows, :cols] = got_ref[:, 2 * k * cols:(2 * k + 1) * cols]
        out_ref[2 * rows:, :cols] = over_ref[:, k * cols:(k + 1) * cols]
        out_ref[:rows, cols:] = sent_ref[:, 2 * len(out_refs) * cols:]
        out_ref[rows:2 * rows, cols:] = got_ref[:, 2 * len(out_refs) * cols:]
        out_ref[2 * rows:, cols:] = over_ref[:, len(out_refs) * cols:]


def grads_z(grads, sent, got, over, wide_count):
    rows, hidden = grads.shape
    count = wide_count // 4
    piece = jax.ShapeDtypeStruct((4 * rows, hidden // wide_count + LANES), grads.dtype)
    return pl.pallas_call(
        grads_z_kernel,
        in_specs=in_vmem(4),
        out_specs=in_vmem(count),
        out_shape=[piece] * count,
        compiler_params=params(16),
        cost_estimate=pl.CostEstimate(flops=0, bytes_accessed=1, transcendentals=0),
    )(grads, sent, got, over)


def rotate_kernel(act_count, done, *refs):
    act_refs, basis_ref, out_ref = refs[:act_count], refs[act_count], refs[-1]
    depth, width = basis_ref.shape
    if done:
        out_ref[:, :done] = refs[act_count + 1][...]
    for k in range(width // depth):
        cols = slice(k * depth, (k + 1) * depth)
        act = jnp.concatenate([ref[:, cols] for ref in act_refs], axis=0)
        turned = jnp.dot(act, basis_ref[:, cols], preferred_element_type=jnp.float32)
        out_ref[cols, done:] = turned.astype(jnp.bfloat16).T


def rotate(act_pieces, basis, after, first=None):
    width = basis.shape[1]
    done = 0 if first is None else first.shape[1]
    tokens = done + sum(x.shape[0] for x in act_pieces)
    more = [after] if first is None else [first]
    return pl.pallas_call(
        functools.partial(rotate_kernel, len(act_pieces), done),
        in_specs=in_vmem(len(act_pieces) + 1) + (in_place(1) if first is None else in_vmem(1)),
        out_specs=in_vmem(1)[0],
        out_shape=jax.ShapeDtypeStruct((width, tokens), jnp.bfloat16),
        compiler_params=params(16 if tokens <= 256 else 32),
        cost_estimate=pl.CostEstimate(flops=0, bytes_accessed=1, transcendentals=0),
    )(*act_pieces, basis, *more)


def image_kernel(batch_count, total, per, rot_ref, *refs):
    left_refs, half_refs = refs[:batch_count], refs[batch_count:3 * batch_count]
    eig_ref, out_ref, right_ref, turn_ref, pre_a, pre_b = refs[3 * batch_count:]
    rows, chunk = eig_ref.shape
    tile = min(256, chunk)
    s = pl.program_id(0)

    @pl.when(s == 0)
    def _():
        side = right_ref.shape[2] // 2
        for b in range(batch_count):
            for other in range(2):
                at = pl.multiple_of(((lax.axis_index("wide") & 1) ^ other) * side, side)
                right_ref[b, :, pl.ds(at, side)] = half_refs[2 * b + other][...]

    @pl.when(jnp.logical_and(lax.rem(s, per) == 0, s < total))
    def _():
        for b in range(batch_count):
            turn_ref[b] = left_refs[b][...].T

    @pl.when(lax.rem(s, per) == 1)
    def _():
        out_ref[...] = jnp.zeros_like(out_ref)

    def produce(pre):
        start = lax.rem(s, per) * chunk
        for at in range(0, chunk, tile):
            cols = pl.ds(pl.multiple_of(start + at, tile), tile)
            damped = eig_ref[:, at:at + tile].astype(jnp.float32) + damping
            inverse = pl.reciprocal(damped, approx=True)
            for b in range(batch_count):
                outer_sum = jnp.dot(
                    turn_ref[b], right_ref[b, :, cols], preferred_element_type=jnp.float32
                )
                pre[b * rows:(b + 1) * rows, at:at + tile] = (
                    outer_sum * inverse
                ).astype(jnp.bfloat16)

    def absorb(pre):
        rot = rot_ref[pl.ds(pl.multiple_of(lax.rem(s - 1, per) * chunk, chunk), chunk), :]
        for b in range(batch_count):
            out_ref[b] += jnp.dot(
                pre[b * rows:(b + 1) * rows, :], rot, preferred_element_type=jnp.float32
            )

    between = jnp.logical_and(s > 0, s < total)
    odd = lax.rem(s, 2) == 1

    @pl.when(s == 0)
    def _():
        produce(pre_a)

    @pl.when(jnp.logical_and(between, odd))
    def _():
        produce(pre_b)
        absorb(pre_a)

    @pl.when(jnp.logical_and(between, jnp.logical_not(odd)))
    def _():
        produce(pre_a)
        absorb(pre_b)

    @pl.when(s == total)
    def _():
        absorb(pre_a if total % 2 else pre_b)


def images(rot, lefts, halves, eigenvalues):
    batch_count, tokens = len(lefts), rot.shape[1]
    hidden, width = eigenvalues.shape
    rows = min(1024, hidden)
    chunk = min(1024, width // 2)
    per = width // chunk
    total = hidden // rows * per
    now = lambda s: jnp.minimum(s, total - 1)
    before = lambda s: jnp.maximum(s - 1, 0)
    return pl.pallas_call(
        functools.partial(image_kernel, batch_count, total, per),
        grid=(total + 1,),
        in_specs=[whole_block(rot.shape)]
        + [pl.BlockSpec((QT, rows), lambda s: (0, now(s) // per)) for _ in lefts]
        + [whole_block(x.shape) for x in halves]
        + [pl.BlockSpec((rows, chunk), lambda s: (now(s) // per, now(s) % per))],
        out_specs=pl.BlockSpec((batch_count, rows, tokens), lambda s: (0, before(s) // per, 0)),
        out_shape=jax.ShapeDtypeStruct((batch_count, hidden, tokens), jnp.float32),
        scratch_shapes=[
            pltpu.VMEM((batch_count, QT, width), jnp.bfloat16),
            pltpu.VMEM((batch_count, rows, QT), jnp.bfloat16),
            pltpu.VMEM((batch_count * rows, chunk), jnp.bfloat16),
            pltpu.VMEM((batch_count * rows, chunk), jnp.bfloat16),
        ],
        compiler_params=params(32 if tokens <= 256 else 48),
        cost_estimate=pl.CostEstimate(
            flops=2 * hidden * width * (tokens + 256) * batch_count,
            bytes_accessed=2 * hidden * width,
            transcendentals=0,
        ),
    )(rot, *lefts, *halves, eigenvalues)


def score_kernel(batch_count, ranks, count, *refs):
    grad_refs, ids_refs = refs[:count], refs[count:2 * count]
    basis_ref, image_ref, out_ref, token_ref = refs[2 * count:]
    step = pl.program_id(0)
    rows = grad_refs[0].shape[0] // 4

    def tokens_of(pieces):
        return jnp.concatenate(
            [pieces[r // 4][r % 4 * rows:(r % 4 + 1) * rows, :] for r in ranks], axis=0
        )

    @pl.when(step == 0)
    def _():
        token_ref[...] = jnp.zeros_like(token_ref)

    turned = jnp.dot(tokens_of(grad_refs), basis_ref[...], preferred_element_type=jnp.float32)
    turned = turned.astype(jnp.bfloat16).T.astype(jnp.float32)
    for b in range(batch_count):
        token_ref[b:b + 1, :] += jnp.sum(image_ref[b] * turned, axis=0, keepdims=True)

    @pl.when(step == pl.num_programs(0) - 1)
    def _():
        ids = tokens_of(ids_refs).astype(jnp.float32)
        seqs = lax.broadcasted_iota(jnp.int32, ids.shape, 1).astype(jnp.float32)
        member = jnp.where(ids == seqs, 1.0, 0.0).T
        own = lax.rem(lax.axis_index("groups"), batch_count)
        for b in range(batch_count):
            sums = jnp.sum(member * token_ref[b:b + 1, :], axis=1, keepdims=True)
            out_ref[lax.rem(own + b, batch_count)] = sums[:out_ref.shape[1], :]


def score_parts(grad_pieces, ranks, grad_basis, image, seq_count):
    batch_count, hidden, tokens = image.shape
    count = len(grad_pieces)
    rows = grad_pieces[0].shape[0]
    inner = min(grad_basis.shape[0], hidden)
    return pl.pallas_call(
        functools.partial(score_kernel, batch_count, ranks, count),
        grid=(hidden // inner,),
        in_specs=[pl.BlockSpec((rows, inner), lambda i: (0, i))] * count
        + [pl.BlockSpec((rows, LANES), lambda i: (0, hidden // LANES))] * count
        + [
            pl.BlockSpec((grad_basis.shape[0], inner), lambda i: (0, i)),
            pl.BlockSpec((batch_count, inner, tokens), lambda i: (0, i, 0)),
        ],
        out_specs=pl.BlockSpec((batch_count, seq_count, 1), lambda i: (0, 0, 0)),
        out_shape=jax.ShapeDtypeStruct((batch_count, seq_count, 1), jnp.float32),
        scratch_shapes=[pltpu.VMEM((8, tokens), jnp.float32)],
        compiler_params=params(32 if tokens <= 256 else 48),
        cost_estimate=pl.CostEstimate(
            flops=2 * tokens * hidden * grad_basis.shape[0],
            bytes_accessed=4 * image.size,
            transcendentals=0,
        ),
    )(*grad_pieces, *grad_pieces, grad_basis, image)


def per_device(
    train_act, train_grad, seq_ids, act_basis, grad_basis, eigenvalues, query_factors, owners
):
    wide_count = lax.axis_size("wide")
    along_z = range(wide_count // 4)
    tok_local = train_act.shape[0]
    seq_count = tok_local * wide_count // SEQ_MEAN
    cols = grad_basis.shape[1]
    hidden = train_grad.shape[1]
    batch_count = owners.shape[0]
    score_scale = 1.0 / math.sqrt(FF * D * QT * SEQ_MEAN)

    half = (query_factors.shape[2] - hidden) // 2
    order = [4 * k + r for r in (0, 2, 1, 3) for k in along_z]
    keep, give = cut_factors(query_factors, order, hidden, batch_count)
    flags = owner_flags(owners, keep)
    keep, give = pick(flags, keep, swap(give, "wide", 1), 0, cols, half, [])
    grads_sent = grads_core(seq_ids, train_grad, give)
    grads_got = swap(grads_sent, "wide", 1)
    grads_over = grads_y(train_grad, grads_sent, grads_got, give)
    parts = pick(flags, keep, swap(give, "wide", 2), 1, cols, half, [grads_over])
    grads_over = swap(grads_over, "wide", 2)
    sent = grads_z(train_grad, grads_sent, grads_got, grads_over, wide_count)
    acts = join([train_act] + [swap(train_act, "wide", 4 * k) for k in along_z if k], parts[0])
    ranks = [4 * k for k in along_z]
    over = swap(acts, "wide", 2)
    first = rotate([acts], act_basis, parts[0])
    parts = [swap(parts[k], "wide", 4 * k) if k else parts[0] for k in along_z]
    left, right = pick_one(flags, parts, cols, [over, first, sent[0]])

    lefts = [left, swap(left, "groups", 1)]
    other = swap(right, "groups", 1)
    halves = []
    for x in (right, other):
        halves += [x, swap(x, "wide", 1)]
    over = gate(over, [right])
    rot = rotate([over, swap(gate(acts, [right]), "wide", 1), swap(over, "wide", 1)], act_basis, None, first)
    ranks = [r + more for more in (0, 2, 1, 3) for r in ranks]

    grads = [swap(sent[k], "wide", 4 * k) if k else sent[0] for k in along_z]

    image = images(rot, lefts, halves, eigenvalues)
    parts = score_parts(grads, ranks, grad_basis, image, seq_count)
    for step, count in ((1, 4), (4, wide_count // 4)):
        parts = parts + sum(swap(parts, "wide", step * n) for n in range(1, count))
    return parts[:, :, 0].T * score_scale


def solution(mesh):
    return jax.shard_map(
        per_device,
        mesh=mesh,
        in_specs=(
            P(("groups", "wide"), None),
            P(("groups", "wide"), None),
            P(("groups", "wide")),
            P(),
            P(None, "wide"),
            P("wide", None),
            P("wide", None, None),
            P(),
        ),
        out_specs=P("groups", None),
        check_vma=False,
    )
```

```python
import functools
import math

import jax
import jax.numpy as jnp
from jax import lax
from jax.experimental import pallas as pl
from jax.experimental.pallas import tpu as pltpu
from jax.sharding import PartitionSpec as P

D = 4096
FF = 32768
SEQ_MEAN = 32
QT = 16
LANES = 128


damping = 0.1


def params(mib):
    return pltpu.CompilerParams(vmem_limit_bytes=mib * 1024 * 1024)


def whole_block(shape):
    return pl.BlockSpec(shape, lambda *_: (0,) * len(shape), pipeline_mode=pl.Buffered(1))


def swap(x, axis, bit):
    count = lax.axis_size(axis)
    return lax.ppermute(x, axis, [(i, i ^ bit) for i in range(count)])


def in_smem(n):
    return [pl.BlockSpec(memory_space=pltpu.SMEM)] * n


def in_vmem(n):
    return [pl.BlockSpec(memory_space=pltpu.VMEM)] * n


def in_place(n):
    return [pl.BlockSpec(memory_space=pl.ANY)] * n


def cut_factors_kernel(order, hidden, batch_count, fac_ref, keep_ref, give_ref):
    cols = hidden // len(order)
    half = (fac_ref.shape[2] - hidden) // 2
    me, batch = lax.axis_index("wide"), lax.rem(lax.axis_index("groups"), batch_count)
    for part, out_ref in enumerate((keep_ref, give_ref)):
        picked = order[part * len(order) // 2:(part + 1) * len(order) // 2]
        for at, r in enumerate(picked):
            src = pl.multiple_of((me ^ r) * cols, cols)
            out_ref[:, at * cols:(at + 1) * cols] = fac_ref[batch, :, pl.ds(src, cols)]
        src = pl.multiple_of(hidden + ((me & 1) ^ part) * half, LANES)
        out_ref[:, len(picked) * cols:] = fac_ref[batch, :, pl.ds(src, half)]


def cut_factors(factors, order, hidden, batch_count):
    rows, width = factors.shape[1:]
    half = jax.ShapeDtypeStruct((rows, width // 2), factors.dtype)
    return pl.pallas_call(
        functools.partial(cut_factors_kernel, order, hidden, batch_count),
        in_specs=in_vmem(1),
        out_specs=in_vmem(2),
        out_shape=[half] * 2,
        compiler_params=params(16),
        cost_estimate=pl.CostEstimate(flops=0, bytes_accessed=1, transcendentals=0),
    )(factors)


def flags_kernel(batch_count, owners_ref, _, flag_ref):
    me, batch = lax.axis_index("wide"), lax.rem(lax.axis_index("groups"), batch_count)
    apart = owners_ref[batch] ^ me
    lane = lax.broadcasted_iota(jnp.int32, flag_ref.shape, 1)
    flags = jnp.where(lane - 2 == apart // 4, 1.0, 0.0)
    for step in range(2):
        same = jnp.where((apart & (1 << step)) == 0, 1.0, 0.0)
        flags = jnp.where(lane == step, same, flags)
    flag_ref[...] = flags.astype(flag_ref.dtype)


def owner_flags(owners, after):
    return pl.pallas_call(
        functools.partial(flags_kernel, owners.shape[0]),
        in_specs=in_smem(1) + in_place(1),
        out_specs=in_vmem(1)[0],
        out_shape=jax.ShapeDtypeStruct((after.shape[0], LANES), after.dtype),
        compiler_params=params(16),
        cost_estimate=pl.CostEstimate(flops=0, bytes_accessed=1, transcendentals=0),
    )(owners, after)


def pick_kernel(step, cols, half, flag_ref, keep_ref, got_ref, *refs):
    out_refs = refs[-2:] if step == 0 else refs[-((keep_ref.shape[1] - half) // cols):]
    same = flag_ref[:, step:step + 1]
    differs = 1 - same

    def chosen(at, size):
        place = slice(at, at + size)
        return keep_ref[:, place] * same + got_ref[:, place] * differs

    size = out_refs[0].shape[1] - half
    shared = chosen(len(out_refs) * size, half)
    for n, out_ref in enumerate(out_refs):
        out_ref[:, :size] = chosen(n * size, size)
        out_ref[:, size:] = shared


def pick(flags, keep, got, step, cols, half, after):
    rows, width = keep.shape
    parts = 2 if step == 0 else (width - half) // cols
    size = (width - half) // parts + half
    return pl.pallas_call(
        functools.partial(pick_kernel, step, cols, half),
        in_specs=in_vmem(3) + in_place(len(after)),
        out_specs=in_vmem(parts),
        out_shape=[jax.ShapeDtypeStruct((rows, size), keep.dtype)] * parts,
        compiler_params=params(16),
        cost_estimate=pl.CostEstimate(flops=0, bytes_accessed=1, transcendentals=0),
    )(flags, keep, got, *after)


def pick_one_kernel(count, flag_ref, *refs):
    left_ref, right_ref = refs[-2:]
    cols = left_ref.shape[1]
    for out_ref, place in ((left_ref, slice(0, cols)), (right_ref, slice(cols, None))):
        out_ref[...] = sum(refs[k][:, place] * flag_ref[:, 2 + k:3 + k] for k in range(count))


def pick_one(flags, pieces, cols, after):
    rows, width = pieces[0].shape
    return pl.pallas_call(
        functools.partial(pick_one_kernel, len(pieces)),
        in_specs=in_vmem(1 + len(pieces)) + in_place(len(after)),
        out_specs=in_vmem(2),
        out_shape=[jax.ShapeDtypeStruct((rows, w), pieces[0].dtype) for w in (cols, width - cols)],
        compiler_params=params(16),
        cost_estimate=pl.CostEstimate(flops=0, bytes_accessed=1, transcendentals=0),
    )(flags, *pieces, *after)


def join_kernel(*refs):
    out_ref = refs[-1]
    rows = refs[0].shape[0]
    for n, ref in enumerate(refs[:-2]):
        out_ref[n * rows:(n + 1) * rows, :] = ref[...]


def join(pieces, after):
    rows, width = pieces[0].shape
    return pl.pallas_call(
        join_kernel,
        in_specs=in_vmem(len(pieces)) + in_place(1),
        out_specs=in_vmem(1)[0],
        out_shape=jax.ShapeDtypeStruct((len(pieces) * rows, width), pieces[0].dtype),
        compiler_params=params(16),
        cost_estimate=pl.CostEstimate(flops=0, bytes_accessed=1, transcendentals=0),
    )(*pieces, after)


def gate_kernel(*_):
    pass


def gate(array, after):
    return pl.pallas_call(
        gate_kernel,
        in_specs=in_place(1 + len(after)),
        out_specs=in_place(1)[0],
        out_shape=jax.ShapeDtypeStruct(array.shape, array.dtype),
        input_output_aliases={0: 0},
        compiler_params=params(1),
        cost_estimate=pl.CostEstimate(flops=0, bytes_accessed=1, transcendentals=0),
    )(array, *after)


def grads_core_kernel(ids_ref, grad_ref, _, out_ref):
    rows, hidden = grad_ref.shape
    wide = lax.axis_size("wide")
    cols = hidden // wide
    me = lax.axis_index("wide")
    row = lax.broadcasted_iota(jnp.int32, (rows, LANES), 0)
    ids = jnp.zeros((rows, LANES), jnp.int32)
    for t in range(rows):
        ids = jnp.where(row == t, ids_ref[t], ids)
    out_ref[:, wide // 2 * cols:] = ids.astype(jnp.float32).astype(out_ref.dtype)
    for q in range(wide // 2):
        src = pl.multiple_of((me ^ (2 * q + 1)) * cols, cols)
        out_ref[:, q * cols:(q + 1) * cols] = grad_ref[:, pl.ds(src, cols)]


def grads_core(ids, grads, after):
    rows, hidden = grads.shape
    return pl.pallas_call(
        grads_core_kernel,
        in_specs=in_smem(1) + in_vmem(1) + in_place(1),
        out_specs=in_vmem(1)[0],
        out_shape=jax.ShapeDtypeStruct((rows, hidden // 2 + LANES), grads.dtype),
        compiler_params=params(16),
        cost_estimate=pl.CostEstimate(flops=0, bytes_accessed=1, transcendentals=0),
    )(ids, grads, after)


def grads_y_kernel(grad_ref, sent_ref, got_ref, _, out_ref):
    rows, hidden = grad_ref.shape
    wide = lax.axis_size("wide")
    cols = hidden // wide
    me = lax.axis_index("wide")
    for k in range(wide // 4):
        src = pl.multiple_of((me ^ (4 * k + 2)) * cols, cols)
        place = slice(k * cols, (k + 1) * cols)
        out_ref[:rows, place] = grad_ref[:, pl.ds(src, cols)]
        out_ref[rows:, place] = got_ref[:, (2 * k + 1) * cols:(2 * k + 2) * cols]
    ids = slice(wide // 4 * cols, wide // 4 * cols + LANES)
    out_ref[:rows, ids] = sent_ref[:, wide // 2 * cols:]
    out_ref[rows:, ids] = got_ref[:, wide // 2 * cols:]


def grads_y(grads, sent, got, after):
    rows, hidden = grads.shape
    return pl.pallas_call(
        grads_y_kernel,
        in_specs=in_vmem(3) + in_place(1),
        out_specs=in_vmem(1)[0],
        out_shape=jax.ShapeDtypeStruct((2 * rows, hidden // 4 + LANES), grads.dtype),
        compiler_params=params(16),
        cost_estimate=pl.CostEstimate(flops=0, bytes_accessed=1, transcendentals=0),
    )(grads, sent, got, after)


def grads_z_kernel(grad_ref, sent_ref, got_ref, over_ref, *out_refs):
    rows = grad_ref.shape[0]
    cols = out_refs[0].shape[1] - LANES
    me = lax.axis_index("wide")
    for k, out_ref in enumerate(out_refs):
        src = pl.multiple_of((me ^ (4 * k)) * cols, cols)
        out_ref[:rows, :cols] = grad_ref[:, pl.ds(src, cols)]
        out_ref[rows:2 * rows, :cols] = got_ref[:, 2 * k * cols:(2 * k + 1) * cols]
        out_ref[2 * rows:, :cols] = over_ref[:, k * cols:(k + 1) * cols]
        out_ref[:rows, cols:] = sent_ref[:, 2 * len(out_refs) * cols:]
        out_ref[rows:2 * rows, cols:] = got_ref[:, 2 * len(out_refs) * cols:]
        out_ref[2 * rows:, cols:] = over_ref[:, len(out_refs) * cols:]


def grads_z(grads, sent, got, over, wide_count):
    rows, hidden = grads.shape
    count = wide_count // 4
    piece = jax.ShapeDtypeStruct((4 * rows, hidden // wide_count + LANES), grads.dtype)
    return pl.pallas_call(
        grads_z_kernel,
        in_specs=in_vmem(4),
        out_specs=in_vmem(count),
        out_shape=[piece] * count,
        compiler_params=params(16),
        cost_estimate=pl.CostEstimate(flops=0, bytes_accessed=1, transcendentals=0),
    )(grads, sent, got, over)


def rotate_kernel(act_count, done, *refs):
    act_refs, basis_ref, out_ref = refs[:act_count], refs[act_count], refs[-1]
    depth, width = basis_ref.shape
    if done:
        out_ref[:, :done] = refs[act_count + 1][...]
    for k in range(width // depth):
        cols = slice(k * depth, (k + 1) * depth)
        act = jnp.concatenate([ref[:, cols] for ref in act_refs], axis=0)
        turned = jnp.dot(act, basis_ref[:, cols], preferred_element_type=jnp.float32)
        out_ref[cols, done:] = turned.astype(jnp.bfloat16).T


def rotate(act_pieces, basis, after, first=None):
    width = basis.shape[1]
    done = 0 if first is None else first.shape[1]
    tokens = done + sum(x.shape[0] for x in act_pieces)
    more = [after] if first is None else [first]
    return pl.pallas_call(
        functools.partial(rotate_kernel, len(act_pieces), done),
        in_specs=in_vmem(len(act_pieces) + 1) + (in_place(1) if first is None else in_vmem(1)),
        out_specs=in_vmem(1)[0],
        out_shape=jax.ShapeDtypeStruct((width, tokens), jnp.bfloat16),
        compiler_params=params(16 if tokens <= 256 else 32),
        cost_estimate=pl.CostEstimate(flops=0, bytes_accessed=1, transcendentals=0),
    )(*act_pieces, basis, *more)


def image_kernel(batch_count, total, per, rot_ref, *refs):
    left_refs, half_refs = refs[:batch_count], refs[batch_count:3 * batch_count]
    eig_ref, out_ref, right_ref, turn_ref, pre_a, pre_b = refs[3 * batch_count:]
    rows, chunk = eig_ref.shape
    tile = min(256, chunk)
    s = pl.program_id(0)

    @pl.when(s == 0)
    def _():
        side = right_ref.shape[2] // 2
        for b in range(batch_count):
            for other in range(2):
                at = pl.multiple_of(((lax.axis_index("wide") & 1) ^ other) * side, side)
                right_ref[b, :, pl.ds(at, side)] = half_refs[2 * b + other][...]

    @pl.when(jnp.logical_and(lax.rem(s, per) == 0, s < total))
    def _():
        for b in range(batch_count):
            turn_ref[b] = left_refs[b][...].T

    @pl.when(lax.rem(s, per) == 1)
    def _():
        out_ref[...] = jnp.zeros_like(out_ref)

    def produce(pre):
        start = lax.rem(s, per) * chunk
        for at in range(0, chunk, tile):
            cols = pl.ds(pl.multiple_of(start + at, tile), tile)
            damped = eig_ref[:, at:at + tile].astype(jnp.float32) + damping
            inverse = pl.reciprocal(damped, approx=True)
            for b in range(batch_count):
                outer_sum = jnp.dot(
                    turn_ref[b], right_ref[b, :, cols], preferred_element_type=jnp.float32
                )
                pre[b * rows:(b + 1) * rows, at:at + tile] = (
                    outer_sum * inverse
                ).astype(jnp.bfloat16)

    def absorb(pre):
        rot = rot_ref[pl.ds(pl.multiple_of(lax.rem(s - 1, per) * chunk, chunk), chunk), :]
        for b in range(batch_count):
            out_ref[b] += jnp.dot(
                pre[b * rows:(b + 1) * rows, :], rot, preferred_element_type=jnp.float32
            )

    between = jnp.logical_and(s > 0, s < total)
    odd = lax.rem(s, 2) == 1

    @pl.when(s == 0)
    def _():
        produce(pre_a)

    @pl.when(jnp.logical_and(between, odd))
    def _():
        produce(pre_b)
        absorb(pre_a)

    @pl.when(jnp.logical_and(between, jnp.logical_not(odd)))
    def _():
        produce(pre_a)
        absorb(pre_b)

    @pl.when(s == total)
    def _():
        absorb(pre_a if total % 2 else pre_b)


def images(rot, lefts, halves, eigenvalues):
    batch_count, tokens = len(lefts), rot.shape[1]
    hidden, width = eigenvalues.shape
    rows = min(1024, hidden)
    chunk = min(1024, width // 2)
    per = width // chunk
    total = hidden // rows * per
    now = lambda s: jnp.minimum(s, total - 1)
    before = lambda s: jnp.maximum(s - 1, 0)
    return pl.pallas_call(
        functools.partial(image_kernel, batch_count, total, per),
        grid=(total + 1,),
        in_specs=[whole_block(rot.shape)]
        + [pl.BlockSpec((QT, rows), lambda s: (0, now(s) // per)) for _ in lefts]
        + [whole_block(x.shape) for x in halves]
        + [pl.BlockSpec((rows, chunk), lambda s: (now(s) // per, now(s) % per))],
        out_specs=pl.BlockSpec((batch_count, rows, tokens), lambda s: (0, before(s) // per, 0)),
        out_shape=jax.ShapeDtypeStruct((batch_count, hidden, tokens), jnp.float32),
        scratch_shapes=[
            pltpu.VMEM((batch_count, QT, width), jnp.bfloat16),
            pltpu.VMEM((batch_count, rows, QT), jnp.bfloat16),
            pltpu.VMEM((batch_count * rows, chunk), jnp.bfloat16),
            pltpu.VMEM((batch_count * rows, chunk), jnp.bfloat16),
        ],
        compiler_params=params(32 if tokens <= 256 else 48),
        cost_estimate=pl.CostEstimate(
            flops=2 * hidden * width * (tokens + 256) * batch_count,
            bytes_accessed=2 * hidden * width,
            transcendentals=0,
        ),
    )(rot, *lefts, *halves, eigenvalues)


def score_kernel(batch_count, ranks, count, *refs):
    grad_refs, ids_refs = refs[:count], refs[count:2 * count]
    basis_ref, image_ref, out_ref, token_ref = refs[2 * count:]
    step = pl.program_id(0)
    rows = grad_refs[0].shape[0] // 4

    def tokens_of(pieces):
        return jnp.concatenate(
            [pieces[r // 4][r % 4 * rows:(r % 4 + 1) * rows, :] for r in ranks], axis=0
        )

    @pl.when(step == 0)
    def _():
        token_ref[...] = jnp.zeros_like(token_ref)

    turned = jnp.dot(tokens_of(grad_refs), basis_ref[...], preferred_element_type=jnp.float32)
    turned = turned.astype(jnp.bfloat16).T.astype(jnp.float32)
    for b in range(batch_count):
        token_ref[b:b + 1, :] += jnp.sum(image_ref[b] * turned, axis=0, keepdims=True)

    @pl.when(step == pl.num_programs(0) - 1)
    def _():
        ids = tokens_of(ids_refs).astype(jnp.float32)
        seqs = lax.broadcasted_iota(jnp.int32, ids.shape, 1).astype(jnp.float32)
        member = jnp.where(ids == seqs, 1.0, 0.0).T
        own = lax.rem(lax.axis_index("groups"), batch_count)
        for b in range(batch_count):
            sums = jnp.sum(member * token_ref[b:b + 1, :], axis=1, keepdims=True)
            out_ref[lax.rem(own + b, batch_count)] = sums[:out_ref.shape[1], :]


def score_parts(grad_pieces, ranks, grad_basis, image, seq_count):
    batch_count, hidden, tokens = image.shape
    count = len(grad_pieces)
    rows = grad_pieces[0].shape[0]
    inner = min(grad_basis.shape[0], hidden)
    return pl.pallas_call(
        functools.partial(score_kernel, batch_count, ranks, count),
        grid=(hidden // inner,),
        in_specs=[pl.BlockSpec((rows, inner), lambda i: (0, i))] * count
        + [pl.BlockSpec((rows, LANES), lambda i: (0, hidden // LANES))] * count
        + [
            pl.BlockSpec((grad_basis.shape[0], inner), lambda i: (0, i)),
            pl.BlockSpec((batch_count, inner, tokens), lambda i: (0, i, 0)),
        ],
        out_specs=pl.BlockSpec((batch_count, seq_count, 1), lambda i: (0, 0, 0)),
        out_shape=jax.ShapeDtypeStruct((batch_count, seq_count, 1), jnp.float32),
        scratch_shapes=[pltpu.VMEM((8, tokens), jnp.float32)],
        compiler_params=params(32 if tokens <= 256 else 48),
        cost_estimate=pl.CostEstimate(
            flops=2 * tokens * hidden * grad_basis.shape[0],
            bytes_accessed=4 * image.size,
            transcendentals=0,
        ),
    )(*grad_pieces, *grad_pieces, grad_basis, image)


def per_device(
    train_act, train_grad, seq_ids, act_basis, grad_basis, eigenvalues, query_factors, owners
):
    wide_count = lax.axis_size("wide")
    along_z = range(wide_count // 4)
    tok_local = train_act.shape[0]
    seq_count = tok_local * wide_count // SEQ_MEAN
    cols = grad_basis.shape[1]
    hidden = train_grad.shape[1]
    batch_count = owners.shape[0]
    score_scale = 1.0 / math.sqrt(FF * D * QT * SEQ_MEAN)

    half = (query_factors.shape[2] - hidden) // 2
    order = [4 * k + r for r in (0, 2, 1, 3) for k in along_z]
    keep, give = cut_factors(query_factors, order, hidden, batch_count)
    flags = owner_flags(owners, keep)
    grads_sent = grads_core(seq_ids, train_grad, keep)
    keep, give = pick(flags, keep, swap(give, "wide", 1), 0, cols, half, [grads_sent])
    grads_got = swap(grads_sent, "wide", 1)
    grads_over = grads_y(train_grad, grads_sent, grads_got, give)
    parts = pick(flags, keep, swap(give, "wide", 2), 1, cols, half, [grads_over])
    grads_over = swap(grads_over, "wide", 2)
    sent = grads_z(train_grad, grads_sent, grads_got, grads_over, wide_count)
    acts = join([train_act] + [swap(train_act, "wide", 4 * k) for k in along_z if k], parts[0])
    ranks = [4 * k for k in along_z]
    over = swap(acts, "wide", 2)
    first = rotate([acts], act_basis, parts[0])
    parts = [swap(parts[k], "wide", 4 * k) if k else parts[0] for k in along_z]
    left, right = pick_one(flags, parts, cols, [over, first, sent[0]])

    lefts = [left, swap(left, "groups", 1)]
    other = swap(right, "groups", 1)
    halves = []
    for x in (right, other):
        halves += [x, swap(x, "wide", 1)]
    over = gate(over, [right])
    rot = rotate([over, swap(gate(acts, [right]), "wide", 1), swap(over, "wide", 1)], act_basis, None, first)
    ranks = [r + more for more in (0, 2, 1, 3) for r in ranks]

    grads = [swap(sent[k], "wide", 4 * k) if k else sent[0] for k in along_z]

    image = images(rot, lefts, halves, eigenvalues)
    parts = score_parts(grads, ranks, grad_basis, image, seq_count)
    for step, count in ((1, 4), (4, wide_count // 4)):
        parts = parts + sum(swap(parts, "wide", step * n) for n in range(1, count))
    return parts[:, :, 0].T * score_scale


def solution(mesh):
    return jax.shard_map(
        per_device,
        mesh=mesh,
        in_specs=(
            P(("groups", "wide"), None),
            P(("groups", "wide"), None),
            P(("groups", "wide")),
            P(),
            P(None, "wide"),
            P("wide", None),
            P("wide", None, None),
            P(),
        ),
        out_specs=P("groups", None),
        check_vma=False,
    )
```

```python
import functools
import math

import jax
import jax.numpy as jnp
from jax import lax
from jax.experimental import pallas as pl
from jax.experimental.pallas import tpu as pltpu
from jax.sharding import PartitionSpec as P

D = 4096
FF = 32768
SEQ_MEAN = 32
QT = 16
LANES = 128


damping = 0.1


def params(mib):
    return pltpu.CompilerParams(vmem_limit_bytes=mib * 1024 * 1024)


def whole_block(shape):
    return pl.BlockSpec(shape, lambda *_: (0,) * len(shape), pipeline_mode=pl.Buffered(1))


def swap(x, axis, bit):
    count = lax.axis_size(axis)
    return lax.ppermute(x, axis, [(i, i ^ bit) for i in range(count)])


def in_smem(n):
    return [pl.BlockSpec(memory_space=pltpu.SMEM)] * n


def in_vmem(n):
    return [pl.BlockSpec(memory_space=pltpu.VMEM)] * n


def in_place(n):
    return [pl.BlockSpec(memory_space=pl.ANY)] * n


def cut_factors_kernel(order, hidden, batch_count, fac_ref, keep_ref, give_ref):
    cols = hidden // len(order)
    half = (fac_ref.shape[2] - hidden) // 2
    me, batch = lax.axis_index("wide"), lax.rem(lax.axis_index("groups"), batch_count)
    for part, out_ref in enumerate((keep_ref, give_ref)):
        picked = order[part * len(order) // 2:(part + 1) * len(order) // 2]
        for at, r in enumerate(picked):
            src = pl.multiple_of((me ^ r) * cols, cols)
            out_ref[:, at * cols:(at + 1) * cols] = fac_ref[batch, :, pl.ds(src, cols)]
        src = pl.multiple_of(hidden + ((me & 1) ^ part) * half, LANES)
        out_ref[:, len(picked) * cols:] = fac_ref[batch, :, pl.ds(src, half)]


def cut_factors(factors, order, hidden, batch_count):
    rows, width = factors.shape[1:]
    half = jax.ShapeDtypeStruct((rows, width // 2), factors.dtype)
    return pl.pallas_call(
        functools.partial(cut_factors_kernel, order, hidden, batch_count),
        in_specs=in_vmem(1),
        out_specs=in_vmem(2),
        out_shape=[half] * 2,
        compiler_params=params(16),
        cost_estimate=pl.CostEstimate(flops=0, bytes_accessed=1, transcendentals=0),
    )(factors)


def flags_kernel(batch_count, owners_ref, _, flag_ref):
    me, batch = lax.axis_index("wide"), lax.rem(lax.axis_index("groups"), batch_count)
    apart = owners_ref[batch] ^ me
    lane = lax.broadcasted_iota(jnp.int32, flag_ref.shape, 1)
    flags = jnp.where(lane - 2 == apart // 4, 1.0, 0.0)
    for step in range(2):
        same = jnp.where((apart & (1 << step)) == 0, 1.0, 0.0)
        flags = jnp.where(lane == step, same, flags)
    flag_ref[...] = flags.astype(flag_ref.dtype)


def owner_flags(owners, after):
    return pl.pallas_call(
        functools.partial(flags_kernel, owners.shape[0]),
        in_specs=in_smem(1) + in_place(1),
        out_specs=in_vmem(1)[0],
        out_shape=jax.ShapeDtypeStruct((after.shape[0], LANES), after.dtype),
        compiler_params=params(16),
        cost_estimate=pl.CostEstimate(flops=0, bytes_accessed=1, transcendentals=0),
    )(owners, after)


def pick_kernel(step, cols, half, flag_ref, keep_ref, got_ref, *refs):
    out_refs = refs[-2:] if step == 0 else refs[-((keep_ref.shape[1] - half) // cols):]
    same = flag_ref[:, step:step + 1]
    differs = 1 - same

    def chosen(at, size):
        place = slice(at, at + size)
        return keep_ref[:, place] * same + got_ref[:, place] * differs

    size = out_refs[0].shape[1] - half
    shared = chosen(len(out_refs) * size, half)
    for n, out_ref in enumerate(out_refs):
        out_ref[:, :size] = chosen(n * size, size)
        out_ref[:, size:] = shared


def pick(flags, keep, got, step, cols, half, after):
    rows, width = keep.shape
    parts = 2 if step == 0 else (width - half) // cols
    size = (width - half) // parts + half
    return pl.pallas_call(
        functools.partial(pick_kernel, step, cols, half),
        in_specs=in_vmem(3) + in_place(len(after)),
        out_specs=in_vmem(parts),
        out_shape=[jax.ShapeDtypeStruct((rows, size), keep.dtype)] * parts,
        compiler_params=params(16),
        cost_estimate=pl.CostEstimate(flops=0, bytes_accessed=1, transcendentals=0),
    )(flags, keep, got, *after)


def pick_one_kernel(count, flag_ref, *refs):
    refs[-1][...] = sum(refs[k][...] * flag_ref[:, 2 + k:3 + k] for k in range(count))


def pick_one(flags, pieces, after):
    return pl.pallas_call(
        functools.partial(pick_one_kernel, len(pieces)),
        in_specs=in_vmem(1 + len(pieces)) + in_place(len(after)),
        out_specs=in_vmem(1)[0],
        out_shape=jax.ShapeDtypeStruct(pieces[0].shape, pieces[0].dtype),
        compiler_params=params(16),
        cost_estimate=pl.CostEstimate(flops=0, bytes_accessed=1, transcendentals=0),
    )(flags, *pieces, *after)


def join_kernel(*refs):
    out_ref = refs[-1]
    rows = refs[0].shape[0]
    for n, ref in enumerate(refs[:-2]):
        out_ref[n * rows:(n + 1) * rows, :] = ref[...]


def join(pieces, after):
    rows, width = pieces[0].shape
    return pl.pallas_call(
        join_kernel,
        in_specs=in_vmem(len(pieces)) + in_place(1),
        out_specs=in_vmem(1)[0],
        out_shape=jax.ShapeDtypeStruct((len(pieces) * rows, width), pieces[0].dtype),
        compiler_params=params(16),
        cost_estimate=pl.CostEstimate(flops=0, bytes_accessed=1, transcendentals=0),
    )(*pieces, after)


def gate_kernel(*_):
    pass


def gate(array, after):
    return pl.pallas_call(
        gate_kernel,
        in_specs=in_place(1 + len(after)),
        out_specs=in_place(1)[0],
        out_shape=jax.ShapeDtypeStruct(array.shape, array.dtype),
        input_output_aliases={0: 0},
        compiler_params=params(1),
        cost_estimate=pl.CostEstimate(flops=0, bytes_accessed=1, transcendentals=0),
    )(array, *after)


def grads_core_kernel(ids_ref, grad_ref, _, out_ref):
    rows, hidden = grad_ref.shape
    wide = lax.axis_size("wide")
    cols = hidden // wide
    me = lax.axis_index("wide")
    row = lax.broadcasted_iota(jnp.int32, (rows, LANES), 0)
    ids = jnp.zeros((rows, LANES), jnp.int32)
    for t in range(rows):
        ids = jnp.where(row == t, ids_ref[t], ids)
    out_ref[:, wide // 2 * cols:] = ids.astype(jnp.float32).astype(out_ref.dtype)
    for q in range(wide // 2):
        src = pl.multiple_of((me ^ (2 * q + 1)) * cols, cols)
        out_ref[:, q * cols:(q + 1) * cols] = grad_ref[:, pl.ds(src, cols)]


def grads_core(ids, grads, after):
    rows, hidden = grads.shape
    return pl.pallas_call(
        grads_core_kernel,
        in_specs=in_smem(1) + in_vmem(1) + in_place(1),
        out_specs=in_vmem(1)[0],
        out_shape=jax.ShapeDtypeStruct((rows, hidden // 2 + LANES), grads.dtype),
        compiler_params=params(16),
        cost_estimate=pl.CostEstimate(flops=0, bytes_accessed=1, transcendentals=0),
    )(ids, grads, after)


def grads_y_kernel(grad_ref, sent_ref, got_ref, _, out_ref):
    rows, hidden = grad_ref.shape
    wide = lax.axis_size("wide")
    cols = hidden // wide
    me = lax.axis_index("wide")
    for k in range(wide // 4):
        src = pl.multiple_of((me ^ (4 * k + 2)) * cols, cols)
        place = slice(k * cols, (k + 1) * cols)
        out_ref[:rows, place] = grad_ref[:, pl.ds(src, cols)]
        out_ref[rows:, place] = got_ref[:, (2 * k + 1) * cols:(2 * k + 2) * cols]
    ids = slice(wide // 4 * cols, wide // 4 * cols + LANES)
    out_ref[:rows, ids] = sent_ref[:, wide // 2 * cols:]
    out_ref[rows:, ids] = got_ref[:, wide // 2 * cols:]


def grads_y(grads, sent, got, after):
    rows, hidden = grads.shape
    return pl.pallas_call(
        grads_y_kernel,
        in_specs=in_vmem(3) + in_place(1),
        out_specs=in_vmem(1)[0],
        out_shape=jax.ShapeDtypeStruct((2 * rows, hidden // 4 + LANES), grads.dtype),
        compiler_params=params(16),
        cost_estimate=pl.CostEstimate(flops=0, bytes_accessed=1, transcendentals=0),
    )(grads, sent, got, after)


def grads_z_kernel(grad_ref, sent_ref, got_ref, over_ref, *out_refs):
    rows = grad_ref.shape[0]
    cols = out_refs[0].shape[1] - LANES
    me = lax.axis_index("wide")
    for k, out_ref in enumerate(out_refs):
        src = pl.multiple_of((me ^ (4 * k)) * cols, cols)
        out_ref[:rows, :cols] = grad_ref[:, pl.ds(src, cols)]
        out_ref[rows:2 * rows, :cols] = got_ref[:, 2 * k * cols:(2 * k + 1) * cols]
        out_ref[2 * rows:, :cols] = over_ref[:, k * cols:(k + 1) * cols]
        out_ref[:rows, cols:] = sent_ref[:, 2 * len(out_refs) * cols:]
        out_ref[rows:2 * rows, cols:] = got_ref[:, 2 * len(out_refs) * cols:]
        out_ref[2 * rows:, cols:] = over_ref[:, len(out_refs) * cols:]


def grads_z(grads, sent, got, over, wide_count):
    rows, hidden = grads.shape
    count = wide_count // 4
    piece = jax.ShapeDtypeStruct((4 * rows, hidden // wide_count + LANES), grads.dtype)
    return pl.pallas_call(
        grads_z_kernel,
        in_specs=in_vmem(4),
        out_specs=in_vmem(count),
        out_shape=[piece] * count,
        compiler_params=params(16),
        cost_estimate=pl.CostEstimate(flops=0, bytes_accessed=1, transcendentals=0),
    )(grads, sent, got, over)


def rotate_kernel(act_count, done, *refs):
    act_refs, basis_ref, out_ref = refs[:act_count], refs[act_count], refs[-1]
    depth, width = basis_ref.shape
    if done:
        out_ref[:, :done] = refs[act_count + 1][...]
    for k in range(width // depth):
        cols = slice(k * depth, (k + 1) * depth)
        act = jnp.concatenate([ref[:, cols] for ref in act_refs], axis=0)
        turned = jnp.dot(act, basis_ref[:, cols], preferred_element_type=jnp.float32)
        out_ref[cols, done:] = turned.astype(jnp.bfloat16).T


def rotate(act_pieces, basis, after, first=None):
    width = basis.shape[1]
    done = 0 if first is None else first.shape[1]
    tokens = done + sum(x.shape[0] for x in act_pieces)
    more = [after] if first is None else [first]
    return pl.pallas_call(
        functools.partial(rotate_kernel, len(act_pieces), done),
        in_specs=in_vmem(len(act_pieces) + 1) + (in_place(1) if first is None else in_vmem(1)),
        out_specs=in_vmem(1)[0],
        out_shape=jax.ShapeDtypeStruct((width, tokens), jnp.bfloat16),
        compiler_params=params(16 if tokens <= 256 else 32),
        cost_estimate=pl.CostEstimate(flops=0, bytes_accessed=1, transcendentals=0),
    )(*act_pieces, basis, *more)


def image_kernel(batch_count, total, per, rot_ref, *refs):
    left_refs, half_refs = refs[:batch_count], refs[batch_count:3 * batch_count]
    eig_ref, out_ref, right_ref, turn_ref, pre_a, pre_b = refs[3 * batch_count:]
    rows, chunk = eig_ref.shape
    tile = min(256, chunk)
    s = pl.program_id(0)

    @pl.when(s == 0)
    def _():
        side = right_ref.shape[2] // 2
        for b in range(batch_count):
            for other in range(2):
                at = pl.multiple_of(((lax.axis_index("wide") & 1) ^ other) * side, side)
                ref = half_refs[2 * b + other]
                right_ref[b, :, pl.ds(at, side)] = ref[:, ref.shape[1] - side:]

    @pl.when(jnp.logical_and(lax.rem(s, per) == 0, s < total))
    def _():
        for b in range(batch_count):
            turn_ref[b] = left_refs[b][...].T

    @pl.when(lax.rem(s, per) == 1)
    def _():
        out_ref[...] = jnp.zeros_like(out_ref)

    def produce(pre):
        start = lax.rem(s, per) * chunk
        for at in range(0, chunk, tile):
            cols = pl.ds(pl.multiple_of(start + at, tile), tile)
            damped = eig_ref[:, at:at + tile].astype(jnp.float32) + damping
            inverse = pl.reciprocal(damped, approx=True)
            for b in range(batch_count):
                outer_sum = jnp.dot(
                    turn_ref[b], right_ref[b, :, cols], preferred_element_type=jnp.float32
                )
                pre[b * rows:(b + 1) * rows, at:at + tile] = (
                    outer_sum * inverse
                ).astype(jnp.bfloat16)

    def absorb(pre):
        rot = rot_ref[pl.ds(pl.multiple_of(lax.rem(s - 1, per) * chunk, chunk), chunk), :]
        for b in range(batch_count):
            out_ref[b] += jnp.dot(
                pre[b * rows:(b + 1) * rows, :], rot, preferred_element_type=jnp.float32
            )

    between = jnp.logical_and(s > 0, s < total)
    odd = lax.rem(s, 2) == 1

    @pl.when(s == 0)
    def _():
        produce(pre_a)

    @pl.when(jnp.logical_and(between, odd))
    def _():
        produce(pre_b)
        absorb(pre_a)

    @pl.when(jnp.logical_and(between, jnp.logical_not(odd)))
    def _():
        produce(pre_a)
        absorb(pre_b)

    @pl.when(s == total)
    def _():
        absorb(pre_a if total % 2 else pre_b)


def images(rot, lefts, halves, eigenvalues):
    batch_count, tokens = len(lefts), rot.shape[1]
    hidden, width = eigenvalues.shape
    rows = min(1024, hidden)
    chunk = min(1024, width // 2)
    per = width // chunk
    total = hidden // rows * per
    now = lambda s: jnp.minimum(s, total - 1)
    before = lambda s: jnp.maximum(s - 1, 0)
    return pl.pallas_call(
        functools.partial(image_kernel, batch_count, total, per),
        grid=(total + 1,),
        in_specs=[whole_block(rot.shape)]
        + [pl.BlockSpec((QT, rows), lambda s: (0, now(s) // per)) for _ in lefts]
        + [whole_block(x.shape) for x in halves]
        + [pl.BlockSpec((rows, chunk), lambda s: (now(s) // per, now(s) % per))],
        out_specs=pl.BlockSpec((batch_count, rows, tokens), lambda s: (0, before(s) // per, 0)),
        out_shape=jax.ShapeDtypeStruct((batch_count, hidden, tokens), jnp.float32),
        scratch_shapes=[
            pltpu.VMEM((batch_count, QT, width), jnp.bfloat16),
            pltpu.VMEM((batch_count, rows, QT), jnp.bfloat16),
            pltpu.VMEM((batch_count * rows, chunk), jnp.bfloat16),
            pltpu.VMEM((batch_count * rows, chunk), jnp.bfloat16),
        ],
        compiler_params=params(32 if tokens <= 256 else 48),
        cost_estimate=pl.CostEstimate(flops=0, bytes_accessed=1, transcendentals=0),
    )(rot, *lefts, *halves, eigenvalues)


def score_kernel(batch_count, ranks, count, *refs):
    grad_refs, ids_refs = refs[:count], refs[count:2 * count]
    basis_ref, image_ref, out_ref, token_ref = refs[2 * count:]
    step = pl.program_id(0)
    rows = grad_refs[0].shape[0] // 4

    def tokens_of(pieces):
        return jnp.concatenate(
            [pieces[r // 4][r % 4 * rows:(r % 4 + 1) * rows, :] for r in ranks], axis=0
        )

    @pl.when(step == 0)
    def _():
        token_ref[...] = jnp.zeros_like(token_ref)

    turned = jnp.dot(tokens_of(grad_refs), basis_ref[...], preferred_element_type=jnp.float32)
    turned = turned.astype(jnp.bfloat16).T.astype(jnp.float32)
    for b in range(batch_count):
        token_ref[b:b + 1, :] += jnp.sum(image_ref[b] * turned, axis=0, keepdims=True)

    @pl.when(step == pl.num_programs(0) - 1)
    def _():
        ids = tokens_of(ids_refs).astype(jnp.float32)
        seqs = lax.broadcasted_iota(jnp.int32, ids.shape, 1).astype(jnp.float32)
        member = jnp.where(ids == seqs, 1.0, 0.0).T
        own = lax.rem(lax.axis_index("groups"), batch_count)
        for b in range(batch_count):
            sums = jnp.sum(member * token_ref[b:b + 1, :], axis=1, keepdims=True)
            out_ref[lax.rem(own + b, batch_count)] = sums[:out_ref.shape[1], :]


def score_parts(grad_pieces, ranks, grad_basis, image, seq_count):
    batch_count, hidden, tokens = image.shape
    count = len(grad_pieces)
    rows = grad_pieces[0].shape[0]
    inner = min(grad_basis.shape[0], hidden)
    return pl.pallas_call(
        functools.partial(score_kernel, batch_count, ranks, count),
        grid=(hidden // inner,),
        in_specs=[pl.BlockSpec((rows, inner), lambda i: (0, i))] * count
        + [pl.BlockSpec((rows, LANES), lambda i: (0, hidden // LANES))] * count
        + [
            pl.BlockSpec((grad_basis.shape[0], inner), lambda i: (0, i)),
            pl.BlockSpec((batch_count, inner, tokens), lambda i: (0, i, 0)),
        ],
        out_specs=pl.BlockSpec((batch_count, seq_count, 1), lambda i: (0, 0, 0)),
        out_shape=jax.ShapeDtypeStruct((batch_count, seq_count, 1), jnp.float32),
        scratch_shapes=[pltpu.VMEM((8, tokens), jnp.float32)],
        compiler_params=params(32 if tokens <= 256 else 48),
        cost_estimate=pl.CostEstimate(
            flops=2 * tokens * hidden * grad_basis.shape[0],
            bytes_accessed=4 * image.size,
            transcendentals=0,
        ),
    )(*grad_pieces, *grad_pieces, grad_basis, image)


def per_device(
    train_act, train_grad, seq_ids, act_basis, grad_basis, eigenvalues, query_factors, owners
):
    wide_count = lax.axis_size("wide")
    along_z = range(wide_count // 4)
    tok_local = train_act.shape[0]
    seq_count = tok_local * wide_count // SEQ_MEAN
    cols = grad_basis.shape[1]
    hidden = train_grad.shape[1]
    batch_count = owners.shape[0]
    score_scale = 1.0 / math.sqrt(FF * D * QT * SEQ_MEAN)

    half = (query_factors.shape[2] - hidden) // 2
    order = [4 * k + r for r in (0, 2, 1, 3) for k in along_z]
    keep, give = cut_factors(query_factors, order, hidden, batch_count)
    flags = owner_flags(owners, keep)
    grads_sent = grads_core(seq_ids, train_grad, keep)
    keep, give = pick(flags, keep, swap(give, "wide", 1), 0, cols, half, [grads_sent])
    grads_got = swap(grads_sent, "wide", 1)
    grads_over = grads_y(train_grad, grads_sent, grads_got, give)
    parts = pick(flags, keep, swap(give, "wide", 2), 1, cols, half, [grads_over])
    grads_over = swap(grads_over, "wide", 2)
    sent = grads_z(train_grad, grads_sent, grads_got, grads_over, wide_count)
    acts = join([train_act] + [swap(train_act, "wide", 4 * k) for k in along_z if k], parts[0])
    ranks = [4 * k for k in along_z]
    over = swap(acts, "wide", 2)
    first = rotate([acts], act_basis, parts[0])
    parts = [swap(parts[k], "wide", 4 * k) if k else parts[0] for k in along_z]
    held = pick_one(flags, parts, [over, first, sent[0]])

    lefts = [held, swap(held, "groups", 1)]
    halves = []
    for x in lefts:
        halves += [x, swap(x, "wide", 1)]
    over = gate(over, [held])
    rot = rotate([over, swap(gate(acts, [held]), "wide", 1), swap(over, "wide", 1)], act_basis, None, first)
    ranks = [r + more for more in (0, 2, 1, 3) for r in ranks]

    grads = [swap(sent[k], "wide", 4 * k) if k else sent[0] for k in along_z]

    image = images(rot, lefts, halves, eigenvalues)
    parts = score_parts(grads, ranks, grad_basis, image, seq_count)
    for step, count in ((1, 4), (4, wide_count // 4)):
        parts = parts + sum(swap(parts, "wide", step * n) for n in range(1, count))
    return parts[:, :, 0].T * score_scale


def solution(mesh):
    return jax.shard_map(
        per_device,
        mesh=mesh,
        in_specs=(
            P(("groups", "wide"), None),
            P(("groups", "wide"), None),
            P(("groups", "wide")),
            P(),
            P(None, "wide"),
            P("wide", None),
            P("wide", None, None),
            P(),
        ),
        out_specs=P("groups", None),
        check_vma=False,
    )
```

```python
import functools
import math

import jax
import jax.numpy as jnp
from jax import lax
from jax.experimental import pallas as pl
from jax.experimental.pallas import tpu as pltpu
from jax.sharding import PartitionSpec as P

D = 4096
FF = 32768
SEQ_MEAN = 32
QT = 16
LANES = 128
SCORE_SCALE = 1.0 / math.sqrt(FF * D * QT * SEQ_MEAN)


damping = 0.1


def params(mib):
    return pltpu.CompilerParams(vmem_limit_bytes=mib * 1024 * 1024)


def whole_block(shape):
    return pl.BlockSpec(shape, lambda *_: (0,) * len(shape), pipeline_mode=pl.Buffered(1))


def swap(x, axis, bit):
    count = lax.axis_size(axis)
    return lax.ppermute(x, axis, [(i, i ^ bit) for i in range(count)])


def in_smem(n):
    return [pl.BlockSpec(memory_space=pltpu.SMEM)] * n


def in_vmem(n):
    return [pl.BlockSpec(memory_space=pltpu.VMEM)] * n


def in_place(n):
    return [pl.BlockSpec(memory_space=pl.ANY)] * n


def cut_factors_kernel(order, hidden, batch_count, fac_ref, keep_ref, give_ref):
    cols = hidden // len(order)
    half = (fac_ref.shape[2] - hidden) // 2
    me, batch = lax.axis_index("wide"), lax.rem(lax.axis_index("groups"), batch_count)
    for part, out_ref in enumerate((keep_ref, give_ref)):
        picked = order[part * len(order) // 2:(part + 1) * len(order) // 2]
        for at, r in enumerate(picked):
            src = pl.multiple_of((me ^ r) * cols, cols)
            out_ref[:, at * cols:(at + 1) * cols] = fac_ref[batch, :, pl.ds(src, cols)]
        src = pl.multiple_of(hidden + ((me & 1) ^ part) * half, LANES)
        out_ref[:, len(picked) * cols:] = fac_ref[batch, :, pl.ds(src, half)]


def cut_factors(factors, order, hidden, batch_count):
    rows, width = factors.shape[1:]
    half = jax.ShapeDtypeStruct((rows, width // 2), factors.dtype)
    return pl.pallas_call(
        functools.partial(cut_factors_kernel, order, hidden, batch_count),
        in_specs=in_vmem(1),
        out_specs=in_vmem(2),
        out_shape=[half] * 2,
        compiler_params=params(16),
        cost_estimate=pl.CostEstimate(flops=0, bytes_accessed=1, transcendentals=0),
    )(factors)


def flags_kernel(batch_count, owners_ref, _, flag_ref):
    me, batch = lax.axis_index("wide"), lax.rem(lax.axis_index("groups"), batch_count)
    apart = owners_ref[batch] ^ me
    lane = lax.broadcasted_iota(jnp.int32, flag_ref.shape, 1)
    flags = jnp.where(lane - 2 == apart // 4, 1.0, 0.0)
    for step in range(2):
        same = jnp.where((apart & (1 << step)) == 0, 1.0, 0.0)
        flags = jnp.where(lane == step, same, flags)
    flag_ref[...] = flags.astype(flag_ref.dtype)


def owner_flags(owners, after):
    return pl.pallas_call(
        functools.partial(flags_kernel, owners.shape[0]),
        in_specs=in_smem(1) + in_place(1),
        out_specs=in_vmem(1)[0],
        out_shape=jax.ShapeDtypeStruct((after.shape[0], LANES), after.dtype),
        compiler_params=params(16),
        cost_estimate=pl.CostEstimate(flops=0, bytes_accessed=1, transcendentals=0),
    )(owners, after)


def pick_kernel(step, cols, half, flag_ref, keep_ref, got_ref, *refs):
    out_refs = refs[-2:] if step == 0 else refs[-((keep_ref.shape[1] - half) // cols):]
    same = flag_ref[:, step:step + 1]
    differs = 1 - same

    def chosen(at, size):
        place = slice(at, at + size)
        return keep_ref[:, place] * same + got_ref[:, place] * differs

    size = out_refs[0].shape[1] - half
    shared = chosen(len(out_refs) * size, half)
    for n, out_ref in enumerate(out_refs):
        out_ref[:, :size] = chosen(n * size, size)
        out_ref[:, size:] = shared


def pick(flags, keep, got, step, cols, half, after):
    rows, width = keep.shape
    parts = 2 if step == 0 else (width - half) // cols
    size = (width - half) // parts + half
    return pl.pallas_call(
        functools.partial(pick_kernel, step, cols, half),
        in_specs=in_vmem(3) + in_place(len(after)),
        out_specs=in_vmem(parts),
        out_shape=[jax.ShapeDtypeStruct((rows, size), keep.dtype)] * parts,
        compiler_params=params(16),
        cost_estimate=pl.CostEstimate(flops=0, bytes_accessed=1, transcendentals=0),
    )(flags, keep, got, *after)


def pick_one_kernel(count, flag_ref, *refs):
    refs[-1][...] = sum(refs[k][...] * flag_ref[:, 2 + k:3 + k] for k in range(count))


def pick_one(flags, pieces, after):
    return pl.pallas_call(
        functools.partial(pick_one_kernel, len(pieces)),
        in_specs=in_vmem(1 + len(pieces)) + in_place(len(after)),
        out_specs=in_vmem(1)[0],
        out_shape=jax.ShapeDtypeStruct(pieces[0].shape, pieces[0].dtype),
        compiler_params=params(16),
        cost_estimate=pl.CostEstimate(flops=0, bytes_accessed=1, transcendentals=0),
    )(flags, *pieces, *after)


def join_kernel(*refs):
    out_ref = refs[-1]
    rows = refs[0].shape[0]
    for n, ref in enumerate(refs[:-2]):
        out_ref[n * rows:(n + 1) * rows, :] = ref[...]


def join(pieces, after):
    rows, width = pieces[0].shape
    return pl.pallas_call(
        join_kernel,
        in_specs=in_vmem(len(pieces)) + in_place(1),
        out_specs=in_vmem(1)[0],
        out_shape=jax.ShapeDtypeStruct((len(pieces) * rows, width), pieces[0].dtype),
        compiler_params=params(16),
        cost_estimate=pl.CostEstimate(flops=0, bytes_accessed=1, transcendentals=0),
    )(*pieces, after)


def gate_kernel(*_):
    pass


def gate(array, after):
    return pl.pallas_call(
        gate_kernel,
        in_specs=in_place(1 + len(after)),
        out_specs=in_place(1)[0],
        out_shape=jax.ShapeDtypeStruct(array.shape, array.dtype),
        input_output_aliases={0: 0},
        compiler_params=params(1),
        cost_estimate=pl.CostEstimate(flops=0, bytes_accessed=1, transcendentals=0),
    )(array, *after)


def grads_core_kernel(ids_ref, grad_ref, _, out_ref):
    rows, hidden = grad_ref.shape
    wide = lax.axis_size("wide")
    cols = hidden // wide
    me = lax.axis_index("wide")
    row = lax.broadcasted_iota(jnp.int32, (rows, LANES), 0)
    ids = jnp.zeros((rows, LANES), jnp.int32)
    for t in range(rows):
        ids = jnp.where(row == t, ids_ref[t], ids)
    out_ref[:, wide // 2 * cols:] = ids.astype(jnp.float32).astype(out_ref.dtype)
    for q in range(wide // 2):
        src = pl.multiple_of((me ^ (2 * q + 1)) * cols, cols)
        out_ref[:, q * cols:(q + 1) * cols] = grad_ref[:, pl.ds(src, cols)]


def grads_core(ids, grads, after):
    rows, hidden = grads.shape
    return pl.pallas_call(
        grads_core_kernel,
        in_specs=in_smem(1) + in_vmem(1) + in_place(1),
        out_specs=in_vmem(1)[0],
        out_shape=jax.ShapeDtypeStruct((rows, hidden // 2 + LANES), grads.dtype),
        compiler_params=params(16),
        cost_estimate=pl.CostEstimate(flops=0, bytes_accessed=1, transcendentals=0),
    )(ids, grads, after)


def grads_y_kernel(grad_ref, sent_ref, got_ref, _, out_ref):
    rows, hidden = grad_ref.shape
    wide = lax.axis_size("wide")
    cols = hidden // wide
    me = lax.axis_index("wide")
    for k in range(wide // 4):
        src = pl.multiple_of((me ^ (4 * k + 2)) * cols, cols)
        place = slice(k * cols, (k + 1) * cols)
        out_ref[:rows, place] = grad_ref[:, pl.ds(src, cols)]
        out_ref[rows:, place] = got_ref[:, (2 * k + 1) * cols:(2 * k + 2) * cols]
    ids = slice(wide // 4 * cols, wide // 4 * cols + LANES)
    out_ref[:rows, ids] = sent_ref[:, wide // 2 * cols:]
    out_ref[rows:, ids] = got_ref[:, wide // 2 * cols:]


def grads_y(grads, sent, got, after):
    rows, hidden = grads.shape
    return pl.pallas_call(
        grads_y_kernel,
        in_specs=in_vmem(3) + in_place(1),
        out_specs=in_vmem(1)[0],
        out_shape=jax.ShapeDtypeStruct((2 * rows, hidden // 4 + LANES), grads.dtype),
        compiler_params=params(16),
        cost_estimate=pl.CostEstimate(flops=0, bytes_accessed=1, transcendentals=0),
    )(grads, sent, got, after)


def grads_z_kernel(grad_ref, sent_ref, got_ref, over_ref, *out_refs):
    rows = grad_ref.shape[0]
    cols = out_refs[0].shape[1] - LANES
    me = lax.axis_index("wide")
    for k, out_ref in enumerate(out_refs):
        src = pl.multiple_of((me ^ (4 * k)) * cols, cols)
        out_ref[:rows, :cols] = grad_ref[:, pl.ds(src, cols)]
        out_ref[rows:2 * rows, :cols] = got_ref[:, 2 * k * cols:(2 * k + 1) * cols]
        out_ref[2 * rows:, :cols] = over_ref[:, k * cols:(k + 1) * cols]
        out_ref[:rows, cols:] = sent_ref[:, 2 * len(out_refs) * cols:]
        out_ref[rows:2 * rows, cols:] = got_ref[:, 2 * len(out_refs) * cols:]
        out_ref[2 * rows:, cols:] = over_ref[:, len(out_refs) * cols:]


def grads_z(grads, sent, got, over, wide_count):
    rows, hidden = grads.shape
    count = wide_count // 4
    piece = jax.ShapeDtypeStruct((4 * rows, hidden // wide_count + LANES), grads.dtype)
    return pl.pallas_call(
        grads_z_kernel,
        in_specs=in_vmem(4),
        out_specs=in_vmem(count),
        out_shape=[piece] * count,
        compiler_params=params(16),
        cost_estimate=pl.CostEstimate(flops=0, bytes_accessed=1, transcendentals=0),
    )(grads, sent, got, over)


def rotate_kernel(act_count, done, *refs):
    act_refs, basis_ref, out_ref = refs[:act_count], refs[act_count], refs[-1]
    depth, width = basis_ref.shape
    if done:
        out_ref[:, :done] = refs[act_count + 1][...]
    for k in range(width // depth):
        cols = slice(k * depth, (k + 1) * depth)
        act = jnp.concatenate([ref[:, cols] for ref in act_refs], axis=0)
        turned = jnp.dot(act, basis_ref[:, cols], preferred_element_type=jnp.float32)
        out_ref[cols, done:] = turned.astype(jnp.bfloat16).T


def rotate(act_pieces, basis, after, first=None):
    width = basis.shape[1]
    done = 0 if first is None else first.shape[1]
    tokens = done + sum(x.shape[0] for x in act_pieces)
    more = [after] if first is None else [first]
    return pl.pallas_call(
        functools.partial(rotate_kernel, len(act_pieces), done),
        in_specs=in_vmem(len(act_pieces) + 1) + (in_place(1) if first is None else in_vmem(1)),
        out_specs=in_vmem(1)[0],
        out_shape=jax.ShapeDtypeStruct((width, tokens), jnp.bfloat16),
        compiler_params=params(16 if tokens <= 256 else 32),
        cost_estimate=pl.CostEstimate(flops=0, bytes_accessed=1, transcendentals=0),
    )(*act_pieces, basis, *more)


def image_kernel(batch_count, total, per, rot_ref, *refs):
    left_refs, half_refs = refs[:batch_count], refs[batch_count:3 * batch_count]
    eig_ref, out_ref, right_ref, turn_ref, pre_a, pre_b = refs[3 * batch_count:]
    rows, chunk = eig_ref.shape
    tile = min(256, chunk)
    s = pl.program_id(0)

    @pl.when(s == 0)
    def _():
        side = right_ref.shape[2] // 2
        right_ref[...] = jnp.zeros_like(right_ref)
        turn_ref[...] = jnp.zeros_like(turn_ref)
        for b in range(batch_count):
            for other in range(2):
                at = pl.multiple_of(((lax.axis_index("wide") & 1) ^ other) * side, side)
                ref = half_refs[2 * b + other]
                right_ref[b, :QT, pl.ds(at, side)] = ref[:, ref.shape[1] - side:]

    @pl.when(jnp.logical_and(lax.rem(s, per) == 0, s < total))
    def _():
        for b in range(batch_count):
            turn_ref[b, :, :QT] = left_refs[b][...].T

    @pl.when(lax.rem(s, per) == 1)
    def _():
        out_ref[...] = jnp.zeros_like(out_ref)

    def produce(pre):
        start = lax.rem(s, per) * chunk
        for at in range(0, chunk, tile):
            cols = pl.ds(pl.multiple_of(start + at, tile), tile)
            damped = eig_ref[:, at:at + tile].astype(jnp.float32) + damping
            inverse = pl.reciprocal(damped, approx=True)
            for b in range(batch_count):
                outer_sum = jnp.dot(
                    turn_ref[b], right_ref[b, :, cols], preferred_element_type=jnp.float32
                )
                pre[b * rows:(b + 1) * rows, at:at + tile] = (
                    outer_sum * inverse
                ).astype(jnp.bfloat16)

    def absorb(pre):
        rot = rot_ref[pl.ds(pl.multiple_of(lax.rem(s - 1, per) * chunk, chunk), chunk), :]
        for b in range(batch_count):
            out_ref[b] += jnp.dot(
                pre[b * rows:(b + 1) * rows, :], rot, preferred_element_type=jnp.float32
            )

    between = jnp.logical_and(s > 0, s < total)
    odd = lax.rem(s, 2) == 1

    @pl.when(s == 0)
    def _():
        produce(pre_a)

    @pl.when(jnp.logical_and(between, odd))
    def _():
        produce(pre_b)
        absorb(pre_a)

    @pl.when(jnp.logical_and(between, jnp.logical_not(odd)))
    def _():
        produce(pre_a)
        absorb(pre_b)

    @pl.when(s == total)
    def _():
        absorb(pre_a if total % 2 else pre_b)


def images(rot, lefts, halves, eigenvalues):
    batch_count, tokens = len(lefts), rot.shape[1]
    hidden, width = eigenvalues.shape
    rows = min(1024, hidden)
    chunk = min(1024, width // 2)
    per = width // chunk
    total = hidden // rows * per
    now = lambda s: jnp.minimum(s, total - 1)
    before = lambda s: jnp.maximum(s - 1, 0)
    return pl.pallas_call(
        functools.partial(image_kernel, batch_count, total, per),
        grid=(total + 1,),
        in_specs=[whole_block(rot.shape)]
        + [pl.BlockSpec((QT, rows), lambda s: (0, now(s) // per)) for _ in lefts]
        + [whole_block(x.shape) for x in halves]
        + [pl.BlockSpec((rows, chunk), lambda s: (now(s) // per, now(s) % per))],
        out_specs=pl.BlockSpec((batch_count, rows, tokens), lambda s: (0, before(s) // per, 0)),
        out_shape=jax.ShapeDtypeStruct((batch_count, hidden, tokens), jnp.float32),
        scratch_shapes=[
            pltpu.VMEM((batch_count, LANES, width), jnp.bfloat16),
            pltpu.VMEM((batch_count, rows, LANES), jnp.bfloat16),
            pltpu.VMEM((batch_count * rows, chunk), jnp.bfloat16),
            pltpu.VMEM((batch_count * rows, chunk), jnp.bfloat16),
        ],
        compiler_params=params(32 if tokens <= 256 else 48),
        cost_estimate=pl.CostEstimate(flops=10**9, bytes_accessed=1, transcendentals=0),
    )(rot, *lefts, *halves, eigenvalues)


def score_kernel(batch_count, ranks, count, *refs):
    grad_refs, ids_refs = refs[:count], refs[count:2 * count]
    basis_ref, image_ref, out_ref, token_ref = refs[2 * count:]
    step = pl.program_id(0)
    rows = grad_refs[0].shape[0] // 4

    def tokens_of(pieces):
        return jnp.concatenate(
            [pieces[r // 4][r % 4 * rows:(r % 4 + 1) * rows, :] for r in ranks], axis=0
        )

    @pl.when(step == 0)
    def _():
        token_ref[...] = jnp.zeros_like(token_ref)

    turned = jnp.dot(tokens_of(grad_refs), basis_ref[...], preferred_element_type=jnp.float32)
    turned = turned.astype(jnp.bfloat16).T.astype(jnp.float32)
    for b in range(batch_count):
        token_ref[b:b + 1, :] += jnp.sum(image_ref[b] * turned, axis=0, keepdims=True)

    @pl.when(step == pl.num_programs(0) - 1)
    def _():
        ids = tokens_of(ids_refs).astype(jnp.float32)
        seqs = lax.broadcasted_iota(jnp.int32, ids.shape, 1).astype(jnp.float32)
        member = jnp.where(ids == seqs, 1.0, 0.0).T
        own = lax.rem(lax.axis_index("groups"), batch_count)
        for b in range(batch_count):
            sums = jnp.sum(member * token_ref[b:b + 1, :], axis=1, keepdims=True)
            out_ref[lax.rem(own + b, batch_count)] = sums[:out_ref.shape[1], :] * SCORE_SCALE


def score_parts(grad_pieces, ranks, grad_basis, image, seq_count):
    batch_count, hidden, tokens = image.shape
    count = len(grad_pieces)
    rows = grad_pieces[0].shape[0]
    inner = min(grad_basis.shape[0], hidden)
    return pl.pallas_call(
        functools.partial(score_kernel, batch_count, ranks, count),
        grid=(hidden // inner,),
        in_specs=[pl.BlockSpec((rows, inner), lambda i: (0, i))] * count
        + [pl.BlockSpec((rows, LANES), lambda i: (0, hidden // LANES))] * count
        + [
            pl.BlockSpec((grad_basis.shape[0], inner), lambda i: (0, i)),
            pl.BlockSpec((batch_count, inner, tokens), lambda i: (0, i, 0)),
        ],
        out_specs=pl.BlockSpec((batch_count, seq_count, 1), lambda i: (0, 0, 0)),
        out_shape=jax.ShapeDtypeStruct((batch_count, seq_count, 1), jnp.float32),
        scratch_shapes=[pltpu.VMEM((8, tokens), jnp.float32)],
        compiler_params=params(32 if tokens <= 256 else 48),
        cost_estimate=pl.CostEstimate(
            flops=2 * tokens * hidden * grad_basis.shape[0],
            bytes_accessed=4 * image.size,
            transcendentals=0,
        ),
    )(*grad_pieces, *grad_pieces, grad_basis, image)


def per_device(
    train_act, train_grad, seq_ids, act_basis, grad_basis, eigenvalues, query_factors, owners
):
    wide_count = lax.axis_size("wide")
    along_z = range(wide_count // 4)
    tok_local = train_act.shape[0]
    seq_count = tok_local * wide_count // SEQ_MEAN
    cols = grad_basis.shape[1]
    hidden = train_grad.shape[1]
    batch_count = owners.shape[0]

    half = (query_factors.shape[2] - hidden) // 2
    order = [4 * k + r for r in (0, 2, 1, 3) for k in along_z]
    keep, give = cut_factors(query_factors, order, hidden, batch_count)
    flags = owner_flags(owners, keep)
    grads_sent = grads_core(seq_ids, train_grad, keep)
    keep, give = pick(flags, keep, swap(give, "wide", 1), 0, cols, half, [grads_sent])
    grads_got = swap(grads_sent, "wide", 1)
    grads_over = grads_y(train_grad, grads_sent, grads_got, give)
    parts = pick(flags, keep, swap(give, "wide", 2), 1, cols, half, [grads_over])
    grads_over = swap(grads_over, "wide", 2)
    sent = grads_z(train_grad, grads_sent, grads_got, grads_over, wide_count)
    acts = join([train_act] + [swap(train_act, "wide", 4 * k) for k in along_z if k], parts[0])
    ranks = [4 * k for k in along_z]
    over = swap(acts, "wide", 2)
    first = rotate([acts], act_basis, parts[0])
    parts = [swap(parts[k], "wide", 4 * k) if k else parts[0] for k in along_z]
    held = pick_one(flags, parts, [over, first, sent[0]])

    over = gate(over, [held])
    rot = rotate([over, swap(gate(acts, [held]), "wide", 1), swap(over, "wide", 1)], act_basis, None, first)
    ranks = [r + more for more in (0, 2, 1, 3) for r in ranks]
    lefts = [held, gate(swap(held, "groups", 1), [rot])]
    halves = []
    for x in lefts:
        halves += [x, swap(x, "wide", 1)]
    grads = [swap(sent[k], "wide", 4 * k) if k else sent[0] for k in along_z]

    image = images(rot, lefts, halves, eigenvalues)
    parts = score_parts(grads, ranks, grad_basis, image, seq_count)
    for step, count in ((1, 4), (4, wide_count // 4)):
        parts = parts + sum(swap(parts, "wide", step * n) for n in range(1, count))
    return parts[:, :, 0].T


def solution(mesh):
    return jax.shard_map(
        per_device,
        mesh=mesh,
        in_specs=(
            P(("groups", "wide"), None),
            P(("groups", "wide"), None),
            P(("groups", "wide")),
            P(),
            P(None, "wide"),
            P("wide", None),
            P("wide", None, None),
            P(),
        ),
        out_specs=P("groups", None),
        check_vma=False,
    )
```

```python
import functools
import math

import jax
import jax.numpy as jnp
from jax import lax
from jax.experimental import pallas as pl
from jax.experimental.pallas import tpu as pltpu
from jax.sharding import PartitionSpec as P

D = 4096
FF = 32768
SEQ_MEAN = 32
QT = 16
LANES = 128
SCORE_SCALE = 1.0 / math.sqrt(FF * D * QT * SEQ_MEAN)


damping = 0.1


def params(mib):
    return pltpu.CompilerParams(vmem_limit_bytes=mib * 1024 * 1024)


def whole_block(shape):
    return pl.BlockSpec(shape, lambda *_: (0,) * len(shape), pipeline_mode=pl.Buffered(1))


def swap(x, axis, bit):
    count = lax.axis_size(axis)
    return lax.ppermute(x, axis, [(i, i ^ bit) for i in range(count)])


def in_smem(n):
    return [pl.BlockSpec(memory_space=pltpu.SMEM)] * n


def in_vmem(n):
    return [pl.BlockSpec(memory_space=pltpu.VMEM)] * n


def in_place(n):
    return [pl.BlockSpec(memory_space=pl.ANY)] * n


def cut_factors_kernel(order, hidden, batch_count, fac_ref, keep_ref, give_ref):
    cols = hidden // len(order)
    half = (fac_ref.shape[2] - hidden) // 2
    me, batch = lax.axis_index("wide"), lax.rem(lax.axis_index("groups"), batch_count)
    for part, out_ref in enumerate((keep_ref, give_ref)):
        picked = order[part * len(order) // 2:(part + 1) * len(order) // 2]
        for at, r in enumerate(picked):
            src = pl.multiple_of((me ^ r) * cols, cols)
            out_ref[:, at * cols:(at + 1) * cols] = fac_ref[batch, :, pl.ds(src, cols)]
        src = pl.multiple_of(hidden + ((me & 1) ^ part) * half, LANES)
        out_ref[:, len(picked) * cols:] = fac_ref[batch, :, pl.ds(src, half)]


def cut_factors(factors, order, hidden, batch_count):
    rows, width = factors.shape[1:]
    half = jax.ShapeDtypeStruct((rows, width // 2), factors.dtype)
    return pl.pallas_call(
        functools.partial(cut_factors_kernel, order, hidden, batch_count),
        in_specs=in_vmem(1),
        out_specs=in_vmem(2),
        out_shape=[half] * 2,
        compiler_params=params(16),
        cost_estimate=pl.CostEstimate(flops=0, bytes_accessed=1, transcendentals=0),
    )(factors)


def flags_kernel(batch_count, owners_ref, _, flag_ref):
    me, batch = lax.axis_index("wide"), lax.rem(lax.axis_index("groups"), batch_count)
    apart = owners_ref[batch] ^ me
    lane = lax.broadcasted_iota(jnp.int32, flag_ref.shape, 1)
    flags = jnp.where(lane - 2 == apart // 4, 1.0, 0.0)
    for step in range(2):
        same = jnp.where((apart & (1 << step)) == 0, 1.0, 0.0)
        flags = jnp.where(lane == step, same, flags)
    flag_ref[...] = flags.astype(flag_ref.dtype)


def owner_flags(owners, after):
    return pl.pallas_call(
        functools.partial(flags_kernel, owners.shape[0]),
        in_specs=in_smem(1) + in_place(1),
        out_specs=in_vmem(1)[0],
        out_shape=jax.ShapeDtypeStruct((after.shape[0], LANES), after.dtype),
        compiler_params=params(16),
        cost_estimate=pl.CostEstimate(flops=0, bytes_accessed=1, transcendentals=0),
    )(owners, after)


def pick_kernel(step, cols, half, flag_ref, keep_ref, got_ref, *refs):
    out_refs = refs[-2:] if step == 0 else refs[-((keep_ref.shape[1] - half) // cols):]
    same = flag_ref[:, step:step + 1]
    differs = 1 - same

    def chosen(at, size):
        place = slice(at, at + size)
        return keep_ref[:, place] * same + got_ref[:, place] * differs

    size = out_refs[0].shape[1] - half
    shared = chosen(len(out_refs) * size, half)
    for n, out_ref in enumerate(out_refs):
        out_ref[:, :size] = chosen(n * size, size)
        out_ref[:, size:] = shared


def pick(flags, keep, got, step, cols, half, after):
    rows, width = keep.shape
    parts = 2 if step == 0 else (width - half) // cols
    size = (width - half) // parts + half
    return pl.pallas_call(
        functools.partial(pick_kernel, step, cols, half),
        in_specs=in_vmem(3) + in_place(len(after)),
        out_specs=in_vmem(parts),
        out_shape=[jax.ShapeDtypeStruct((rows, size), keep.dtype)] * parts,
        compiler_params=params(16),
        cost_estimate=pl.CostEstimate(flops=0, bytes_accessed=1, transcendentals=0),
    )(flags, keep, got, *after)


def pick_one_kernel(count, flag_ref, *refs):
    refs[-1][...] = sum(refs[k][...] * flag_ref[:, 2 + k:3 + k] for k in range(count))


def pick_one(flags, pieces, after):
    return pl.pallas_call(
        functools.partial(pick_one_kernel, len(pieces)),
        in_specs=in_vmem(1 + len(pieces)) + in_place(len(after)),
        out_specs=in_vmem(1)[0],
        out_shape=jax.ShapeDtypeStruct(pieces[0].shape, pieces[0].dtype),
        compiler_params=params(16),
        cost_estimate=pl.CostEstimate(flops=0, bytes_accessed=1, transcendentals=0),
    )(flags, *pieces, *after)


def join_kernel(*refs):
    out_ref = refs[-1]
    rows = refs[0].shape[0]
    for n, ref in enumerate(refs[:-2]):
        out_ref[n * rows:(n + 1) * rows, :] = ref[...]


def join(pieces, after):
    rows, width = pieces[0].shape
    return pl.pallas_call(
        join_kernel,
        in_specs=in_vmem(len(pieces)) + in_place(1),
        out_specs=in_vmem(1)[0],
        out_shape=jax.ShapeDtypeStruct((len(pieces) * rows, width), pieces[0].dtype),
        compiler_params=params(16),
        cost_estimate=pl.CostEstimate(flops=0, bytes_accessed=1, transcendentals=0),
    )(*pieces, after)


def gate_kernel(*_):
    pass


def gate(array, after):
    return pl.pallas_call(
        gate_kernel,
        in_specs=in_place(1 + len(after)),
        out_specs=in_place(1)[0],
        out_shape=jax.ShapeDtypeStruct(array.shape, array.dtype),
        input_output_aliases={0: 0},
        compiler_params=params(1),
        cost_estimate=pl.CostEstimate(flops=0, bytes_accessed=1, transcendentals=0),
    )(array, *after)


def grads_core_kernel(ids_ref, grad_ref, _, out_ref):
    rows, hidden = grad_ref.shape
    wide = lax.axis_size("wide")
    cols = hidden // wide
    me = lax.axis_index("wide")
    row = lax.broadcasted_iota(jnp.int32, (rows, LANES), 0)
    ids = jnp.zeros((rows, LANES), jnp.int32)
    for t in range(rows):
        ids = jnp.where(row == t, ids_ref[t], ids)
    out_ref[:, wide // 2 * cols:] = ids.astype(jnp.float32).astype(out_ref.dtype)
    for q in range(wide // 2):
        src = pl.multiple_of((me ^ (2 * q + 1)) * cols, cols)
        out_ref[:, q * cols:(q + 1) * cols] = grad_ref[:, pl.ds(src, cols)]


def grads_core(ids, grads, after):
    rows, hidden = grads.shape
    return pl.pallas_call(
        grads_core_kernel,
        in_specs=in_smem(1) + in_vmem(1) + in_place(1),
        out_specs=in_vmem(1)[0],
        out_shape=jax.ShapeDtypeStruct((rows, hidden // 2 + LANES), grads.dtype),
        compiler_params=params(16),
        cost_estimate=pl.CostEstimate(flops=0, bytes_accessed=1, transcendentals=0),
    )(ids, grads, after)


def grads_y_kernel(grad_ref, sent_ref, got_ref, _, out_ref):
    rows, hidden = grad_ref.shape
    wide = lax.axis_size("wide")
    cols = hidden // wide
    me = lax.axis_index("wide")
    for k in range(wide // 4):
        src = pl.multiple_of((me ^ (4 * k + 2)) * cols, cols)
        place = slice(k * cols, (k + 1) * cols)
        out_ref[:rows, place] = grad_ref[:, pl.ds(src, cols)]
        out_ref[rows:, place] = got_ref[:, (2 * k + 1) * cols:(2 * k + 2) * cols]
    ids = slice(wide // 4 * cols, wide // 4 * cols + LANES)
    out_ref[:rows, ids] = sent_ref[:, wide // 2 * cols:]
    out_ref[rows:, ids] = got_ref[:, wide // 2 * cols:]


def grads_y(grads, sent, got, after):
    rows, hidden = grads.shape
    return pl.pallas_call(
        grads_y_kernel,
        in_specs=in_vmem(3) + in_place(1),
        out_specs=in_vmem(1)[0],
        out_shape=jax.ShapeDtypeStruct((2 * rows, hidden // 4 + LANES), grads.dtype),
        compiler_params=params(16),
        cost_estimate=pl.CostEstimate(flops=0, bytes_accessed=1, transcendentals=0),
    )(grads, sent, got, after)


def grads_z_kernel(grad_ref, sent_ref, got_ref, over_ref, *out_refs):
    rows = grad_ref.shape[0]
    cols = out_refs[0].shape[1] - LANES
    me = lax.axis_index("wide")
    for k, out_ref in enumerate(out_refs):
        src = pl.multiple_of((me ^ (4 * k)) * cols, cols)
        out_ref[:rows, :cols] = grad_ref[:, pl.ds(src, cols)]
        out_ref[rows:2 * rows, :cols] = got_ref[:, 2 * k * cols:(2 * k + 1) * cols]
        out_ref[2 * rows:, :cols] = over_ref[:, k * cols:(k + 1) * cols]
        out_ref[:rows, cols:] = sent_ref[:, 2 * len(out_refs) * cols:]
        out_ref[rows:2 * rows, cols:] = got_ref[:, 2 * len(out_refs) * cols:]
        out_ref[2 * rows:, cols:] = over_ref[:, len(out_refs) * cols:]


def grads_z(grads, sent, got, over, wide_count):
    rows, hidden = grads.shape
    count = wide_count // 4
    piece = jax.ShapeDtypeStruct((4 * rows, hidden // wide_count + LANES), grads.dtype)
    return pl.pallas_call(
        grads_z_kernel,
        in_specs=in_vmem(4),
        out_specs=in_vmem(count),
        out_shape=[piece] * count,
        compiler_params=params(16),
        cost_estimate=pl.CostEstimate(flops=0, bytes_accessed=1, transcendentals=0),
    )(grads, sent, got, over)


def rotate_kernel(act_count, done, *refs):
    act_refs, basis_ref, out_ref = refs[:act_count], refs[act_count], refs[-1]
    depth, width = basis_ref.shape
    if done:
        out_ref[:, :done] = refs[act_count + 1][...]
    for k in range(width // depth):
        cols = slice(k * depth, (k + 1) * depth)
        act = jnp.concatenate([ref[:, cols] for ref in act_refs], axis=0)
        turned = jnp.dot(act, basis_ref[:, cols], preferred_element_type=jnp.float32)
        out_ref[cols, done:] = turned.astype(jnp.bfloat16).T


def rotate(act_pieces, basis, after, first=None):
    width = basis.shape[1]
    done = 0 if first is None else first.shape[1]
    tokens = done + sum(x.shape[0] for x in act_pieces)
    more = [after] if first is None else [first]
    return pl.pallas_call(
        functools.partial(rotate_kernel, len(act_pieces), done),
        in_specs=in_vmem(len(act_pieces) + 1) + (in_place(1) if first is None else in_vmem(1)),
        out_specs=in_vmem(1)[0],
        out_shape=jax.ShapeDtypeStruct((width, tokens), jnp.bfloat16),
        compiler_params=params(16 if tokens <= 256 else 32),
        cost_estimate=pl.CostEstimate(flops=0, bytes_accessed=1, transcendentals=0),
    )(*act_pieces, basis, *more)


def image_kernel(batch_count, total, per, rot_ref, *refs):
    left_refs, half_refs = refs[:batch_count], refs[batch_count:3 * batch_count]
    eig_ref, out_ref, right_ref, turn_ref, pre_a, pre_b = refs[3 * batch_count:]
    rows, chunk = eig_ref.shape
    tile = min(256, chunk)
    s = pl.program_id(0)

    @pl.when(s == 0)
    def _():
        side = right_ref.shape[2] // 2
        for b in range(batch_count):
            for other in range(2):
                at = pl.multiple_of(((lax.axis_index("wide") & 1) ^ other) * side, side)
                ref = half_refs[2 * b + other]
                right_ref[b, :, pl.ds(at, side)] = ref[:, ref.shape[1] - side:]

    @pl.when(jnp.logical_and(lax.rem(s, per) == 0, s < total))
    def _():
        for b in range(batch_count):
            turn_ref[b] = left_refs[b][...].T

    @pl.when(lax.rem(s, per) == 1)
    def _():
        out_ref[...] = jnp.zeros_like(out_ref)

    def produce(pre):
        start = lax.rem(s, per) * chunk
        for at in range(0, chunk, tile):
            cols = pl.ds(pl.multiple_of(start + at, tile), tile)
            damped = eig_ref[:, at:at + tile].astype(jnp.float32) + damping
            inverse = pl.reciprocal(damped, approx=True)
            for b in range(batch_count):
                outer_sum = jnp.dot(
                    turn_ref[b], right_ref[b, :, cols], preferred_element_type=jnp.float32
                )
                pre[b * rows:(b + 1) * rows, at:at + tile] = (
                    outer_sum * inverse
                ).astype(jnp.bfloat16)

    def absorb(pre):
        rot = rot_ref[pl.ds(pl.multiple_of(lax.rem(s - 1, per) * chunk, chunk), chunk), :]
        for b in range(batch_count):
            out_ref[b] += jnp.dot(
                pre[b * rows:(b + 1) * rows, :], rot, preferred_element_type=jnp.float32
            )

    between = jnp.logical_and(s > 0, s < total)
    odd = lax.rem(s, 2) == 1

    @pl.when(s == 0)
    def _():
        produce(pre_a)

    @pl.when(jnp.logical_and(between, odd))
    def _():
        produce(pre_b)
        absorb(pre_a)

    @pl.when(jnp.logical_and(between, jnp.logical_not(odd)))
    def _():
        produce(pre_a)
        absorb(pre_b)

    @pl.when(s == total)
    def _():
        absorb(pre_a if total % 2 else pre_b)


def images(rot, lefts, halves, eigenvalues):
    batch_count, tokens = len(lefts), rot.shape[1]
    hidden, width = eigenvalues.shape
    rows = min(1024, hidden)
    chunk = min(1024, width // 2)
    per = width // chunk
    total = hidden // rows * per
    now = lambda s: jnp.minimum(s, total - 1)
    before = lambda s: jnp.maximum(s - 1, 0)
    return pl.pallas_call(
        functools.partial(image_kernel, batch_count, total, per),
        grid=(total + 1,),
        in_specs=[whole_block(rot.shape)]
        + [pl.BlockSpec((QT, rows), lambda s: (0, now(s) // per)) for _ in lefts]
        + [whole_block(x.shape) for x in halves]
        + [pl.BlockSpec((rows, chunk), lambda s: (now(s) // per, now(s) % per))],
        out_specs=pl.BlockSpec((batch_count, rows, tokens), lambda s: (0, before(s) // per, 0)),
        out_shape=jax.ShapeDtypeStruct((batch_count, hidden, tokens), jnp.float32),
        scratch_shapes=[
            pltpu.VMEM((batch_count, QT, width), jnp.bfloat16),
            pltpu.VMEM((batch_count, rows, QT), jnp.bfloat16),
            pltpu.VMEM((batch_count * rows, chunk), jnp.bfloat16),
            pltpu.VMEM((batch_count * rows, chunk), jnp.bfloat16),
        ],
        compiler_params=params(32 if tokens <= 256 else 48),
        cost_estimate=pl.CostEstimate(flops=10**9, bytes_accessed=1, transcendentals=0),
    )(rot, *lefts, *halves, eigenvalues)


def score_kernel(batch_count, ranks, count, *refs):
    grad_refs, ids_refs = refs[:count], refs[count:2 * count]
    basis_ref, image_ref, out_ref, token_ref = refs[2 * count:]
    step = pl.program_id(0)
    rows = grad_refs[0].shape[0] // 4

    def tokens_of(pieces):
        return jnp.concatenate(
            [pieces[r // 4][r % 4 * rows:(r % 4 + 1) * rows, :] for r in ranks], axis=0
        )

    @pl.when(step == 0)
    def _():
        token_ref[...] = jnp.zeros_like(token_ref)

    turned = jnp.dot(tokens_of(grad_refs), basis_ref[...], preferred_element_type=jnp.float32)
    turned = turned.astype(jnp.bfloat16).T.astype(jnp.float32)
    for b in range(batch_count):
        token_ref[b:b + 1, :] += jnp.sum(image_ref[b] * turned, axis=0, keepdims=True)

    @pl.when(step == pl.num_programs(0) - 1)
    def _():
        ids = tokens_of(ids_refs).astype(jnp.float32)
        seqs = lax.broadcasted_iota(jnp.int32, ids.shape, 1).astype(jnp.float32)
        member = jnp.where(ids == seqs, 1.0, 0.0).T
        own = lax.rem(lax.axis_index("groups"), batch_count)
        for b in range(batch_count):
            sums = jnp.sum(member * token_ref[b:b + 1, :], axis=1, keepdims=True)
            out_ref[lax.rem(own + b, batch_count)] = sums[:out_ref.shape[1], :] * SCORE_SCALE


def score_parts(grad_pieces, ranks, grad_basis, image, seq_count):
    batch_count, hidden, tokens = image.shape
    count = len(grad_pieces)
    rows = grad_pieces[0].shape[0]
    inner = min(grad_basis.shape[0], hidden)
    return pl.pallas_call(
        functools.partial(score_kernel, batch_count, ranks, count),
        grid=(hidden // inner,),
        in_specs=[pl.BlockSpec((rows, inner), lambda i: (0, i))] * count
        + [pl.BlockSpec((rows, LANES), lambda i: (0, hidden // LANES))] * count
        + [
            pl.BlockSpec((grad_basis.shape[0], inner), lambda i: (0, i)),
            pl.BlockSpec((batch_count, inner, tokens), lambda i: (0, i, 0)),
        ],
        out_specs=pl.BlockSpec((batch_count, seq_count, 1), lambda i: (0, 0, 0)),
        out_shape=jax.ShapeDtypeStruct((batch_count, seq_count, 1), jnp.float32),
        scratch_shapes=[pltpu.VMEM((8, tokens), jnp.float32)],
        compiler_params=params(32 if tokens <= 256 else 48),
        cost_estimate=pl.CostEstimate(
            flops=2 * tokens * hidden * grad_basis.shape[0],
            bytes_accessed=4 * image.size,
            transcendentals=0,
        ),
    )(*grad_pieces, *grad_pieces, grad_basis, image)


def per_device(
    train_act, train_grad, seq_ids, act_basis, grad_basis, eigenvalues, query_factors, owners
):
    wide_count = lax.axis_size("wide")
    along_z = range(wide_count // 4)
    tok_local = train_act.shape[0]
    seq_count = tok_local * wide_count // SEQ_MEAN
    cols = grad_basis.shape[1]
    hidden = train_grad.shape[1]
    batch_count = owners.shape[0]

    half = (query_factors.shape[2] - hidden) // 2
    order = [4 * k + r for r in (0, 2, 1, 3) for k in along_z]
    keep, give = cut_factors(query_factors, order, hidden, batch_count)
    flags = owner_flags(owners, keep)
    grads_sent = grads_core(seq_ids, train_grad, keep)
    keep, give = pick(flags, keep, swap(give, "wide", 1), 0, cols, half, [grads_sent])
    grads_got = swap(grads_sent, "wide", 1)
    grads_over = grads_y(train_grad, grads_sent, grads_got, give)
    parts = pick(flags, keep, swap(give, "wide", 2), 1, cols, half, [grads_over])
    grads_over = swap(grads_over, "wide", 2)
    sent = grads_z(train_grad, grads_sent, grads_got, grads_over, wide_count)
    acts = join([train_act] + [swap(train_act, "wide", 4 * k) for k in along_z if k], parts[0])
    ranks = [4 * k for k in along_z]
    over = swap(acts, "wide", 2)
    first = rotate([acts], act_basis, parts[0])
    parts = [swap(parts[k], "wide", 4 * k) if k else parts[0] for k in along_z]
    held = pick_one(flags, parts, [over, first, sent[0]])

    over = gate(over, [held])
    rot = rotate([over, swap(gate(acts, [held]), "wide", 1), swap(over, "wide", 1)], act_basis, None, first)
    ranks = [r + more for more in (0, 2, 1, 3) for r in ranks]
    lefts = [held, gate(swap(held, "groups", 1), [rot])]
    halves = []
    for x in lefts:
        halves += [x, swap(x, "wide", 1)]
    grads = [swap(sent[k], "wide", 4 * k) if k else sent[0] for k in along_z]

    image = images(rot, lefts, halves, eigenvalues)
    parts = score_parts(grads, ranks, grad_basis, image, seq_count)
    for step, count in ((1, 4), (4, wide_count // 4)):
        parts = parts + sum(swap(parts, "wide", step * n) for n in range(count - 1, 0, -1))
    return parts[:, :, 0].T


def solution(mesh):
    return jax.shard_map(
        per_device,
        mesh=mesh,
        in_specs=(
            P(("groups", "wide"), None),
            P(("groups", "wide"), None),
            P(("groups", "wide")),
            P(),
            P(None, "wide"),
            P("wide", None),
            P("wide", None, None),
            P(),
        ),
        out_specs=P("groups", None),
        check_vma=False,
    )
```

```python
import functools
import math

import jax
import jax.numpy as jnp
from jax import lax
from jax.experimental import pallas as pl
from jax.experimental.pallas import tpu as pltpu
from jax.sharding import PartitionSpec as P

D = 4096
FF = 32768
SEQ_MEAN = 32
QT = 16
LANES = 128
SCORE_SCALE = 1.0 / math.sqrt(FF * D * QT * SEQ_MEAN)


damping = 0.1


def params(mib):
    return pltpu.CompilerParams(vmem_limit_bytes=mib * 1024 * 1024)


def whole_block(shape):
    return pl.BlockSpec(shape, lambda *_: (0,) * len(shape), pipeline_mode=pl.Buffered(1))


def swap(x, axis, bit):
    count = lax.axis_size(axis)
    return lax.ppermute(x, axis, [(i, i ^ bit) for i in range(count)])


def in_smem(n):
    return [pl.BlockSpec(memory_space=pltpu.SMEM)] * n


def in_vmem(n):
    return [pl.BlockSpec(memory_space=pltpu.VMEM)] * n


def in_place(n):
    return [pl.BlockSpec(memory_space=pl.ANY)] * n


def cut_factors_kernel(order, hidden, batch_count, fac_ref, keep_ref, give_ref):
    cols = hidden // len(order)
    half = (fac_ref.shape[2] - hidden) // 2
    me, batch = lax.axis_index("wide"), lax.rem(lax.axis_index("groups"), batch_count)
    for part, out_ref in enumerate((keep_ref, give_ref)):
        picked = order[part * len(order) // 2:(part + 1) * len(order) // 2]
        for at, r in enumerate(picked):
            src = pl.multiple_of((me ^ r) * cols, cols)
            out_ref[:, at * cols:(at + 1) * cols] = fac_ref[batch, :, pl.ds(src, cols)]
        src = pl.multiple_of(hidden + ((me & 1) ^ part) * half, LANES)
        out_ref[:, len(picked) * cols:] = fac_ref[batch, :, pl.ds(src, half)]


def cut_factors(factors, order, hidden, batch_count):
    rows, width = factors.shape[1:]
    half = jax.ShapeDtypeStruct((rows, width // 2), factors.dtype)
    return pl.pallas_call(
        functools.partial(cut_factors_kernel, order, hidden, batch_count),
        in_specs=in_vmem(1),
        out_specs=in_vmem(2),
        out_shape=[half] * 2,
        compiler_params=params(16),
        cost_estimate=pl.CostEstimate(flops=0, bytes_accessed=1, transcendentals=0),
    )(factors)


def flags_kernel(batch_count, owners_ref, _, flag_ref):
    me, batch = lax.axis_index("wide"), lax.rem(lax.axis_index("groups"), batch_count)
    apart = owners_ref[batch] ^ me
    lane = lax.broadcasted_iota(jnp.int32, flag_ref.shape, 1)
    flags = jnp.where(lane - 2 == apart // 4, 1.0, 0.0)
    for step in range(2):
        same = jnp.where((apart & (1 << step)) == 0, 1.0, 0.0)
        flags = jnp.where(lane == step, same, flags)
    flag_ref[...] = flags.astype(flag_ref.dtype)


def owner_flags(owners, after):
    return pl.pallas_call(
        functools.partial(flags_kernel, owners.shape[0]),
        in_specs=in_smem(1) + in_place(1),
        out_specs=in_vmem(1)[0],
        out_shape=jax.ShapeDtypeStruct((after.shape[0], LANES), after.dtype),
        compiler_params=params(16),
        cost_estimate=pl.CostEstimate(flops=0, bytes_accessed=1, transcendentals=0),
    )(owners, after)


def pick_kernel(step, cols, half, flag_ref, keep_ref, got_ref, *refs):
    out_refs = refs[-2:] if step == 0 else refs[-((keep_ref.shape[1] - half) // cols):]
    same = flag_ref[:, step:step + 1]
    differs = 1 - same

    def chosen(at, size):
        place = slice(at, at + size)
        return keep_ref[:, place] * same + got_ref[:, place] * differs

    size = out_refs[0].shape[1] - half
    shared = chosen(len(out_refs) * size, half)
    for n, out_ref in enumerate(out_refs):
        out_ref[:, :size] = chosen(n * size, size)
        out_ref[:, size:] = shared


def pick(flags, keep, got, step, cols, half, after):
    rows, width = keep.shape
    parts = 2 if step == 0 else (width - half) // cols
    size = (width - half) // parts + half
    return pl.pallas_call(
        functools.partial(pick_kernel, step, cols, half),
        in_specs=in_vmem(3) + in_place(len(after)),
        out_specs=in_vmem(parts),
        out_shape=[jax.ShapeDtypeStruct((rows, size), keep.dtype)] * parts,
        compiler_params=params(16),
        cost_estimate=pl.CostEstimate(flops=0, bytes_accessed=1, transcendentals=0),
    )(flags, keep, got, *after)


def pick_one_kernel(count, flag_ref, *refs):
    refs[-1][...] = sum(refs[k][...] * flag_ref[:, 2 + k:3 + k] for k in range(count))


def pick_one(flags, pieces, after):
    return pl.pallas_call(
        functools.partial(pick_one_kernel, len(pieces)),
        in_specs=in_vmem(1 + len(pieces)) + in_place(len(after)),
        out_specs=in_vmem(1)[0],
        out_shape=jax.ShapeDtypeStruct(pieces[0].shape, pieces[0].dtype),
        compiler_params=params(16),
        cost_estimate=pl.CostEstimate(flops=0, bytes_accessed=1, transcendentals=0),
    )(flags, *pieces, *after)


def join_kernel(*refs):
    out_ref = refs[-1]
    rows = refs[0].shape[0]
    for n, ref in enumerate(refs[:-2]):
        out_ref[n * rows:(n + 1) * rows, :] = ref[...]


def join(pieces, after):
    rows, width = pieces[0].shape
    return pl.pallas_call(
        join_kernel,
        in_specs=in_vmem(len(pieces)) + in_place(1),
        out_specs=in_vmem(1)[0],
        out_shape=jax.ShapeDtypeStruct((len(pieces) * rows, width), pieces[0].dtype),
        compiler_params=params(16),
        cost_estimate=pl.CostEstimate(flops=0, bytes_accessed=1, transcendentals=0),
    )(*pieces, after)


def gate_kernel(*_):
    pass


def gate(array, after):
    return pl.pallas_call(
        gate_kernel,
        in_specs=in_place(1 + len(after)),
        out_specs=in_place(1)[0],
        out_shape=jax.ShapeDtypeStruct(array.shape, array.dtype),
        input_output_aliases={0: 0},
        compiler_params=params(1),
        cost_estimate=pl.CostEstimate(flops=0, bytes_accessed=1, transcendentals=0),
    )(array, *after)


def grads_core_kernel(ids_ref, grad_ref, _, out_ref):
    rows, hidden = grad_ref.shape
    wide = lax.axis_size("wide")
    cols = hidden // wide
    me = lax.axis_index("wide")
    row = lax.broadcasted_iota(jnp.int32, (rows, LANES), 0)
    ids = jnp.zeros((rows, LANES), jnp.int32)
    for t in range(rows):
        ids = jnp.where(row == t, ids_ref[t], ids)
    out_ref[:, wide // 2 * cols:] = ids.astype(jnp.float32).astype(out_ref.dtype)
    for q in range(wide // 2):
        src = pl.multiple_of((me ^ (2 * q + 1)) * cols, cols)
        out_ref[:, q * cols:(q + 1) * cols] = grad_ref[:, pl.ds(src, cols)]


def grads_core(ids, grads, after):
    rows, hidden = grads.shape
    return pl.pallas_call(
        grads_core_kernel,
        in_specs=in_smem(1) + in_vmem(1) + in_place(1),
        out_specs=in_vmem(1)[0],
        out_shape=jax.ShapeDtypeStruct((rows, hidden // 2 + LANES), grads.dtype),
        compiler_params=params(16),
        cost_estimate=pl.CostEstimate(flops=0, bytes_accessed=1, transcendentals=0),
    )(ids, grads, after)


def grads_y_kernel(grad_ref, sent_ref, got_ref, _, out_ref):
    rows, hidden = grad_ref.shape
    wide = lax.axis_size("wide")
    cols = hidden // wide
    me = lax.axis_index("wide")
    for k in range(wide // 4):
        src = pl.multiple_of((me ^ (4 * k + 2)) * cols, cols)
        place = slice(k * cols, (k + 1) * cols)
        out_ref[:rows, place] = grad_ref[:, pl.ds(src, cols)]
        out_ref[rows:, place] = got_ref[:, (2 * k + 1) * cols:(2 * k + 2) * cols]
    ids = slice(wide // 4 * cols, wide // 4 * cols + LANES)
    out_ref[:rows, ids] = sent_ref[:, wide // 2 * cols:]
    out_ref[rows:, ids] = got_ref[:, wide // 2 * cols:]


def grads_y(grads, sent, got, after):
    rows, hidden = grads.shape
    return pl.pallas_call(
        grads_y_kernel,
        in_specs=in_vmem(3) + in_place(1),
        out_specs=in_vmem(1)[0],
        out_shape=jax.ShapeDtypeStruct((2 * rows, hidden // 4 + LANES), grads.dtype),
        compiler_params=params(16),
        cost_estimate=pl.CostEstimate(flops=0, bytes_accessed=1, transcendentals=0),
    )(grads, sent, got, after)


def grads_z_kernel(grad_ref, sent_ref, got_ref, over_ref, *out_refs):
    rows = grad_ref.shape[0]
    cols = out_refs[0].shape[1] - LANES
    me = lax.axis_index("wide")
    for k, out_ref in enumerate(out_refs):
        src = pl.multiple_of((me ^ (4 * k)) * cols, cols)
        out_ref[:rows, :cols] = grad_ref[:, pl.ds(src, cols)]
        out_ref[rows:2 * rows, :cols] = got_ref[:, 2 * k * cols:(2 * k + 1) * cols]
        out_ref[2 * rows:, :cols] = over_ref[:, k * cols:(k + 1) * cols]
        out_ref[:rows, cols:] = sent_ref[:, 2 * len(out_refs) * cols:]
        out_ref[rows:2 * rows, cols:] = got_ref[:, 2 * len(out_refs) * cols:]
        out_ref[2 * rows:, cols:] = over_ref[:, len(out_refs) * cols:]


def grads_z(grads, sent, got, over, wide_count):
    rows, hidden = grads.shape
    count = wide_count // 4
    piece = jax.ShapeDtypeStruct((4 * rows, hidden // wide_count + LANES), grads.dtype)
    return pl.pallas_call(
        grads_z_kernel,
        in_specs=in_vmem(4),
        out_specs=in_vmem(count),
        out_shape=[piece] * count,
        compiler_params=params(16),
        cost_estimate=pl.CostEstimate(flops=0, bytes_accessed=1, transcendentals=0),
    )(grads, sent, got, over)


def rotate_kernel(act_count, done, *refs):
    act_refs, basis_ref, out_ref = refs[:act_count], refs[act_count], refs[-1]
    depth, width = basis_ref.shape
    if done:
        out_ref[:, :done] = refs[act_count + 1][...]
    for k in range(width // depth):
        cols = slice(k * depth, (k + 1) * depth)
        act = jnp.concatenate([ref[:, cols] for ref in act_refs], axis=0)
        turned = jnp.dot(act, basis_ref[:, cols], preferred_element_type=jnp.float32)
        out_ref[cols, done:] = turned.astype(jnp.bfloat16).T


def rotate(act_pieces, basis, after, first=None):
    width = basis.shape[1]
    done = 0 if first is None else first.shape[1]
    tokens = done + sum(x.shape[0] for x in act_pieces)
    more = [after] if first is None else [first]
    return pl.pallas_call(
        functools.partial(rotate_kernel, len(act_pieces), done),
        in_specs=in_vmem(len(act_pieces) + 1) + (in_place(1) if first is None else in_vmem(1)),
        out_specs=in_vmem(1)[0],
        out_shape=jax.ShapeDtypeStruct((width, tokens), jnp.bfloat16),
        compiler_params=params(16 if tokens <= 256 else 32),
        cost_estimate=pl.CostEstimate(flops=0, bytes_accessed=1, transcendentals=0),
    )(*act_pieces, basis, *more)


def image_kernel(batch_count, total, per, rot_ref, *refs):
    left_refs, half_refs = refs[:batch_count], refs[batch_count:3 * batch_count]
    eig_ref, out_ref, right_ref, turn_ref, pre_a, pre_b = refs[3 * batch_count:]
    rows, chunk = eig_ref.shape
    tile = min(256, chunk)
    s = pl.program_id(0)

    @pl.when(s == 0)
    def _():
        side = right_ref.shape[2] // 2
        for b in range(batch_count):
            for other in range(2):
                at = pl.multiple_of(((lax.axis_index("wide") & 1) ^ other) * side, side)
                ref = half_refs[2 * b + other]
                right_ref[b, :, pl.ds(at, side)] = ref[:, ref.shape[1] - side:]

    @pl.when(jnp.logical_and(lax.rem(s, per) == 0, s < total))
    def _():
        for b in range(batch_count):
            turn_ref[b] = left_refs[b][...].T

    @pl.when(lax.rem(s, per) == 1)
    def _():
        out_ref[...] = jnp.zeros_like(out_ref)

    def produce(pre):
        start = lax.rem(s, per) * chunk
        for at in range(0, chunk, tile):
            cols = pl.ds(pl.multiple_of(start + at, tile), tile)
            damped = eig_ref[:, at:at + tile].astype(jnp.float32) + damping
            inverse = pl.reciprocal(damped, approx=True)
            for b in range(batch_count):
                outer_sum = jnp.dot(
                    turn_ref[b], right_ref[b, :, cols], preferred_element_type=jnp.float32
                )
                pre[b * rows:(b + 1) * rows, at:at + tile] = (
                    outer_sum * inverse
                ).astype(jnp.bfloat16)

    def absorb(pre):
        rot = rot_ref[pl.ds(pl.multiple_of(lax.rem(s - 1, per) * chunk, chunk), chunk), :]
        for b in range(batch_count):
            out_ref[b] += jnp.dot(
                pre[b * rows:(b + 1) * rows, :], rot, preferred_element_type=jnp.float32
            )

    between = jnp.logical_and(s > 0, s < total)
    odd = lax.rem(s, 2) == 1

    @pl.when(s == 0)
    def _():
        produce(pre_a)

    @pl.when(jnp.logical_and(between, odd))
    def _():
        produce(pre_b)
        absorb(pre_a)

    @pl.when(jnp.logical_and(between, jnp.logical_not(odd)))
    def _():
        produce(pre_a)
        absorb(pre_b)

    @pl.when(s == total)
    def _():
        absorb(pre_a if total % 2 else pre_b)


def images(rot, lefts, halves, eigenvalues):
    batch_count, tokens = len(lefts), rot.shape[1]
    hidden, width = eigenvalues.shape
    rows = min(1024, hidden)
    chunk = min(1024, width // 2)
    per = width // chunk
    total = hidden // rows * per
    now = lambda s: jnp.minimum(s, total - 1)
    before = lambda s: jnp.maximum(s - 1, 0)
    return pl.pallas_call(
        functools.partial(image_kernel, batch_count, total, per),
        grid=(total + 1,),
        in_specs=[whole_block(rot.shape)]
        + [pl.BlockSpec((QT, rows), lambda s: (0, now(s) // per)) for _ in lefts]
        + [whole_block(x.shape) for x in halves]
        + [pl.BlockSpec((rows, chunk), lambda s: (now(s) // per, now(s) % per))],
        out_specs=pl.BlockSpec((batch_count, rows, tokens), lambda s: (0, before(s) // per, 0)),
        out_shape=jax.ShapeDtypeStruct((batch_count, hidden, tokens), jnp.float32),
        scratch_shapes=[
            pltpu.VMEM((batch_count, QT, width), jnp.bfloat16),
            pltpu.VMEM((batch_count, rows, QT), jnp.bfloat16),
            pltpu.VMEM((batch_count * rows, chunk), jnp.bfloat16),
            pltpu.VMEM((batch_count * rows, chunk), jnp.bfloat16),
        ],
        compiler_params=params(32 if tokens <= 256 else 48),
        cost_estimate=pl.CostEstimate(flops=10**9, bytes_accessed=1, transcendentals=0),
    )(rot, *lefts, *halves, eigenvalues)


def score_kernel(batch_count, ranks, count, *refs):
    grad_refs, ids_refs = refs[:count], refs[count:2 * count]
    basis_ref, image_ref, out_ref, token_ref = refs[2 * count:]
    step = pl.program_id(0)
    rows = grad_refs[0].shape[0] // 4

    def tokens_of(pieces):
        return jnp.concatenate(
            [pieces[r // 4][r % 4 * rows:(r % 4 + 1) * rows, :] for r in ranks], axis=0
        )

    @pl.when(step == 0)
    def _():
        token_ref[...] = jnp.zeros_like(token_ref)

    turned = jnp.dot(tokens_of(grad_refs), basis_ref[...], preferred_element_type=jnp.float32)
    turned = turned.astype(jnp.bfloat16).T.astype(jnp.float32)
    for b in range(batch_count):
        token_ref[b:b + 1, :] += jnp.sum(image_ref[b] * turned, axis=0, keepdims=True)

    @pl.when(step == pl.num_programs(0) - 1)
    def _():
        ids = tokens_of(ids_refs).astype(jnp.float32)
        seqs = lax.broadcasted_iota(jnp.int32, ids.shape, 1).astype(jnp.float32)
        member = jnp.where(ids == seqs, 1.0, 0.0).T
        own = lax.rem(lax.axis_index("groups"), batch_count)
        for b in range(batch_count):
            sums = jnp.sum(member * token_ref[b:b + 1, :], axis=1, keepdims=True)
            out_ref[lax.rem(own + b, batch_count)] = sums[:out_ref.shape[1], :] * SCORE_SCALE


def score_parts(grad_pieces, ranks, grad_basis, image, seq_count):
    batch_count, hidden, tokens = image.shape
    count = len(grad_pieces)
    rows = grad_pieces[0].shape[0]
    inner = min(grad_basis.shape[0], hidden)
    return pl.pallas_call(
        functools.partial(score_kernel, batch_count, ranks, count),
        grid=(hidden // inner,),
        in_specs=[pl.BlockSpec((rows, inner), lambda i: (0, i))] * count
        + [pl.BlockSpec((rows, LANES), lambda i: (0, hidden // LANES))] * count
        + [
            pl.BlockSpec((grad_basis.shape[0], inner), lambda i: (0, i)),
            pl.BlockSpec((batch_count, inner, tokens), lambda i: (0, i, 0)),
        ],
        out_specs=pl.BlockSpec((batch_count, seq_count, 1), lambda i: (0, 0, 0)),
        out_shape=jax.ShapeDtypeStruct((batch_count, seq_count, 1), jnp.float32),
        scratch_shapes=[pltpu.VMEM((8, tokens), jnp.float32)],
        compiler_params=params(32 if tokens <= 256 else 48),
        cost_estimate=pl.CostEstimate(
            flops=2 * tokens * hidden * grad_basis.shape[0],
            bytes_accessed=4 * image.size,
            transcendentals=0,
        ),
    )(*grad_pieces, *grad_pieces, grad_basis, image)


def per_device(
    train_act, train_grad, seq_ids, act_basis, grad_basis, eigenvalues, query_factors, owners
):
    wide_count = lax.axis_size("wide")
    along_z = range(wide_count // 4)
    tok_local = train_act.shape[0]
    seq_count = tok_local * wide_count // SEQ_MEAN
    cols = grad_basis.shape[1]
    hidden = train_grad.shape[1]
    batch_count = owners.shape[0]

    half = (query_factors.shape[2] - hidden) // 2
    order = [4 * k + r for r in (0, 2, 1, 3) for k in along_z]
    keep, give = cut_factors(query_factors, order, hidden, batch_count)
    flags = owner_flags(owners, keep)
    grads_sent = grads_core(seq_ids, train_grad, keep)
    keep, give = pick(flags, keep, swap(give, "wide", 1), 0, cols, half, [grads_sent])
    grads_got = swap(grads_sent, "wide", 1)
    grads_over = grads_y(train_grad, grads_sent, grads_got, give)
    parts = pick(flags, keep, swap(give, "wide", 2), 1, cols, half, [grads_over])
    grads_over = swap(grads_over, "wide", 2)
    sent = grads_z(train_grad, grads_sent, grads_got, grads_over, wide_count)
    acts = join([train_act] + [swap(train_act, "wide", 4 * k) for k in along_z if k], parts[0])
    ranks = [4 * k for k in along_z]
    over = swap(acts, "wide", 2)
    first = rotate([acts], act_basis, parts[0])
    parts = [swap(parts[k], "wide", 4 * k) if k else parts[0] for k in along_z]
    held = pick_one(flags, parts, [over, first, sent[0]])

    over = gate(over, [held])
    rot = rotate([over, swap(gate(acts, [held]), "wide", 1), swap(over, "wide", 1)], act_basis, None, first)
    ranks = [r + more for more in (0, 2, 1, 3) for r in ranks]
    lefts = [held, gate(swap(held, "groups", 1), [rot])]
    halves = []
    for x in lefts:
        halves += [x, swap(x, "wide", 1)]
    grads = [swap(sent[k], "wide", 4 * k) if k else sent[0] for k in along_z]

    image = images(rot, lefts, halves, eigenvalues)
    parts = score_parts(grads, ranks, grad_basis, image, seq_count)
    parts = parts + sum(swap(parts, "wide", r) for r in (3, 2, 1))
    bit = 4
    while bit < wide_count:
        parts = parts + swap(parts, "wide", bit)
        bit *= 2
    return parts[:, :, 0].T


def solution(mesh):
    return jax.shard_map(
        per_device,
        mesh=mesh,
        in_specs=(
            P(("groups", "wide"), None),
            P(("groups", "wide"), None),
            P(("groups", "wide")),
            P(),
            P(None, "wide"),
            P("wide", None),
            P("wide", None, None),
            P(),
        ),
        out_specs=P("groups", None),
        check_vma=False,
    )
```

```python
import functools
import math

import jax
import jax.numpy as jnp
from jax import lax
from jax.experimental import pallas as pl
from jax.experimental.pallas import tpu as pltpu
from jax.sharding import PartitionSpec as P

D = 4096
FF = 32768
SEQ_MEAN = 32
QT = 16
LANES = 128
SCORE_SCALE = 1.0 / math.sqrt(FF * D * QT * SEQ_MEAN)


damping = 0.1


def params(mib):
    return pltpu.CompilerParams(vmem_limit_bytes=mib * 1024 * 1024)


def whole_block(shape):
    return pl.BlockSpec(shape, lambda *_: (0,) * len(shape), pipeline_mode=pl.Buffered(1))


def swap(x, axis, bit):
    count = lax.axis_size(axis)
    return lax.ppermute(x, axis, [(i, i ^ bit) for i in range(count)])


def in_smem(n):
    return [pl.BlockSpec(memory_space=pltpu.SMEM)] * n


def in_vmem(n):
    return [pl.BlockSpec(memory_space=pltpu.VMEM)] * n


def in_place(n):
    return [pl.BlockSpec(memory_space=pl.ANY)] * n


def cut_factors_kernel(order, hidden, batch_count, fac_ref, keep_ref, give_ref):
    cols = hidden // len(order)
    half = (fac_ref.shape[2] - hidden) // 2
    me, batch = lax.axis_index("wide"), lax.rem(lax.axis_index("groups"), batch_count)
    for part, out_ref in enumerate((keep_ref, give_ref)):
        picked = order[part * len(order) // 2:(part + 1) * len(order) // 2]
        for at, r in enumerate(picked):
            src = pl.multiple_of((me ^ r) * cols, cols)
            out_ref[:, at * cols:(at + 1) * cols] = fac_ref[batch, :, pl.ds(src, cols)]
        src = pl.multiple_of(hidden + ((me & 1) ^ part) * half, LANES)
        out_ref[:, len(picked) * cols:] = fac_ref[batch, :, pl.ds(src, half)]


def cut_factors(factors, order, hidden, batch_count):
    rows, width = factors.shape[1:]
    half = jax.ShapeDtypeStruct((rows, width // 2), factors.dtype)
    return pl.pallas_call(
        functools.partial(cut_factors_kernel, order, hidden, batch_count),
        in_specs=in_vmem(1),
        out_specs=in_vmem(2),
        out_shape=[half] * 2,
        compiler_params=params(16),
        cost_estimate=pl.CostEstimate(flops=0, bytes_accessed=1, transcendentals=0),
    )(factors)


def flags_kernel(batch_count, owners_ref, _, flag_ref):
    me, batch = lax.axis_index("wide"), lax.rem(lax.axis_index("groups"), batch_count)
    apart = owners_ref[batch] ^ me
    lane = lax.broadcasted_iota(jnp.int32, flag_ref.shape, 1)
    flags = jnp.where(lane - 2 == apart // 4, 1.0, 0.0)
    for step in range(2):
        same = jnp.where((apart & (1 << step)) == 0, 1.0, 0.0)
        flags = jnp.where(lane == step, same, flags)
    flag_ref[...] = flags.astype(flag_ref.dtype)


def owner_flags(owners, after):
    return pl.pallas_call(
        functools.partial(flags_kernel, owners.shape[0]),
        in_specs=in_smem(1) + in_place(1),
        out_specs=in_vmem(1)[0],
        out_shape=jax.ShapeDtypeStruct((after.shape[0], LANES), after.dtype),
        compiler_params=params(16),
        cost_estimate=pl.CostEstimate(flops=0, bytes_accessed=1, transcendentals=0),
    )(owners, after)


def pick_kernel(step, cols, half, flag_ref, keep_ref, got_ref, *refs):
    out_refs = refs[-2:] if step == 0 else refs[-((keep_ref.shape[1] - half) // cols):]
    same = flag_ref[:, step:step + 1]
    differs = 1 - same

    def chosen(at, size):
        place = slice(at, at + size)
        return keep_ref[:, place] * same + got_ref[:, place] * differs

    size = out_refs[0].shape[1] - half
    shared = chosen(len(out_refs) * size, half)
    for n, out_ref in enumerate(out_refs):
        out_ref[:, :size] = chosen(n * size, size)
        out_ref[:, size:] = shared


def pick(flags, keep, got, step, cols, half, after):
    rows, width = keep.shape
    parts = 2 if step == 0 else (width - half) // cols
    size = (width - half) // parts + half
    return pl.pallas_call(
        functools.partial(pick_kernel, step, cols, half),
        in_specs=in_vmem(3) + in_place(len(after)),
        out_specs=in_vmem(parts),
        out_shape=[jax.ShapeDtypeStruct((rows, size), keep.dtype)] * parts,
        compiler_params=params(16),
        cost_estimate=pl.CostEstimate(flops=0, bytes_accessed=1, transcendentals=0),
    )(flags, keep, got, *after)


def pick_one_kernel(count, flag_ref, *refs):
    refs[-1][...] = sum(refs[k][...] * flag_ref[:, 2 + k:3 + k] for k in range(count))


def pick_one(flags, pieces, after):
    return pl.pallas_call(
        functools.partial(pick_one_kernel, len(pieces)),
        in_specs=in_vmem(1 + len(pieces)) + in_place(len(after)),
        out_specs=in_vmem(1)[0],
        out_shape=jax.ShapeDtypeStruct(pieces[0].shape, pieces[0].dtype),
        compiler_params=params(16),
        cost_estimate=pl.CostEstimate(flops=0, bytes_accessed=1, transcendentals=0),
    )(flags, *pieces, *after)


def join_kernel(*refs):
    out_ref = refs[-1]
    rows = refs[0].shape[0]
    for n, ref in enumerate(refs[:-2]):
        out_ref[n * rows:(n + 1) * rows, :] = ref[...]


def join(pieces, after):
    rows, width = pieces[0].shape
    return pl.pallas_call(
        join_kernel,
        in_specs=in_vmem(len(pieces)) + in_place(1),
        out_specs=in_vmem(1)[0],
        out_shape=jax.ShapeDtypeStruct((len(pieces) * rows, width), pieces[0].dtype),
        compiler_params=params(16),
        cost_estimate=pl.CostEstimate(flops=0, bytes_accessed=1, transcendentals=0),
    )(*pieces, after)


def gate_kernel(*_):
    pass


def gate(array, after):
    return pl.pallas_call(
        gate_kernel,
        in_specs=in_place(1 + len(after)),
        out_specs=in_place(1)[0],
        out_shape=jax.ShapeDtypeStruct(array.shape, array.dtype),
        input_output_aliases={0: 0},
        compiler_params=params(1),
        cost_estimate=pl.CostEstimate(flops=0, bytes_accessed=1, transcendentals=0),
    )(array, *after)


def grads_core_kernel(ids_ref, grad_ref, _, out_ref):
    rows, hidden = grad_ref.shape
    wide = lax.axis_size("wide")
    cols = hidden // wide
    me = lax.axis_index("wide")
    row = lax.broadcasted_iota(jnp.int32, (rows, LANES), 0)
    ids = jnp.zeros((rows, LANES), jnp.int32)
    for t in range(rows):
        ids = jnp.where(row == t, ids_ref[t], ids)
    out_ref[:, wide // 2 * cols:] = ids.astype(jnp.float32).astype(out_ref.dtype)
    for q in range(wide // 2):
        src = pl.multiple_of((me ^ (2 * q + 1)) * cols, cols)
        out_ref[:, q * cols:(q + 1) * cols] = grad_ref[:, pl.ds(src, cols)]


def grads_core(ids, grads, after):
    rows, hidden = grads.shape
    return pl.pallas_call(
        grads_core_kernel,
        in_specs=in_smem(1) + in_vmem(1) + in_place(1),
        out_specs=in_vmem(1)[0],
        out_shape=jax.ShapeDtypeStruct((rows, hidden // 2 + LANES), grads.dtype),
        compiler_params=params(16),
        cost_estimate=pl.CostEstimate(flops=0, bytes_accessed=1, transcendentals=0),
    )(ids, grads, after)


def grads_y_kernel(grad_ref, sent_ref, got_ref, _, out_ref):
    rows, hidden = grad_ref.shape
    wide = lax.axis_size("wide")
    cols = hidden // wide
    me = lax.axis_index("wide")
    for k in range(wide // 4):
        src = pl.multiple_of((me ^ (4 * k + 2)) * cols, cols)
        place = slice(k * cols, (k + 1) * cols)
        out_ref[:rows, place] = grad_ref[:, pl.ds(src, cols)]
        out_ref[rows:, place] = got_ref[:, (2 * k + 1) * cols:(2 * k + 2) * cols]
    ids = slice(wide // 4 * cols, wide // 4 * cols + LANES)
    out_ref[:rows, ids] = sent_ref[:, wide // 2 * cols:]
    out_ref[rows:, ids] = got_ref[:, wide // 2 * cols:]


def grads_y(grads, sent, got, after):
    rows, hidden = grads.shape
    return pl.pallas_call(
        grads_y_kernel,
        in_specs=in_vmem(3) + in_place(1),
        out_specs=in_vmem(1)[0],
        out_shape=jax.ShapeDtypeStruct((2 * rows, hidden // 4 + LANES), grads.dtype),
        compiler_params=params(16),
        cost_estimate=pl.CostEstimate(flops=0, bytes_accessed=1, transcendentals=0),
    )(grads, sent, got, after)


def grads_z_kernel(grad_ref, sent_ref, got_ref, over_ref, *out_refs):
    rows = grad_ref.shape[0]
    cols = out_refs[0].shape[1] - LANES
    me = lax.axis_index("wide")
    for k, out_ref in enumerate(out_refs):
        src = pl.multiple_of((me ^ (4 * k)) * cols, cols)
        out_ref[:rows, :cols] = grad_ref[:, pl.ds(src, cols)]
        out_ref[rows:2 * rows, :cols] = got_ref[:, 2 * k * cols:(2 * k + 1) * cols]
        out_ref[2 * rows:, :cols] = over_ref[:, k * cols:(k + 1) * cols]
        out_ref[:rows, cols:] = sent_ref[:, 2 * len(out_refs) * cols:]
        out_ref[rows:2 * rows, cols:] = got_ref[:, 2 * len(out_refs) * cols:]
        out_ref[2 * rows:, cols:] = over_ref[:, len(out_refs) * cols:]


def grads_z(grads, sent, got, over, wide_count):
    rows, hidden = grads.shape
    count = wide_count // 4
    piece = jax.ShapeDtypeStruct((4 * rows, hidden // wide_count + LANES), grads.dtype)
    return pl.pallas_call(
        grads_z_kernel,
        in_specs=in_vmem(4),
        out_specs=in_vmem(count),
        out_shape=[piece] * count,
        compiler_params=params(16),
        cost_estimate=pl.CostEstimate(flops=0, bytes_accessed=1, transcendentals=0),
    )(grads, sent, got, over)


def rotate_kernel(act_count, done, *refs):
    act_refs, basis_ref, out_ref = refs[:act_count], refs[act_count], refs[-1]
    depth, width = basis_ref.shape
    if done:
        out_ref[:, :done] = refs[act_count + 1][...]
    for k in range(width // depth):
        cols = slice(k * depth, (k + 1) * depth)
        act = jnp.concatenate([ref[:, cols] for ref in act_refs], axis=0)
        turned = jnp.dot(act, basis_ref[:, cols], preferred_element_type=jnp.float32)
        out_ref[cols, done:] = turned.astype(jnp.bfloat16).T


def rotate(act_pieces, basis, after, first=None):
    width = basis.shape[1]
    done = 0 if first is None else first.shape[1]
    tokens = done + sum(x.shape[0] for x in act_pieces)
    more = [after] if first is None else [first]
    return pl.pallas_call(
        functools.partial(rotate_kernel, len(act_pieces), done),
        in_specs=in_vmem(len(act_pieces) + 1) + (in_place(1) if first is None else in_vmem(1)),
        out_specs=in_vmem(1)[0],
        out_shape=jax.ShapeDtypeStruct((width, tokens), jnp.bfloat16),
        compiler_params=params(16 if tokens <= 256 else 32),
        cost_estimate=pl.CostEstimate(flops=0, bytes_accessed=1, transcendentals=0),
    )(*act_pieces, basis, *more)


def image_kernel(batch_count, total, per, rot_ref, *refs):
    left_refs, half_refs = refs[:batch_count], refs[batch_count:3 * batch_count]
    eig_ref, out_ref, right_ref, turn_ref, pre_a, pre_b = refs[3 * batch_count:]
    rows, chunk = eig_ref.shape
    tile = min(512, chunk)
    s = pl.program_id(0)

    @pl.when(s == 0)
    def _():
        side = right_ref.shape[2] // 2
        for b in range(batch_count):
            for other in range(2):
                at = pl.multiple_of(((lax.axis_index("wide") & 1) ^ other) * side, side)
                ref = half_refs[2 * b + other]
                right_ref[b, :, pl.ds(at, side)] = ref[:, ref.shape[1] - side:]

    @pl.when(jnp.logical_and(lax.rem(s, per) == 0, s < total))
    def _():
        for b in range(batch_count):
            turn_ref[b] = left_refs[b][...].T

    @pl.when(lax.rem(s, per) == 1)
    def _():
        out_ref[...] = jnp.zeros_like(out_ref)

    def produce(pre):
        start = lax.rem(s, per) * chunk
        for at in range(0, chunk, tile):
            cols = pl.ds(pl.multiple_of(start + at, tile), tile)
            damped = eig_ref[:, at:at + tile].astype(jnp.float32) + damping
            inverse = pl.reciprocal(damped, approx=True)
            for b in range(batch_count):
                outer_sum = jnp.dot(
                    turn_ref[b], right_ref[b, :, cols], preferred_element_type=jnp.float32
                )
                pre[b * rows:(b + 1) * rows, at:at + tile] = (
                    outer_sum * inverse
                ).astype(jnp.bfloat16)

    def absorb(pre):
        rot = rot_ref[pl.ds(pl.multiple_of(lax.rem(s - 1, per) * chunk, chunk), chunk), :]
        for b in range(batch_count):
            out_ref[b] += jnp.dot(
                pre[b * rows:(b + 1) * rows, :], rot, preferred_element_type=jnp.float32
            )

    between = jnp.logical_and(s > 0, s < total)
    odd = lax.rem(s, 2) == 1

    @pl.when(s == 0)
    def _():
        produce(pre_a)

    @pl.when(jnp.logical_and(between, odd))
    def _():
        produce(pre_b)
        absorb(pre_a)

    @pl.when(jnp.logical_and(between, jnp.logical_not(odd)))
    def _():
        produce(pre_a)
        absorb(pre_b)

    @pl.when(s == total)
    def _():
        absorb(pre_a if total % 2 else pre_b)


def images(rot, lefts, halves, eigenvalues):
    batch_count, tokens = len(lefts), rot.shape[1]
    hidden, width = eigenvalues.shape
    rows = min(1024, hidden)
    chunk = min(1024, width // 2)
    per = width // chunk
    total = hidden // rows * per
    now = lambda s: jnp.minimum(s, total - 1)
    before = lambda s: jnp.maximum(s - 1, 0)
    return pl.pallas_call(
        functools.partial(image_kernel, batch_count, total, per),
        grid=(total + 1,),
        in_specs=[whole_block(rot.shape)]
        + [pl.BlockSpec((QT, rows), lambda s: (0, now(s) // per)) for _ in lefts]
        + [whole_block(x.shape) for x in halves]
        + [pl.BlockSpec((rows, chunk), lambda s: (now(s) // per, now(s) % per))],
        out_specs=pl.BlockSpec((batch_count, rows, tokens), lambda s: (0, before(s) // per, 0)),
        out_shape=jax.ShapeDtypeStruct((batch_count, hidden, tokens), jnp.float32),
        scratch_shapes=[
            pltpu.VMEM((batch_count, QT, width), jnp.bfloat16),
            pltpu.VMEM((batch_count, rows, QT), jnp.bfloat16),
            pltpu.VMEM((batch_count * rows, chunk), jnp.bfloat16),
            pltpu.VMEM((batch_count * rows, chunk), jnp.bfloat16),
        ],
        compiler_params=params(32 if tokens <= 256 else 48),
        cost_estimate=pl.CostEstimate(flops=10**9, bytes_accessed=1, transcendentals=0),
    )(rot, *lefts, *halves, eigenvalues)


def score_kernel(batch_count, ranks, count, *refs):
    grad_refs, ids_refs = refs[:count], refs[count:2 * count]
    basis_ref, image_ref, out_ref, token_ref = refs[2 * count:]
    step = pl.program_id(0)
    rows = grad_refs[0].shape[0] // 4

    def tokens_of(pieces):
        return jnp.concatenate(
            [pieces[r // 4][r % 4 * rows:(r % 4 + 1) * rows, :] for r in ranks], axis=0
        )

    @pl.when(step == 0)
    def _():
        token_ref[...] = jnp.zeros_like(token_ref)

    turned = jnp.dot(tokens_of(grad_refs), basis_ref[...], preferred_element_type=jnp.float32)
    turned = turned.astype(jnp.bfloat16).T.astype(jnp.float32)
    for b in range(batch_count):
        token_ref[b:b + 1, :] += jnp.sum(image_ref[b] * turned, axis=0, keepdims=True)

    @pl.when(step == pl.num_programs(0) - 1)
    def _():
        ids = tokens_of(ids_refs).astype(jnp.float32)
        seqs = lax.broadcasted_iota(jnp.int32, ids.shape, 1).astype(jnp.float32)
        member = jnp.where(ids == seqs, 1.0, 0.0).T
        own = lax.rem(lax.axis_index("groups"), batch_count)
        for b in range(batch_count):
            sums = jnp.sum(member * token_ref[b:b + 1, :], axis=1, keepdims=True)
            out_ref[lax.rem(own + b, batch_count)] = sums[:out_ref.shape[1], :] * SCORE_SCALE


def score_parts(grad_pieces, ranks, grad_basis, image, seq_count):
    batch_count, hidden, tokens = image.shape
    count = len(grad_pieces)
    rows = grad_pieces[0].shape[0]
    inner = min(grad_basis.shape[0], hidden)
    return pl.pallas_call(
        functools.partial(score_kernel, batch_count, ranks, count),
        grid=(hidden // inner,),
        in_specs=[pl.BlockSpec((rows, inner), lambda i: (0, i))] * count
        + [pl.BlockSpec((rows, LANES), lambda i: (0, hidden // LANES))] * count
        + [
            pl.BlockSpec((grad_basis.shape[0], inner), lambda i: (0, i)),
            pl.BlockSpec((batch_count, inner, tokens), lambda i: (0, i, 0)),
        ],
        out_specs=pl.BlockSpec((batch_count, seq_count, 1), lambda i: (0, 0, 0)),
        out_shape=jax.ShapeDtypeStruct((batch_count, seq_count, 1), jnp.float32),
        scratch_shapes=[pltpu.VMEM((8, tokens), jnp.float32)],
        compiler_params=params(32 if tokens <= 256 else 48),
        cost_estimate=pl.CostEstimate(
            flops=2 * tokens * hidden * grad_basis.shape[0],
            bytes_accessed=4 * image.size,
            transcendentals=0,
        ),
    )(*grad_pieces, *grad_pieces, grad_basis, image)


def per_device(
    train_act, train_grad, seq_ids, act_basis, grad_basis, eigenvalues, query_factors, owners
):
    wide_count = lax.axis_size("wide")
    along_z = range(wide_count // 4)
    tok_local = train_act.shape[0]
    seq_count = tok_local * wide_count // SEQ_MEAN
    cols = grad_basis.shape[1]
    hidden = train_grad.shape[1]
    batch_count = owners.shape[0]

    half = (query_factors.shape[2] - hidden) // 2
    order = [4 * k + r for r in (0, 2, 1, 3) for k in along_z]
    keep, give = cut_factors(query_factors, order, hidden, batch_count)
    flags = owner_flags(owners, keep)
    grads_sent = grads_core(seq_ids, train_grad, keep)
    keep, give = pick(flags, keep, swap(give, "wide", 1), 0, cols, half, [grads_sent])
    grads_got = swap(grads_sent, "wide", 1)
    grads_over = grads_y(train_grad, grads_sent, grads_got, give)
    parts = pick(flags, keep, swap(give, "wide", 2), 1, cols, half, [grads_over])
    grads_over = swap(grads_over, "wide", 2)
    sent = grads_z(train_grad, grads_sent, grads_got, grads_over, wide_count)
    acts = join([train_act] + [swap(train_act, "wide", 4 * k) for k in along_z if k], parts[0])
    ranks = [4 * k for k in along_z]
    over = swap(acts, "wide", 2)
    first = rotate([acts], act_basis, parts[0])
    parts = [swap(parts[k], "wide", 4 * k) if k else parts[0] for k in along_z]
    held = pick_one(flags, parts, [over, first, sent[0]])

    over = gate(over, [held])
    rot = rotate([over, swap(gate(acts, [held]), "wide", 1), swap(over, "wide", 1)], act_basis, None, first)
    ranks = [r + more for more in (0, 2, 1, 3) for r in ranks]
    lefts = [held, gate(swap(held, "groups", 1), [rot])]
    halves = []
    for x in lefts:
        halves += [x, swap(x, "wide", 1)]
    grads = [swap(sent[k], "wide", 4 * k) if k else sent[0] for k in along_z]

    image = images(rot, lefts, halves, eigenvalues)
    parts = score_parts(grads, ranks, grad_basis, image, seq_count)
    parts = parts + sum(swap(parts, "wide", r) for r in (3, 2, 1))
    bit = 4
    while bit < wide_count:
        parts = parts + swap(parts, "wide", bit)
        bit *= 2
    return parts[:, :, 0].T


def solution(mesh):
    return jax.shard_map(
        per_device,
        mesh=mesh,
        in_specs=(
            P(("groups", "wide"), None),
            P(("groups", "wide"), None),
            P(("groups", "wide")),
            P(),
            P(None, "wide"),
            P("wide", None),
            P("wide", None, None),
            P(),
        ),
        out_specs=P("groups", None),
        check_vma=False,
    )
```

```python
import functools
import math

import jax
import jax.numpy as jnp
from jax import lax
from jax.experimental import pallas as pl
from jax.experimental.pallas import tpu as pltpu
from jax.sharding import PartitionSpec as P

D = 4096
FF = 32768
SEQ_MEAN = 32
QT = 16
LANES = 128
SCORE_SCALE = 1.0 / math.sqrt(FF * D * QT * SEQ_MEAN)


damping = 0.1


def params(mib):
    return pltpu.CompilerParams(vmem_limit_bytes=mib * 1024 * 1024)


def whole_block(shape):
    return pl.BlockSpec(shape, lambda *_: (0,) * len(shape), pipeline_mode=pl.Buffered(1))


def swap(x, axis, bit):
    count = lax.axis_size(axis)
    return lax.ppermute(x, axis, [(i, i ^ bit) for i in range(count)])


def in_smem(n):
    return [pl.BlockSpec(memory_space=pltpu.SMEM)] * n


def in_vmem(n):
    return [pl.BlockSpec(memory_space=pltpu.VMEM)] * n


def in_place(n):
    return [pl.BlockSpec(memory_space=pl.ANY)] * n


def cut_factors_kernel(order, hidden, batch_count, fac_ref, keep_ref, give_ref):
    cols = hidden // len(order)
    half = (fac_ref.shape[2] - hidden) // 2
    me, batch = lax.axis_index("wide"), lax.rem(lax.axis_index("groups"), batch_count)
    for part, out_ref in enumerate((keep_ref, give_ref)):
        picked = order[part * len(order) // 2:(part + 1) * len(order) // 2]
        for at, r in enumerate(picked):
            src = pl.multiple_of((me ^ r) * cols, cols)
            out_ref[:, at * cols:(at + 1) * cols] = fac_ref[batch, :, pl.ds(src, cols)]
        src = pl.multiple_of(hidden + ((me & 1) ^ part) * half, LANES)
        out_ref[:, len(picked) * cols:] = fac_ref[batch, :, pl.ds(src, half)]


def cut_factors(factors, order, hidden, batch_count):
    rows, width = factors.shape[1:]
    half = jax.ShapeDtypeStruct((rows, width // 2), factors.dtype)
    return pl.pallas_call(
        functools.partial(cut_factors_kernel, order, hidden, batch_count),
        in_specs=in_vmem(1),
        out_specs=in_vmem(2),
        out_shape=[half] * 2,
        compiler_params=params(16),
        cost_estimate=pl.CostEstimate(flops=0, bytes_accessed=1, transcendentals=0),
    )(factors)


def pick_kernel(step, cols, half, flag_ref, keep_ref, got_ref, *refs):
    out_refs = refs[-2:] if step == 0 else refs[-((keep_ref.shape[1] - half) // cols):]
    same = flag_ref[:, step:step + 1]
    differs = 1 - same

    def chosen(at, size):
        place = slice(at, at + size)
        return keep_ref[:, place] * same + got_ref[:, place] * differs

    size = out_refs[0].shape[1] - half
    shared = chosen(len(out_refs) * size, half)
    for n, out_ref in enumerate(out_refs):
        out_ref[:, :size] = chosen(n * size, size)
        out_ref[:, size:] = shared


def pick(flags, keep, got, step, cols, half, after):
    rows, width = keep.shape
    parts = 2 if step == 0 else (width - half) // cols
    size = (width - half) // parts + half
    return pl.pallas_call(
        functools.partial(pick_kernel, step, cols, half),
        in_specs=in_vmem(3) + in_place(len(after)),
        out_specs=in_vmem(parts),
        out_shape=[jax.ShapeDtypeStruct((rows, size), keep.dtype)] * parts,
        compiler_params=params(16),
        cost_estimate=pl.CostEstimate(flops=0, bytes_accessed=1, transcendentals=0),
    )(flags, keep, got, *after)


def pick_one_kernel(count, flag_ref, *refs):
    refs[-1][...] = sum(refs[k][...] * flag_ref[:, 2 + k:3 + k] for k in range(count))


def pick_one(flags, pieces, after):
    return pl.pallas_call(
        functools.partial(pick_one_kernel, len(pieces)),
        in_specs=in_vmem(1 + len(pieces)) + in_place(len(after)),
        out_specs=in_vmem(1)[0],
        out_shape=jax.ShapeDtypeStruct(pieces[0].shape, pieces[0].dtype),
        compiler_params=params(16),
        cost_estimate=pl.CostEstimate(flops=0, bytes_accessed=1, transcendentals=0),
    )(flags, *pieces, *after)


def join_kernel(*refs):
    out_ref = refs[-1]
    rows = refs[0].shape[0]
    for n, ref in enumerate(refs[:-2]):
        out_ref[n * rows:(n + 1) * rows, :] = ref[...]


def join(pieces, after):
    rows, width = pieces[0].shape
    return pl.pallas_call(
        join_kernel,
        in_specs=in_vmem(len(pieces)) + in_place(1),
        out_specs=in_vmem(1)[0],
        out_shape=jax.ShapeDtypeStruct((len(pieces) * rows, width), pieces[0].dtype),
        compiler_params=params(16),
        cost_estimate=pl.CostEstimate(flops=0, bytes_accessed=1, transcendentals=0),
    )(*pieces, after)


def gate_kernel(*_):
    pass


def gate(array, after):
    return pl.pallas_call(
        gate_kernel,
        in_specs=in_place(1 + len(after)),
        out_specs=in_place(1)[0],
        out_shape=jax.ShapeDtypeStruct(array.shape, array.dtype),
        input_output_aliases={0: 0},
        compiler_params=params(1),
        cost_estimate=pl.CostEstimate(flops=0, bytes_accessed=1, transcendentals=0),
    )(array, *after)


def grads_core_kernel(batch_count, owners_ref, ids_ref, grad_ref, _, flag_ref, out_ref):
    rows, hidden = grad_ref.shape
    wide = lax.axis_size("wide")
    cols = hidden // wide
    me, batch = lax.axis_index("wide"), lax.rem(lax.axis_index("groups"), batch_count)
    apart = owners_ref[batch] ^ me
    lane = lax.broadcasted_iota(jnp.int32, flag_ref.shape, 1)
    flags = jnp.where(lane - 2 == apart // 4, 1.0, 0.0)
    for step in range(2):
        same = jnp.where((apart & (1 << step)) == 0, 1.0, 0.0)
        flags = jnp.where(lane == step, same, flags)
    flag_ref[...] = flags.astype(flag_ref.dtype)
    row = lax.broadcasted_iota(jnp.int32, (rows, LANES), 0)
    ids = jnp.zeros((rows, LANES), jnp.int32)
    for t in range(rows):
        ids = jnp.where(row == t, ids_ref[t], ids)
    out_ref[:, wide // 2 * cols:] = ids.astype(jnp.float32).astype(out_ref.dtype)
    for q in range(wide // 2):
        src = pl.multiple_of((me ^ (2 * q + 1)) * cols, cols)
        out_ref[:, q * cols:(q + 1) * cols] = grad_ref[:, pl.ds(src, cols)]


def grads_core(owners, ids, grads, after):
    rows, hidden = grads.shape
    return pl.pallas_call(
        functools.partial(grads_core_kernel, owners.shape[0]),
        in_specs=in_smem(2) + in_vmem(1) + in_place(1),
        out_specs=in_vmem(2),
        out_shape=[
            jax.ShapeDtypeStruct((QT, LANES), grads.dtype),
            jax.ShapeDtypeStruct((rows, hidden // 2 + LANES), grads.dtype),
        ],
        compiler_params=params(16),
        cost_estimate=pl.CostEstimate(flops=0, bytes_accessed=1, transcendentals=0),
    )(owners, ids, grads, after)


def grads_y_kernel(grad_ref, sent_ref, got_ref, _, out_ref):
    rows, hidden = grad_ref.shape
    wide = lax.axis_size("wide")
    cols = hidden // wide
    me = lax.axis_index("wide")
    for k in range(wide // 4):
        src = pl.multiple_of((me ^ (4 * k + 2)) * cols, cols)
        place = slice(k * cols, (k + 1) * cols)
        out_ref[:rows, place] = grad_ref[:, pl.ds(src, cols)]
        out_ref[rows:, place] = got_ref[:, (2 * k + 1) * cols:(2 * k + 2) * cols]
    ids = slice(wide // 4 * cols, wide // 4 * cols + LANES)
    out_ref[:rows, ids] = sent_ref[:, wide // 2 * cols:]
    out_ref[rows:, ids] = got_ref[:, wide // 2 * cols:]


def grads_y(grads, sent, got, after):
    rows, hidden = grads.shape
    return pl.pallas_call(
        grads_y_kernel,
        in_specs=in_vmem(3) + in_place(1),
        out_specs=in_vmem(1)[0],
        out_shape=jax.ShapeDtypeStruct((2 * rows, hidden // 4 + LANES), grads.dtype),
        compiler_params=params(16),
        cost_estimate=pl.CostEstimate(flops=0, bytes_accessed=1, transcendentals=0),
    )(grads, sent, got, after)


def grads_z_kernel(grad_ref, sent_ref, got_ref, over_ref, *out_refs):
    rows = grad_ref.shape[0]
    cols = out_refs[0].shape[1] - LANES
    me = lax.axis_index("wide")
    for k, out_ref in enumerate(out_refs):
        src = pl.multiple_of((me ^ (4 * k)) * cols, cols)
        out_ref[:rows, :cols] = grad_ref[:, pl.ds(src, cols)]
        out_ref[rows:2 * rows, :cols] = got_ref[:, 2 * k * cols:(2 * k + 1) * cols]
        out_ref[2 * rows:, :cols] = over_ref[:, k * cols:(k + 1) * cols]
        out_ref[:rows, cols:] = sent_ref[:, 2 * len(out_refs) * cols:]
        out_ref[rows:2 * rows, cols:] = got_ref[:, 2 * len(out_refs) * cols:]
        out_ref[2 * rows:, cols:] = over_ref[:, len(out_refs) * cols:]


def grads_z(grads, sent, got, over, wide_count):
    rows, hidden = grads.shape
    count = wide_count // 4
    piece = jax.ShapeDtypeStruct((4 * rows, hidden // wide_count + LANES), grads.dtype)
    return pl.pallas_call(
        grads_z_kernel,
        in_specs=in_vmem(4),
        out_specs=in_vmem(count),
        out_shape=[piece] * count,
        compiler_params=params(16),
        cost_estimate=pl.CostEstimate(flops=0, bytes_accessed=1, transcendentals=0),
    )(grads, sent, got, over)


def rotate_kernel(act_count, done, *refs):
    act_refs, basis_ref, out_ref = refs[:act_count], refs[act_count], refs[-1]
    depth, width = basis_ref.shape
    if done:
        out_ref[:, :done] = refs[act_count + 1][...]
    for k in range(width // depth):
        cols = slice(k * depth, (k + 1) * depth)
        act = jnp.concatenate([ref[:, cols] for ref in act_refs], axis=0)
        turned = jnp.dot(act, basis_ref[:, cols], preferred_element_type=jnp.float32)
        out_ref[cols, done:] = turned.astype(jnp.bfloat16).T


def rotate(act_pieces, basis, after, first=None):
    width = basis.shape[1]
    done = 0 if first is None else first.shape[1]
    tokens = done + sum(x.shape[0] for x in act_pieces)
    more = [after] if first is None else [first]
    return pl.pallas_call(
        functools.partial(rotate_kernel, len(act_pieces), done),
        in_specs=in_vmem(len(act_pieces) + 1) + (in_place(1) if first is None else in_vmem(1)),
        out_specs=in_vmem(1)[0],
        out_shape=jax.ShapeDtypeStruct((width, tokens), jnp.bfloat16),
        compiler_params=params(16 if tokens <= 256 else 32),
        cost_estimate=pl.CostEstimate(flops=0, bytes_accessed=1, transcendentals=0),
    )(*act_pieces, basis, *more)


def image_kernel(batch_count, total, per, rot_ref, *refs):
    left_refs, half_refs = refs[:batch_count], refs[batch_count:3 * batch_count]
    eig_ref, out_ref, right_ref, turn_ref, pre_a, pre_b = refs[3 * batch_count:]
    rows, chunk = eig_ref.shape
    tile = min(256, chunk)
    s = pl.program_id(0)

    @pl.when(s == 0)
    def _():
        side = right_ref.shape[2] // 2
        for b in range(batch_count):
            for other in range(2):
                at = pl.multiple_of(((lax.axis_index("wide") & 1) ^ other) * side, side)
                ref = half_refs[2 * b + other]
                right_ref[b, :, pl.ds(at, side)] = ref[:, ref.shape[1] - side:]

    @pl.when(jnp.logical_and(lax.rem(s, per) == 0, s < total))
    def _():
        for b in range(batch_count):
            turn_ref[b] = left_refs[b][...].T

    @pl.when(lax.rem(s, per) == 1)
    def _():
        out_ref[...] = jnp.zeros_like(out_ref)

    def produce(pre):
        start = lax.rem(s, per) * chunk
        for at in range(0, chunk, tile):
            cols = pl.ds(pl.multiple_of(start + at, tile), tile)
            damped = eig_ref[:, at:at + tile].astype(jnp.float32) + damping
            inverse = pl.reciprocal(damped, approx=True)
            for b in range(batch_count):
                outer_sum = jnp.dot(
                    turn_ref[b], right_ref[b, :, cols], preferred_element_type=jnp.float32
                )
                pre[b * rows:(b + 1) * rows, at:at + tile] = (
                    outer_sum * inverse
                ).astype(jnp.bfloat16)

    def absorb(pre):
        rot = rot_ref[pl.ds(pl.multiple_of(lax.rem(s - 1, per) * chunk, chunk), chunk), :]
        for b in range(batch_count):
            out_ref[b] += jnp.dot(
                pre[b * rows:(b + 1) * rows, :], rot, preferred_element_type=jnp.float32
            )

    between = jnp.logical_and(s > 0, s < total)
    odd = lax.rem(s, 2) == 1

    @pl.when(s == 0)
    def _():
        produce(pre_a)

    @pl.when(jnp.logical_and(between, odd))
    def _():
        produce(pre_b)
        absorb(pre_a)

    @pl.when(jnp.logical_and(between, jnp.logical_not(odd)))
    def _():
        produce(pre_a)
        absorb(pre_b)

    @pl.when(s == total)
    def _():
        absorb(pre_a if total % 2 else pre_b)


def images(rot, lefts, halves, eigenvalues):
    batch_count, tokens = len(lefts), rot.shape[1]
    hidden, width = eigenvalues.shape
    rows = min(1024, hidden)
    chunk = min(1024, width // 2)
    per = width // chunk
    total = hidden // rows * per
    now = lambda s: jnp.minimum(s, total - 1)
    before = lambda s: jnp.maximum(s - 1, 0)
    return pl.pallas_call(
        functools.partial(image_kernel, batch_count, total, per),
        grid=(total + 1,),
        in_specs=[whole_block(rot.shape)]
        + [pl.BlockSpec((QT, rows), lambda s: (0, now(s) // per)) for _ in lefts]
        + [whole_block(x.shape) for x in halves]
        + [pl.BlockSpec((rows, chunk), lambda s: (now(s) // per, now(s) % per))],
        out_specs=pl.BlockSpec((batch_count, rows, tokens), lambda s: (0, before(s) // per, 0)),
        out_shape=jax.ShapeDtypeStruct((batch_count, hidden, tokens), jnp.float32),
        scratch_shapes=[
            pltpu.VMEM((batch_count, QT, width), jnp.bfloat16),
            pltpu.VMEM((batch_count, rows, QT), jnp.bfloat16),
            pltpu.VMEM((batch_count * rows, chunk), jnp.bfloat16),
            pltpu.VMEM((batch_count * rows, chunk), jnp.bfloat16),
        ],
        compiler_params=params(32 if tokens <= 256 else 48),
        cost_estimate=pl.CostEstimate(flops=10**9, bytes_accessed=1, transcendentals=0),
    )(rot, *lefts, *halves, eigenvalues)


def score_kernel(batch_count, ranks, count, *refs):
    grad_refs, ids_refs = refs[:count], refs[count:2 * count]
    basis_ref, image_ref, out_ref, token_ref = refs[2 * count:]
    step = pl.program_id(0)
    rows = grad_refs[0].shape[0] // 4

    def tokens_of(pieces):
        return jnp.concatenate(
            [pieces[r // 4][r % 4 * rows:(r % 4 + 1) * rows, :] for r in ranks], axis=0
        )

    @pl.when(step == 0)
    def _():
        token_ref[...] = jnp.zeros_like(token_ref)

    turned = jnp.dot(tokens_of(grad_refs), basis_ref[...], preferred_element_type=jnp.float32)
    turned = turned.astype(jnp.bfloat16).T.astype(jnp.float32)
    for b in range(batch_count):
        token_ref[b:b + 1, :] += jnp.sum(image_ref[b] * turned, axis=0, keepdims=True)

    @pl.when(step == pl.num_programs(0) - 1)
    def _():
        ids = tokens_of(ids_refs).astype(jnp.float32)
        seqs = lax.broadcasted_iota(jnp.int32, ids.shape, 1).astype(jnp.float32)
        member = jnp.where(ids == seqs, 1.0, 0.0).T
        own = lax.rem(lax.axis_index("groups"), batch_count)
        for b in range(batch_count):
            sums = jnp.sum(member * token_ref[b:b + 1, :], axis=1, keepdims=True)
            out_ref[lax.rem(own + b, batch_count)] = sums[:out_ref.shape[1], :] * SCORE_SCALE


def score_parts(grad_pieces, ranks, grad_basis, image, seq_count):
    batch_count, hidden, tokens = image.shape
    count = len(grad_pieces)
    rows = grad_pieces[0].shape[0]
    inner = min(grad_basis.shape[0], hidden)
    return pl.pallas_call(
        functools.partial(score_kernel, batch_count, ranks, count),
        grid=(hidden // inner,),
        in_specs=[pl.BlockSpec((rows, inner), lambda i: (0, i))] * count
        + [pl.BlockSpec((rows, LANES), lambda i: (0, hidden // LANES))] * count
        + [
            pl.BlockSpec((grad_basis.shape[0], inner), lambda i: (0, i)),
            pl.BlockSpec((batch_count, inner, tokens), lambda i: (0, i, 0)),
        ],
        out_specs=pl.BlockSpec((batch_count, seq_count, 1), lambda i: (0, 0, 0)),
        out_shape=jax.ShapeDtypeStruct((batch_count, seq_count, 1), jnp.float32),
        scratch_shapes=[pltpu.VMEM((8, tokens), jnp.float32)],
        compiler_params=params(32 if tokens <= 256 else 48),
        cost_estimate=pl.CostEstimate(
            flops=2 * tokens * hidden * grad_basis.shape[0],
            bytes_accessed=4 * image.size,
            transcendentals=0,
        ),
    )(*grad_pieces, *grad_pieces, grad_basis, image)


def per_device(
    train_act, train_grad, seq_ids, act_basis, grad_basis, eigenvalues, query_factors, owners
):
    wide_count = lax.axis_size("wide")
    along_z = range(wide_count // 4)
    tok_local = train_act.shape[0]
    seq_count = tok_local * wide_count // SEQ_MEAN
    cols = grad_basis.shape[1]
    hidden = train_grad.shape[1]
    batch_count = owners.shape[0]

    half = (query_factors.shape[2] - hidden) // 2
    order = [4 * k + r for r in (0, 2, 1, 3) for k in along_z]
    keep, give = cut_factors(query_factors, order, hidden, batch_count)
    flags, grads_sent = grads_core(owners, seq_ids, train_grad, keep)
    keep, give = pick(flags, keep, swap(give, "wide", 1), 0, cols, half, [grads_sent])
    grads_got = swap(grads_sent, "wide", 1)
    grads_over = grads_y(train_grad, grads_sent, grads_got, give)
    parts = pick(flags, keep, swap(give, "wide", 2), 1, cols, half, [grads_over])
    grads_over = swap(grads_over, "wide", 2)
    sent = grads_z(train_grad, grads_sent, grads_got, grads_over, wide_count)
    acts = join([train_act] + [swap(train_act, "wide", 4 * k) for k in along_z if k], parts[0])
    ranks = [4 * k for k in along_z]
    over = swap(acts, "wide", 2)
    first = rotate([acts], act_basis, parts[0])
    parts = [swap(parts[k], "wide", 4 * k) if k else parts[0] for k in along_z]
    held = pick_one(flags, parts, [over, first, sent[0]])

    over = gate(over, [held])
    rot = rotate([over, swap(gate(acts, [held]), "wide", 1), swap(over, "wide", 1)], act_basis, None, first)
    ranks = [r + more for more in (0, 2, 1, 3) for r in ranks]
    lefts = [held, gate(swap(held, "groups", 1), [rot])]
    halves = []
    for x in lefts:
        halves += [x, swap(x, "wide", 1)]
    grads = [swap(sent[k], "wide", 4 * k) if k else sent[0] for k in along_z]

    image = images(rot, lefts, halves, eigenvalues)
    parts = score_parts(grads, ranks, grad_basis, image, seq_count)
    parts = parts + sum(swap(parts, "wide", r) for r in (3, 2, 1))
    bit = 4
    while bit < wide_count:
        parts = parts + swap(parts, "wide", bit)
        bit *= 2
    return parts[:, :, 0].T


def solution(mesh):
    return jax.shard_map(
        per_device,
        mesh=mesh,
        in_specs=(
            P(("groups", "wide"), None),
            P(("groups", "wide"), None),
            P(("groups", "wide")),
            P(),
            P(None, "wide"),
            P("wide", None),
            P("wide", None, None),
            P(),
        ),
        out_specs=P("groups", None),
        check_vma=False,
    )
```

```python
import functools
import math

import jax
import jax.numpy as jnp
from jax import lax
from jax.experimental import pallas as pl
from jax.experimental.pallas import tpu as pltpu
from jax.sharding import PartitionSpec as P

D = 4096
FF = 32768
SEQ_MEAN = 32
QT = 16
LANES = 128
SCORE_SCALE = 1.0 / math.sqrt(FF * D * QT * SEQ_MEAN)


damping = 0.1


def params(mib):
    return pltpu.CompilerParams(vmem_limit_bytes=mib * 1024 * 1024)


def whole_block(shape):
    return pl.BlockSpec(shape, lambda *_: (0,) * len(shape), pipeline_mode=pl.Buffered(1))


def swap(x, axis, bit):
    count = lax.axis_size(axis)
    return lax.ppermute(x, axis, [(i, i ^ bit) for i in range(count)])


def in_smem(n):
    return [pl.BlockSpec(memory_space=pltpu.SMEM)] * n


def in_vmem(n):
    return [pl.BlockSpec(memory_space=pltpu.VMEM)] * n


def in_place(n):
    return [pl.BlockSpec(memory_space=pl.ANY)] * n


def cut_factors_kernel(order, hidden, batch_count, fac_ref, keep_ref, give_ref):
    cols = hidden // len(order)
    half = (fac_ref.shape[2] - hidden) // 2
    me, batch = lax.axis_index("wide"), lax.rem(lax.axis_index("groups"), batch_count)
    for part, out_ref in enumerate((keep_ref, give_ref)):
        picked = order[part * len(order) // 2:(part + 1) * len(order) // 2]
        for at, r in enumerate(picked):
            src = pl.multiple_of((me ^ r) * cols, cols)
            out_ref[:, at * cols:(at + 1) * cols] = fac_ref[batch, :, pl.ds(src, cols)]
        src = pl.multiple_of(hidden + ((me & 1) ^ part) * half, LANES)
        out_ref[:, len(picked) * cols:] = fac_ref[batch, :, pl.ds(src, half)]


def cut_factors(factors, order, hidden, batch_count):
    rows, width = factors.shape[1:]
    half = jax.ShapeDtypeStruct((rows, width // 2), factors.dtype)
    return pl.pallas_call(
        functools.partial(cut_factors_kernel, order, hidden, batch_count),
        in_specs=in_vmem(1),
        out_specs=in_vmem(2),
        out_shape=[half] * 2,
        compiler_params=params(16),
        cost_estimate=pl.CostEstimate(flops=0, bytes_accessed=1, transcendentals=0),
    )(factors)


def flags_kernel(batch_count, owners_ref, _, flag_ref):
    me, batch = lax.axis_index("wide"), lax.rem(lax.axis_index("groups"), batch_count)
    apart = owners_ref[batch] ^ me
    lane = lax.broadcasted_iota(jnp.int32, flag_ref.shape, 1)
    flags = jnp.where(lane - 2 == apart // 4, 1.0, 0.0)
    for step in range(2):
        same = jnp.where((apart & (1 << step)) == 0, 1.0, 0.0)
        flags = jnp.where(lane == step, same, flags)
    flag_ref[...] = flags.astype(flag_ref.dtype)


def owner_flags(owners, after):
    return pl.pallas_call(
        functools.partial(flags_kernel, owners.shape[0]),
        in_specs=in_smem(1) + in_place(1),
        out_specs=in_vmem(1)[0],
        out_shape=jax.ShapeDtypeStruct((after.shape[0], LANES), after.dtype),
        compiler_params=params(16),
        cost_estimate=pl.CostEstimate(flops=0, bytes_accessed=1, transcendentals=0),
    )(owners, after)


def pick_kernel(step, cols, half, flag_ref, keep_ref, got_ref, *refs):
    out_refs = refs[-2:] if step == 0 else refs[-((keep_ref.shape[1] - half) // cols):]
    same = flag_ref[:, step:step + 1]
    differs = 1 - same

    def chosen(at, size):
        place = slice(at, at + size)
        return keep_ref[:, place] * same + got_ref[:, place] * differs

    size = out_refs[0].shape[1] - half
    shared = chosen(len(out_refs) * size, half)
    for n, out_ref in enumerate(out_refs):
        out_ref[:, :size] = chosen(n * size, size)
        out_ref[:, size:] = shared


def pick(flags, keep, got, step, cols, half, after):
    rows, width = keep.shape
    parts = 2 if step == 0 else (width - half) // cols
    size = (width - half) // parts + half
    return pl.pallas_call(
        functools.partial(pick_kernel, step, cols, half),
        in_specs=in_vmem(3) + in_place(len(after)),
        out_specs=in_vmem(parts),
        out_shape=[jax.ShapeDtypeStruct((rows, size), keep.dtype)] * parts,
        compiler_params=params(16),
        cost_estimate=pl.CostEstimate(flops=0, bytes_accessed=1, transcendentals=0),
    )(flags, keep, got, *after)


def pick_one_kernel(count, flag_ref, *refs):
    refs[-1][...] = sum(refs[k][...] * flag_ref[:, 2 + k:3 + k] for k in range(count))


def pick_one(flags, pieces, after):
    return pl.pallas_call(
        functools.partial(pick_one_kernel, len(pieces)),
        in_specs=in_vmem(1 + len(pieces)) + in_place(len(after)),
        out_specs=in_vmem(1)[0],
        out_shape=jax.ShapeDtypeStruct(pieces[0].shape, pieces[0].dtype),
        compiler_params=params(16),
        cost_estimate=pl.CostEstimate(flops=0, bytes_accessed=1, transcendentals=0),
    )(flags, *pieces, *after)


def join_kernel(*refs):
    out_ref = refs[-1]
    rows = refs[0].shape[0]
    for n, ref in enumerate(refs[:-2]):
        out_ref[n * rows:(n + 1) * rows, :] = ref[...]


def join(pieces, after):
    rows, width = pieces[0].shape
    return pl.pallas_call(
        join_kernel,
        in_specs=in_vmem(len(pieces)) + in_place(1),
        out_specs=in_vmem(1)[0],
        out_shape=jax.ShapeDtypeStruct((len(pieces) * rows, width), pieces[0].dtype),
        compiler_params=params(16),
        cost_estimate=pl.CostEstimate(flops=0, bytes_accessed=1, transcendentals=0),
    )(*pieces, after)


def gate_kernel(*_):
    pass


def gate(array, after):
    return pl.pallas_call(
        gate_kernel,
        in_specs=in_place(1 + len(after)),
        out_specs=in_place(1)[0],
        out_shape=jax.ShapeDtypeStruct(array.shape, array.dtype),
        input_output_aliases={0: 0},
        compiler_params=params(1),
        cost_estimate=pl.CostEstimate(flops=0, bytes_accessed=1, transcendentals=0),
    )(array, *after)


def grads_core_kernel(ids_ref, grad_ref, _, out_ref):
    rows, hidden = grad_ref.shape
    wide = lax.axis_size("wide")
    cols = hidden // wide
    me = lax.axis_index("wide")
    row = lax.broadcasted_iota(jnp.int32, (rows, LANES), 0)
    ids = jnp.zeros((rows, LANES), jnp.int32)
    for t in range(rows):
        ids = jnp.where(row == t, ids_ref[t], ids)
    out_ref[:, wide // 2 * cols:] = ids.astype(jnp.float32).astype(out_ref.dtype)
    for q in range(wide // 2):
        src = pl.multiple_of((me ^ (2 * q + 1)) * cols, cols)
        out_ref[:, q * cols:(q + 1) * cols] = grad_ref[:, pl.ds(src, cols)]


def grads_core(ids, grads, after):
    rows, hidden = grads.shape
    return pl.pallas_call(
        grads_core_kernel,
        in_specs=in_smem(1) + in_vmem(1) + in_place(1),
        out_specs=in_vmem(1)[0],
        out_shape=jax.ShapeDtypeStruct((rows, hidden // 2 + LANES), grads.dtype),
        compiler_params=params(16),
        cost_estimate=pl.CostEstimate(flops=0, bytes_accessed=1, transcendentals=0),
    )(ids, grads, after)


def grads_y_kernel(grad_ref, sent_ref, got_ref, _, out_ref):
    rows, hidden = grad_ref.shape
    wide = lax.axis_size("wide")
    cols = hidden // wide
    me = lax.axis_index("wide")
    for k in range(wide // 4):
        src = pl.multiple_of((me ^ (4 * k + 2)) * cols, cols)
        place = slice(k * cols, (k + 1) * cols)
        out_ref[:rows, place] = grad_ref[:, pl.ds(src, cols)]
        out_ref[rows:, place] = got_ref[:, (2 * k + 1) * cols:(2 * k + 2) * cols]
    ids = slice(wide // 4 * cols, wide // 4 * cols + LANES)
    out_ref[:rows, ids] = sent_ref[:, wide // 2 * cols:]
    out_ref[rows:, ids] = got_ref[:, wide // 2 * cols:]


def grads_y(grads, sent, got, after):
    rows, hidden = grads.shape
    return pl.pallas_call(
        grads_y_kernel,
        in_specs=in_vmem(3) + in_place(1),
        out_specs=in_vmem(1)[0],
        out_shape=jax.ShapeDtypeStruct((2 * rows, hidden // 4 + LANES), grads.dtype),
        compiler_params=params(16),
        cost_estimate=pl.CostEstimate(flops=0, bytes_accessed=1, transcendentals=0),
    )(grads, sent, got, after)


def grads_z_kernel(grad_ref, sent_ref, got_ref, over_ref, *out_refs):
    rows = grad_ref.shape[0]
    cols = out_refs[0].shape[1] - LANES
    me = lax.axis_index("wide")
    for k, out_ref in enumerate(out_refs):
        src = pl.multiple_of((me ^ (4 * k)) * cols, cols)
        out_ref[:rows, :cols] = grad_ref[:, pl.ds(src, cols)]
        out_ref[rows:2 * rows, :cols] = got_ref[:, 2 * k * cols:(2 * k + 1) * cols]
        out_ref[2 * rows:, :cols] = over_ref[:, k * cols:(k + 1) * cols]
        out_ref[:rows, cols:] = sent_ref[:, 2 * len(out_refs) * cols:]
        out_ref[rows:2 * rows, cols:] = got_ref[:, 2 * len(out_refs) * cols:]
        out_ref[2 * rows:, cols:] = over_ref[:, len(out_refs) * cols:]


def grads_z(grads, sent, got, over, wide_count):
    rows, hidden = grads.shape
    count = wide_count // 4
    piece = jax.ShapeDtypeStruct((4 * rows, hidden // wide_count + LANES), grads.dtype)
    return pl.pallas_call(
        grads_z_kernel,
        in_specs=in_vmem(4),
        out_specs=in_vmem(count),
        out_shape=[piece] * count,
        compiler_params=params(16),
        cost_estimate=pl.CostEstimate(flops=0, bytes_accessed=1, transcendentals=0),
    )(grads, sent, got, over)


def rotate_kernel(act_count, done, *refs):
    act_refs, basis_ref, out_ref = refs[:act_count], refs[act_count], refs[-1]
    depth, width = basis_ref.shape
    if done:
        out_ref[:, :done] = refs[act_count + 1][...]
    for k in range(width // depth):
        cols = slice(k * depth, (k + 1) * depth)
        act = jnp.concatenate([ref[:, cols] for ref in act_refs], axis=0)
        turned = jnp.dot(act, basis_ref[:, cols], preferred_element_type=jnp.float32)
        out_ref[cols, done:] = turned.astype(jnp.bfloat16).T


def rotate(act_pieces, basis, after, first=None):
    width = basis.shape[1]
    done = 0 if first is None else first.shape[1]
    tokens = done + sum(x.shape[0] for x in act_pieces)
    more = [after] if first is None else [first]
    return pl.pallas_call(
        functools.partial(rotate_kernel, len(act_pieces), done),
        in_specs=in_vmem(len(act_pieces) + 1) + (in_place(1) if first is None else in_vmem(1)),
        out_specs=in_vmem(1)[0],
        out_shape=jax.ShapeDtypeStruct((width, tokens), jnp.bfloat16),
        compiler_params=params(16 if tokens <= 256 else 32),
        cost_estimate=pl.CostEstimate(flops=0, bytes_accessed=1, transcendentals=0),
    )(*act_pieces, basis, *more)


def image_kernel(batch_count, total, per, rot_ref, *refs):
    left_refs, half_refs = refs[:batch_count], refs[batch_count:3 * batch_count]
    eig_ref, out_ref, right_ref, turn_ref, pre_a, pre_b = refs[3 * batch_count:]
    rows, chunk = eig_ref.shape
    tile = min(256, chunk)
    s = pl.program_id(0)

    @pl.when(s == 0)
    def _():
        side = right_ref.shape[2] // 2
        for b in range(batch_count):
            for other in range(2):
                at = pl.multiple_of(((lax.axis_index("wide") & 1) ^ other) * side, side)
                ref = half_refs[2 * b + other]
                right_ref[b, :, pl.ds(at, side)] = ref[:, ref.shape[1] - side:]

    @pl.when(jnp.logical_and(lax.rem(s, per) == 0, s < total))
    def _():
        for b in range(batch_count):
            turn_ref[b] = left_refs[b][...].T

    @pl.when(lax.rem(s, per) == 1)
    def _():
        out_ref[...] = jnp.zeros_like(out_ref)

    def produce(pre):
        start = lax.rem(s, per) * chunk
        for at in range(0, chunk, tile):
            cols = pl.ds(pl.multiple_of(start + at, tile), tile)
            damped = eig_ref[:, at:at + tile].astype(jnp.float32) + damping
            inverse = pl.reciprocal(damped, approx=True)
            for b in range(batch_count):
                outer_sum = jnp.dot(
                    turn_ref[b], right_ref[b, :, cols], preferred_element_type=jnp.float32
                )
                pre[b * rows:(b + 1) * rows, at:at + tile] = (
                    outer_sum * inverse
                ).astype(jnp.bfloat16)

    def absorb(pre):
        rot = rot_ref[pl.ds(pl.multiple_of(lax.rem(s - 1, per) * chunk, chunk), chunk), :]
        for b in range(batch_count):
            out_ref[b] += jnp.dot(
                pre[b * rows:(b + 1) * rows, :], rot, preferred_element_type=jnp.float32
            )

    between = jnp.logical_and(s > 0, s < total)
    odd = lax.rem(s, 2) == 1

    @pl.when(s == 0)
    def _():
        produce(pre_a)

    @pl.when(jnp.logical_and(between, odd))
    def _():
        produce(pre_b)
        absorb(pre_a)

    @pl.when(jnp.logical_and(between, jnp.logical_not(odd)))
    def _():
        produce(pre_a)
        absorb(pre_b)

    @pl.when(s == total)
    def _():
        absorb(pre_a if total % 2 else pre_b)


def images(rot, lefts, halves, eigenvalues):
    batch_count, tokens = len(lefts), rot.shape[1]
    hidden, width = eigenvalues.shape
    rows = min(1024, hidden)
    chunk = min(1024, width // 2)
    per = width // chunk
    total = hidden // rows * per
    now = lambda s: jnp.minimum(s, total - 1)
    before = lambda s: jnp.maximum(s - 1, 0)
    return pl.pallas_call(
        functools.partial(image_kernel, batch_count, total, per),
        grid=(total + 1,),
        in_specs=[whole_block(rot.shape)]
        + [pl.BlockSpec((QT, rows), lambda s: (0, now(s) // per)) for _ in lefts]
        + [whole_block(x.shape) for x in halves]
        + [pl.BlockSpec((rows, chunk), lambda s: (now(s) // per, now(s) % per))],
        out_specs=pl.BlockSpec((batch_count, rows, tokens), lambda s: (0, before(s) // per, 0)),
        out_shape=jax.ShapeDtypeStruct((batch_count, hidden, tokens), jnp.float32),
        scratch_shapes=[
            pltpu.VMEM((batch_count, QT, width), jnp.bfloat16),
            pltpu.VMEM((batch_count, rows, QT), jnp.bfloat16),
            pltpu.VMEM((batch_count * rows, chunk), jnp.bfloat16),
            pltpu.VMEM((batch_count * rows, chunk), jnp.bfloat16),
        ],
        compiler_params=params(32 if tokens <= 256 else 48),
        cost_estimate=pl.CostEstimate(flops=10**9, bytes_accessed=1, transcendentals=0),
    )(rot, *lefts, *halves, eigenvalues)


def score_kernel(batch_count, ranks, count, *refs):
    grad_refs, ids_refs = refs[:count], refs[count:2 * count]
    basis_ref, image_ref, out_ref, token_ref = refs[2 * count:]
    step = pl.program_id(0)
    rows = grad_refs[0].shape[0] // 4

    def tokens_of(pieces):
        return jnp.concatenate(
            [pieces[r // 4][r % 4 * rows:(r % 4 + 1) * rows, :] for r in ranks], axis=0
        )

    @pl.when(step == 0)
    def _():
        token_ref[...] = jnp.zeros_like(token_ref)

    turned = jnp.dot(tokens_of(grad_refs), basis_ref[...], preferred_element_type=jnp.float32)
    turned = turned.astype(jnp.bfloat16).T.astype(jnp.float32)
    for b in range(batch_count):
        token_ref[b:b + 1, :] += jnp.sum(image_ref[b] * turned, axis=0, keepdims=True)

    @pl.when(step == pl.num_programs(0) - 1)
    def _():
        ids = tokens_of(ids_refs).astype(jnp.float32)
        seqs = lax.broadcasted_iota(jnp.int32, ids.shape, 1).astype(jnp.float32)
        member = jnp.where(ids == seqs, 1.0, 0.0).T
        own = lax.rem(lax.axis_index("groups"), batch_count)
        for b in range(batch_count):
            sums = jnp.sum(member * token_ref[b:b + 1, :], axis=1, keepdims=True)
            out_ref[lax.rem(own + b, batch_count)] = sums[:out_ref.shape[1], :] * SCORE_SCALE


def score_parts(grad_pieces, ranks, grad_basis, image, seq_count):
    batch_count, hidden, tokens = image.shape
    count = len(grad_pieces)
    rows = grad_pieces[0].shape[0]
    inner = min(grad_basis.shape[0], hidden)
    return pl.pallas_call(
        functools.partial(score_kernel, batch_count, ranks, count),
        grid=(hidden // inner,),
        in_specs=[pl.BlockSpec((rows, inner), lambda i: (0, i))] * count
        + [pl.BlockSpec((rows, LANES), lambda i: (0, hidden // LANES))] * count
        + [
            pl.BlockSpec((grad_basis.shape[0], inner), lambda i: (0, i)),
            pl.BlockSpec((batch_count, inner, tokens), lambda i: (0, i, 0)),
        ],
        out_specs=pl.BlockSpec((batch_count, seq_count, 1), lambda i: (0, 0, 0)),
        out_shape=jax.ShapeDtypeStruct((batch_count, seq_count, 1), jnp.float32),
        scratch_shapes=[pltpu.VMEM((8, tokens), jnp.float32)],
        compiler_params=params(32 if tokens <= 256 else 48),
        cost_estimate=pl.CostEstimate(
            flops=2 * tokens * hidden * grad_basis.shape[0],
            bytes_accessed=4 * image.size,
            transcendentals=0,
        ),
    )(*grad_pieces, *grad_pieces, grad_basis, image)


def per_device(
    train_act, train_grad, seq_ids, act_basis, grad_basis, eigenvalues, query_factors, owners
):
    wide_count = lax.axis_size("wide")
    along_z = range(wide_count // 4)
    tok_local = train_act.shape[0]
    seq_count = tok_local * wide_count // SEQ_MEAN
    cols = grad_basis.shape[1]
    hidden = train_grad.shape[1]
    batch_count = owners.shape[0]

    half = (query_factors.shape[2] - hidden) // 2
    order = [4 * k + r for r in (0, 2, 1, 3) for k in along_z]
    keep, give = cut_factors(query_factors, order, hidden, batch_count)
    flags = owner_flags(owners, keep)
    grads_sent = grads_core(seq_ids, train_grad, keep)
    keep, give = pick(flags, keep, swap(give, "wide", 1), 0, cols, half, [grads_sent])
    grads_got = swap(grads_sent, "wide", 1)
    grads_over = grads_y(train_grad, grads_sent, grads_got, give)
    parts = pick(flags, keep, swap(give, "wide", 2), 1, cols, half, [grads_over])
    grads_over = swap(grads_over, "wide", 2)
    sent = grads_z(train_grad, grads_sent, grads_got, grads_over, wide_count)
    acts = join([train_act] + [swap(train_act, "wide", 4 * k) for k in along_z if k], parts[0])
    ranks = [4 * k for k in along_z]
    over = swap(acts, "wide", 2)
    first = rotate([acts], act_basis, parts[0])
    parts = [swap(parts[k], "wide", 4 * k) if k else parts[0] for k in along_z]
    held = pick_one(flags, parts, [over, first, sent[0]])

    over = gate(over, [held])
    rot = rotate([over, swap(gate(acts, [held]), "wide", 1), swap(over, "wide", 1)], act_basis, None, first)
    ranks = [r + more for more in (0, 2, 1, 3) for r in ranks]
    lefts = [held, gate(swap(held, "groups", 1), [rot])]
    halves = []
    for x in lefts:
        halves += [x, swap(x, "wide", 1)]
    grads = [swap(sent[k], "wide", 4 * k) if k else sent[0] for k in along_z]

    image = images(rot, lefts, halves, eigenvalues)
    parts = score_parts(grads, ranks, grad_basis, image, seq_count)
    bit = 1
    while bit < wide_count:
        parts = parts + swap(parts, "wide", bit)
        bit *= 2
    return parts[:, :, 0].T


def solution(mesh):
    return jax.shard_map(
        per_device,
        mesh=mesh,
        in_specs=(
            P(("groups", "wide"), None),
            P(("groups", "wide"), None),
            P(("groups", "wide")),
            P(),
            P(None, "wide"),
            P("wide", None),
            P("wide", None, None),
            P(),
        ),
        out_specs=P("groups", None),
        check_vma=False,
    )
```
